128 devices in a mesh: img: 2 (over x_lo), ctx: 16 (over z, y), tp: 4 (over x_hi, core).
Axes of the slice: x: 4 (x_hi: 2, x_lo: 2; x = x_hi * 2 + x_lo), y: 4, z: 4, core: 2. Of those that a mesh axis runs over, the one named last changes fastest.
Arguments:
- features: bfloat16 [1, 32768, 1152], P(None, ('img', 'ctx')), may hold values from -60 to 60
- ln_gain: bfloat16 [1, 4, 1152], replicated, may hold values from 0.099609375 to 1.8984375
- ln_bias: bfloat16 [1, 4, 1152], replicated, may hold values from -3 to 3
- projection: bfloat16 [1, 4, 1152, 4096], P(None, None, 'ctx', 'tp'), may hold values from -0.09375 to 0.09375
- stream: bfloat16 [16384, 4096], P(('img', 'ctx'), 'tp'), may hold values from -12 to 12
- norm_gain: bfloat16 [1, 4096], P(None, 'tp'), may hold values from 0.099609375 to 1.8984375
- cotangent: bfloat16 [1, 16384, 4096], P(None, ('img', 'ctx'), 'tp'), may hold values from -6 to 6
- slots: int32 [8192], P(('img', 'ctx')), may hold values from 0 to 16383, as said below
Outputs:
- new_stream: bfloat16 [16384, 4096], P(('img', 'ctx'), 'tp')
- feature_grad: bfloat16 [1, 32768, 1152], P(None, ('img', 'ctx'))
The draws below stay inside these ranges and needn't reach their ends.
Inputs may be any that keep to these rules, and one draw needn't show every extreme that they name: `slots`: the 8192 positions are distinct. Of the 256 tokens of one device of img+ctx, at most 16 fall into any aligned block of 512 positions, and in every draw one block holds exactly 16 tokens of every device.
All inputs are finite; a program needn't handle non-finite values.
Results may differ from the reference program's by a relative error of at most 0.0049.
Values may be sent and summed in bfloat16 or wider, within the bound.
No kernel may reach another device: no remote copies, remote signals or barrier semaphores. Data moves between devices by JAX's collectives and lax.ppermute only.
A program may use at most 128 MiB of HBM per device.

```python
import math
import jax
import jax.numpy as jnp
from jax import lax

VD = 1152
D = 4096
WIN = 4
DEPTHS = 1
MERGED_DEV = 256
TOK_DEV = 512
PATCHES = 32768
VTOK = 8192
TOKENS = 16384
N_IMG = 2
N_CTX = 16


def draw_features(key, part):
    key = jax.random.fold_in(key, 5)
    base_key, row_key, col_key = jax.random.split(key, 3)
    shape = (DEPTHS, PATCHES, VD)
    base = jnp.clip(jax.random.normal(base_key, shape, jnp.float32), -4.0, 4.0)
    row_scale = jnp.exp(jax.random.uniform(row_key, (DEPTHS, PATCHES, 1), jnp.float32, 0.0, math.log(10.0)))
    ramp = jnp.exp(math.log(3.0) * jnp.arange(VD, dtype=jnp.float32) / VD)
    col_scale = ramp[None, None, :] * jnp.exp(jax.random.uniform(col_key, (DEPTHS, 1, VD), jnp.float32, -0.3, 0.3))
    return jnp.clip(base * row_scale * col_scale, -60.0, 60.0).astype(jnp.bfloat16)


def draw_stream(key, part):
    key = jax.random.fold_in(key, 7)
    base_key, col_key = jax.random.split(key, 2)
    shape = (TOKENS, D)
    base = jnp.clip(jax.random.normal(base_key, shape, jnp.float32), -4.0, 4.0)
    ramp = jnp.exp(math.log(3.0) * jnp.arange(D, dtype=jnp.float32) / D)
    col_scale = ramp[None, :] * jnp.exp(jax.random.uniform(col_key, (1, D), jnp.float32, -0.3, 0.3))
    return jnp.clip(base * col_scale, -12.0, 12.0).astype(jnp.bfloat16)


def draw_slots(key, part):
    key = jax.random.fold_in(key, 11)
    owners = N_IMG * N_CTX
    capacity = 2 * MERGED_DEV // owners
    table_key, route_key, pick_key = jax.random.split(key, 3)
    scores = jax.random.randint(table_key, (owners, TOK_DEV), 0, 2 ** 18) * TOK_DEV + jnp.arange(TOK_DEV)[None, :]
    orders = jnp.argsort(scores, axis=1)
    chosen = jax.random.randint(pick_key, (), 0, owners)
    slot_range = jnp.arange(owners * capacity)

    def one_device(device_key, device_index):
        slot_ids = jax.random.permutation(device_key, owners * capacity)
        priority = jnp.where(slot_ids // capacity == chosen, slot_range - owners * capacity, slot_range)
        ordered = slot_ids[jnp.argsort(priority)]
        taken = ordered[:MERGED_DEV]
        owner_ids = taken // capacity
        within = taken % capacity
        offsets = orders[owner_ids, device_index * capacity + within]
        return owner_ids * TOK_DEV + offsets
    device_keys = jax.random.split(route_key, owners)
    return jax.vmap(one_device)(device_keys, jnp.arange(owners)).reshape(-1).astype(jnp.int32)


def block_scale(stream_key, dims, cuts, least, top_value):
    level, own = 1.0, jax.random.fold_in(stream_key, 6)
    for dim, blocks in cuts:
        draws = jnp.exp(jax.random.uniform(jax.random.fold_in(own, dim), (blocks,), jnp.float32, least / len(cuts), top_value / len(cuts)))
        level = level * jnp.repeat(draws, dims[dim] // blocks).reshape([-1 if axis == dim else 1 for axis in range(len(dims))])
    return level


def gaussian(key, extent, width, limit, shards=(), kind=jnp.bfloat16):
    drawn = width * jax.random.normal(key, extent, jnp.float32)
    if shards:
        drawn = drawn * block_scale(key, extent, shards, -0.22, 0.18)
    return jnp.clip(drawn, -limit, limit).astype(kind)


def setup_inputs(seed: int = 0) -> dict:
    key_list = jax.random.split(jax.random.key(seed), 9)
    return {
        "features": draw_features(jax.random.fold_in(key_list[8], 71), 0),
        "ln_gain": jnp.clip(1.0 + 0.18 * jax.random.normal(key_list[1], (DEPTHS, WIN, VD), jnp.float32), 0.099609375, 1.8984375).astype(jnp.bfloat16),
        "ln_bias": gaussian(key_list[2], (DEPTHS, WIN, VD), 0.5, 3.0),
        "projection": gaussian(key_list[3], (DEPTHS, WIN, VD, D), (WIN * VD) ** -0.5, 0.09375, ((2, 16), (3, 4))),
        "stream": draw_stream(jax.random.fold_in(key_list[8], 71), 0),
        "norm_gain": jnp.clip(1.0 + 0.18 * jax.random.normal(key_list[5], (DEPTHS, D), jnp.float32), 0.099609375, 1.8984375).astype(jnp.bfloat16),
        "cotangent": gaussian(key_list[6], (DEPTHS, TOKENS, D), 1.0, 6.0, ((1, 32), (2, 4))),
        "slots": draw_slots(jax.random.fold_in(key_list[8], 71), 0),
    }


def layer_norm_rows(windows):
    row_mean = lax.optimization_barrier(jnp.mean(windows, axis=1, keepdims=True))
    square_mean = lax.optimization_barrier(jnp.mean(windows * windows, axis=1, keepdims=True))
    inv_std = lax.rsqrt(square_mean - row_mean * row_mean + 1e-05)
    return ((windows - row_mean) * inv_std, inv_std)

def reference(features, ln_gain, ln_bias, projection, stream, norm_gain, cotangent, slots):
    current = stream.astype(jnp.float32)
    history = []
    for depth_index in range(DEPTHS):
        windows = features[depth_index].astype(jnp.float32).reshape(VTOK, WIN * VD)
        normed, inv_std = layer_norm_rows(windows)
        gain_row = ln_gain[depth_index].astype(jnp.float32).reshape(1, WIN * VD)
        bias_row = ln_bias[depth_index].astype(jnp.float32).reshape(1, WIN * VD)
        lifted = (normed * gain_row + bias_row).astype(jnp.bfloat16)
        weights = projection[depth_index].reshape(WIN * VD, D)
        visual = jnp.dot(lifted, weights, preferred_element_type=jnp.float32).astype(jnp.bfloat16)
        current = current.at[slots].add(visual.astype(jnp.float32))
        history.append((current, normed, inv_std))
    new_stream = current.astype(jnp.bfloat16)
    stream_grad = jnp.zeros((TOKENS, D), jnp.float32)
    grads = [None] * DEPTHS
    for depth_index in reversed(range(DEPTHS)):
        current, normed, inv_std = history[depth_index]
        upstream = norm_gain[depth_index].astype(jnp.float32)[None, :] * cotangent[depth_index].astype(jnp.float32)
        inv_rms = lax.rsqrt(lax.optimization_barrier(jnp.mean(current * current, axis=1, keepdims=True)) + 1e-06)
        inner = lax.optimization_barrier(jnp.mean(upstream * current, axis=1, keepdims=True))
        stream_grad = stream_grad + inv_rms * upstream - current * (inv_rms * inv_rms * inv_rms * inner)
        picked = stream_grad[slots].astype(jnp.bfloat16)
        weights = projection[depth_index].reshape(WIN * VD, D)
        lifted_grad = jnp.dot(picked, weights.T, preferred_element_type=jnp.float32)
        gain_row = ln_gain[depth_index].astype(jnp.float32).reshape(1, WIN * VD)
        scaled = lifted_grad * gain_row
        centered = scaled - lax.optimization_barrier(jnp.mean(scaled, axis=1, keepdims=True)) - normed * lax.optimization_barrier(jnp.mean(scaled * normed, axis=1, keepdims=True))
        grads[depth_index] = (inv_std * centered).reshape(PATCHES, VD).astype(jnp.bfloat16)
    return (new_stream, jnp.stack(grads))
```

```python
import jax
import jax.numpy as jnp
from jax import lax
from jax.experimental import pallas as pl
from jax.experimental.pallas import tpu as pltpu
from jax.sharding import PartitionSpec as P

BF = jnp.bfloat16
F32 = jnp.float32
VMEM_LIMIT = 48 * 1024 * 1024
VMEM = pltpu.VMEM
SMEM = pltpu.SMEM


def params():
    return pltpu.CompilerParams(vmem_limit_bytes=VMEM_LIMIT)


def whole():
    return pl.BlockSpec(memory_space=VMEM)


def cost(flops, moved):
    return pl.CostEstimate(flops=flops, bytes_accessed=moved, transcendentals=0)


def eq_hot(shape, dim, index):
    return (lax.broadcasted_iota(jnp.int32, shape, dim) == index).astype(BF)


def window_major(tokens, window):
    n = tokens * window
    row = lax.broadcasted_iota(jnp.int32, (n, n), 0)
    col = lax.broadcasted_iota(jnp.int32, (n, n), 1)
    return (col == (row % tokens) * window + row // tokens).astype(BF)


def patch_major(tokens, window):
    n = tokens * window
    row = lax.broadcasted_iota(jnp.int32, (n, n), 0)
    col = lax.broadcasted_iota(jnp.int32, (n, n), 1)
    return (col == (row % window) * tokens + row // window).astype(BF)


def norm_kernel(x_ref, gain_ref, bias_ref, lifted_ref, xw_ref, stat_ref):
    window = gain_ref.shape[0]
    tokens = x_ref.shape[0] // window
    full = window * x_ref.shape[1]
    x = jnp.dot(
        window_major(tokens, window), x_ref[...], preferred_element_type=F32
    )
    parts = [x[w * tokens : (w + 1) * tokens] for w in range(window)]
    total = sum(jnp.sum(p, axis=1, keepdims=True) for p in parts)
    squares = sum(jnp.sum(p * p, axis=1, keepdims=True) for p in parts)
    mean = total / full
    inv = lax.rsqrt(squares / full - mean * mean + 1e-05)
    for w, p in enumerate(parts):
        normed = (p - mean) * inv
        lifted_ref[w] = (
            normed * gain_ref[w : w + 1].astype(F32) + bias_ref[w : w + 1].astype(F32)
        ).astype(BF)
        xw_ref[w] = p.astype(BF)
    lane = lax.broadcasted_iota(jnp.int32, stat_ref.shape, 1)
    stat_ref[...] = jnp.where(lane == 0, mean, inv)


def layer_norm(features, gain, bias):
    rows, width = features.shape
    window = gain.shape[0]
    merged = rows // window
    block = 64
    return pl.pallas_call(
        norm_kernel,
        grid=(merged // block,),
        in_specs=[
            pl.BlockSpec((block * window, width), lambda i: (i, 0)),
            pl.BlockSpec((window, width), lambda i: (0, 0)),
            pl.BlockSpec((window, width), lambda i: (0, 0)),
        ],
        out_specs=[
            pl.BlockSpec((window, block, width), lambda i: (0, i, 0)),
            pl.BlockSpec((window, block, width), lambda i: (0, i, 0)),
            pl.BlockSpec((block, 128), lambda i: (i, 0)),
        ],
        out_shape=[
            jax.ShapeDtypeStruct((window, merged, width), BF),
            jax.ShapeDtypeStruct((window, merged, width), BF),
            jax.ShapeDtypeStruct((merged, 128), F32),
        ],
        compiler_params=params(),
        cost_estimate=cost(2 * rows * block * window * width, 6 * rows * width),
        name="layer_norm",
    )(features, gain, bias)


def collect_kernel(pos_ref, stream_ref, cot_ref, out_ref):
    slots = pos_ref.shape[0]
    rows, width = stream_ref.shape
    pick = eq_hot((slots, rows), 1, pos_ref[...])
    out_ref[:, :width] = jnp.dot(pick, stream_ref[...], preferred_element_type=F32).astype(BF)
    out_ref[:, width:] = jnp.dot(pick, cot_ref[...], preferred_element_type=F32).astype(BF)


def collect(pos, stream, cot):
    slots = pos.shape[0]
    rows, width = stream.shape
    return pl.pallas_call(
        collect_kernel,
        in_specs=[whole()] * 3,
        out_specs=whole(),
        out_shape=jax.ShapeDtypeStruct((slots, 2 * width), BF),
        compiler_params=params(),
        cost_estimate=cost(4 * slots * rows * width, 8 * rows * width),
        name="collect",
    )(pos, stream, cot)


def forward_kernel(lifted_ref, w_ref, row_ref, came_ref, ngain_ref,
                   state_ref, up_ref, send_ref, stat_ref, acc_ref):
    step = pl.program_id(0) * pl.num_programs(1) + pl.program_id(1)
    last = pl.num_programs(0) * pl.num_programs(1) - 1
    part = jnp.dot(lifted_ref[0], w_ref[0], preferred_element_type=F32)

    @pl.when(step == 0)
    def _():
        acc_ref[...] = part

    @pl.when(step > 0)
    def _():
        acc_ref[...] += part

    @pl.when(step == last)
    def _():
        slots = came_ref.shape[0]
        tokens, width = acc_ref.shape
        pack = eq_hot((slots, tokens), 0, row_ref[...])
        visual = acc_ref[...].astype(BF)
        send_ref[...] = jnp.dot(pack, visual, preferred_element_type=F32).astype(BF)
        held = lax.dot_general(
            pack, came_ref[...], (((0,), (0,)), ((), ())), preferred_element_type=F32
        )
        state = held[:, :width] + visual.astype(F32)
        up = held[:, width:] * ngain_ref[...].astype(F32)
        state_ref[...] = state
        up_ref[...] = up
        lane = lax.broadcasted_iota(jnp.int32, stat_ref.shape, 1)
        stat_ref[...] = jnp.where(
            lane == 0,
            jnp.sum(state * state, axis=1, keepdims=True),
            jnp.sum(up * state, axis=1, keepdims=True),
        )


def forward(lifted, weight, slot_row, came, ngain):
    window, tokens, depth = lifted.shape
    width = weight.shape[2]
    slots = came.shape[0]
    block = 384
    return pl.pallas_call(
        forward_kernel,
        grid=(window, depth // block),
        in_specs=[
            pl.BlockSpec((1, tokens, block), lambda w, k: (w, 0, k)),
            pl.BlockSpec((1, block, width), lambda w, k: (w, k, 0)),
            pl.BlockSpec((1, tokens), lambda w, k: (0, 0)),
            pl.BlockSpec((slots, 2 * width), lambda w, k: (0, 0)),
            pl.BlockSpec((1, width), lambda w, k: (0, 0)),
        ],
        out_specs=[
            pl.BlockSpec((tokens, width), lambda w, k: (0, 0)),
            pl.BlockSpec((tokens, width), lambda w, k: (0, 0)),
            pl.BlockSpec((slots, width), lambda w, k: (0, 0)),
            pl.BlockSpec((tokens, 128), lambda w, k: (0, 0)),
        ],
        out_shape=[
            jax.ShapeDtypeStruct((tokens, width), F32),
            jax.ShapeDtypeStruct((tokens, width), F32),
            jax.ShapeDtypeStruct((slots, width), BF),
            jax.ShapeDtypeStruct((tokens, 128), F32),
        ],
        scratch_shapes=[pltpu.VMEM((tokens, width), F32)],
        compiler_params=params(),
        cost_estimate=cost(2 * window * depth * tokens * width, 2 * window * depth * width),
        name="forward",
    )(lifted, weight, slot_row, came, ngain)


def backward_kernel(full_width, chunk, rows, core_ref, state_ref, up_ref, stat_a_ref, stat_b_ref, w_ref,
                    mine_ref, other_ref, picked_ref):
    step = pl.program_id(0) * pl.num_programs(1) + pl.program_id(1)
    tokens = state_ref.shape[0]
    half = tokens // 2

    @pl.when(step == 0)
    def _():
        core = core_ref[0]
        for place, owner in enumerate((core, 1 - core)):
            start = pl.multiple_of(owner * half + chunk * rows, rows)
            at = pl.ds(start, rows)
            sums = stat_a_ref[at, :] + stat_b_ref[at, :]
            inv = lax.rsqrt(sums[:, 0:1] / full_width + 1e-06)
            inner = sums[:, 1:2] / full_width
            grad = inv * up_ref[at, :] - state_ref[at, :] * (inv * inv * inv * inner)
            picked_ref[place * rows : (place + 1) * rows, :] = grad.astype(BF)

    both = lax.dot_general(
        picked_ref[...], w_ref[0], (((1,), (1,)), ((), ())), preferred_element_type=F32
    )
    mine_ref[0] = both[:rows]
    other_ref[0] = both[rows:].astype(BF)


def backward(core, state, up, stat_a, stat_b, weight, chunk, rows, full_width):
    window, depth, width = weight.shape
    tokens = state.shape[0]
    block = 384
    fixed = lambda w, k: (0, 0)
    return pl.pallas_call(
        lambda *refs: backward_kernel(full_width, chunk, rows, *refs),
        grid=(window, depth // block),
        in_specs=[
            pl.BlockSpec(memory_space=SMEM),
            pl.BlockSpec((tokens, width), fixed),
            pl.BlockSpec((tokens, width), fixed),
            pl.BlockSpec((tokens, 128), fixed),
            pl.BlockSpec((tokens, 128), fixed),
            pl.BlockSpec((1, block, width), lambda w, k: (w, k, 0)),
        ],
        out_specs=[
            pl.BlockSpec((1, rows, block), lambda w, k: (w, 0, k)),
            pl.BlockSpec((1, rows, block), lambda w, k: (w, 0, k)),
        ],
        out_shape=[
            jax.ShapeDtypeStruct((window, rows, depth), F32),
            jax.ShapeDtypeStruct((window, rows, depth), BF),
        ],
        scratch_shapes=[pltpu.VMEM((2 * rows, width), BF)],
        compiler_params=params(),
        cost_estimate=cost(4 * window * depth * rows * width, 2 * window * depth * width),
        name="backward",
    )(core, state, up, stat_a, stat_b, weight)


def finish_kernel(block_ref, own_ref, far_ref, xw_ref, stat_ref, gain_ref, out_ref):
    window, tokens, width = own_ref.shape
    full = window * width
    mean = stat_ref[:, 0:1]
    inv = stat_ref[:, 1:2]
    scaled = []
    total = 0.0
    inner = 0.0
    for w in range(window):
        g = (own_ref[w].astype(F32) + far_ref[w].astype(F32)) * gain_ref[w : w + 1].astype(F32)
        normed = (xw_ref[w].astype(F32) - mean) * inv
        total = total + jnp.sum(g, axis=1, keepdims=True)
        inner = inner + jnp.sum(g * normed, axis=1, keepdims=True)
        scaled.append((g, normed))
    total = total / full
    inner = inner / full
    rows = jnp.concatenate(
        [(inv * (g - total - normed * inner)).astype(BF) for g, normed in scaled], axis=0
    )
    out_ref[...] = jnp.dot(
        patch_major(tokens, window), rows, preferred_element_type=F32
    ).astype(BF)


def finish(block, own, far, xw, stat, gain):
    window, tokens, width = own.shape
    return pl.pallas_call(
        finish_kernel,
        grid_spec=pltpu.PrefetchScalarGridSpec(
            num_scalar_prefetch=1,
            grid=(1,),
            in_specs=[
                pl.BlockSpec((window, tokens, width), lambda i, b: (0, 0, 0)),
                pl.BlockSpec((window, tokens, width), lambda i, b: (0, 0, 0)),
                pl.BlockSpec((window, tokens, width), lambda i, b: (0, b[0], 0)),
                pl.BlockSpec((tokens, 128), lambda i, b: (b[0], 0)),
                pl.BlockSpec((window, width), lambda i, b: (0, 0)),
            ],
            out_specs=pl.BlockSpec((tokens * window, width), lambda i, b: (0, 0)),
        ),
        out_shape=jax.ShapeDtypeStruct((tokens * window, width), BF),
        compiler_params=params(),
        cost_estimate=cost(2 * (tokens * window) ** 2 * width, 8 * window * tokens * width),
        name="finish",
    )(block, own, far, xw, stat, gain)


def place_kernel(pos_ref, came_ref, stream_ref, out_ref):
    slots = came_ref.shape[0]
    rows, width = stream_ref.shape
    put = eq_hot((rows, slots), 0, pos_ref[...])
    out_ref[...] = (
        stream_ref[...].astype(F32) + jnp.dot(put, came_ref[...], preferred_element_type=F32)
    ).astype(BF)


def place(pos, came, stream):
    rows, width = stream.shape
    return pl.pallas_call(
        place_kernel,
        in_specs=[whole()] * 3,
        out_specs=whole(),
        out_shape=jax.ShapeDtypeStruct((rows, width), BF),
        compiler_params=params(),
        cost_estimate=cost(2 * came.shape[0] * rows * width, 6 * rows * width),
        name="place",
    )(pos, came, stream)


def shards(features, ln_gain, ln_bias, projection, stream, norm_gain, cotangent, slots):
    n_img = lax.axis_size("img")
    n_ctx = lax.axis_size("ctx")
    n_tp = lax.axis_size("tp")
    merged = slots.shape[0]
    window = ln_gain.shape[1]
    tok_rows, width = stream.shape
    owners = n_img * n_ctx
    capacity = 2 * merged // owners
    slot_count = owners * capacity
    full_width = width * n_tp

    core_pairs = [(t, t ^ 1) for t in range(n_tp)]
    far_pairs = [(t, t ^ 2) for t in range(n_tp)]
    core = lax.axis_index("tp") % 2

    weight = lax.all_gather(projection, "ctx", axis=2, tiled=True)[0]

    target = slots // tok_rows
    ids = jnp.arange(merged)
    earlier = (target[:, None] == target[None, :]) & (ids[:, None] < ids[None, :])
    rank = jnp.sum(earlier.astype(jnp.int32), axis=0)
    slot = target * capacity + rank
    local = slots - target * tok_rows
    packed = jnp.max(
        jnp.where(jnp.arange(slot_count)[:, None] == slot[None, :], local[None, :], -1), axis=1
    )
    asked = lax.all_to_all(
        packed.reshape(owners, capacity), ("img", "ctx"), split_axis=0, concat_axis=0, tiled=True
    )

    held = collect(asked.reshape(slot_count, 1), stream, cotangent[0])
    came = lax.all_to_all(
        held.reshape(owners, capacity, 2 * width),
        ("img", "ctx"), split_axis=0, concat_axis=0, tiled=True,
    ).reshape(slot_count, 2 * width)

    gain = ln_gain[0]
    lifted, xw, stat = layer_norm(features[0], gain, ln_bias[0])

    state, up, send, sums = forward(lifted, weight, slot.reshape(1, merged), came, norm_gain)

    near = sums + lax.ppermute(sums, "tp", core_pairs)
    far = lax.ppermute(near, "tp", far_pairs)

    arrived = lax.all_to_all(
        send.reshape(owners, capacity, width),
        ("img", "ctx"), split_axis=0, concat_axis=0, tiled=True,
    ).reshape(slot_count, width)
    new_stream = place(asked.reshape(1, slot_count), arrived, stream)

    chunks = 2
    rows = merged // 2 // chunks
    core_in = core.reshape(1).astype(jnp.int32)
    own_out, got_out = [], []
    for chunk in range(chunks):
        mine, other = backward(core_in, state, up, near, far, weight, chunk, rows, full_width)
        got = lax.ppermute(other, "tp", core_pairs)
        pair = (mine + got.astype(F32)).astype(BF)
        beyond = lax.ppermute(pair, "tp", far_pairs)
        out = finish((core_in * chunks + chunk), pair, beyond, xw, stat, gain)
        own_out.append(out)
        got_out.append(lax.ppermute(out, "tp", core_pairs))
    first = core == 0
    own = jnp.concatenate(own_out, axis=0)
    got = jnp.concatenate(got_out, axis=0)
    grad = jnp.concatenate([jnp.where(first, own, got), jnp.where(first, got, own)], axis=0)
    return (new_stream, grad[None])


def solution(mesh):
    placed = (
        P(None, ("img", "ctx"), None),
        P(),
        P(),
        P(None, None, "ctx", "tp"),
        P(("img", "ctx"), "tp"),
        P(None, "tp"),
        P(None, ("img", "ctx"), "tp"),
        P(("img", "ctx")),
    )
    return jax.shard_map(
        shards,
        mesh=mesh,
        in_specs=placed,
        out_specs=(P(("img", "ctx"), "tp"), P(None, ("img", "ctx"), None)),
        check_vma=False,
    )
```

```python
import jax
import jax.numpy as jnp
from jax import lax
from jax.experimental import pallas as pl
from jax.experimental.pallas import tpu as pltpu
from jax.sharding import PartitionSpec as P

BF = jnp.bfloat16
F32 = jnp.float32
VMEM = pltpu.VMEM
SMEM = pltpu.SMEM


def params(mib):
    return pltpu.CompilerParams(vmem_limit_bytes=mib * 1024 * 1024)


def whole():
    return pl.BlockSpec(memory_space=VMEM)


def cost(flops, moved):
    return pl.CostEstimate(flops=flops, bytes_accessed=moved, transcendentals=0)


def eq_hot(shape, dim, index):
    return (lax.broadcasted_iota(jnp.int32, shape, dim) == index).astype(BF)


def window_major(tokens, window):
    n = tokens * window
    row = lax.broadcasted_iota(jnp.int32, (n, n), 0)
    col = lax.broadcasted_iota(jnp.int32, (n, n), 1)
    return (col == (row % tokens) * window + row // tokens).astype(BF)


def patch_major(tokens, window):
    n = tokens * window
    row = lax.broadcasted_iota(jnp.int32, (n, n), 0)
    col = lax.broadcasted_iota(jnp.int32, (n, n), 1)
    return (col == (row % window) * tokens + row // window).astype(BF)


SIDE = 4


def piece_slices(window, share):
    half = window // 2
    pieces = []
    for first in range(SIDE):
        pieces.append([(w, (first * SIDE + y) * share) for y in range(SIDE) for w in range(half)])
    for first in range(SIDE):
        pieces.append(
            [(w, (z * SIDE + first) * share) for z in range(SIDE) for w in range(half, window)]
        )
    return pieces


def norm_kernel(x_ref, gain_ref, bias_ref, lifted_ref, xw_ref, stat_ref):
    window, width = gain_ref.shape
    tokens = x_ref.shape[0] // window
    full = window * width
    share = width // (SIDE * SIDE)
    x = jnp.dot(
        window_major(tokens, window), x_ref[...], preferred_element_type=F32
    )
    parts = [x[w * tokens : (w + 1) * tokens] for w in range(window)]
    total = sum(jnp.sum(p, axis=1, keepdims=True) for p in parts)
    squares = sum(jnp.sum(p * p, axis=1, keepdims=True) for p in parts)
    mean = total / full
    inv = lax.rsqrt(squares / full - mean * mean + 1e-05)
    lifted = []
    for w, p in enumerate(parts):
        normed = (p - mean) * inv
        lifted.append(
            normed * gain_ref[w : w + 1].astype(F32) + bias_ref[w : w + 1].astype(F32)
        )
        xw_ref[w] = p.astype(BF)
    for index, piece in enumerate(piece_slices(window, share)):
        lifted_ref[index] = jnp.concatenate(
            [lifted[w][:, at : at + share] for w, at in piece], axis=1
        ).astype(BF)
    lane = lax.broadcasted_iota(jnp.int32, stat_ref.shape, 1)
    stat_ref[...] = jnp.where(lane == 0, mean, inv)


def layer_norm(features, gain, bias):
    rows, width = features.shape
    window = gain.shape[0]
    merged = rows // window
    block = 64
    piece = window * width // (2 * SIDE)
    return pl.pallas_call(
        norm_kernel,
        grid=(merged // block,),
        in_specs=[
            pl.BlockSpec((block * window, width), lambda i: (i, 0)),
            pl.BlockSpec((window, width), lambda i: (0, 0)),
            pl.BlockSpec((window, width), lambda i: (0, 0)),
        ],
        out_specs=[
            pl.BlockSpec((2 * SIDE, block, piece), lambda i: (0, i, 0)),
            pl.BlockSpec((window, block, width), lambda i: (0, i, 0)),
            pl.BlockSpec((block, 128), lambda i: (i, 0)),
        ],
        out_shape=[
            jax.ShapeDtypeStruct((2 * SIDE, merged, piece), BF),
            jax.ShapeDtypeStruct((window, merged, width), BF),
            jax.ShapeDtypeStruct((merged, 128), F32),
        ],
        compiler_params=params(24),
        cost_estimate=cost(2 * rows * block * window * width, 6 * rows * width),
        name="layer_norm",
    )(features, gain, bias)


def collect_kernel(pos_ref, stream_ref, cot_ref, out_ref):
    slots = pos_ref.shape[0]
    rows, width = stream_ref.shape
    pick = eq_hot((slots, rows), 1, pos_ref[...])
    out_ref[:, :width] = jnp.dot(pick, stream_ref[...], preferred_element_type=F32).astype(BF)
    out_ref[:, width:] = jnp.dot(pick, cot_ref[...], preferred_element_type=F32).astype(BF)


def collect(pos, stream, cot):
    slots = pos.shape[0]
    rows, width = stream.shape
    return pl.pallas_call(
        collect_kernel,
        in_specs=[whole()] * 3,
        out_specs=whole(),
        out_shape=jax.ShapeDtypeStruct((slots, 2 * width), BF),
        compiler_params=params(24),
        cost_estimate=cost(4 * slots * rows * width, 8 * rows * width),
        name="collect",
    )(pos, stream, cot)


def unpack_kernel(slot_ref, came_ref, ngain_ref, base_ref, up_ref):
    tokens, width = base_ref.shape
    slots = came_ref.shape[0]
    take = eq_hot((tokens, slots), 1, slot_ref[...])
    base_ref[...] = jnp.dot(take, came_ref[:, :width], preferred_element_type=F32)
    up_ref[...] = jnp.dot(take, came_ref[:, width:], preferred_element_type=F32) * ngain_ref[
        ...
    ].astype(F32)


def unpack(slot_col, came, ngain):
    tokens = slot_col.shape[0]
    slots, both = came.shape
    width = both // 2
    return pl.pallas_call(
        unpack_kernel,
        in_specs=[whole()] * 3,
        out_specs=[whole()] * 2,
        out_shape=[jax.ShapeDtypeStruct((tokens, width), F32)] * 2,
        compiler_params=params(16),
        cost_estimate=cost(4 * slots * tokens * width, 8 * tokens * width),
        name="unpack",
    )(slot_col, came, ngain)


def stack_kernel(me_ref, *refs):
    out_ref = refs[-1]
    me = me_ref[0]
    for away, ref in zip((0, SIDE - 1, 1, 2), refs[:-1]):
        out_ref[lax.rem(me + away, SIDE)] = ref[...]


def stack(me, blocks):
    rows, width = blocks[0].shape
    return pl.pallas_call(
        stack_kernel,
        in_specs=[pl.BlockSpec(memory_space=SMEM)] + [whole()] * 4,
        out_specs=whole(),
        out_shape=jax.ShapeDtypeStruct((SIDE, rows, width), BF),
        compiler_params=params(8),
        cost_estimate=cost(0, 16 * rows * width),
        name="stack",
    )(me, *blocks)


def multiply_kernel(plan, count, zy_ref, lifted_ref, *refs):
    total = None
    if len(refs) > count + 1:
        total = refs[count][...]
    for (axis, away, start, stop), ref in zip(plan, refs[:count]):
        index = axis * SIDE + lax.rem(zy_ref[axis] + away, SIDE)
        rows = ref.shape[0]
        left = lifted_ref[index][:, start:stop]
        part = jnp.dot(left, ref[...], preferred_element_type=F32)
        total = part if total is None else total + part
    refs[-1][...] = total


def multiply(zy, lifted, pieces, plan, before=None):
    tokens = lifted.shape[1]
    width = pieces[0].shape[1]
    extra = [] if before is None else [before]
    depth = sum(p.shape[0] for p in pieces)
    return pl.pallas_call(
        lambda *refs: multiply_kernel(plan, len(pieces), *refs),
        in_specs=[pl.BlockSpec(memory_space=SMEM)] + [whole()] * (1 + len(pieces) + len(extra)),
        out_specs=whole(),
        out_shape=jax.ShapeDtypeStruct((tokens, width), F32),
        compiler_params=params(24),
        cost_estimate=cost(2 * depth * tokens * width, 2 * depth * width),
        name="multiply",
    )(zy, lifted, *pieces, *extra)


def merge_kernel(acc_ref, base_ref, up_ref, visual_ref, state_ref, stat_ref):
    visual = acc_ref[...].astype(BF)
    visual_ref[...] = visual
    state = base_ref[...] + visual.astype(F32)
    state_ref[...] = state
    lane = lax.broadcasted_iota(jnp.int32, stat_ref.shape, 1)
    stat_ref[...] = jnp.where(
        lane == 0,
        jnp.sum(state * state, axis=1, keepdims=True),
        jnp.sum(up_ref[...] * state, axis=1, keepdims=True),
    )


def merge(acc, base, up):
    tokens, width = acc.shape
    return pl.pallas_call(
        merge_kernel,
        in_specs=[whole()] * 3,
        out_specs=[whole()] * 3,
        out_shape=[
            jax.ShapeDtypeStruct((tokens, width), BF),
            jax.ShapeDtypeStruct((tokens, width), F32),
            jax.ShapeDtypeStruct((tokens, 128), F32),
        ],
        compiler_params=params(16),
        cost_estimate=cost(8 * tokens * width, 18 * tokens * width),
        name="merge",
    )(acc, base, up)


def pack_kernel(slot_ref, visual_ref, out_ref):
    slots = out_ref.shape[0]
    tokens = visual_ref.shape[0]
    put = eq_hot((slots, tokens), 0, slot_ref[...])
    out_ref[...] = jnp.dot(put, visual_ref[...], preferred_element_type=F32).astype(BF)


def pack(slot_row, visual, slots):
    tokens, width = visual.shape
    return pl.pallas_call(
        pack_kernel,
        in_specs=[whole()] * 2,
        out_specs=whole(),
        out_shape=jax.ShapeDtypeStruct((slots, width), BF),
        compiler_params=params(16),
        cost_estimate=cost(2 * slots * tokens * width, 2 * (slots + tokens) * width),
        name="pack",
    )(slot_row, visual)


def assemble_kernel(plan, zy_ref, *refs):
    out_ref = refs[-1]
    for (axis, away, start, stop), ref in zip(plan, refs[:-1]):
        index = axis * SIDE + lax.rem(zy_ref[axis] + away, SIDE)
        out_ref[index, start:stop, :] = ref[...]


def assemble(zy, pieces, plan):
    depth = sum(p.shape[0] for p in pieces)
    width = pieces[0].shape[1]
    return pl.pallas_call(
        lambda *refs: assemble_kernel(plan, *refs),
        in_specs=[pl.BlockSpec(memory_space=SMEM)] + [whole()] * len(pieces),
        out_specs=whole(),
        out_shape=jax.ShapeDtypeStruct((2 * SIDE, depth // (2 * SIDE), width), BF),
        compiler_params=params(32),
        cost_estimate=cost(0, 4 * depth * width),
        name="assemble",
    )(zy, *pieces)


def backward_kernel(full_width, chunks, core_ref, state_ref, up_ref, stat_a_ref, stat_b_ref, w_ref, *refs):
    picked_ref = refs[-1]
    tokens = state_ref.shape[0]
    half = tokens // 2
    rows = half // chunks
    core = core_ref[0]
    for place, owner in enumerate((core, 1 - core)):
        at = pl.ds(pl.multiple_of(owner * half, half), half)
        sums = stat_a_ref[at, :] + stat_b_ref[at, :]
        inv = lax.rsqrt(sums[:, 0:1] / full_width + 1e-06)
        inner = sums[:, 1:2] / full_width
        grad = inv * up_ref[at, :] - state_ref[at, :] * (inv * inv * inv * inner)
        picked_ref[place * half : (place + 1) * half, :] = grad.astype(BF)
    depth = w_ref.shape[0]
    block = depth // SIDE
    for step in range(SIDE):
        cols = slice(step * block, (step + 1) * block)
        both = lax.dot_general(
            picked_ref[...], w_ref[cols, :], (((1,), (1,)), ((), ())), preferred_element_type=F32
        )
        for chunk in range(chunks):
            refs[chunk][:, cols] = both[chunk * rows : (chunk + 1) * rows]
            refs[chunks + chunk][:, cols] = both[
                half + chunk * rows : half + (chunk + 1) * rows
            ].astype(BF)


def backward(core, state, up, stat_a, stat_b, weight, chunks, full_width):
    depth, width = weight.shape
    tokens = state.shape[0]
    rows = tokens // 2 // chunks
    return pl.pallas_call(
        lambda *refs: backward_kernel(full_width, chunks, *refs),
        in_specs=[pl.BlockSpec(memory_space=SMEM)] + [whole()] * 5,
        out_specs=[whole()] * (2 * chunks),
        out_shape=[jax.ShapeDtypeStruct((rows, depth), F32)] * chunks
        + [jax.ShapeDtypeStruct((rows, depth), BF)] * chunks,
        scratch_shapes=[pltpu.VMEM((tokens, width), BF)],
        compiler_params=params(32),
        cost_estimate=cost(2 * depth * tokens * width, 2 * depth * width),
        name="backward",
    )(core, state, up, stat_a, stat_b, weight)


def finish_kernel(block_ref, own_ref, far_ref, xw_ref, stat_ref, gain_ref, out_ref):
    window, tokens, width = xw_ref.shape
    full = window * width
    share = width // (SIDE * SIDE)
    piece = full // (2 * SIDE)
    mean = stat_ref[:, 0:1]
    inv = stat_ref[:, 1:2]
    lifted = own_ref[...].astype(F32) + far_ref[...].astype(F32)
    where = {}
    for index, slices in enumerate(piece_slices(window, share)):
        for place, key in enumerate(slices):
            where[key] = index * piece + place * share
    scaled = []
    total = 0.0
    inner = 0.0
    for w in range(window):
        starts = [where[(w, at)] for at in range(0, width, share)]
        g = jnp.concatenate([lifted[:, at : at + share] for at in starts], axis=1)
        g = g * gain_ref[w : w + 1].astype(F32)
        normed = (xw_ref[w].astype(F32) - mean) * inv
        total = total + jnp.sum(g, axis=1, keepdims=True)
        inner = inner + jnp.sum(g * normed, axis=1, keepdims=True)
        scaled.append((g, normed))
    total = total / full
    inner = inner / full
    rows = jnp.concatenate(
        [(inv * (g - total - normed * inner)).astype(BF) for g, normed in scaled], axis=0
    )
    out_ref[...] = jnp.dot(
        patch_major(tokens, window), rows, preferred_element_type=F32
    ).astype(BF)


def finish(block, own, far, xw, stat, gain):
    tokens, full = own.shape
    window, width = gain.shape
    return pl.pallas_call(
        finish_kernel,
        grid_spec=pltpu.PrefetchScalarGridSpec(
            num_scalar_prefetch=1,
            grid=(1,),
            in_specs=[
                pl.BlockSpec((tokens, full), lambda i, b: (0, 0)),
                pl.BlockSpec((tokens, full), lambda i, b: (0, 0)),
                pl.BlockSpec((window, tokens, width), lambda i, b: (0, b[0], 0)),
                pl.BlockSpec((tokens, 128), lambda i, b: (b[0], 0)),
                pl.BlockSpec((window, width), lambda i, b: (0, 0)),
            ],
            out_specs=pl.BlockSpec((tokens * window, width), lambda i, b: (0, 0)),
        ),
        out_shape=jax.ShapeDtypeStruct((tokens * window, width), BF),
        compiler_params=params(24),
        cost_estimate=cost(2 * (tokens * window) ** 2 * width, 8 * window * tokens * width),
        name="finish",
    )(block, own, far, xw, stat, gain)


def place_kernel(pos_ref, came_ref, stream_ref, out_ref):
    slots = came_ref.shape[0]
    rows, width = stream_ref.shape
    put = eq_hot((rows, slots), 0, pos_ref[...])
    out_ref[...] = (
        stream_ref[...].astype(F32) + jnp.dot(put, came_ref[...], preferred_element_type=F32)
    ).astype(BF)


def place(pos, came, stream):
    rows, width = stream.shape
    return pl.pallas_call(
        place_kernel,
        in_specs=[whole()] * 3,
        out_specs=whole(),
        out_shape=jax.ShapeDtypeStruct((rows, width), BF),
        compiler_params=params(16),
        cost_estimate=cost(2 * came.shape[0] * rows * width, 6 * rows * width),
        name="place",
    )(pos, came, stream)


def shards(features, ln_gain, ln_bias, projection, stream, norm_gain, cotangent, slots):
    n_img = lax.axis_size("img")
    n_ctx = lax.axis_size("ctx")
    n_tp = lax.axis_size("tp")
    merged = slots.shape[0]
    window = ln_gain.shape[1]
    tok_rows, width = stream.shape
    owners = n_img * n_ctx
    capacity = 2 * merged // owners
    slot_count = owners * capacity
    full_width = width * n_tp

    core_pairs = [(t, t ^ 1) for t in range(n_tp)]
    far_pairs = [(t, t ^ 2) for t in range(n_tp)]
    core = (lax.axis_index("tp") % 2).astype(jnp.int32).reshape(1)

    zy = jnp.stack([lax.axis_index("ctx") // SIDE, lax.axis_index("ctx") % SIDE]).astype(jnp.int32)

    def moved(array, axis, by):
        pairs = []
        for z in range(SIDE):
            for y in range(SIDE):
                to = ((z + by) % SIDE, y) if axis == 0 else (z, (y + by) % SIDE)
                pairs.append((z * SIDE + y, to[0] * SIDE + to[1]))
        return lax.ppermute(array, "ctx", pairs)

    half = window // 2
    share = projection.shape[2]
    mine_a = projection[0, :half].reshape(half * share, width)
    mine_b = projection[0, half:].reshape(half * share, width)
    first_a = [mine_a] + [moved(mine_a, 1, by) for by in (1, -1, 2)]
    first_b = [mine_b] + [moved(mine_b, 0, by) for by in (1, -1, 2)]

    target = slots // tok_rows
    ids = jnp.arange(merged)
    earlier = (target[:, None] == target[None, :]) & (ids[:, None] < ids[None, :])
    rank = jnp.sum(earlier.astype(jnp.int32), axis=0)
    slot = target * capacity + rank
    local = slots - target * tok_rows
    packed = jnp.max(
        jnp.where(jnp.arange(slot_count)[:, None] == slot[None, :], local[None, :], -1), axis=1
    )
    asked = lax.all_to_all(
        packed.reshape(owners, capacity), ("img", "ctx"), split_axis=0, concat_axis=0, tiled=True
    )
    held = collect(asked.reshape(slot_count, 1), stream, cotangent[0])
    came = lax.all_to_all(
        held.reshape(owners, capacity, 2 * width),
        ("img", "ctx"), split_axis=0, concat_axis=0, tiled=True,
    ).reshape(slot_count, 2 * width)

    gain = ln_gain[0]
    lifted, xw, stat = layer_norm(features[0], gain, ln_bias[0])

    stack_a = stack(zy[1:], first_a).reshape(SIDE * half * share, width)
    stack_b = stack(zy[:1], first_b).reshape(SIDE * half * share, width)
    pieces, plan, far_pieces, far_plan = [], [], [], []
    for axis, block in ((0, stack_a), (1, stack_b)):
        rows = block.shape[0]
        before = moved(block, axis, 1)
        after = moved(block, axis, -1)
        pieces += [block, before, after]
        plan += [(axis, 0, 0, rows), (axis, SIDE - 1, 0, rows), (axis, 1, 0, rows)]
        far_pieces += [moved(before[: rows // 2], axis, 1), moved(after[rows // 2 :], axis, -1)]
        far_plan += [(axis, 2, 0, rows // 2), (axis, 2, rows // 2, rows)]

    base, up = unpack(slot.reshape(merged, 1), came, norm_gain)
    acc = multiply(zy, lifted, pieces, plan)
    acc = multiply(zy, lifted, far_pieces, far_plan, acc)
    visual, state, sums = merge(acc, base, up)

    near = sums + lax.ppermute(sums, "tp", core_pairs)
    far = lax.ppermute(near, "tp", far_pairs)
    weight = assemble(zy, pieces + far_pieces, plan + far_plan).reshape(-1, width)

    send = pack(slot.reshape(1, merged), visual, slot_count)
    arrived = lax.all_to_all(
        send.reshape(owners, capacity, width),
        ("img", "ctx"), split_axis=0, concat_axis=0, tiled=True,
    ).reshape(slot_count, width)
    new_stream = place(asked.reshape(1, slot_count), arrived, stream)

    chunks = 2
    parts = backward(core, state, up, near, far, weight, chunks, full_width)
    own_out, got_out = [], []
    for chunk in range(chunks):
        got = lax.ppermute(parts[chunks + chunk], "tp", core_pairs)
        pair = (parts[chunk] + got.astype(F32)).astype(BF)
        beyond = lax.ppermute(pair, "tp", far_pairs)
        out = finish(core * chunks + chunk, pair, beyond, xw, stat, gain)
        own_out.append(out)
        got_out.append(lax.ppermute(out, "tp", core_pairs))
    first = core[0] == 0
    own = jnp.concatenate(own_out, axis=0)
    got = jnp.concatenate(got_out, axis=0)
    grad = jnp.concatenate([jnp.where(first, own, got), jnp.where(first, got, own)], axis=0)
    return (new_stream, grad[None])


def solution(mesh):
    placed = (
        P(None, ("img", "ctx"), None),
        P(),
        P(),
        P(None, None, "ctx", "tp"),
        P(("img", "ctx"), "tp"),
        P(None, "tp"),
        P(None, ("img", "ctx"), "tp"),
        P(("img", "ctx")),
    )
    return jax.shard_map(
        shards,
        mesh=mesh,
        in_specs=placed,
        out_specs=(P(("img", "ctx"), "tp"), P(None, ("img", "ctx"), None)),
        check_vma=False,
    )
```

```python
import jax
import jax.numpy as jnp
from jax import lax
from jax.experimental import pallas as pl
from jax.experimental.pallas import tpu as pltpu
from jax.sharding import PartitionSpec as P

BF = jnp.bfloat16
F32 = jnp.float32
VMEM = pltpu.VMEM
SMEM = pltpu.SMEM


def params(mib):
    return pltpu.CompilerParams(vmem_limit_bytes=mib * 1024 * 1024)


def whole():
    return pl.BlockSpec(memory_space=VMEM)


def cost(flops, moved):
    return pl.CostEstimate(flops=flops, bytes_accessed=moved, transcendentals=0)


def eq_hot(shape, dim, index):
    return (lax.broadcasted_iota(jnp.int32, shape, dim) == index).astype(BF)


def window_major(tokens, window):
    n = tokens * window
    row = lax.broadcasted_iota(jnp.int32, (n, n), 0)
    col = lax.broadcasted_iota(jnp.int32, (n, n), 1)
    return (col == (row % tokens) * window + row // tokens).astype(BF)


def patch_major(tokens, window):
    n = tokens * window
    row = lax.broadcasted_iota(jnp.int32, (n, n), 0)
    col = lax.broadcasted_iota(jnp.int32, (n, n), 1)
    return (col == (row % window) * tokens + row // window).astype(BF)


SIDE = 4
HALVES = 4 * SIDE


def piece_slices(window, share):
    half = window // 2
    pieces = []
    for part in range(2):
        for first in range(SIDE):
            for side in range(2):
                piece = []
                for second in (2 * side, 2 * side + 1):
                    ctx = first * SIDE + second if part == 0 else second * SIDE + first
                    piece += [(w, ctx * share) for w in range(part * half, part * half + half)]
                pieces.append(piece)
    return pieces


def norm_kernel(x_ref, gain_ref, bias_ref, lifted_ref, xw_ref, stat_ref):
    window, width = gain_ref.shape
    tokens = x_ref.shape[0] // window
    full = window * width
    share = width // (SIDE * SIDE)
    x = jnp.dot(
        window_major(tokens, window), x_ref[...], preferred_element_type=F32
    )
    parts = [x[w * tokens : (w + 1) * tokens] for w in range(window)]
    total = sum(jnp.sum(p, axis=1, keepdims=True) for p in parts)
    squares = sum(jnp.sum(p * p, axis=1, keepdims=True) for p in parts)
    mean = total / full
    inv = lax.rsqrt(squares / full - mean * mean + 1e-05)
    lifted = []
    for w, p in enumerate(parts):
        normed = (p - mean) * inv
        lifted.append(
            normed * gain_ref[w : w + 1].astype(F32) + bias_ref[w : w + 1].astype(F32)
        )
        xw_ref[w] = p.astype(BF)
    for index, piece in enumerate(piece_slices(window, share)):
        lifted_ref[index] = jnp.concatenate(
            [lifted[w][:, at : at + share] for w, at in piece], axis=1
        ).astype(BF)
    lane = lax.broadcasted_iota(jnp.int32, stat_ref.shape, 1)
    stat_ref[...] = jnp.where(lane == 0, mean, inv)


def layer_norm(features, gain, bias):
    rows, width = features.shape
    window = gain.shape[0]
    merged = rows // window
    block = 64
    piece = window * width // HALVES
    return pl.pallas_call(
        norm_kernel,
        grid=(merged // block,),
        in_specs=[
            pl.BlockSpec((block * window, width), lambda i: (i, 0)),
            pl.BlockSpec((window, width), lambda i: (0, 0)),
            pl.BlockSpec((window, width), lambda i: (0, 0)),
        ],
        out_specs=[
            pl.BlockSpec((HALVES, block, piece), lambda i: (0, i, 0)),
            pl.BlockSpec((window, block, width), lambda i: (0, i, 0)),
            pl.BlockSpec((block, 128), lambda i: (i, 0)),
        ],
        out_shape=[
            jax.ShapeDtypeStruct((HALVES, merged, piece), BF),
            jax.ShapeDtypeStruct((window, merged, width), BF),
            jax.ShapeDtypeStruct((merged, 128), F32),
        ],
        compiler_params=params(12),
        cost_estimate=cost(2 * rows * block * window * width, 6 * rows * width),
        name="layer_norm",
    )(features, gain, bias)


def collect_kernel(pos_ref, stream_ref, cot_ref, out_ref):
    slots = pos_ref.shape[0]
    rows, width = stream_ref.shape
    pick = eq_hot((slots, rows), 1, pos_ref[...])
    out_ref[:, :width] = jnp.dot(pick, stream_ref[...], preferred_element_type=F32).astype(BF)
    out_ref[:, width:] = jnp.dot(pick, cot_ref[...], preferred_element_type=F32).astype(BF)


def collect(pos, stream, cot):
    slots = pos.shape[0]
    rows, width = stream.shape
    return pl.pallas_call(
        collect_kernel,
        in_specs=[whole()] * 3,
        out_specs=whole(),
        out_shape=jax.ShapeDtypeStruct((slots, 2 * width), BF),
        compiler_params=params(12),
        cost_estimate=cost(4 * slots * rows * width, 8 * rows * width),
        name="collect",
    )(pos, stream, cot)


def unpack_kernel(slot_ref, came_ref, ngain_ref, base_ref, up_ref):
    tokens, width = base_ref.shape
    slots = came_ref.shape[0]
    take = eq_hot((tokens, slots), 1, slot_ref[...])
    base_ref[...] = jnp.dot(take, came_ref[:, :width], preferred_element_type=F32)
    up_ref[...] = jnp.dot(take, came_ref[:, width:], preferred_element_type=F32) * ngain_ref[
        ...
    ].astype(F32)


def unpack(slot_col, came, ngain):
    tokens = slot_col.shape[0]
    slots, both = came.shape
    width = both // 2
    return pl.pallas_call(
        unpack_kernel,
        in_specs=[whole()] * 3,
        out_specs=[whole()] * 2,
        out_shape=[jax.ShapeDtypeStruct((tokens, width), F32)] * 2,
        compiler_params=params(12),
        cost_estimate=cost(4 * slots * tokens * width, 8 * tokens * width),
        name="unpack",
    )(slot_col, came, ngain)


def stack_kernel(me_ref, *refs):
    me = me_ref[0]
    for away, ref in zip((0, SIDE - 1, 1, 2), refs[:SIDE]):
        place = lax.rem(me + away, SIDE)
        for side in range(2):

            @pl.when(place // 2 == side)
            def _():
                refs[SIDE + side][lax.rem(place, 2)] = ref[...]


def stack(me, blocks):
    rows, width = blocks[0].shape
    halves = pl.pallas_call(
        stack_kernel,
        in_specs=[pl.BlockSpec(memory_space=SMEM)] + [whole()] * SIDE,
        out_specs=[whole()] * 2,
        out_shape=[jax.ShapeDtypeStruct((2, rows, width), BF)] * 2,
        compiler_params=params(6),
        cost_estimate=cost(0, 16 * rows * width),
        name="stack",
    )(me, *blocks)
    return [h.reshape(2 * rows, width) for h in halves]


def place_of(zy_ref, entry):
    part, away, side = entry
    return part * 2 * SIDE + 2 * lax.rem(zy_ref[part] + away, SIDE) + side


def product(plan, zy_ref, lifted_ref, refs):
    total = None
    for entry, ref in zip(plan, refs):
        part = jnp.dot(
            lifted_ref[place_of(zy_ref, entry)], ref[...], preferred_element_type=F32
        )
        total = part if total is None else total + part
    return total


def multiply_kernel(plan, zy_ref, lifted_ref, *refs):
    refs[-1][...] = product(plan, zy_ref, lifted_ref, refs[:-1])


def multiply(zy, lifted, pieces, plan):
    tokens = lifted.shape[1]
    width = pieces[0].shape[1]
    depth = sum(p.shape[0] for p in pieces)
    return pl.pallas_call(
        lambda *refs: multiply_kernel(plan, *refs),
        in_specs=[pl.BlockSpec(memory_space=SMEM)] + [whole()] * (1 + len(pieces)),
        out_specs=whole(),
        out_shape=jax.ShapeDtypeStruct((tokens, width), F32),
        compiler_params=params(16),
        cost_estimate=cost(2 * depth * tokens * width, 2 * depth * width),
        name="multiply",
    )(zy, lifted, *pieces)


def merge_kernel(plan, zy_ref, lifted_ref, *refs):
    acc_ref, base_ref, up_ref, visual_ref, state_ref, stat_ref = refs[len(plan) :]
    total = acc_ref[...] + product(plan, zy_ref, lifted_ref, refs[: len(plan)])
    visual = total.astype(BF)
    visual_ref[...] = visual
    state = base_ref[...] + visual.astype(F32)
    state_ref[...] = state
    lane = lax.broadcasted_iota(jnp.int32, (state.shape[0], 128), 1)
    sums = jnp.where(
        lane == 0,
        jnp.sum(state * state, axis=1, keepdims=True),
        jnp.sum(up_ref[...] * state, axis=1, keepdims=True),
    )
    stat_ref[...] = sums.T[: stat_ref.shape[0]]


def merge(zy, lifted, pieces, plan, acc, base, up):
    tokens, width = acc.shape
    depth = sum(p.shape[0] for p in pieces)
    return pl.pallas_call(
        lambda *refs: merge_kernel(plan, *refs),
        in_specs=[pl.BlockSpec(memory_space=SMEM)] + [whole()] * (4 + len(pieces)),
        out_specs=[whole()] * 3,
        out_shape=[
            jax.ShapeDtypeStruct((tokens, width), BF),
            jax.ShapeDtypeStruct((tokens, width), F32),
            jax.ShapeDtypeStruct((8, tokens), F32),
        ],
        compiler_params=params(16),
        cost_estimate=cost(2 * depth * tokens * width, 18 * tokens * width),
        name="merge",
    )(zy, lifted, *pieces, acc, base, up)


def pack_kernel(slot_ref, visual_ref, stay_ref, cross_ref):
    tokens = visual_ref.shape[0]
    slots = stay_ref.shape[0]
    for shift, out_ref in ((0, stay_ref), (slots, cross_ref)):
        put = eq_hot((slots, tokens), 0, slot_ref[...] - shift)
        out_ref[...] = jnp.dot(put, visual_ref[...], preferred_element_type=F32).astype(BF)


def pack(slot_row, visual, slots):
    tokens, width = visual.shape
    return pl.pallas_call(
        pack_kernel,
        in_specs=[whole()] * 2,
        out_specs=[whole()] * 2,
        out_shape=[jax.ShapeDtypeStruct((slots // 2, width), BF)] * 2,
        compiler_params=params(8),
        cost_estimate=cost(2 * slots * tokens * width, 2 * (slots + tokens) * width),
        name="pack",
    )(slot_row, visual)


def assemble_kernel(plan, zy_ref, *refs):
    for entry, ref in zip(plan, refs[:-1]):
        refs[-1][place_of(zy_ref, entry)] = ref[...]


def assemble(zy, pieces, plan):
    rows, width = pieces[0].shape
    return pl.pallas_call(
        lambda *refs: assemble_kernel(plan, *refs),
        in_specs=[pl.BlockSpec(memory_space=SMEM)] + [whole()] * len(pieces),
        out_specs=whole(),
        out_shape=jax.ShapeDtypeStruct((HALVES, rows, width), BF),
        compiler_params=params(22),
        cost_estimate=cost(0, 4 * HALVES * rows * width),
        name="assemble",
    )(zy, *pieces)


def backward_kernel(full_width, chunks, core_ref, state_ref, up_ref, stat_a_ref, stat_b_ref, w_ref, *refs):
    picked_ref, sums_ref = refs[-2:]
    tokens = state_ref.shape[0]
    half = tokens // 2
    rows = half // chunks
    core = core_ref[0]
    sums_ref[...] = (stat_a_ref[...] + stat_b_ref[...]).T
    for place, owner in enumerate((core, 1 - core)):
        at = pl.ds(pl.multiple_of(owner * half, half), half)
        sums = sums_ref[at, :]
        inv = lax.rsqrt(sums[:, 0:1] / full_width + 1e-06)
        inner = sums[:, 1:2] / full_width
        grad = inv * up_ref[at, :] - state_ref[at, :] * (inv * inv * inv * inner)
        picked_ref[place * half : (place + 1) * half, :] = grad.astype(BF)
    depth = w_ref.shape[0]
    block = depth // SIDE
    for step in range(SIDE):
        cols = slice(step * block, (step + 1) * block)
        both = lax.dot_general(
            picked_ref[...], w_ref[cols, :], (((1,), (1,)), ((), ())), preferred_element_type=F32
        )
        for chunk in range(chunks):
            refs[chunk][:, cols] = both[chunk * rows : (chunk + 1) * rows]
            refs[chunks + chunk][:, cols] = both[
                half + chunk * rows : half + (chunk + 1) * rows
            ].astype(BF)


def backward(core, state, up, stat_a, stat_b, weight, chunks, full_width):
    depth, width = weight.shape
    tokens = state.shape[0]
    rows = tokens // 2 // chunks
    return pl.pallas_call(
        lambda *refs: backward_kernel(full_width, chunks, *refs),
        in_specs=[pl.BlockSpec(memory_space=SMEM)] + [whole()] * 5,
        out_specs=[whole()] * (2 * chunks),
        out_shape=[jax.ShapeDtypeStruct((rows, depth), F32)] * chunks
        + [jax.ShapeDtypeStruct((rows, depth), BF)] * chunks,
        scratch_shapes=[pltpu.VMEM((tokens, width), BF), pltpu.VMEM((tokens, 8), F32)],
        compiler_params=params(22),
        cost_estimate=cost(2 * depth * tokens * width, 2 * depth * width),
        name="backward",
    )(core, state, up, stat_a, stat_b, weight)


def finish_kernel(block_ref, own_ref, far_ref, xw_ref, stat_ref, gain_ref, out_ref):
    window, tokens, width = xw_ref.shape
    full = window * width
    share = width // (SIDE * SIDE)
    piece = full // HALVES
    mean = stat_ref[:, 0:1]
    inv = stat_ref[:, 1:2]
    lifted = own_ref[...].astype(F32) + far_ref[...].astype(F32)
    where = {}
    for index, slices in enumerate(piece_slices(window, share)):
        for place, key in enumerate(slices):
            where[key] = index * piece + place * share
    scaled = []
    total = 0.0
    inner = 0.0
    for w in range(window):
        starts = [where[(w, at)] for at in range(0, width, share)]
        g = jnp.concatenate([lifted[:, at : at + share] for at in starts], axis=1)
        g = g * gain_ref[w : w + 1].astype(F32)
        normed = (xw_ref[w].astype(F32) - mean) * inv
        total = total + jnp.sum(g, axis=1, keepdims=True)
        inner = inner + jnp.sum(g * normed, axis=1, keepdims=True)
        scaled.append((g, normed))
    total = total / full
    inner = inner / full
    rows = jnp.concatenate(
        [(inv * (g - total - normed * inner)).astype(BF) for g, normed in scaled], axis=0
    )
    out_ref[...] = jnp.dot(
        patch_major(tokens, window), rows, preferred_element_type=F32
    ).astype(BF)


def finish(block, own, far, xw, stat, gain):
    tokens, full = own.shape
    window, width = gain.shape
    return pl.pallas_call(
        finish_kernel,
        grid_spec=pltpu.PrefetchScalarGridSpec(
            num_scalar_prefetch=1,
            grid=(1,),
            in_specs=[
                pl.BlockSpec((tokens, full), lambda i, b: (0, 0)),
                pl.BlockSpec((tokens, full), lambda i, b: (0, 0)),
                pl.BlockSpec((window, tokens, width), lambda i, b: (0, b[0], 0)),
                pl.BlockSpec((tokens, 128), lambda i, b: (b[0], 0)),
                pl.BlockSpec((window, width), lambda i, b: (0, 0)),
            ],
            out_specs=pl.BlockSpec((tokens * window, width), lambda i, b: (0, 0)),
        ),
        out_shape=jax.ShapeDtypeStruct((tokens * window, width), BF),
        compiler_params=params(12),
        cost_estimate=cost(2 * (tokens * window) ** 2 * width, 8 * window * tokens * width),
        name="finish",
    )(block, own, far, xw, stat, gain)


def place_kernel(pos_ref, came_ref, stream_ref, out_ref):
    slots = came_ref.shape[0]
    rows, width = stream_ref.shape
    put = eq_hot((rows, slots), 0, pos_ref[...])
    out_ref[...] = (
        stream_ref[...].astype(F32) + jnp.dot(put, came_ref[...], preferred_element_type=F32)
    ).astype(BF)


def place(pos, came, stream):
    rows, width = stream.shape
    return pl.pallas_call(
        place_kernel,
        in_specs=[whole()] * 3,
        out_specs=whole(),
        out_shape=jax.ShapeDtypeStruct((rows, width), BF),
        compiler_params=params(12),
        cost_estimate=cost(2 * came.shape[0] * rows * width, 6 * rows * width),
        name="place",
    )(pos, came, stream)


def lay_kernel(core_ref, *refs):
    out_ref, sems = refs[-2:]
    chunks = (len(refs) - 2) // 2
    rows = refs[0].shape[0]
    copies = []
    for index, ref in enumerate(refs[:-2]):
        owner = core_ref[0] if index < chunks else 1 - core_ref[0]
        start = pl.multiple_of((owner * chunks + index % chunks) * rows, rows)
        copies.append(pltpu.make_async_copy(ref, out_ref.at[pl.ds(start, rows)], sems.at[index]))
    for copy in copies:
        copy.start()
    for copy in copies:
        copy.wait()


def lay(core, blocks):
    rows, width = blocks[0].shape
    return pl.pallas_call(
        lay_kernel,
        in_specs=[pl.BlockSpec(memory_space=SMEM)] + [whole()] * len(blocks),
        out_specs=pl.BlockSpec(memory_space=pl.ANY),
        out_shape=jax.ShapeDtypeStruct((len(blocks) * rows, width), BF),
        scratch_shapes=[pltpu.SemaphoreType.DMA((len(blocks),))],
        compiler_params=params(6),
        cost_estimate=cost(0, 4 * len(blocks) * rows * width),
        name="lay",
    )(core, *blocks)


def shards(features, ln_gain, ln_bias, projection, stream, norm_gain, cotangent, slots):
    n_img = lax.axis_size("img")
    n_ctx = lax.axis_size("ctx")
    n_tp = lax.axis_size("tp")
    merged = slots.shape[0]
    window = ln_gain.shape[1]
    tok_rows, width = stream.shape
    owners = n_img * n_ctx
    capacity = 2 * merged // owners
    slot_count = owners * capacity
    full_width = width * n_tp

    core_pairs = [(t, t ^ 1) for t in range(n_tp)]
    far_pairs = [(t, t ^ 2) for t in range(n_tp)]
    core = (lax.axis_index("tp") % 2).astype(jnp.int32).reshape(1)

    zy = jnp.stack([lax.axis_index("ctx") // SIDE, lax.axis_index("ctx") % SIDE]).astype(jnp.int32)

    def moved(array, axis, by):
        pairs = []
        for z in range(SIDE):
            for y in range(SIDE):
                to = ((z + by) % SIDE, y) if axis == 0 else (z, (y + by) % SIDE)
                pairs.append((z * SIDE + y, to[0] * SIDE + to[1]))
        return lax.ppermute(array, "ctx", pairs)

    half = window // 2
    share = projection.shape[2]
    mine_a = projection[0, :half].reshape(half * share, width)
    mine_b = projection[0, half:].reshape(half * share, width)
    first_a = [mine_a] + [moved(mine_a, 1, by) for by in (1, -1, 2)]
    first_b = [mine_b] + [moved(mine_b, 0, by) for by in (1, -1, 2)]

    target = slots // tok_rows
    ids = jnp.arange(merged)
    earlier = (target[:, None] == target[None, :]) & (ids[:, None] < ids[None, :])
    rank = jnp.sum(earlier.astype(jnp.int32), axis=0)
    slot = target * capacity + rank
    local = slots - target * tok_rows
    packed = jnp.max(
        jnp.where(jnp.arange(slot_count)[:, None] == slot[None, :], local[None, :], -1), axis=1
    )
    asked = lax.all_to_all(
        packed.reshape(owners, capacity), ("img", "ctx"), split_axis=0, concat_axis=0, tiled=True
    )
    asked, first_a, first_b = lax.optimization_barrier((asked, first_a, first_b))

    halves = [stack(zy[1:], first_a), stack(zy[:1], first_b)]
    before = [[moved(h, part, 1) for h in halves[part]] for part in range(2)]
    after = [[moved(h, part, -1) for h in halves[part]] for part in range(2)]

    held = collect(asked.reshape(slot_count, 1), stream, cotangent[0])
    came = lax.all_to_all(
        held.reshape(owners, capacity, 2 * width),
        ("img", "ctx"), split_axis=0, concat_axis=0, tiled=True,
    ).reshape(slot_count, 2 * width)

    gain = ln_gain[0]
    lifted, xw, stat = layer_norm(features[0], gain, ln_bias[0])
    lifted, before, after = lax.optimization_barrier((lifted, before, after))

    pieces, plan, far_pieces, far_plan = [], [], [], []
    for part in range(2):
        for away, sides in ((0, halves[part]), (SIDE - 1, before[part]), (1, after[part])):
            pieces += sides
            plan += [(part, away, 0), (part, away, 1)]
        far_pieces += [moved(before[part][0], part, 1), moved(after[part][1], part, -1)]
        far_plan += [(part, 2, 0), (part, 2, 1)]

    acc = multiply(zy, lifted, pieces, plan)
    base, up = unpack(slot.reshape(merged, 1), came, norm_gain)
    visual, state, sums = merge(zy, lifted, far_pieces, far_plan, acc, base, up)

    near = sums + lax.ppermute(sums, "tp", core_pairs)
    far = lax.ppermute(near, "tp", far_pairs)
    weight = assemble(zy, pieces + far_pieces, plan + far_plan).reshape(-1, width)

    img = lax.axis_index("img").astype(jnp.int32)
    in_img = slot_count // n_img
    relative = lax.rem(slot + img * in_img, slot_count)
    stay, cross = pack(relative.reshape(1, merged), visual, slot_count)
    crossed = lax.ppermute(cross, "img", [(i, 1 - i) for i in range(n_img)])

    chunks = 2
    parts = backward(core, state, up, near, far, weight, chunks, full_width)
    pairs = []
    for chunk in range(chunks):
        got = lax.ppermute(parts[chunks + chunk], "tp", core_pairs)
        pairs.append((parts[chunk] + got.astype(F32)).astype(BF))
    beyond = [lax.ppermute(pair, "tp", far_pairs) for pair in pairs]

    stay, crossed, pairs[0] = lax.optimization_barrier((stay, crossed, pairs[0]))
    send = jnp.concatenate(
        [x.reshape(n_ctx, capacity, width) for x in (stay, crossed)], axis=1
    )
    arrived = lax.all_to_all(send, "ctx", split_axis=0, concat_axis=0, tiled=True)
    by_img = jnp.stack([
        lax.dynamic_index_in_dim(asked.reshape(n_img, n_ctx, capacity), i, 0, keepdims=False)
        for i in (img, 1 - img)
    ], axis=1)
    new_stream = place(
        by_img.reshape(1, slot_count), arrived.reshape(slot_count, width), stream
    )

    own_out, got_out = [], []
    for chunk in range(chunks):
        out = finish(core * chunks + chunk, pairs[chunk], beyond[chunk], xw, stat, gain)
        own_out.append(out)
        got_out.append(lax.ppermute(out, "tp", core_pairs))
    grad = lay(core, own_out + got_out)
    return (new_stream, grad[None])


def solution(mesh):
    placed = (
        P(None, ("img", "ctx"), None),
        P(),
        P(),
        P(None, None, "ctx", "tp"),
        P(("img", "ctx"), "tp"),
        P(None, "tp"),
        P(None, ("img", "ctx"), "tp"),
        P(("img", "ctx")),
    )
    return jax.shard_map(
        shards,
        mesh=mesh,
        in_specs=placed,
        out_specs=(P(("img", "ctx"), "tp"), P(None, ("img", "ctx"), None)),
        check_vma=False,
    )
```

```python
import jax
import jax.numpy as jnp
from jax import lax
from jax.experimental import pallas as pl
from jax.experimental.pallas import tpu as pltpu
from jax.sharding import PartitionSpec as P

BF = jnp.bfloat16
F32 = jnp.float32
VMEM = pltpu.VMEM
SMEM = pltpu.SMEM


def params(mib):
    return pltpu.CompilerParams(vmem_limit_bytes=mib * 1024 * 1024)


def whole():
    return pl.BlockSpec(memory_space=VMEM)


def cost(flops, moved):
    return pl.CostEstimate(flops=flops, bytes_accessed=moved, transcendentals=0)


def eq_hot(shape, dim, index):
    return (lax.broadcasted_iota(jnp.int32, shape, dim) == index).astype(BF)


def window_major(tokens, window):
    n = tokens * window
    row = lax.broadcasted_iota(jnp.int32, (n, n), 0)
    col = lax.broadcasted_iota(jnp.int32, (n, n), 1)
    return (col == (row % tokens) * window + row // tokens).astype(BF)


def patch_major(tokens, window):
    n = tokens * window
    row = lax.broadcasted_iota(jnp.int32, (n, n), 0)
    col = lax.broadcasted_iota(jnp.int32, (n, n), 1)
    return (col == (row % window) * tokens + row // window).astype(BF)


SIDE = 4


def second_half(window, share):
    blocks = SIDE * SIDE
    return [(w, c * share) for c in range(blocks) for w in range(window // 2, window)]


def norm_kernel(x_ref, gain_ref, bias_ref, first_ref, second_ref, xw_ref, stat_ref):
    window, width = gain_ref.shape
    tokens = x_ref.shape[0] // window
    full = window * width
    share = width // (SIDE * SIDE)
    x = jnp.dot(
        window_major(tokens, window), x_ref[...], preferred_element_type=F32
    )
    parts = [x[w * tokens : (w + 1) * tokens] for w in range(window)]
    total = sum(jnp.sum(p, axis=1, keepdims=True) for p in parts)
    squares = sum(jnp.sum(p * p, axis=1, keepdims=True) for p in parts)
    mean = total / full
    inv = lax.rsqrt(squares / full - mean * mean + 1e-05)
    lifted = []
    for w, p in enumerate(parts):
        normed = (p - mean) * inv
        lifted.append(
            normed * gain_ref[w : w + 1].astype(F32) + bias_ref[w : w + 1].astype(F32)
        )
        xw_ref[w] = p.astype(BF)
    for w in range(window // 2):
        first_ref[:, w * width : (w + 1) * width] = lifted[w].astype(BF)
    second_ref[...] = jnp.concatenate(
        [lifted[w][:, at : at + share] for w, at in second_half(window, share)], axis=1
    ).astype(BF)
    lane = lax.broadcasted_iota(jnp.int32, stat_ref.shape, 1)
    stat_ref[...] = jnp.where(lane == 0, mean, inv)


def layer_norm(features, gain, bias):
    rows, width = features.shape
    window = gain.shape[0]
    merged = rows // window
    block = 64
    half = window * width // 2
    return pl.pallas_call(
        norm_kernel,
        grid=(merged // block,),
        in_specs=[
            pl.BlockSpec((block * window, width), lambda i: (i, 0)),
            pl.BlockSpec((window, width), lambda i: (0, 0)),
            pl.BlockSpec((window, width), lambda i: (0, 0)),
        ],
        out_specs=[
            pl.BlockSpec((block, half), lambda i: (i, 0)),
            pl.BlockSpec((block, half), lambda i: (i, 0)),
            pl.BlockSpec((window, block, width), lambda i: (0, i, 0)),
            pl.BlockSpec((block, 128), lambda i: (i, 0)),
        ],
        out_shape=[
            jax.ShapeDtypeStruct((merged, half), BF),
            jax.ShapeDtypeStruct((merged, half), BF),
            jax.ShapeDtypeStruct((window, merged, width), BF),
            jax.ShapeDtypeStruct((merged, 128), F32),
        ],
        compiler_params=params(12),
        cost_estimate=cost(2 * rows * block * window * width, 6 * rows * width),
        name="layer_norm",
    )(features, gain, bias)


def collect_kernel(pos_ref, stream_ref, cot_ref, out_ref):
    slots = pos_ref.shape[0]
    rows, width = stream_ref.shape
    pick = eq_hot((slots, rows), 1, pos_ref[...])
    out_ref[:, :width] = jnp.dot(pick, stream_ref[...], preferred_element_type=F32).astype(BF)
    out_ref[:, width:] = jnp.dot(pick, cot_ref[...], preferred_element_type=F32).astype(BF)


def collect(pos, stream, cot):
    slots = pos.shape[0]
    rows, width = stream.shape
    return pl.pallas_call(
        collect_kernel,
        in_specs=[whole()] * 3,
        out_specs=whole(),
        out_shape=jax.ShapeDtypeStruct((slots, 2 * width), BF),
        compiler_params=params(12),
        cost_estimate=cost(4 * slots * rows * width, 8 * rows * width),
        name="collect",
    )(pos, stream, cot)


def unpack_kernel(slot_ref, came_ref, ngain_ref, base_ref, up_ref):
    tokens, width = base_ref.shape
    slots = came_ref.shape[0]
    take = eq_hot((tokens, slots), 1, slot_ref[...])
    base_ref[...] = jnp.dot(take, came_ref[:, :width], preferred_element_type=F32)
    up_ref[...] = jnp.dot(take, came_ref[:, width:], preferred_element_type=F32) * ngain_ref[
        ...
    ].astype(F32)


def unpack(slot_col, came, ngain):
    tokens = slot_col.shape[0]
    slots, both = came.shape
    width = both // 2
    return pl.pallas_call(
        unpack_kernel,
        in_specs=[whole()] * 3,
        out_specs=[whole()] * 2,
        out_shape=[jax.ShapeDtypeStruct((tokens, width), F32)] * 2,
        compiler_params=params(12),
        cost_estimate=cost(4 * slots * tokens * width, 8 * tokens * width),
        name="unpack",
    )(slot_col, came, ngain)


AWAY = (0, SIDE - 1, 1, 2)


def stack_kernel(me_ref, *refs):
    for away, ref in zip(AWAY, refs[:SIDE]):
        refs[SIDE][lax.rem(me_ref[0] + away, SIDE)] = ref[...]


def stack(me, blocks):
    rows, width = blocks[0].shape
    return pl.pallas_call(
        stack_kernel,
        in_specs=[pl.BlockSpec(memory_space=SMEM)] + [whole()] * SIDE,
        out_specs=whole(),
        out_shape=jax.ShapeDtypeStruct((SIDE, rows, width), BF),
        compiler_params=params(4),
        cost_estimate=cost(0, 16 * rows * width),
        name="stack",
    )(me, *blocks)


def second_kernel(zy_ref, lifted_ref, *refs):
    acc_ref, out_ref, held_ref, sems, out_sem = refs[2 * SIDE :]
    cut = refs[0].shape[2]
    copies = []
    for index, ref in enumerate(refs[: 2 * SIDE]):
        part, away = index // SIDE, AWAY[index % SIDE]
        place = lax.rem(zy_ref[part] + away, SIDE)
        to = held_ref.at[place, :, :, :cut] if part == 0 else held_ref.at[:, place, :, cut:]
        copies.append(pltpu.make_async_copy(ref, to, sems.at[index]))
    for copy in copies:
        copy.start()
    for copy in copies:
        copy.wait()
    keep = pltpu.make_async_copy(held_ref, out_ref, out_sem)
    keep.start()
    depth = lifted_ref.shape[1]
    acc_ref[...] = jnp.dot(
        lifted_ref[...], held_ref[...].reshape(depth, -1), preferred_element_type=F32
    )
    keep.wait()


def second(zy, lifted, pieces):
    tokens, depth = lifted.shape
    rows, cut = pieces[0].shape[1:]
    width = 2 * cut
    held = (SIDE, SIDE, rows, width)
    return pl.pallas_call(
        second_kernel,
        in_specs=[pl.BlockSpec(memory_space=SMEM), whole()]
        + [pl.BlockSpec(memory_space=pl.ANY)] * len(pieces),
        out_specs=[whole(), pl.BlockSpec(memory_space=pl.ANY)],
        out_shape=[
            jax.ShapeDtypeStruct((tokens, width), F32),
            jax.ShapeDtypeStruct(held, BF),
        ],
        scratch_shapes=[
            pltpu.VMEM(held, BF),
            pltpu.SemaphoreType.DMA((len(pieces),)),
            pltpu.SemaphoreType.DMA,
        ],
        compiler_params=params(16),
        cost_estimate=cost(2 * depth * tokens * width, 6 * depth * width),
        name="second",
    )(zy, lifted, *pieces)


BLOCK = 768


def merge_kernel(lifted_ref, acc_ref, base_ref, up_ref, w_ref, visual_ref, state_ref, stat_ref, held_ref, sems):
    steps = range(w_ref.shape[0] // BLOCK)
    copies = []
    for step in steps:
        at = pl.ds(step * BLOCK, BLOCK)
        copies.append(pltpu.make_async_copy(w_ref.at[at], held_ref.at[at], sems.at[step]))
        copies[step].start()
    total = acc_ref[...]
    for step in steps:
        at = slice(step * BLOCK, (step + 1) * BLOCK)
        copies[step].wait()
        total = total + jnp.dot(lifted_ref[:, at], held_ref[at, :], preferred_element_type=F32)
    visual = total.astype(BF)
    visual_ref[...] = visual
    state = base_ref[...] + visual.astype(F32)
    state_ref[...] = state
    lane = lax.broadcasted_iota(jnp.int32, (state.shape[0], 128), 1)
    sums = jnp.where(
        lane == 0,
        jnp.sum(state * state, axis=1, keepdims=True),
        jnp.sum(up_ref[...] * state, axis=1, keepdims=True),
    )
    stat_ref[...] = sums.T[: stat_ref.shape[0]]


def merge(lifted, acc, base, up, weight):
    tokens, width = acc.shape
    depth = weight.shape[0]
    return pl.pallas_call(
        merge_kernel,
        in_specs=[whole()] * 4 + [pl.BlockSpec(memory_space=pl.ANY)],
        out_specs=[whole()] * 3,
        out_shape=[
            jax.ShapeDtypeStruct((tokens, width), BF),
            jax.ShapeDtypeStruct((tokens, width), F32),
            jax.ShapeDtypeStruct((8, tokens), F32),
        ],
        scratch_shapes=[
            pltpu.VMEM((depth, width), BF),
            pltpu.SemaphoreType.DMA((depth // BLOCK,)),
        ],
        compiler_params=params(18),
        cost_estimate=cost(2 * depth * tokens * width, 2 * depth * width),
        name="merge",
    )(lifted, acc, base, up, weight)


def pack_kernel(slot_ref, visual_ref, stay_ref, cross_ref):
    tokens = visual_ref.shape[0]
    slots = stay_ref.shape[0]
    for shift, out_ref in ((0, stay_ref), (slots, cross_ref)):
        put = eq_hot((slots, tokens), 0, slot_ref[...] - shift)
        out_ref[...] = jnp.dot(put, visual_ref[...], preferred_element_type=F32).astype(BF)


def pack(slot_row, visual, slots):
    tokens, width = visual.shape
    return pl.pallas_call(
        pack_kernel,
        in_specs=[whole()] * 2,
        out_specs=[whole()] * 2,
        out_shape=[jax.ShapeDtypeStruct((slots // 2, width), BF)] * 2,
        compiler_params=params(8),
        cost_estimate=cost(2 * slots * tokens * width, 2 * (slots + tokens) * width),
        name="pack",
    )(slot_row, visual)


def backward_kernel(full_width, chunks, core_ref, state_ref, up_ref, stat_a_ref, stat_b_ref, *refs):
    weights, outs = refs[:2], refs[2 : 2 + 2 * chunks]
    picked_ref, sums_ref, held_ref, sems = refs[2 + 2 * chunks :]
    copies = []
    for ref in weights:
        for start in range(0, ref.shape[0], BLOCK):
            step = len(copies)
            copies.append(
                pltpu.make_async_copy(
                    ref.at[pl.ds(start, BLOCK)], held_ref.at[pl.ds(step * BLOCK, BLOCK)], sems.at[step]
                )
            )
            copies[step].start()
    tokens = state_ref.shape[0]
    half = tokens // 2
    rows = half // chunks
    core = core_ref[0]
    sums_ref[...] = (stat_a_ref[...] + stat_b_ref[...]).T
    for place, owner in enumerate((core, 1 - core)):
        at = pl.ds(pl.multiple_of(owner * half, half), half)
        sums = sums_ref[at, :]
        inv = lax.rsqrt(sums[:, 0:1] / full_width + 1e-06)
        inner = sums[:, 1:2] / full_width
        grad = inv * up_ref[at, :] - state_ref[at, :] * (inv * inv * inv * inner)
        picked_ref[place * half : (place + 1) * half, :] = grad.astype(BF)
    for step, copy in enumerate(copies):
        cols = slice(step * BLOCK, (step + 1) * BLOCK)
        copy.wait()
        both = lax.dot_general(
            picked_ref[...], held_ref[cols, :], (((1,), (1,)), ((), ())), preferred_element_type=F32
        )
        for chunk in range(chunks):
            outs[chunk][:, cols] = both[chunk * rows : (chunk + 1) * rows]
            outs[chunks + chunk][:, cols] = both[
                half + chunk * rows : half + (chunk + 1) * rows
            ].astype(BF)


def backward(core, state, up, stat_a, stat_b, weights, chunks, full_width):
    width = weights[0].shape[1]
    depth = sum(w.shape[0] for w in weights)
    tokens = state.shape[0]
    rows = tokens // 2 // chunks
    return pl.pallas_call(
        lambda *refs: backward_kernel(full_width, chunks, *refs),
        in_specs=[pl.BlockSpec(memory_space=SMEM)] + [whole()] * 4
        + [pl.BlockSpec(memory_space=pl.ANY)] * 2,
        out_specs=[whole()] * (2 * chunks),
        out_shape=[jax.ShapeDtypeStruct((rows, depth), F32)] * chunks
        + [jax.ShapeDtypeStruct((rows, depth), BF)] * chunks,
        scratch_shapes=[
            pltpu.VMEM((tokens, width), BF),
            pltpu.VMEM((tokens, 8), F32),
            pltpu.VMEM((depth, width), BF),
            pltpu.SemaphoreType.DMA((depth // BLOCK,)),
        ],
        compiler_params=params(24),
        cost_estimate=cost(2 * depth * tokens * width, 2 * depth * width),
        name="backward",
    )(core, state, up, stat_a, stat_b, *weights)


def finish_kernel(block_ref, own_ref, far_ref, xw_ref, stat_ref, gain_ref, out_ref):
    window, tokens, width = xw_ref.shape
    full = window * width
    share = width // (SIDE * SIDE)
    mean = stat_ref[:, 0:1]
    inv = stat_ref[:, 1:2]
    lifted = own_ref[...].astype(F32) + far_ref[...].astype(F32)
    order = second_half(window, share)
    scaled = []
    total = 0.0
    inner = 0.0
    for w in range(window):
        if w < window // 2:
            g = lifted[:, w * width : (w + 1) * width]
        else:
            starts = [full // 2 + i * share for i, (v, _) in enumerate(order) if v == w]
            g = jnp.concatenate([lifted[:, at : at + share] for at in starts], axis=1)
        g = g * gain_ref[w : w + 1].astype(F32)
        normed = (xw_ref[w].astype(F32) - mean) * inv
        total = total + jnp.sum(g, axis=1, keepdims=True)
        inner = inner + jnp.sum(g * normed, axis=1, keepdims=True)
        scaled.append((g, normed))
    total = total / full
    inner = inner / full
    rows = jnp.concatenate(
        [(inv * (g - total - normed * inner)).astype(BF) for g, normed in scaled], axis=0
    )
    out_ref[...] = jnp.dot(
        patch_major(tokens, window), rows, preferred_element_type=F32
    ).astype(BF)


def finish(block, own, far, xw, stat, gain):
    tokens, full = own.shape
    window, width = gain.shape
    return pl.pallas_call(
        finish_kernel,
        grid_spec=pltpu.PrefetchScalarGridSpec(
            num_scalar_prefetch=1,
            grid=(1,),
            in_specs=[
                pl.BlockSpec((tokens, full), lambda i, b: (0, 0)),
                pl.BlockSpec((tokens, full), lambda i, b: (0, 0)),
                pl.BlockSpec((window, tokens, width), lambda i, b: (0, b[0], 0)),
                pl.BlockSpec((tokens, 128), lambda i, b: (b[0], 0)),
                pl.BlockSpec((window, width), lambda i, b: (0, 0)),
            ],
            out_specs=pl.BlockSpec((tokens * window, width), lambda i, b: (0, 0)),
        ),
        out_shape=jax.ShapeDtypeStruct((tokens * window, width), BF),
        compiler_params=params(12),
        cost_estimate=cost(2 * (tokens * window) ** 2 * width, 8 * window * tokens * width),
        name="finish",
    )(block, own, far, xw, stat, gain)


def place_kernel(pos_ref, came_ref, stream_ref, out_ref):
    slots = came_ref.shape[0]
    rows, width = stream_ref.shape
    put = eq_hot((rows, slots), 0, pos_ref[...])
    out_ref[...] = (
        stream_ref[...].astype(F32) + jnp.dot(put, came_ref[...], preferred_element_type=F32)
    ).astype(BF)


def place(pos, came, stream):
    rows, width = stream.shape
    return pl.pallas_call(
        place_kernel,
        in_specs=[whole()] * 3,
        out_specs=whole(),
        out_shape=jax.ShapeDtypeStruct((rows, width), BF),
        compiler_params=params(12),
        cost_estimate=cost(2 * came.shape[0] * rows * width, 6 * rows * width),
        name="place",
    )(pos, came, stream)


def lay_kernel(core_ref, *refs):
    out_ref, sems = refs[-2:]
    chunks = (len(refs) - 2) // 2
    rows = refs[0].shape[0]
    copies = []
    for index, ref in enumerate(refs[:-2]):
        owner = core_ref[0] if index < chunks else 1 - core_ref[0]
        start = pl.multiple_of((owner * chunks + index % chunks) * rows, rows)
        copies.append(pltpu.make_async_copy(ref, out_ref.at[pl.ds(start, rows)], sems.at[index]))
    for copy in copies:
        copy.start()
    for copy in copies:
        copy.wait()


def lay(core, blocks):
    rows, width = blocks[0].shape
    return pl.pallas_call(
        lay_kernel,
        in_specs=[pl.BlockSpec(memory_space=SMEM)] + [whole()] * len(blocks),
        out_specs=pl.BlockSpec(memory_space=pl.ANY),
        out_shape=jax.ShapeDtypeStruct((len(blocks) * rows, width), BF),
        scratch_shapes=[pltpu.SemaphoreType.DMA((len(blocks),))],
        compiler_params=params(6),
        cost_estimate=cost(0, 4 * len(blocks) * rows * width),
        name="lay",
    )(core, *blocks)


def shards(features, ln_gain, ln_bias, projection, stream, norm_gain, cotangent, slots):
    n_img = lax.axis_size("img")
    n_ctx = lax.axis_size("ctx")
    n_tp = lax.axis_size("tp")
    merged = slots.shape[0]
    window = ln_gain.shape[1]
    tok_rows, width = stream.shape
    owners = n_img * n_ctx
    capacity = 2 * merged // owners
    slot_count = owners * capacity
    full_width = width * n_tp

    core_pairs = [(t, t ^ 1) for t in range(n_tp)]
    far_pairs = [(t, t ^ 2) for t in range(n_tp)]
    core = (lax.axis_index("tp") % 2).astype(jnp.int32).reshape(1)

    zy = jnp.stack([lax.axis_index("ctx") // SIDE, lax.axis_index("ctx") % SIDE]).astype(jnp.int32)

    def moved(array, axis, by):
        pairs = []
        for z in range(SIDE):
            for y in range(SIDE):
                to = ((z + by) % SIDE, y) if axis == 0 else (z, (y + by) % SIDE)
                pairs.append((z * SIDE + y, to[0] * SIDE + to[1]))
        return lax.ppermute(array, "ctx", pairs)

    half = window // 2
    share = projection.shape[2]
    first_weight = lax.all_gather(projection[0, :half], "ctx", axis=1, tiled=True)
    first_weight = first_weight.reshape(-1, width)
    block = projection[0, half:].reshape(half * share, width)
    cuts = (block[:, : width // 2], block[:, width // 2 :])
    moves = (1, -1, 2)
    near_blocks = [[cuts[part]] + [moved(cuts[part], 1 - part, by) for by in moves] for part in range(2)]

    target = slots // tok_rows
    ids = jnp.arange(merged)
    earlier = (target[:, None] == target[None, :]) & (ids[:, None] < ids[None, :])
    rank = jnp.sum(earlier.astype(jnp.int32), axis=0)
    slot = target * capacity + rank
    local = slots - target * tok_rows
    packed = jnp.max(
        jnp.where(jnp.arange(slot_count)[:, None] == slot[None, :], local[None, :], -1), axis=1
    )
    asked = lax.all_to_all(
        packed.reshape(owners, capacity), ("img", "ctx"), split_axis=0, concat_axis=0, tiled=True
    )
    asked, near_blocks = lax.optimization_barrier((asked, near_blocks))

    held = collect(asked.reshape(slot_count, 1), stream, cotangent[0])
    came = lax.all_to_all(
        held.reshape(owners, capacity, 2 * width),
        ("img", "ctx"), split_axis=0, concat_axis=0, tiled=True,
    ).reshape(slot_count, 2 * width)

    pieces = []
    for part in range(2):
        stacked = stack(zy[1 - part : 2 - part], near_blocks[part])
        pieces += [stacked] + [moved(stacked, part, by) for by in moves]

    gain = ln_gain[0]
    lifted_first, lifted_second, xw, stat = layer_norm(features[0], gain, ln_bias[0])
    acc, second_weight = second(zy, lifted_second, pieces)
    second_weight = second_weight.reshape(-1, width)
    base, up = unpack(slot.reshape(merged, 1), came, norm_gain)
    visual, state, sums = merge(lifted_first, acc, base, up, first_weight)

    near = sums + lax.ppermute(sums, "tp", core_pairs)
    far = lax.ppermute(near, "tp", far_pairs)

    img = lax.axis_index("img").astype(jnp.int32)
    in_img = slot_count // n_img
    relative = lax.rem(slot + img * in_img, slot_count)
    stay, cross = pack(relative.reshape(1, merged), visual, slot_count)
    crossed = lax.ppermute(cross, "img", [(i, 1 - i) for i in range(n_img)])

    chunks = 2
    weights = (first_weight, second_weight)
    parts = backward(core, state, up, near, far, weights, chunks, full_width)
    parts, crossed = lax.optimization_barrier((parts, crossed))
    pairs = []
    for chunk in range(chunks):
        got = lax.ppermute(parts[chunks + chunk], "tp", core_pairs)
        pairs.append((parts[chunk] + got.astype(F32)).astype(BF))
    beyond = [lax.ppermute(pair, "tp", far_pairs) for pair in pairs]

    stay, crossed, pairs[0] = lax.optimization_barrier((stay, crossed, pairs[0]))
    send = jnp.concatenate(
        [x.reshape(n_ctx, capacity, width) for x in (stay, crossed)], axis=1
    )
    arrived = lax.all_to_all(send, "ctx", split_axis=0, concat_axis=0, tiled=True)
    by_img = jnp.stack([
        lax.dynamic_index_in_dim(asked.reshape(n_img, n_ctx, capacity), i, 0, keepdims=False)
        for i in (img, 1 - img)
    ], axis=1)
    new_stream = place(
        by_img.reshape(1, slot_count), arrived.reshape(slot_count, width), stream
    )

    own_out, got_out = [], []
    for chunk in range(chunks):
        out = finish(core * chunks + chunk, pairs[chunk], beyond[chunk], xw, stat, gain)
        own_out.append(out)
        got_out.append(lax.ppermute(out, "tp", core_pairs))
    grad = lay(core, own_out + got_out)
    return (new_stream, grad[None])


def solution(mesh):
    placed = (
        P(None, ("img", "ctx"), None),
        P(),
        P(),
        P(None, None, "ctx", "tp"),
        P(("img", "ctx"), "tp"),
        P(None, "tp"),
        P(None, ("img", "ctx"), "tp"),
        P(("img", "ctx")),
    )
    return jax.shard_map(
        shards,
        mesh=mesh,
        in_specs=placed,
        out_specs=(P(("img", "ctx"), "tp"), P(None, ("img", "ctx"), None)),
        check_vma=False,
    )
```

```python
import jax
import jax.numpy as jnp
from jax import lax
from jax.experimental import pallas as pl
from jax.experimental.pallas import tpu as pltpu
from jax.sharding import PartitionSpec as P


BF = jnp.bfloat16
F32 = jnp.float32
BLOCK = 768


def params(mib):
    return pltpu.CompilerParams(vmem_limit_bytes=mib * 1024 * 1024)


def whole():
    return pl.BlockSpec(memory_space=pltpu.VMEM)


def scalars():
    return pl.BlockSpec(memory_space=pltpu.SMEM)


def anywhere():
    return pl.BlockSpec(memory_space=pl.ANY)


def cost(flops, moved):
    return pl.CostEstimate(flops=flops, bytes_accessed=moved, transcendentals=0)


def eq_hot(shape, dim, index):
    return (lax.broadcasted_iota(jnp.int32, shape, dim) == index).astype(BF)


def window_major(tokens, window):
    n = tokens * window
    row = lax.broadcasted_iota(jnp.int32, (n, n), 0)
    col = lax.broadcasted_iota(jnp.int32, (n, n), 1)
    return (col == (row % tokens) * window + row // tokens).astype(BF)


def patch_major(tokens, window):
    n = tokens * window
    row = lax.broadcasted_iota(jnp.int32, (n, n), 0)
    col = lax.broadcasted_iota(jnp.int32, (n, n), 1)
    return (col == (row % window) * tokens + row // window).astype(BF)


def norm_kernel(core_ref, x_ref, gain_ref, bias_ref, lifted_ref, xw_ref, stat_ref):
    window, width = gain_ref.shape
    tokens = x_ref.shape[0] // window
    full = window * width
    x = jnp.dot(window_major(tokens, window), x_ref[...], preferred_element_type=F32)
    parts = [x[w * tokens : (w + 1) * tokens] for w in range(window)]
    total = sum(jnp.sum(p, axis=1, keepdims=True) for p in parts)
    squares = sum(jnp.sum(p * p, axis=1, keepdims=True) for p in parts)
    mean = total / full
    inv = lax.rsqrt(squares / full - mean * mean + 1e-05)
    for w, p in enumerate(parts):
        normed = (p - mean) * inv
        lifted_ref[:, w * width : (w + 1) * width] = (
            normed * gain_ref[w : w + 1].astype(F32) + bias_ref[w : w + 1].astype(F32)
        ).astype(BF)
        xw_ref[w] = p.astype(BF)
    lane = lax.broadcasted_iota(jnp.int32, stat_ref.shape, 1)
    stat_ref[...] = jnp.where(lane == 0, mean, inv)


def layer_norm(core, features, gain, bias):
    rows, width = features.shape
    window = gain.shape[0]
    merged = rows // window
    block = 64
    steps = merged // block
    return pl.pallas_call(
        norm_kernel,
        grid_spec=pltpu.PrefetchScalarGridSpec(
            num_scalar_prefetch=1,
            grid=(steps,),
            in_specs=[
                pl.BlockSpec(
                    (block * window, width),
                    lambda i, c: (lax.rem(i + c[0] * (steps // 2), steps), 0),
                ),
                pl.BlockSpec((window, width), lambda i, c: (0, 0)),
                pl.BlockSpec((window, width), lambda i, c: (0, 0)),
            ],
            out_specs=[
                pl.BlockSpec((block, window * width), lambda i, c: (i, 0)),
                pl.BlockSpec((window, block, width), lambda i, c: (0, i, 0)),
                pl.BlockSpec((block, 128), lambda i, c: (i, 0)),
            ],
        ),
        out_shape=[
            jax.ShapeDtypeStruct((merged, window * width), BF),
            jax.ShapeDtypeStruct((window, merged, width), BF),
            jax.ShapeDtypeStruct((merged, 128), F32),
        ],
        compiler_params=params(12),
        cost_estimate=cost(2 * rows * block * window * width, 6 * rows * width),
        name="layer_norm",
    )(core, features, gain, bias)


def collect_kernel(pos_ref, stream_ref, cot_ref, out_ref):
    slots = pos_ref.shape[0]
    rows, width = stream_ref.shape
    cut = width // 2
    pick = eq_hot((slots, rows), 1, pos_ref[...])
    for img in range(2):
        at = slice(img * cut, (img + 1) * cut)
        for place, ref in enumerate((stream_ref, cot_ref)):
            out_ref[img, :, place * cut : (place + 1) * cut] = jnp.dot(
                pick, ref[:, at], preferred_element_type=F32
            ).astype(BF)


def collect(pos, stream, cot):
    slots = pos.shape[0]
    rows, width = stream.shape
    return pl.pallas_call(
        collect_kernel,
        in_specs=[whole()] * 3,
        out_specs=whole(),
        out_shape=jax.ShapeDtypeStruct((2, slots, width), BF),
        compiler_params=params(12),
        cost_estimate=cost(4 * slots * rows * width, 8 * rows * width),
        name="collect",
    )(pos, stream, cot)


def unpack_kernel(slot_ref, came_ref, ngain_ref, base_ref, up_ref):
    tokens, width = base_ref.shape
    slots = came_ref.shape[0]
    take = eq_hot((tokens, slots), 1, slot_ref[...])
    base_ref[...] = jnp.dot(take, came_ref[:, :width], preferred_element_type=F32)
    up_ref[...] = jnp.dot(take, came_ref[:, width:], preferred_element_type=F32) * ngain_ref[
        ...
    ].astype(F32)


def unpack(slot_col, came, ngain):
    tokens = slot_col.shape[0]
    slots, both = came.shape
    width = both // 2
    return pl.pallas_call(
        unpack_kernel,
        in_specs=[whole()] * 3,
        out_specs=[whole()] * 2,
        out_shape=[jax.ShapeDtypeStruct((tokens, width), F32)] * 2,
        compiler_params=params(12),
        cost_estimate=cost(4 * slots * tokens * width, 8 * tokens * width),
        name="unpack",
    )(slot_col, came, ngain)


def merge_kernel(base_ref, up_ref, w_ref, *refs):
    lifted, (visual_ref, state_ref, stat_ref, held_ref, left_ref, sems) = refs[:-6], refs[-6:]
    steps = range(w_ref.shape[0] // BLOCK)
    copies = []
    for step in steps:
        at = pl.ds(step * BLOCK, BLOCK)
        start = 0
        group = []
        for ref in lifted:
            rows = ref.shape[0]
            group.append((ref.at[:, at], left_ref.at[pl.ds(start, rows), at]))
            start += rows
        group.append((w_ref.at[at], held_ref.at[at]))
        copies.append(
            [pltpu.make_async_copy(a, b, sems.at[step, i]) for i, (a, b) in enumerate(group)]
        )
        for copy in copies[step]:
            copy.start()
    total = None
    for step in steps:
        at = slice(step * BLOCK, (step + 1) * BLOCK)
        for copy in copies[step]:
            copy.wait()
        part = jnp.dot(left_ref[:, at], held_ref[at, :], preferred_element_type=F32)
        total = part if total is None else total + part
    visual = total.astype(BF)
    visual_ref[...] = visual
    state = base_ref[...] + visual.astype(F32)
    state_ref[...] = state
    lane = lax.broadcasted_iota(jnp.int32, (state.shape[0], 128), 1)
    sums = jnp.where(
        lane == 0,
        jnp.sum(state * state, axis=1, keepdims=True),
        jnp.sum(up_ref[...] * state, axis=1, keepdims=True),
    )
    stat_ref[...] = sums.T[: stat_ref.shape[0]]


def merge(base, up, weight, lifted):
    tokens, width = base.shape
    depth = weight.shape[0]
    return pl.pallas_call(
        merge_kernel,
        in_specs=[whole()] * 2 + [anywhere()] * (1 + len(lifted)),
        out_specs=[whole()] * 3,
        out_shape=[
            jax.ShapeDtypeStruct((tokens, width), BF),
            jax.ShapeDtypeStruct((tokens, width), F32),
            jax.ShapeDtypeStruct((8, tokens), F32),
        ],
        scratch_shapes=[
            pltpu.VMEM((depth, width), BF),
            pltpu.VMEM((tokens, depth), BF),
            pltpu.SemaphoreType.DMA((depth // BLOCK, 1 + len(lifted))),
        ],
        compiler_params=params(22),
        cost_estimate=cost(2 * depth * tokens * width, 2 * depth * width),
        name="merge",
    )(base, up, weight, *lifted)


def pack_kernel(slot_ref, visual_ref, stay_ref, cross_ref):
    tokens = visual_ref.shape[0]
    slots = stay_ref.shape[0]
    for shift, out_ref in ((0, stay_ref), (slots, cross_ref)):
        put = eq_hot((slots, tokens), 0, slot_ref[...] - shift)
        out_ref[...] = jnp.dot(put, visual_ref[...], preferred_element_type=F32).astype(BF)


def pack(slot_row, visual, slots):
    tokens, width = visual.shape
    return pl.pallas_call(
        pack_kernel,
        in_specs=[whole()] * 2,
        out_specs=[whole()] * 2,
        out_shape=[jax.ShapeDtypeStruct((slots // 2, width), BF)] * 2,
        compiler_params=params(8),
        cost_estimate=cost(2 * slots * tokens * width, 2 * (slots + tokens) * width),
        name="pack",
    )(slot_row, visual)


RING = 4


def backward_kernel(full_width, chunks, at_ref, state_ref, up_ref, w_ref, *refs):
    stats, refs = refs[:RING], refs[RING:]
    outs, (picked_ref, sums_ref, held_ref, sems) = refs[: 3 * chunks], refs[3 * chunks :]
    copies = []
    for step in range(w_ref.shape[0] // BLOCK):
        at = pl.ds(step * BLOCK, BLOCK)
        copies.append(pltpu.make_async_copy(w_ref.at[at], held_ref.at[at], sems.at[step]))
        copies[step].start()
    tokens = state_ref.shape[0]
    rows = tokens // 2 // RING // chunks
    total = stats[0][...]
    for ref in stats[1:]:
        total = total + ref[...]
    sums_ref[...] = total.T
    img, far = at_ref[0], at_ref[1]
    for core in range(2):
        for chunk in range(chunks):
            for away in range(RING):
                there = lax.rem(2 * far + img + away, RING)
                partner = lax.rem(there + img, 2)
                begin = partner * (tokens // 2) + core * (tokens // 4) + (there // 2) * (tokens // 8)
                at = pl.ds(pl.multiple_of(begin + chunk * rows, rows), rows)
                sums = sums_ref[at, :]
                inv = lax.rsqrt(sums[:, 0:1] / full_width + 1e-06)
                inner = sums[:, 1:2] / full_width
                grad = inv * up_ref[at, :] - state_ref[at, :] * (inv * inv * inv * inner)
                to = ((core * chunks + chunk) * RING + away) * rows
                picked_ref[to : to + rows, :] = grad.astype(BF)
    for step, copy in enumerate(copies):
        cols = slice(step * BLOCK, (step + 1) * BLOCK)
        copy.wait()
        both = lax.dot_general(
            picked_ref[...], held_ref[cols, :], (((1,), (1,)), ((), ())), preferred_element_type=F32
        )
        for chunk in range(chunks):
            own, rest, other = outs[chunk], outs[chunks + chunk], outs[2 * chunks + chunk]
            start = chunk * RING * rows
            own[:, cols] = both[start : start + rows]
            rest[:, cols] = both[start + rows : start + RING * rows]
            start += tokens // 2
            other[:, cols] = both[start : start + RING * rows].astype(BF)


def backward(at, state, up, stats, weight, chunks, full_width):
    depth, width = weight.shape
    tokens = state.shape[0]
    rows = tokens // 2 // RING // chunks
    return pl.pallas_call(
        lambda *refs: backward_kernel(full_width, chunks, *refs),
        in_specs=[scalars()] + [whole()] * 2 + [anywhere()] + [whole()] * RING,
        out_specs=[whole()] * (3 * chunks),
        out_shape=[jax.ShapeDtypeStruct((rows, depth), F32)] * chunks
        + [jax.ShapeDtypeStruct(((RING - 1) * rows, depth), F32)] * chunks
        + [jax.ShapeDtypeStruct((RING * rows, depth), BF)] * chunks,
        scratch_shapes=[
            pltpu.VMEM((tokens, width), BF),
            pltpu.VMEM((tokens, 8), F32),
            pltpu.VMEM((depth, width), BF),
            pltpu.SemaphoreType.DMA((depth // BLOCK,)),
        ],
        compiler_params=params(24),
        cost_estimate=cost(2 * depth * tokens * width, 2 * depth * width),
        name="backward",
    )(at, state, up, weight, *stats)


def pair_kernel(rest_ref, got_ref, *outs):
    rows = outs[0].shape[0]
    for away, out in enumerate(outs):
        at = slice(away * rows, (away + 1) * rows)
        got = slice((away + 1) * rows, (away + 2) * rows)
        out[...] = (rest_ref[at, :] + got_ref[got, :].astype(F32)).astype(BF)


def pair(rest, got):
    rows, depth = got.shape[0] // RING, got.shape[1]
    return pl.pallas_call(
        pair_kernel,
        in_specs=[whole()] * 2,
        out_specs=[whole()] * (RING - 1),
        out_shape=[jax.ShapeDtypeStruct((rows, depth), BF)] * (RING - 1),
        compiler_params=params(12),
        cost_estimate=cost(4 * rows * depth, 24 * rows * depth),
        name="pair",
    )(rest, got)


def finish_kernel(block_ref, own_ref, got_ref, *refs):
    came, (xw_ref, stat_ref, gain_ref, out_ref) = refs[: RING - 1], refs[RING - 1 :]
    window, tokens, width = xw_ref.shape
    full = window * width
    mean = stat_ref[:, 0:1]
    inv = stat_ref[:, 1:2]
    lifted = own_ref[...] + got_ref[...].astype(F32)
    for ref in came:
        lifted = lifted + ref[...].astype(F32)
    scaled = []
    total = 0.0
    inner = 0.0
    for w in range(window):
        g = lifted[:, w * width : (w + 1) * width] * gain_ref[w : w + 1].astype(F32)
        normed = (xw_ref[w].astype(F32) - mean) * inv
        total = total + jnp.sum(g, axis=1, keepdims=True)
        inner = inner + jnp.sum(g * normed, axis=1, keepdims=True)
        scaled.append((g, normed))
    total = total / full
    inner = inner / full
    rows = jnp.concatenate(
        [(inv * (g - total - normed * inner)).astype(BF) for g, normed in scaled], axis=0
    )
    out_ref[...] = jnp.dot(
        patch_major(tokens, window), rows, preferred_element_type=F32
    ).astype(BF)


def finish(block, own, got, came, xw, stat, gain):
    tokens, full = own.shape
    window, width = gain.shape
    same = pl.BlockSpec((tokens, full), lambda i, b: (0, 0))
    return pl.pallas_call(
        finish_kernel,
        grid_spec=pltpu.PrefetchScalarGridSpec(
            num_scalar_prefetch=1,
            grid=(1,),
            in_specs=[same] * (1 + RING)
            + [
                pl.BlockSpec((window, tokens, width), lambda i, b: (0, b[0], 0)),
                pl.BlockSpec((tokens, 128), lambda i, b: (b[0], 0)),
                pl.BlockSpec((window, width), lambda i, b: (0, 0)),
            ],
            out_specs=pl.BlockSpec((tokens * window, width), lambda i, b: (0, 0)),
        ),
        out_shape=jax.ShapeDtypeStruct((tokens * window, width), BF),
        compiler_params=params(12),
        cost_estimate=cost(2 * (tokens * window) ** 2 * width, 8 * window * tokens * width),
        name="finish",
    )(block, own, got, *came, xw, stat, gain)


def place_kernel(img_ref, pos_ref, came_ref, stream_ref, out_ref):
    rows, width = stream_ref.shape
    cut = width // 2
    slots = pos_ref.shape[1]
    put = eq_hot((rows, slots), 0, pos_ref[...])
    for relative in range(2):
        start = pl.multiple_of((img_ref[0] ^ relative) * cut, cut)
        at = pl.ds(start, cut)
        out_ref[:, at] = (
            stream_ref[:, at].astype(F32)
            + jnp.dot(put, came_ref[relative], preferred_element_type=F32)
        ).astype(BF)


def place(img, pos, came, stream):
    rows, width = stream.shape
    return pl.pallas_call(
        place_kernel,
        in_specs=[scalars()] + [whole()] * 3,
        out_specs=whole(),
        out_shape=jax.ShapeDtypeStruct((rows, width), BF),
        compiler_params=params(12),
        cost_estimate=cost(2 * pos.shape[1] * rows * width, 6 * rows * width),
        name="place",
    )(img, pos, came, stream)


def lay_kernel(chunks, at_ref, *refs):
    blocks, (out_ref, sems) = refs[:-2], refs[-2:]
    rows = blocks[0].shape[0]
    copies = []
    for index, ref in enumerate(blocks):
        quarter, chunk = index // chunks, index % chunks
        owner = 2 * (at_ref[0] ^ (quarter // 2)) + (at_ref[1] ^ (quarter % 2))
        start = pl.multiple_of((owner * chunks + chunk) * rows, rows)
        copies.append(pltpu.make_async_copy(ref, out_ref.at[pl.ds(start, rows)], sems.at[index]))
    for copy in copies:
        copy.start()
    for copy in copies:
        copy.wait()


def lay(at, blocks, chunks):
    rows, width = blocks[0].shape
    return pl.pallas_call(
        lambda *refs: lay_kernel(chunks, *refs),
        in_specs=[scalars()] + [anywhere()] * len(blocks),
        out_specs=anywhere(),
        out_shape=jax.ShapeDtypeStruct((len(blocks) * rows, width), BF),
        scratch_shapes=[pltpu.SemaphoreType.DMA((len(blocks),))],
        compiler_params=params(4),
        cost_estimate=cost(0, 4 * len(blocks) * rows * width),
        name="lay",
    )(at, *blocks)


def swap_lanes(array, count):
    cuts = [array[:, i : i + count] for i in range(0, array.shape[1], count)]
    return jnp.concatenate([cuts[i ^ 1] for i in range(len(cuts))], axis=1)


def shards(features, ln_gain, ln_bias, projection, stream, norm_gain, cotangent, slots):
    n_img = lax.axis_size("img")
    n_ctx = lax.axis_size("ctx")
    n_tp = lax.axis_size("tp")
    merged = slots.shape[0]
    tok_rows, width = stream.shape
    owners = n_img * n_ctx
    capacity = 2 * merged // owners
    slot_count = owners * capacity
    full_width = width * n_tp
    cut = width // n_img

    img = lax.axis_index("img").astype(jnp.int32)
    tp = lax.axis_index("tp").astype(jnp.int32)
    core, far_half = tp % 2, tp // 2
    core_in = core.reshape(1)

    flip = [(i, 1 - i) for i in range(n_img)]
    core_pairs = [(t, t ^ 1) for t in range(n_tp)]
    far_pairs = [(t, t ^ 2) for t in range(n_tp)]

    def along_x(array, by):
        pairs = []
        for i in range(n_img):
            for t in range(n_tp):
                x = (2 * (t // 2) + i + by) % RING
                pairs.append((i * n_tp + t, (x % 2) * n_tp + 2 * (x // 2) + t % 2))
        return lax.ppermute(array, ("img", "tp"), pairs)

    own_columns = lax.dynamic_slice_in_dim(projection[0], img * cut, cut, axis=2)
    weight = lax.all_gather(own_columns, "ctx", axis=1, tiled=True).reshape(-1, cut)

    slots = jnp.roll(slots, -core * (merged // 2))
    target = slots // tok_rows
    ids = jnp.arange(merged)
    earlier = (target[:, None] == target[None, :]) & (ids[:, None] < ids[None, :])
    rank = jnp.sum(earlier.astype(jnp.int32), axis=0)
    slot = target * capacity + rank
    local = slots - target * tok_rows
    packed = jnp.max(
        jnp.where(jnp.arange(slot_count)[:, None] == slot[None, :], local[None, :], -1), axis=1
    )
    asked = lax.all_to_all(
        packed.reshape(owners, capacity), ("img", "ctx"), split_axis=0, concat_axis=0, tiled=True
    )
    asked = asked.reshape(n_img, n_ctx, capacity).transpose(1, 0, 2)
    held = collect(asked.reshape(slot_count, 1), stream, cotangent[0])
    came = lax.all_to_all(
        held.reshape(owners, n_img * capacity, width),
        ("img", "ctx"), split_axis=0, concat_axis=0, tiled=True,
    ).reshape(n_img * slot_count, width)
    paired = target * (n_img * capacity) + rank + img * capacity
    paired = jnp.concatenate([paired, lax.ppermute(paired, "img", flip)])

    gain = ln_gain[0]
    lifted, xw, stat = layer_norm(core_in, features[0], gain, ln_bias[0])
    next_mine = lax.ppermute(lifted[: merged // 2], "img", flip)
    next_other = lax.ppermute(next_mine, "tp", core_pairs)

    own_gain = lax.dynamic_slice_in_dim(norm_gain, img * cut, cut, axis=1)
    base, up = unpack(paired.reshape(-1, 1), came, own_gain)
    visual, state, sums = merge(base, up, weight, (lifted, next_mine, next_other))

    quarter = merged // 2
    near = sums + lax.ppermute(swap_lanes(sums, quarter), "tp", core_pairs)
    turned = swap_lanes(near, merged)
    stats = [near] + [along_x(near if by == 2 else turned, by) for by in (1, 2, 3)]

    in_img = n_img * slot_count // 2
    relative = lax.rem(paired + img * in_img, 2 * in_img)
    stay, cross = pack(relative.reshape(1, -1), visual, 2 * in_img)
    cross, stats = lax.optimization_barrier((cross, stats))
    crossed = lax.ppermute(cross, "img", flip)

    chunks = 2
    at = jnp.stack([img, far_half])
    parts = backward(at, state, up, stats, weight, chunks, full_width)
    own, rest, other = (parts[i * chunks : (i + 1) * chunks] for i in range(3))
    got = [lax.ppermute(o, "tp", core_pairs) for o in other]
    got[0], crossed = lax.optimization_barrier((got[0], crossed))
    sent = [pair(rest[c], got[c]) for c in range(chunks)]
    came_back = [[along_x(sent[c][by - 1], by) for by in (1, 2, 3)] for c in range(chunks)]

    stay, crossed, sent[0] = lax.optimization_barrier((stay, crossed, sent[0]))
    send = jnp.concatenate(
        [x.reshape(n_ctx, 1, n_img * capacity, cut) for x in (stay, crossed)], axis=1
    )
    arrived = lax.all_to_all(send, "ctx", split_axis=0, concat_axis=0, tiled=True)
    arrived = arrived.transpose(1, 0, 2, 3).reshape(n_img, slot_count, cut)
    new_stream = place(img.reshape(1), asked.reshape(1, slot_count), arrived, stream)

    quarters = [[], [], [], []]
    for c in range(chunks):
        block = (far_half * chunks + c).reshape(1)
        out = finish(block, own[c], got[c], came_back[c], xw, stat, gain)
        beyond = lax.ppermute(out, "tp", far_pairs)
        quarters[0].append(out)
        quarters[1].append(beyond)
        quarters[2].append(lax.ppermute(out, "tp", core_pairs))
        quarters[3].append(lax.ppermute(beyond, "tp", core_pairs))
    grad = lay(jnp.stack([core, far_half]), sum(quarters, []), chunks)
    return (new_stream, grad[None])


def solution(mesh):
    placed = (
        P(None, ("img", "ctx"), None),
        P(),
        P(),
        P(None, None, "ctx", "tp"),
        P(("img", "ctx"), "tp"),
        P(None, "tp"),
        P(None, ("img", "ctx"), "tp"),
        P(("img", "ctx")),
    )
    return jax.shard_map(
        shards,
        mesh=mesh,
        in_specs=placed,
        out_specs=(P(("img", "ctx"), "tp"), P(None, ("img", "ctx"), None)),
        check_vma=False,
    )
```

```python
import jax
import jax.numpy as jnp
from jax import lax
from jax.experimental import pallas as pl
from jax.experimental.pallas import tpu as pltpu
from jax.sharding import PartitionSpec as P


BF = jnp.bfloat16
F32 = jnp.float32
BLOCK = 768


def params():
    return pltpu.CompilerParams(vmem_limit_bytes=60 * 1024 * 1024)


def full(array):
    return pl.BlockSpec(array.shape, lambda *_: (0,) * len(array.shape))


def fulls(arrays):
    return [full(a) for a in arrays]


def shape(dims, kind):
    return jax.ShapeDtypeStruct(dims, kind)


def scalars():
    return pl.BlockSpec(memory_space=pltpu.SMEM)


def anywhere():
    return pl.BlockSpec(memory_space=pl.ANY)


def cost(flops, moved):
    return pl.CostEstimate(flops=flops, bytes_accessed=moved, transcendentals=0)


def eq_hot(shape, dim, index):
    return (lax.broadcasted_iota(jnp.int32, shape, dim) == index).astype(BF)


def window_major(tokens, window):
    n = tokens * window
    row = lax.broadcasted_iota(jnp.int32, (n, n), 0)
    col = lax.broadcasted_iota(jnp.int32, (n, n), 1)
    return (col == (row % tokens) * window + row // tokens).astype(BF)


def patch_major(tokens, window):
    n = tokens * window
    row = lax.broadcasted_iota(jnp.int32, (n, n), 0)
    col = lax.broadcasted_iota(jnp.int32, (n, n), 1)
    return (col == (row % window) * tokens + row // window).astype(BF)


def norm_kernel(core_ref, x_ref, gain_ref, bias_ref, lifted_ref, xw_ref, stat_ref):
    window, width = gain_ref.shape
    tokens = x_ref.shape[0] // window
    full = window * width
    x = jnp.dot(window_major(tokens, window), x_ref[...], preferred_element_type=F32)
    parts = [x[w * tokens : (w + 1) * tokens] for w in range(window)]
    total = sum(jnp.sum(p, axis=1, keepdims=True) for p in parts)
    squares = sum(jnp.sum(p * p, axis=1, keepdims=True) for p in parts)
    mean = total / full
    inv = lax.rsqrt(squares / full - mean * mean + 1e-05)
    for w, p in enumerate(parts):
        normed = (p - mean) * inv
        lifted_ref[:, w * width : (w + 1) * width] = (
            normed * gain_ref[w : w + 1].astype(F32) + bias_ref[w : w + 1].astype(F32)
        ).astype(BF)
        xw_ref[w] = p.astype(BF)
    lane = lax.broadcasted_iota(jnp.int32, stat_ref.shape, 1)
    stat_ref[...] = jnp.where(lane == 0, mean, inv)


def layer_norm(core, features, gain, bias):
    rows, width = features.shape
    window = gain.shape[0]
    merged = rows // window
    block = 64
    steps = merged // block
    return pl.pallas_call(
        norm_kernel,
        grid_spec=pltpu.PrefetchScalarGridSpec(
            num_scalar_prefetch=1,
            grid=(steps,),
            in_specs=[
                pl.BlockSpec(
                    (block * window, width),
                    lambda i, c: (lax.rem(i + c[0] * (steps // 2), steps), 0),
                ),
                pl.BlockSpec((window, width), lambda i, c: (0, 0)),
                pl.BlockSpec((window, width), lambda i, c: (0, 0)),
            ],
            out_specs=[
                pl.BlockSpec((block, window * width), lambda i, c: (i, 0)),
                pl.BlockSpec((window, block, width), lambda i, c: (0, i, 0)),
                pl.BlockSpec((block, 128), lambda i, c: (i, 0)),
            ],
        ),
        out_shape=[
            shape((merged, window * width), BF),
            shape((window, merged, width), BF),
            shape((merged, 128), F32),
        ],
        compiler_params=params(),
        cost_estimate=cost(2 * rows * block * window * width, 6 * rows * width),
        name="layer_norm",
    )(core, features, gain, bias)


def collect_kernel(pos_ref, stream_ref, cot_ref, out_ref):
    slots = pos_ref.shape[0]
    rows, width = stream_ref.shape
    cut = width // 2
    pick = eq_hot((slots, rows), 1, pos_ref[...])
    for img in range(2):
        at = slice(img * cut, (img + 1) * cut)
        for place, ref in enumerate((stream_ref, cot_ref)):
            out_ref[img, :, place * cut : (place + 1) * cut] = jnp.dot(
                pick, ref[:, at], preferred_element_type=F32
            ).astype(BF)


def collect(pos, stream, cot):
    slots = pos.shape[0]
    rows, width = stream.shape
    out = shape((2, slots, width), BF)
    return pl.pallas_call(
        collect_kernel,
        grid=(1,),
        in_specs=fulls((pos, stream, cot)),
        out_specs=full(out),
        out_shape=out,
        compiler_params=params(),
        cost_estimate=cost(4 * slots * rows * width, 8 * rows * width),
        name="collect",
    )(pos, stream, cot)


def unpack_kernel(slot_ref, came_ref, base_ref, cot_ref):
    tokens, width = base_ref.shape
    slots = came_ref.shape[0]
    take = eq_hot((tokens, slots), 1, slot_ref[...])
    for start, out_ref in ((0, base_ref), (width, cot_ref)):
        out_ref[...] = jnp.dot(
            take, came_ref[:, start : start + width], preferred_element_type=F32
        ).astype(BF)


def unpack(slot_col, came):
    tokens = slot_col.shape[0]
    slots, both = came.shape
    width = both // 2
    outs = [shape((tokens, width), BF)] * 2
    return pl.pallas_call(
        unpack_kernel,
        grid=(1,),
        in_specs=fulls((slot_col, came)),
        out_specs=fulls(outs),
        out_shape=outs,
        compiler_params=params(),
        cost_estimate=cost(4 * slots * tokens * width, 8 * tokens * width),
        name="unpack",
    )(slot_col, came)


def merge_kernel(base_ref, cot_ref, ngain_ref, w_ref, *refs):
    lifted, (visual_ref, state_ref, stat_ref, held_ref, left_ref, sems) = refs[:-6], refs[-6:]
    steps = range(w_ref.shape[0] // BLOCK)
    copies = []
    for step in steps:
        at = pl.ds(step * BLOCK, BLOCK)
        start = 0
        group = []
        for ref in lifted:
            rows = ref.shape[0]
            group.append((ref.at[:, at], left_ref.at[pl.ds(start, rows), at]))
            start += rows
        group.append((w_ref.at[at], held_ref.at[at]))
        copies.append(
            [pltpu.make_async_copy(a, b, sems.at[step, i]) for i, (a, b) in enumerate(group)]
        )
        for copy in copies[step]:
            copy.start()
    total = None
    for step in steps:
        at = slice(step * BLOCK, (step + 1) * BLOCK)
        for copy in copies[step]:
            copy.wait()
        part = jnp.dot(left_ref[:, at], held_ref[at, :], preferred_element_type=F32)
        total = part if total is None else total + part
    visual = total.astype(BF)
    visual_ref[...] = visual
    state = base_ref[...].astype(F32) + visual.astype(F32)
    state_ref[...] = state
    up = ngain_ref[...].astype(F32) * cot_ref[...].astype(F32)
    lane = lax.broadcasted_iota(jnp.int32, (state.shape[0], 128), 1)
    sums = jnp.where(
        lane == 0,
        jnp.sum(state * state, axis=1, keepdims=True),
        jnp.sum(up * state, axis=1, keepdims=True),
    )
    stat_ref[...] = sums.T[: stat_ref.shape[0]]


def merge(base, cot, ngain, weight, lifted):
    tokens, width = base.shape
    depth = weight.shape[0]
    outs = [shape((tokens, width), BF), shape((tokens, width), F32), shape((8, tokens), F32)]
    return pl.pallas_call(
        merge_kernel,
        grid=(1,),
        in_specs=fulls((base, cot, ngain)) + [anywhere()] * (1 + len(lifted)),
        out_specs=fulls(outs),
        out_shape=outs,
        scratch_shapes=[
            pltpu.VMEM((depth, width), BF),
            pltpu.VMEM((tokens, depth), BF),
            pltpu.SemaphoreType.DMA((depth // BLOCK, 1 + len(lifted))),
        ],
        compiler_params=params(),
        cost_estimate=cost(2 * depth * tokens * width, 2 * depth * width),
        name="merge",
    )(base, cot, ngain, weight, *lifted)


def pack_kernel(slot_ref, visual_ref, stay_ref, cross_ref):
    tokens = visual_ref.shape[0]
    slots = stay_ref.shape[0]
    for shift, out_ref in ((0, stay_ref), (slots, cross_ref)):
        put = eq_hot((slots, tokens), 0, slot_ref[...] - shift)
        out_ref[...] = jnp.dot(put, visual_ref[...], preferred_element_type=F32).astype(BF)


def pack(slot_row, visual, slots):
    tokens, width = visual.shape
    outs = [shape((slots // 2, width), BF)] * 2
    return pl.pallas_call(
        pack_kernel,
        grid=(1,),
        in_specs=fulls((slot_row, visual)),
        out_specs=fulls(outs),
        out_shape=outs,
        compiler_params=params(),
        cost_estimate=cost(2 * slots * tokens * width, 2 * (slots + tokens) * width),
        name="pack",
    )(slot_row, visual)


RING = 4


def backward_kernel(full_width, chunks, at_ref, state_ref, cot_ref, ngain_ref, w_ref, *refs):
    stats, refs = refs[:RING], refs[RING:]
    outs, (picked_ref, sums_ref) = refs[: 3 * chunks], refs[3 * chunks :]
    tokens = state_ref.shape[0]
    rows = tokens // 2 // RING // chunks

    @pl.when(pl.program_id(0) == 0)
    def _():
        total = stats[0][...]
        for ref in stats[1:]:
            total = total + ref[...]
        sums_ref[...] = total.T
        img, far = at_ref[0], at_ref[1]
        gain = ngain_ref[...].astype(F32)
        for core in range(2):
            for chunk in range(chunks):
                for away in range(RING):
                    there = lax.rem(2 * far + img + away, RING)
                    partner = lax.rem(there + img, 2)
                    begin = partner * (tokens // 2) + core * (tokens // 4) + (there // 2) * (tokens // 8)
                    at = pl.ds(pl.multiple_of(begin + chunk * rows, rows), rows)
                    sums = sums_ref[at, :]
                    inv = lax.rsqrt(sums[:, 0:1] / full_width + 1e-06)
                    inner = sums[:, 1:2] / full_width
                    up = gain * cot_ref[at, :].astype(F32)
                    grad = inv * up - state_ref[at, :] * (inv * inv * inv * inner)
                    to = ((core * chunks + chunk) * RING + away) * rows
                    picked_ref[to : to + rows, :] = grad.astype(BF)

    both = lax.dot_general(
        picked_ref[...], w_ref[...], (((1,), (1,)), ((), ())), preferred_element_type=F32
    )
    for chunk in range(chunks):
        own, rest, other = outs[chunk], outs[chunks + chunk], outs[2 * chunks + chunk]
        start = chunk * RING * rows
        own[...] = both[start : start + rows]
        rest[...] = both[start + rows : start + RING * rows].astype(BF)
        start += tokens // 2
        other[...] = both[start : start + RING * rows].astype(BF)


def backward(at, state, cot, ngain, stats, weight, chunks, full_width):
    depth, width = weight.shape
    tokens = state.shape[0]
    rows = tokens // 2 // RING // chunks
    outs = (
        [shape((rows, depth), F32)] * chunks
        + [shape(((RING - 1) * rows, depth), BF)] * chunks
        + [shape((RING * rows, depth), BF)] * chunks
    )
    return pl.pallas_call(
        lambda *refs: backward_kernel(full_width, chunks, *refs),
        grid=(depth // BLOCK,),
        in_specs=[scalars()]
        + fulls((state, cot, ngain))
        + [pl.BlockSpec((BLOCK, width), lambda i: (i, 0))]
        + fulls(stats),
        out_specs=[pl.BlockSpec((o.shape[0], BLOCK), lambda i: (0, i)) for o in outs],
        out_shape=outs,
        scratch_shapes=[pltpu.VMEM((tokens, width), BF), pltpu.VMEM((tokens, 8), F32)],
        compiler_params=params(),
        cost_estimate=cost(2 * depth * tokens * width, 2 * depth * width),
        name="backward",
    )(at, state, cot, ngain, weight, *stats)


def pair_kernel(rest_ref, got_ref, *outs):
    rows = outs[0].shape[0]
    for away, out in enumerate(outs):
        at = slice(away * rows, (away + 1) * rows)
        got = slice((away + 1) * rows, (away + 2) * rows)
        out[...] = (rest_ref[at, :].astype(F32) + got_ref[got, :].astype(F32)).astype(BF)


def pair(rest, got):
    rows, depth = got.shape[0] // RING, got.shape[1]
    cols = depth // 4
    outs = [shape((rows, depth), BF)] * (RING - 1)
    return pl.pallas_call(
        pair_kernel,
        grid=(depth // cols,),
        in_specs=[pl.BlockSpec((a.shape[0], cols), lambda i: (0, i)) for a in (rest, got)],
        out_specs=[pl.BlockSpec((rows, cols), lambda i: (0, i))] * (RING - 1),
        out_shape=outs,
        compiler_params=params(),
        cost_estimate=cost(4 * rows * depth, 24 * rows * depth),
        name="pair",
    )(rest, got)


def finish_kernel(block_ref, own_ref, got_ref, *refs):
    came, (xw_ref, stat_ref, gain_ref, out_ref) = refs[: RING - 1], refs[RING - 1 :]
    window, tokens, width = xw_ref.shape
    full = window * width
    mean = stat_ref[:, 0:1]
    inv = stat_ref[:, 1:2]
    lifted = own_ref[...] + got_ref[...].astype(F32)
    for ref in came:
        lifted = lifted + ref[...].astype(F32)
    scaled = []
    total = 0.0
    inner = 0.0
    for w in range(window):
        g = lifted[:, w * width : (w + 1) * width] * gain_ref[w : w + 1].astype(F32)
        normed = (xw_ref[w].astype(F32) - mean) * inv
        total = total + jnp.sum(g, axis=1, keepdims=True)
        inner = inner + jnp.sum(g * normed, axis=1, keepdims=True)
        scaled.append((g, normed))
    total = total / full
    inner = inner / full
    rows = jnp.concatenate(
        [(inv * (g - total - normed * inner)).astype(BF) for g, normed in scaled], axis=0
    )
    out_ref[...] = jnp.dot(
        patch_major(tokens, window), rows, preferred_element_type=F32
    ).astype(BF)


def finish(block, own, got, came, xw, stat, gain):
    tokens, depth = own.shape
    window, width = gain.shape
    same = pl.BlockSpec((tokens, depth), lambda i, b: (0, 0))
    return pl.pallas_call(
        finish_kernel,
        grid_spec=pltpu.PrefetchScalarGridSpec(
            num_scalar_prefetch=1,
            grid=(1,),
            in_specs=[same] * (1 + RING)
            + [
                pl.BlockSpec((window, tokens, width), lambda i, b: (0, b[0], 0)),
                pl.BlockSpec((tokens, 128), lambda i, b: (b[0], 0)),
                pl.BlockSpec((window, width), lambda i, b: (0, 0)),
            ],
            out_specs=pl.BlockSpec((tokens * window, width), lambda i, b: (0, 0)),
        ),
        out_shape=shape((tokens * window, width), BF),
        compiler_params=params(),
        cost_estimate=cost(2 * (tokens * window) ** 2 * width, 8 * window * tokens * width),
        name="finish",
    )(block, own, got, *came, xw, stat, gain)


def place_kernel(img_ref, pos_ref, came_ref, stream_ref, out_ref):
    rows, width = stream_ref.shape
    cut = width // 2
    slots = pos_ref.shape[1]
    put = eq_hot((rows, slots), 0, pos_ref[...])
    for relative in range(2):
        start = pl.multiple_of((img_ref[0] ^ relative) * cut, cut)
        at = pl.ds(start, cut)
        out_ref[:, at] = (
            stream_ref[:, at].astype(F32)
            + jnp.dot(put, came_ref[relative], preferred_element_type=F32)
        ).astype(BF)


def place(img, pos, came, stream):
    rows, width = stream.shape
    return pl.pallas_call(
        place_kernel,
        grid=(1,),
        in_specs=[scalars()] + fulls((pos, came, stream)),
        out_specs=full(stream),
        out_shape=shape((rows, width), BF),
        compiler_params=params(),
        cost_estimate=cost(2 * pos.shape[1] * rows * width, 6 * rows * width),
        name="place",
    )(img, pos, came, stream)


def lay_kernel(chunks, at_ref, *refs):
    blocks, (out_ref, sems) = refs[:-2], refs[-2:]
    rows = blocks[0].shape[0]
    copies = []
    for index, ref in enumerate(blocks):
        quarter, chunk = index // chunks, index % chunks
        owner = 2 * (at_ref[0] ^ (quarter // 2)) + (at_ref[1] ^ (quarter % 2))
        start = pl.multiple_of((owner * chunks + chunk) * rows, rows)
        copies.append(pltpu.make_async_copy(ref, out_ref.at[pl.ds(start, rows)], sems.at[index]))
    for copy in copies:
        copy.start()
    for copy in copies:
        copy.wait()


def lay(at, blocks, chunks):
    rows, width = blocks[0].shape
    return pl.pallas_call(
        lambda *refs: lay_kernel(chunks, *refs),
        grid=(1,),
        in_specs=[scalars()] + fulls(blocks),
        out_specs=anywhere(),
        out_shape=shape((len(blocks) * rows, width), BF),
        scratch_shapes=[pltpu.SemaphoreType.DMA((len(blocks),))],
        compiler_params=params(),
        cost_estimate=cost(0, 4 * len(blocks) * rows * width),
        name="lay",
    )(at, *blocks)


def swap_lanes(array, count):
    cuts = [array[:, i : i + count] for i in range(0, array.shape[1], count)]
    return jnp.concatenate([cuts[i ^ 1] for i in range(len(cuts))], axis=1)


def shards(features, ln_gain, ln_bias, projection, stream, norm_gain, cotangent, slots):
    n_img = lax.axis_size("img")
    n_ctx = lax.axis_size("ctx")
    n_tp = lax.axis_size("tp")
    merged = slots.shape[0]
    tok_rows, width = stream.shape
    owners = n_img * n_ctx
    capacity = 2 * merged // owners
    slot_count = owners * capacity
    full_width = width * n_tp
    cut = width // n_img

    img = lax.axis_index("img").astype(jnp.int32)
    tp = lax.axis_index("tp").astype(jnp.int32)
    core, far_half = tp % 2, tp // 2
    core_in = core.reshape(1)

    flip = [(i, 1 - i) for i in range(n_img)]
    core_pairs = [(t, t ^ 1) for t in range(n_tp)]
    far_pairs = [(t, t ^ 2) for t in range(n_tp)]

    def along_x(array, by):
        pairs = []
        for i in range(n_img):
            for t in range(n_tp):
                x = (2 * (t // 2) + i + by) % RING
                pairs.append((i * n_tp + t, (x % 2) * n_tp + 2 * (x // 2) + t % 2))
        return lax.ppermute(array, ("img", "tp"), pairs)

    own_columns = lax.dynamic_slice_in_dim(projection[0], img * cut, cut, axis=2)
    weight = lax.all_gather(own_columns, "ctx", axis=1, tiled=True).reshape(-1, cut)

    slots = jnp.roll(slots, -core * (merged // 2))
    target = slots // tok_rows
    ids = jnp.arange(merged)
    earlier = (target[:, None] == target[None, :]) & (ids[:, None] < ids[None, :])
    rank = jnp.sum(earlier.astype(jnp.int32), axis=0)
    slot = target * capacity + rank
    local = slots - target * tok_rows
    packed = jnp.max(
        jnp.where(jnp.arange(slot_count)[:, None] == slot[None, :], local[None, :], -1), axis=1
    )
    asked = lax.all_to_all(
        packed.reshape(owners, capacity), ("img", "ctx"), split_axis=0, concat_axis=0, tiled=True
    )
    asked = asked.reshape(n_img, n_ctx, capacity).transpose(1, 0, 2)
    features, asked = lax.optimization_barrier((features, asked))
    gain = ln_gain[0]
    lifted, xw, stat = layer_norm(core_in, features[0], gain, ln_bias[0])
    sent_on = [lifted[: merged // 4], lifted[merged // 4 : merged // 2]]
    sent_on, asked = lax.optimization_barrier((sent_on, asked))
    next_mine = [along_x(sent_on[0], 1), along_x(sent_on[1], -1)]
    next_other = [lax.ppermute(x, "tp", core_pairs) for x in next_mine]
    held = collect(asked.reshape(slot_count, 1), stream, cotangent[0])
    came = lax.all_to_all(
        held.reshape(owners, n_img * capacity, width),
        ("img", "ctx"), split_axis=0, concat_axis=0, tiled=True,
    ).reshape(n_img * slot_count, width)
    paired = target * (n_img * capacity) + rank + img * capacity
    paired = jnp.concatenate([paired, lax.ppermute(paired, "img", flip)])

    own_gain = lax.dynamic_slice_in_dim(norm_gain, img * cut, cut, axis=1)
    base, cot = unpack(paired.reshape(-1, 1), came)
    visual, state, sums = merge(base, cot, own_gain, weight, [lifted] + next_mine + next_other)

    quarter = merged // 2
    near = sums + lax.ppermute(swap_lanes(sums, quarter), "tp", core_pairs)
    turned = swap_lanes(near, merged)
    stats = [near] + [along_x(near if by == 2 else turned, by) for by in (1, 2, 3)]

    in_img = n_img * slot_count // 2
    relative = lax.rem(paired + img * in_img, 2 * in_img)
    stay, cross = pack(relative.reshape(1, -1), visual, 2 * in_img)
    cross, stats = lax.optimization_barrier((cross, stats))
    crossed = lax.ppermute(cross, "img", flip)

    chunks = 2
    at = jnp.stack([img, far_half])
    parts = backward(at, state, cot, own_gain, stats, weight, chunks, full_width)
    parts, crossed = lax.optimization_barrier((parts, crossed))
    own, rest, other = (parts[i * chunks : (i + 1) * chunks] for i in range(3))
    got = [lax.ppermute(o, "tp", core_pairs) for o in other]
    sent = [pair(rest[c], got[c]) for c in range(chunks)]
    stay, crossed, sent[1] = lax.optimization_barrier((stay, crossed, sent[1]))
    came_back = [[along_x(sent[c][by - 1], by) for by in (1, 2, 3)] for c in range(chunks)]
    send = jnp.concatenate(
        [x.reshape(n_ctx, 1, n_img * capacity, cut) for x in (stay, crossed)], axis=1
    )
    arrived = lax.all_to_all(send, "ctx", split_axis=0, concat_axis=0, tiled=True)
    arrived = arrived.transpose(1, 0, 2, 3).reshape(n_img, slot_count, cut)
    new_stream = place(img.reshape(1), asked.reshape(1, slot_count), arrived, stream)

    new_stream, came_back[1] = lax.optimization_barrier((new_stream, came_back[1]))

    quarters = [[], [], [], []]
    for c in range(chunks):
        block = (far_half * chunks + c).reshape(1)
        out = finish(block, own[c], got[c], came_back[c], xw, stat, gain)
        beyond = lax.ppermute(out, "tp", far_pairs)
        quarters[0].append(out)
        quarters[1].append(beyond)
        quarters[2].append(lax.ppermute(out, "tp", core_pairs))
        quarters[3].append(lax.ppermute(beyond, "tp", core_pairs))
    grad = lay(jnp.stack([core, far_half]), sum(quarters, []), chunks)
    return (new_stream, grad[None])


def solution(mesh):
    placed = (
        P(None, ("img", "ctx"), None),
        P(),
        P(),
        P(None, None, "ctx", "tp"),
        P(("img", "ctx"), "tp"),
        P(None, "tp"),
        P(None, ("img", "ctx"), "tp"),
        P(("img", "ctx")),
    )
    return jax.shard_map(
        shards,
        mesh=mesh,
        in_specs=placed,
        out_specs=(P(("img", "ctx"), "tp"), P(None, ("img", "ctx"), None)),
        check_vma=False,
    )
```

```python
import jax
import jax.numpy as jnp
from jax import lax
from jax.experimental import pallas as pl
from jax.experimental.pallas import tpu as pltpu
from jax.sharding import PartitionSpec as P


BF = jnp.bfloat16
F32 = jnp.float32
BLOCK = 768
RING = 4
AWAY = (0, 3, 1, 2)


def params(mib):
    return pltpu.CompilerParams(vmem_limit_bytes=mib * 1024 * 1024)


def whole():
    return pl.BlockSpec(memory_space=pltpu.VMEM)


def shape(dims, kind):
    return jax.ShapeDtypeStruct(dims, kind)


def scalars():
    return pl.BlockSpec(memory_space=pltpu.SMEM)


def anywhere():
    return pl.BlockSpec(memory_space=pl.ANY)


def cost(flops, moved):
    return pl.CostEstimate(flops=flops, bytes_accessed=moved, transcendentals=0)


def eq_hot(shape, dim, index):
    return (lax.broadcasted_iota(jnp.int32, shape, dim) == index).astype(BF)


def window_major(tokens, window):
    n = tokens * window
    row = lax.broadcasted_iota(jnp.int32, (n, n), 0)
    col = lax.broadcasted_iota(jnp.int32, (n, n), 1)
    return (col == (row % tokens) * window + row // tokens).astype(BF)


def patch_major(tokens, window):
    n = tokens * window
    row = lax.broadcasted_iota(jnp.int32, (n, n), 0)
    col = lax.broadcasted_iota(jnp.int32, (n, n), 1)
    return (col == (row % window) * tokens + row // window).astype(BF)


def norm_kernel(here_ref, x_ref, gain_ref, bias_ref, after_ref, lifted_ref, xw_ref, stat_ref):
    window, width = gain_ref.shape
    tokens = x_ref.shape[0] // window
    full = window * width
    x = jnp.dot(window_major(tokens, window), x_ref[...], preferred_element_type=F32)
    parts = [x[w * tokens : (w + 1) * tokens] for w in range(window)]
    total = sum(jnp.sum(p, axis=1, keepdims=True) for p in parts)
    squares = sum(jnp.sum(p * p, axis=1, keepdims=True) for p in parts)
    mean = total / full
    inv = lax.rsqrt(squares / full - mean * mean + 1e-05)
    lifted = []
    for w, p in enumerate(parts):
        normed = (p - mean) * inv
        lifted.append(
            normed * gain_ref[w : w + 1].astype(F32) + bias_ref[w : w + 1].astype(F32)
        )
        xw_ref[w] = p.astype(BF)
    share = width // (RING * RING)
    lifted_ref[...] = jnp.concatenate(
        [p[:, at : at + share] for at in range(0, width, share) for p in lifted], axis=1
    ).astype(BF)
    lane = lax.broadcasted_iota(jnp.int32, stat_ref.shape, 1)
    stat_ref[...] = jnp.where(lane == 0, mean, inv)


def layer_norm(here, features, gain, bias, after):
    rows, width = features.shape
    window = gain.shape[0]
    merged = rows // window
    block = 64
    steps = merged // block
    return pl.pallas_call(
        norm_kernel,
        grid_spec=pltpu.PrefetchScalarGridSpec(
            num_scalar_prefetch=1,
            grid=(steps,),
            in_specs=[
                pl.BlockSpec(
                    (block * window, width),
                    lambda i, c: (lax.rem(i + c[0] * (steps // 2), steps), 0),
                ),
                pl.BlockSpec((window, width), lambda i, c: (0, 0)),
                pl.BlockSpec((window, width), lambda i, c: (0, 0)),
                anywhere(),
            ],
            out_specs=[
                pl.BlockSpec((block, window * width), lambda i, c: (i, 0)),
                pl.BlockSpec((window, block, width), lambda i, c: (0, i, 0)),
                pl.BlockSpec((block, 128), lambda i, c: (i, 0)),
            ],
        ),
        out_shape=[
            shape((merged, window * width), BF),
            shape((window, merged, width), BF),
            shape((merged, 128), F32),
        ],
        compiler_params=params(58),
        cost_estimate=cost(2 * rows * block * window * width, 6 * rows * width),
        name="layer_norm",
    )(here, features, gain, bias, after)


def collect_kernel(pos_ref, stream_ref, cot_ref, after_ref, out_ref):
    slots = pos_ref.shape[0]
    rows, width = stream_ref.shape
    cut = width // 2
    pick = eq_hot((slots, rows), 1, pos_ref[...])
    for img in range(2):
        at = slice(img * cut, (img + 1) * cut)
        for place, ref in enumerate((stream_ref, cot_ref)):
            out_ref[img, :, place * cut : (place + 1) * cut] = jnp.dot(
                pick, ref[:, at], preferred_element_type=F32
            ).astype(BF)


def collect(pos, stream, cot, after):
    slots = pos.shape[0]
    rows, width = stream.shape
    out = shape((2, slots, width), BF)
    return pl.pallas_call(
        collect_kernel,
        in_specs=[whole()] * 3 + [anywhere()],
        out_specs=whole(),
        out_shape=out,
        compiler_params=params(20),
        cost_estimate=cost(4 * slots * rows * width, 8 * rows * width),
        name="collect",
    )(pos, stream, cot, after)


def unpack_kernel(slot_ref, came_ref, base_ref, cot_ref):
    tokens, width = base_ref.shape
    slots = came_ref.shape[0]
    take = eq_hot((tokens, slots), 1, slot_ref[...])
    for start, out_ref in ((0, base_ref), (width, cot_ref)):
        out_ref[...] = jnp.dot(
            take, came_ref[:, start : start + width], preferred_element_type=F32
        ).astype(BF)


def unpack(slot_col, came):
    tokens = slot_col.shape[0]
    slots, both = came.shape
    width = both // 2
    outs = [shape((tokens, width), BF)] * 2
    return pl.pallas_call(
        unpack_kernel,
        in_specs=[whole()] * 2,
        out_specs=[whole()] * 2,
        out_shape=outs,
        compiler_params=params(12),
        cost_estimate=cost(4 * slots * tokens * width, 8 * tokens * width),
        name="unpack",
    )(slot_col, came)


def stack_kernel(here_ref, *refs):
    first = jnp.where(here_ref[0] == 0, here_ref[4], here_ref[3])
    for away, ref in zip(AWAY, refs[:RING]):
        refs[RING][lax.rem(first + away, RING)] = ref[...]


def stack(here, blocks):
    rows, width = blocks[0].shape
    return pl.pallas_call(
        stack_kernel,
        in_specs=[scalars()] + [whole()] * RING,
        out_specs=whole(),
        out_shape=shape((RING, rows, width), BF),
        compiler_params=params(6),
        cost_estimate=cost(0, 16 * rows * width),
        name="stack",
    )(here, *blocks)


def fetch(here_ref, stacks, held_ref, sems):
    for index, (away, ref) in enumerate(zip(AWAY, stacks)):

        @pl.when(here_ref[0] == 0)
        def _():
            place = lax.rem(here_ref[3] + away, RING)
            pltpu.make_async_copy(ref, held_ref.at[place], sems.at[index]).start()

        @pl.when(here_ref[0] == 1)
        def _():
            place = lax.rem(here_ref[4] + away, RING)
            pltpu.make_async_copy(ref, held_ref.at[:, place], sems.at[index]).start()

    def wait():
        for index, ref in enumerate(stacks):
            pltpu.make_async_copy(ref, held_ref.at[0], sems.at[index]).wait()

    return wait


def merge_kernel(here_ref, ngain_ref, base_hbm, cot_hbm, *refs):
    stacks, refs = refs[:RING], refs[RING:]
    lifted, refs = refs[:-10], refs[-10:]
    visual_ref, state_ref, stat_ref, held_ref, left_ref, base_ref, cot_ref, w_sems, sems, row_sems = refs
    wait_weight = fetch(here_ref, stacks, held_ref, w_sems)
    depth = left_ref.shape[1]
    steps = range(depth // BLOCK)
    copies = []
    for step in steps:
        at = pl.ds(step * BLOCK, BLOCK)
        start = 0
        group = []
        for index, ref in enumerate(lifted):
            rows = ref.shape[0]
            group.append(
                pltpu.make_async_copy(
                    ref.at[:, at], left_ref.at[pl.ds(start, rows), at], sems.at[step, index]
                )
            )
            group[-1].start()
            start += rows
        copies.append(group)
    row_copies = [
        pltpu.make_async_copy(a, b, row_sems.at[i])
        for i, (a, b) in enumerate(((base_hbm, base_ref), (cot_hbm, cot_ref)))
    ]
    for copy in row_copies:
        copy.start()
    wait_weight()
    weight = held_ref[...].reshape(depth, -1)
    total = None
    for step in steps:
        at = slice(step * BLOCK, (step + 1) * BLOCK)
        for copy in copies[step]:
            copy.wait()
        part = jnp.dot(left_ref[:, at], weight[at], preferred_element_type=F32)
        total = part if total is None else total + part
    for copy in row_copies:
        copy.wait()
    visual = total.astype(BF)
    visual_ref[...] = visual
    state = base_ref[...].astype(F32) + visual.astype(F32)
    state_ref[...] = state
    up = ngain_ref[...].astype(F32) * cot_ref[...].astype(F32)
    lane = lax.broadcasted_iota(jnp.int32, (state.shape[0], 128), 1)
    sums = jnp.where(
        lane == 0,
        jnp.sum(state * state, axis=1, keepdims=True),
        jnp.sum(up * state, axis=1, keepdims=True),
    )
    stat_ref[...] = sums.T[: stat_ref.shape[0]]


def merge(here, base, cot, ngain, stacks, lifted):
    tokens, width = base.shape
    depth = lifted[0].shape[1]
    outs = [shape((tokens, width), BF), shape((tokens, width), F32), shape((8, tokens), F32)]
    return pl.pallas_call(
        merge_kernel,
        in_specs=[scalars(), whole()] + [anywhere()] * (2 + RING + len(lifted)),
        out_specs=[whole()] * 3,
        out_shape=outs,
        scratch_shapes=[
            pltpu.VMEM((RING,) + stacks[0].shape, BF),
            pltpu.VMEM((tokens, depth), BF),
            pltpu.VMEM((tokens, width), BF),
            pltpu.VMEM((tokens, width), BF),
            pltpu.SemaphoreType.DMA((RING,)),
            pltpu.SemaphoreType.DMA((depth // BLOCK, len(lifted))),
            pltpu.SemaphoreType.DMA((2,)),
        ],
        compiler_params=params(56),
        cost_estimate=cost(2 * depth * tokens * width, 2 * depth * width),
        name="merge",
    )(here, ngain, base, cot, *stacks, *lifted)


def add_kernel(sums_ref, got_ref, near_ref, turned_ref):
    count = sums_ref.shape[1] // 4
    cuts = [
        sums_ref[:, i * count : (i + 1) * count] + got_ref[:, (i ^ 1) * count : ((i ^ 1) + 1) * count]
        for i in range(4)
    ]
    near_ref[...] = jnp.concatenate(cuts, axis=1)
    turned_ref[...] = jnp.concatenate(cuts[2:] + cuts[:2], axis=1)


def add(sums, got):
    return pl.pallas_call(
        add_kernel,
        in_specs=[whole()] * 2,
        out_specs=[whole()] * 2,
        out_shape=[shape(sums.shape, F32)] * 2,
        compiler_params=params(4),
        cost_estimate=cost(sums.size, 16 * sums.size),
        name="add",
    )(sums, got)


def pack_kernel(here_ref, slot_ref, visual_ref, after_ref, stay_ref, cross_ref):
    tokens = visual_ref.shape[0]
    slots = stay_ref.shape[0]
    for relative, out_ref in ((0, stay_ref), (1, cross_ref)):
        put = eq_hot((tokens, slots), 1, slot_ref[...] - (here_ref[2] ^ relative) * slots)
        out_ref[...] = lax.dot_general(
            put, visual_ref[...], (((0,), (0,)), ((), ())), preferred_element_type=F32
        ).astype(BF)


def pack(here, slot_col, visual, slots, after):
    tokens, width = visual.shape
    return pl.pallas_call(
        pack_kernel,
        in_specs=[scalars()] + [whole()] * 2 + [anywhere()],
        out_specs=[whole()] * 2,
        out_shape=[shape((slots // 2, width), BF)] * 2,
        compiler_params=params(8),
        cost_estimate=cost(2 * slots * tokens * width, 2 * (slots + tokens) * width),
        name="pack",
    )(here, slot_col, visual, after)


def braid_kernel(stay_ref, crossed_ref, after_ref, out_ref):
    count, _, rows, _ = out_ref.shape
    for c in range(count):
        at = slice(c * rows, (c + 1) * rows)
        out_ref[c, 0] = stay_ref[at, :]
        out_ref[c, 1] = crossed_ref[at, :]


def braid(stay, crossed, count, after):
    rows, width = stay.shape
    return pl.pallas_call(
        braid_kernel,
        in_specs=[whole()] * 2 + [anywhere()],
        out_specs=whole(),
        out_shape=shape((count, 2, rows // count, width), BF),
        compiler_params=params(6),
        cost_estimate=cost(0, 8 * rows * width),
        name="braid",
    )(stay, crossed, after)


def backward_kernel(full_width, chunks, here_ref, state_ref, cot_ref, ngain_ref, *refs):
    stats, stacks, refs = refs[:RING], refs[RING : 2 * RING], refs[2 * RING :]
    outs, (picked_ref, sums_ref, held_ref, sems) = refs[: 3 * chunks], refs[3 * chunks :]
    wait_weight = fetch(here_ref, stacks, held_ref, sems)
    tokens = state_ref.shape[0]
    rows = tokens // 2 // RING // chunks
    total = stats[0][...]
    for ref in stats[1:]:
        total = total + ref[...]
    sums_ref[...] = total.T
    far, img = here_ref[1], here_ref[2]
    gain = ngain_ref[...].astype(F32)
    for core in range(2):
        for away in range(RING):
            there = lax.rem(2 * far + img + away, RING)
            partner = lax.rem(there + img, 2)
            begin = partner * (tokens // 2) + core * (tokens // 4) + (there // 2) * (tokens // 8)
            at = pl.ds(pl.multiple_of(begin, tokens // 8), tokens // 8)
            sums = sums_ref[at, :]
            inv = lax.rsqrt(sums[:, 0:1] / full_width + 1e-06)
            inner = sums[:, 1:2] / full_width
            up = gain * cot_ref[at, :].astype(F32)
            grad = inv * up - state_ref[at, :] * (inv * inv * inv * inner)
            for chunk in range(chunks):
                to = ((core * chunks + chunk) * RING + away) * rows
                picked_ref[to : to + rows, :] = grad[chunk * rows : (chunk + 1) * rows].astype(BF)
    depth = outs[0].shape[1]
    wait_weight()
    weight = held_ref[...].reshape(depth, -1)
    for begin in range(0, depth, BLOCK):
        cols = slice(begin, begin + BLOCK)
        both = lax.dot_general(
            picked_ref[...], weight[cols], (((1,), (1,)), ((), ())), preferred_element_type=F32
        )
        for chunk in range(chunks):
            own, rest, other = outs[chunk], outs[chunks + chunk], outs[2 * chunks + chunk]
            start = chunk * RING * rows
            own[:, cols] = both[start : start + rows]
            rest[:, cols] = both[start + rows : start + RING * rows].astype(BF)
            start += tokens // 2
            other[:, cols] = both[start : start + RING * rows].astype(BF)


def backward(here, state, cot, ngain, stats, stacks, chunks, full_width):
    tokens, width = state.shape
    depth = RING * stacks[0].shape[0] * stacks[0].shape[1]
    rows = tokens // 2 // RING // chunks
    outs = (
        [shape((rows, depth), F32)] * chunks
        + [shape(((RING - 1) * rows, depth), BF)] * chunks
        + [shape((RING * rows, depth), BF)] * chunks
    )
    return pl.pallas_call(
        lambda *refs: backward_kernel(full_width, chunks, *refs),
        in_specs=[scalars()] + [whole()] * (3 + RING) + [anywhere()] * RING,
        out_specs=[whole()] * len(outs),
        out_shape=outs,
        scratch_shapes=[
            pltpu.VMEM((tokens, width), BF),
            pltpu.VMEM((tokens, 8), F32),
            pltpu.VMEM((RING,) + stacks[0].shape, BF),
            pltpu.SemaphoreType.DMA((RING,)),
        ],
        compiler_params=params(24),
        cost_estimate=cost(2 * depth * tokens * width, 2 * depth * width),
        name="backward",
    )(here, state, cot, ngain, *stats, *stacks)


def pair_kernel(rest_ref, got_ref, after_ref, *outs):
    rows = outs[0].shape[0]
    for away, out in enumerate(outs):
        at = slice(away * rows, (away + 1) * rows)
        got = slice((away + 1) * rows, (away + 2) * rows)
        out[...] = (rest_ref[at, :].astype(F32) + got_ref[got, :].astype(F32)).astype(BF)


def pair(rest, got, after):
    rows, depth = got.shape[0] // RING, got.shape[1]
    outs = [shape((rows, depth), BF)] * (RING - 1)
    return pl.pallas_call(
        pair_kernel,
        in_specs=[whole()] * 2 + [anywhere()],
        out_specs=[whole()] * (RING - 1),
        out_shape=outs,
        compiler_params=params(8),
        cost_estimate=cost(4 * rows * depth, 24 * rows * depth),
        name="pair",
    )(rest, got, after)


def finish_kernel(block_ref, own_ref, got_ref, *refs):
    came, (xw_ref, stat_ref, gain_ref, out_ref) = refs[: RING - 1], refs[RING - 1 :]
    window, tokens, width = xw_ref.shape
    full = window * width
    mean = stat_ref[:, 0:1]
    inv = stat_ref[:, 1:2]
    lifted = own_ref[...] + got_ref[...].astype(F32)
    for ref in came:
        lifted = lifted + ref[...].astype(F32)
    share = width // (RING * RING)
    scaled = []
    total = 0.0
    inner = 0.0
    for w in range(window):
        g = jnp.concatenate(
            [lifted[:, at : at + share] for at in range(w * share, full, window * share)], axis=1
        ) * gain_ref[w : w + 1].astype(F32)
        normed = (xw_ref[w].astype(F32) - mean) * inv
        total = total + jnp.sum(g, axis=1, keepdims=True)
        inner = inner + jnp.sum(g * normed, axis=1, keepdims=True)
        scaled.append((g, normed))
    total = total / full
    inner = inner / full
    rows = jnp.concatenate(
        [(inv * (g - total - normed * inner)).astype(BF) for g, normed in scaled], axis=0
    )
    out_ref[...] = jnp.dot(
        patch_major(tokens, window), rows, preferred_element_type=F32
    ).astype(BF)


def finish(block, own, got, came, xw, stat, gain):
    tokens, depth = own.shape
    window, width = gain.shape
    same = pl.BlockSpec((tokens, depth), lambda i, b: (0, 0))
    return pl.pallas_call(
        finish_kernel,
        grid_spec=pltpu.PrefetchScalarGridSpec(
            num_scalar_prefetch=1,
            grid=(1,),
            in_specs=[same] * (1 + RING)
            + [
                pl.BlockSpec((window, tokens, width), lambda i, b: (0, b[0], 0)),
                pl.BlockSpec((tokens, 128), lambda i, b: (b[0], 0)),
                pl.BlockSpec((window, width), lambda i, b: (0, 0)),
            ],
            out_specs=pl.BlockSpec((tokens * window, width), lambda i, b: (0, 0)),
        ),
        out_shape=shape((tokens * window, width), BF),
        compiler_params=params(12),
        cost_estimate=cost(2 * (tokens * window) ** 2 * width, 8 * window * tokens * width),
        name="finish",
    )(block, own, got, *came, xw, stat, gain)


def place_kernel(here_ref, pos_ref, came_ref, stream_ref, out_ref):
    rows, width = stream_ref.shape
    cut = width // 2
    slots = pos_ref.shape[0]
    put = eq_hot((slots, rows), 1, pos_ref[...])
    for relative in range(2):
        start = pl.multiple_of((here_ref[2] ^ relative) * cut, cut)
        at = pl.ds(start, cut)
        out_ref[:, at] = (
            stream_ref[:, at].astype(F32)
            + lax.dot_general(
                put,
                came_ref[:, relative].reshape(slots, cut),
                (((0,), (0,)), ((), ())),
                preferred_element_type=F32,
            )
        ).astype(BF)


def place(here, pos, came, stream):
    rows, width = stream.shape
    return pl.pallas_call(
        place_kernel,
        in_specs=[scalars()] + [whole()] * 3,
        out_specs=whole(),
        out_shape=shape((rows, width), BF),
        compiler_params=params(12),
        cost_estimate=cost(2 * pos.shape[0] * rows * width, 6 * rows * width),
        name="place",
    )(here, pos, came, stream)


def lay_kernel(chunks, at_ref, *refs):
    blocks, (out_ref, sems) = refs[:-2], refs[-2:]
    rows = blocks[0].shape[0]
    copies = []
    for index, ref in enumerate(blocks):
        quarter, chunk = index // chunks, index % chunks
        owner = 2 * (at_ref[0] ^ (quarter // 2)) + (at_ref[1] ^ (quarter % 2))
        start = pl.multiple_of((owner * chunks + chunk) * rows, rows)
        copies.append(pltpu.make_async_copy(ref, out_ref.at[pl.ds(start, rows)], sems.at[index]))
    for copy in copies:
        copy.start()
    for copy in copies:
        copy.wait()


def lay(at, blocks, chunks):
    rows, width = blocks[0].shape
    return pl.pallas_call(
        lambda *refs: lay_kernel(chunks, *refs),
        in_specs=[scalars()] + [whole()] * len(blocks),
        out_specs=anywhere(),
        out_shape=shape((len(blocks) * rows, width), BF),
        scratch_shapes=[pltpu.SemaphoreType.DMA((len(blocks),))],
        compiler_params=params(4),
        cost_estimate=cost(0, 4 * len(blocks) * rows * width),
        name="lay",
    )(at, *blocks)


def shards(features, ln_gain, ln_bias, projection, stream, norm_gain, cotangent, slots):
    n_img = lax.axis_size("img")
    n_ctx = lax.axis_size("ctx")
    n_tp = lax.axis_size("tp")
    merged = slots.shape[0]
    tok_rows, width = stream.shape
    owners = n_img * n_ctx
    capacity = 2 * merged // owners
    slot_count = owners * capacity
    full_width = width * n_tp
    cut = width // n_img

    img = lax.axis_index("img").astype(jnp.int32)
    tp = lax.axis_index("tp").astype(jnp.int32)
    core, far_half = tp % 2, tp // 2
    z, y = lax.axis_index("ctx") // RING, lax.axis_index("ctx") % RING
    here = jnp.stack([core, far_half, img, z, y]).astype(jnp.int32)

    flip = [(i, 1 - i) for i in range(n_img)]
    core_pairs = [(t, t ^ 1) for t in range(n_tp)]
    far_pairs = [(t, t ^ 2) for t in range(n_tp)]

    def along_x(array, by):
        pairs = []
        for i in range(n_img):
            for t in range(n_tp):
                x = (2 * (t // 2) + i + by) % RING
                pairs.append((i * n_tp + t, (x % 2) * n_tp + 2 * (x // 2) + t % 2))
        return lax.ppermute(array, ("img", "tp"), pairs)

    def along_ctx(array, axis, by):
        pairs = []
        for c in range(n_ctx):
            for t in range(n_tp):
                z, y = c // RING, c % RING
                if t % 2 == axis:
                    y = (y + by) % RING
                else:
                    z = (z + by) % RING
                pairs.append((c * n_tp + t, (z * RING + y) * n_tp + t))
        return lax.ppermute(array, ("ctx", "tp"), pairs)

    moves = (1, -1, 2)
    columns = lax.dynamic_slice_in_dim(projection[0], img * cut, cut, axis=2).reshape(-1, cut)
    first = stack(here, [columns] + [along_ctx(columns, 0, by) for by in moves])

    slots = jnp.roll(slots, -core * (merged // 2))
    target = slots // tok_rows
    ids = jnp.arange(merged)
    earlier = (target[:, None] == target[None, :]) & (ids[:, None] < ids[None, :])
    rank = jnp.sum(earlier.astype(jnp.int32), axis=0)
    slot = target * capacity + rank
    local = slots - target * tok_rows
    packed = jnp.max(
        jnp.where(jnp.arange(slot_count)[:, None] == slot[None, :], local[None, :], -1), axis=1
    )
    asked = lax.all_to_all(
        packed.reshape(owners, capacity), ("img", "ctx"), split_axis=0, concat_axis=0, tiled=True
    )
    asked = asked.reshape(n_img, n_ctx, capacity).transpose(1, 0, 2)
    asked = asked.reshape(slot_count, 1)
    held = collect(asked, stream, cotangent[0], first)
    came = lax.all_to_all(
        held.reshape(owners, n_img * capacity, width),
        ("img", "ctx"), split_axis=0, concat_axis=0, tiled=True,
    ).reshape(n_img * slot_count, width)
    paired = target * (n_img * capacity) + rank + img * capacity
    paired = jnp.concatenate([paired, lax.ppermute(paired, "img", flip)]).reshape(-1, 1)

    stacks = [first] + [along_ctx(first, 1, by) for by in moves]

    gain = ln_gain[0]
    lifted, xw, stat = layer_norm(here, features[0], gain, ln_bias[0], held)
    pairs = []
    for i in range(n_img):
        for t in range(n_tp):
            x = (2 * (t // 2) + i + (1 if t % 2 == 0 else -1)) % RING
            pairs.append((i * n_tp + t, (x % 2) * n_tp + 2 * (x // 2) + t % 2))
    next_mine = lax.ppermute(lifted[: merged // 2], ("img", "tp"), pairs)
    next_other = lax.ppermute(next_mine, "tp", core_pairs)

    own_gain = lax.dynamic_slice_in_dim(norm_gain, img * cut, cut, axis=1)
    base, cot = unpack(paired, came)
    visual, state, sums = merge(here, base, cot, own_gain, stacks, [lifted, next_mine, next_other])

    near, turned = add(sums, lax.ppermute(sums, "tp", core_pairs))
    stats = [near] + [along_x(near if by == 2 else turned, by) for by in (1, 2, 3)]
    stay, cross = pack(here, paired, visual, n_img * slot_count, near)
    crossed = lax.ppermute(cross, "img", flip)

    chunks = 2
    parts = backward(here, state, cot, own_gain, stats, stacks, chunks, full_width)
    parts, crossed = lax.optimization_barrier((parts, crossed))
    own, rest, other = (parts[i * chunks : (i + 1) * chunks] for i in range(3))
    got = [lax.ppermute(o, "tp", core_pairs) for o in other]
    sent = [pair(rest[c], got[c], crossed) for c in range(chunks)]
    came_back = [[along_x(sent[c][by - 1], by) for by in (1, 2, 3)] for c in range(chunks)]

    send = braid(stay, crossed, n_ctx, came_back[0][0])
    arrived = lax.all_to_all(send, "ctx", split_axis=0, concat_axis=0, tiled=True)
    new_stream = place(here, asked, arrived, stream)

    quarters = [[], [], [], []]
    for c in range(chunks):
        block = (far_half * chunks + c).reshape(1)
        out = finish(block, own[c], got[c], came_back[c], xw, stat, gain)
        beyond = lax.ppermute(out, "tp", far_pairs)
        quarters[0].append(out)
        quarters[1].append(beyond)
        quarters[2].append(lax.ppermute(out, "tp", core_pairs))
        quarters[3].append(lax.ppermute(beyond, "tp", core_pairs))
    grad = lay(here, sum(quarters, []), chunks)
    return (new_stream, grad[None])


def solution(mesh):
    placed = (
        P(None, ("img", "ctx"), None),
        P(),
        P(),
        P(None, None, "ctx", "tp"),
        P(("img", "ctx"), "tp"),
        P(None, "tp"),
        P(None, ("img", "ctx"), "tp"),
        P(("img", "ctx")),
    )
    return jax.shard_map(
        shards,
        mesh=mesh,
        in_specs=placed,
        out_specs=(P(("img", "ctx"), "tp"), P(None, ("img", "ctx"), None)),
        check_vma=False,
    )
```

```python
import jax
import jax.numpy as jnp
from jax import lax
from jax.experimental import pallas as pl
from jax.experimental.pallas import tpu as pltpu
from jax.sharding import PartitionSpec as P


BF = jnp.bfloat16
F32 = jnp.float32
FREE = pl.CostEstimate(flops=0, bytes_accessed=0, transcendentals=0)
RING = 4
AWAY = (0, 3, 1, 2)


def params(mib):
    return pltpu.CompilerParams(vmem_limit_bytes=mib * 1024 * 1024)


def whole():
    return pl.BlockSpec(memory_space=pltpu.VMEM)


def shape(dims, kind):
    return jax.ShapeDtypeStruct(dims, kind)


def scalars():
    return pl.BlockSpec(memory_space=pltpu.SMEM)


def anywhere():
    return pl.BlockSpec(memory_space=pl.ANY)


def eq_hot(shape, dim, index):
    return (lax.broadcasted_iota(jnp.int32, shape, dim) == index).astype(BF)


def window_major(tokens, window):
    n = tokens * window
    row = lax.broadcasted_iota(jnp.int32, (n, n), 0)
    col = lax.broadcasted_iota(jnp.int32, (n, n), 1)
    return (col == (row % tokens) * window + row // tokens).astype(BF)


def patch_major(tokens, window):
    n = tokens * window
    row = lax.broadcasted_iota(jnp.int32, (n, n), 0)
    col = lax.broadcasted_iota(jnp.int32, (n, n), 1)
    return (col == (row % window) * tokens + row // window).astype(BF)


def norm_kernel(here_ref, x_ref, gain_ref, bias_ref, mine_ref, other_ref, xw_ref, stat_ref):
    window, width = gain_ref.shape
    tokens = x_ref.shape[0] // window
    full = window * width
    x = jnp.dot(window_major(tokens, window), x_ref[...], preferred_element_type=F32)
    parts = [x[w * tokens : (w + 1) * tokens] for w in range(window)]
    total = sum(jnp.sum(p, axis=1, keepdims=True) for p in parts)
    squares = sum(jnp.sum(p * p, axis=1, keepdims=True) for p in parts)
    mean = total / full
    inv = lax.rsqrt(squares / full - mean * mean + 1e-05)
    lifted = []
    for w, p in enumerate(parts):
        normed = (p - mean) * inv
        lifted.append(
            normed * gain_ref[w : w + 1].astype(F32) + bias_ref[w : w + 1].astype(F32)
        )
        xw_ref[w] = p.astype(BF)
    share = width // (RING * RING)
    lifted = jnp.concatenate(
        [p[:, at : at + share] for at in range(0, width, share) for p in lifted], axis=1
    ).astype(BF)
    half = pl.num_programs(0) // 2

    @pl.when(pl.program_id(0) < half)
    def _():
        mine_ref[...] = lifted

    @pl.when(pl.program_id(0) >= half)
    def _():
        other_ref[...] = lifted

    lane = lax.broadcasted_iota(jnp.int32, stat_ref.shape, 1)
    stat_ref[...] = jnp.where(lane == 0, mean, inv)


def layer_norm(here, features, gain, bias):
    rows, width = features.shape
    window = gain.shape[0]
    merged = rows // window
    block = 64
    steps = merged // block
    return pl.pallas_call(
        norm_kernel,
        grid_spec=pltpu.PrefetchScalarGridSpec(
            num_scalar_prefetch=1,
            grid=(steps,),
            in_specs=[
                pl.BlockSpec(
                    (block * window, width),
                    lambda i, c: (lax.rem(i + c[0] * (steps // 2), steps), 0),
                ),
                pl.BlockSpec((window, width), lambda i, c: (0, 0)),
                pl.BlockSpec((window, width), lambda i, c: (0, 0)),
            ],
            out_specs=[
                pl.BlockSpec((block, window * width), lambda i, c: (jnp.minimum(i, steps // 2 - 1), 0)),
                pl.BlockSpec((block, window * width), lambda i, c: (jnp.maximum(i - steps // 2, 0), 0)),
                pl.BlockSpec((window, block, width), lambda i, c: (0, i, 0)),
                pl.BlockSpec((block, 128), lambda i, c: (i, 0)),
            ],
        ),
        out_shape=[
            shape((merged // 2, window * width), BF),
            shape((merged // 2, window * width), BF),
            shape((window, merged, width), BF),
            shape((merged, 128), F32),
        ],
        compiler_params=params(16),
        cost_estimate=FREE,
        name="layer_norm",
    )(here, features, gain, bias)


def collect_kernel(pos_ref, stream_ref, cot_ref, after_ref, norm_ref, out_ref):
    slots = pos_ref.shape[0]
    rows, width = stream_ref.shape
    cut = width // 2
    pick = eq_hot((slots, rows), 1, pos_ref[...])
    for img in range(2):
        at = slice(img * cut, (img + 1) * cut)
        for place, ref in enumerate((stream_ref, cot_ref)):
            out_ref[img, :, place * cut : (place + 1) * cut] = jnp.dot(
                pick, ref[:, at], preferred_element_type=F32
            ).astype(BF)


def collect(pos, stream, cot, *after):
    slots = pos.shape[0]
    rows, width = stream.shape
    out = shape((2, slots, width), BF)
    return pl.pallas_call(
        collect_kernel,
        in_specs=[whole()] * 3 + [anywhere()] * 2,
        out_specs=whole(),
        out_shape=out,
        compiler_params=params(20),
        cost_estimate=FREE,
        name="collect",
    )(pos, stream, cot, *after)


def unpack_kernel(slot_ref, came_ref, base_ref, cot_ref):
    tokens, width = base_ref.shape
    slots = came_ref.shape[0]
    take = eq_hot((tokens, slots), 1, slot_ref[...])
    for start, out_ref in ((0, base_ref), (width, cot_ref)):
        out_ref[...] = jnp.dot(
            take, came_ref[:, start : start + width], preferred_element_type=F32
        ).astype(BF)


def unpack(slot_col, came):
    tokens = slot_col.shape[0]
    slots, both = came.shape
    width = both // 2
    outs = [shape((tokens, width), BF)] * 2
    return pl.pallas_call(
        unpack_kernel,
        in_specs=[whole()] * 2,
        out_specs=[whole()] * 2,
        out_shape=outs,
        compiler_params=params(12),
        cost_estimate=FREE,
        name="unpack",
    )(slot_col, came)


def stack_kernel(here_ref, *refs):
    first = jnp.where(here_ref[0] == 0, here_ref[4], here_ref[3])
    for away, ref in zip(AWAY, refs[:RING]):
        refs[RING][lax.rem(first + away, RING)] = ref[...]


def stack(here, blocks):
    rows, width = blocks[0].shape
    return pl.pallas_call(
        stack_kernel,
        in_specs=[scalars()] + [whole()] * RING,
        out_specs=whole(),
        out_shape=shape((RING, rows, width), BF),
        compiler_params=params(6),
        cost_estimate=FREE,
        name="stack",
    )(here, *blocks)


def fetch(here_ref, stacks, held_ref, sems):
    for index, (away, ref) in enumerate(zip(AWAY, stacks)):

        @pl.when(here_ref[0] == 0)
        def _():
            place = lax.rem(here_ref[3] + away, RING)
            pltpu.make_async_copy(ref, held_ref.at[place], sems.at[index]).start()

        @pl.when(here_ref[0] == 1)
        def _():
            place = lax.rem(here_ref[4] + away, RING)
            pltpu.make_async_copy(ref, held_ref.at[:, place], sems.at[index]).start()

    def wait():
        for index, ref in enumerate(stacks):
            pltpu.make_async_copy(ref, held_ref.at[0], sems.at[index]).wait()

    return wait


def merge_kernel(here_ref, ngain_ref, base_hbm, cot_hbm, *refs):
    stacks, refs = refs[:RING], refs[RING:]
    lifted, refs = refs[:-10], refs[-10:]
    visual_ref, state_ref, stat_ref, held_ref, left_ref, base_ref, cot_ref, w_sems, sems, row_sems = refs
    wait_weight = fetch(here_ref, stacks, held_ref, w_sems)
    depth = left_ref.shape[1]
    block = depth // RING
    steps = range(RING)
    copies = []
    for step in steps:
        at = pl.ds(step * block, block)
        start = 0
        group = []
        for index, ref in enumerate(lifted):
            rows = ref.shape[0]
            group.append(
                pltpu.make_async_copy(
                    ref.at[:, at], left_ref.at[pl.ds(start, rows), at], sems.at[step, index]
                )
            )
            group[-1].start()
            start += rows
        copies.append(group)
    row_copies = [
        pltpu.make_async_copy(a, b, row_sems.at[i])
        for i, (a, b) in enumerate(((base_hbm, base_ref), (cot_hbm, cot_ref)))
    ]
    for copy in row_copies:
        copy.start()
    wait_weight()
    total = None
    for step in steps:
        for copy in copies[step]:
            copy.wait()
        part = jnp.dot(
            left_ref[:, step * block : (step + 1) * block],
            held_ref[step].reshape(block, -1),
            preferred_element_type=F32,
        )
        total = part if total is None else total + part
    for copy in row_copies:
        copy.wait()
    visual = total.astype(BF)
    visual_ref[...] = visual
    state = base_ref[...].astype(F32) + visual.astype(F32)
    state_ref[...] = state
    up = ngain_ref[...].astype(F32) * cot_ref[...].astype(F32)
    lane = lax.broadcasted_iota(jnp.int32, (state.shape[0], 128), 1)
    sums = jnp.where(
        lane == 0,
        jnp.sum(state * state, axis=1, keepdims=True),
        jnp.sum(up * state, axis=1, keepdims=True),
    )
    stat_ref[...] = sums.T[: stat_ref.shape[0]]


def merge(here, base, cot, ngain, stacks, lifted):
    tokens, width = base.shape
    depth = lifted[0].shape[1]
    outs = [shape((tokens, width), BF), shape((tokens, width), F32), shape((8, tokens), F32)]
    return pl.pallas_call(
        merge_kernel,
        in_specs=[scalars(), whole()] + [anywhere()] * (2 + RING + len(lifted)),
        out_specs=[whole()] * 3,
        out_shape=outs,
        scratch_shapes=[
            pltpu.VMEM((RING,) + stacks[0].shape, BF),
            pltpu.VMEM((tokens, depth), BF),
            pltpu.VMEM((tokens, width), BF),
            pltpu.VMEM((tokens, width), BF),
            pltpu.SemaphoreType.DMA((RING,)),
            pltpu.SemaphoreType.DMA((RING, len(lifted))),
            pltpu.SemaphoreType.DMA((2,)),
        ],
        compiler_params=params(56),
        cost_estimate=FREE,
        name="merge",
    )(here, ngain, base, cot, *stacks, *lifted)


def add_kernel(sums_ref, got_ref, near_ref, turned_ref):
    count = sums_ref.shape[1] // 4
    cuts = [
        sums_ref[:, i * count : (i + 1) * count] + got_ref[:, (i ^ 1) * count : ((i ^ 1) + 1) * count]
        for i in range(4)
    ]
    near_ref[...] = jnp.concatenate(cuts, axis=1)
    turned_ref[...] = jnp.concatenate(cuts[2:] + cuts[:2], axis=1)


def add(sums, got):
    return pl.pallas_call(
        add_kernel,
        in_specs=[whole()] * 2,
        out_specs=[whole()] * 2,
        out_shape=[shape(sums.shape, F32)] * 2,
        compiler_params=params(4),
        cost_estimate=FREE,
        name="add",
    )(sums, got)


def pack_kernel(here_ref, slot_ref, visual_ref, after_ref, stay_ref, cross_ref):
    tokens = visual_ref.shape[0]
    slots = stay_ref.shape[0]
    for relative, out_ref in ((0, stay_ref), (1, cross_ref)):
        put = eq_hot((tokens, slots), 1, slot_ref[...] - (here_ref[2] ^ relative) * slots)
        out_ref[...] = lax.dot_general(
            put, visual_ref[...], (((0,), (0,)), ((), ())), preferred_element_type=F32
        ).astype(BF)


def pack(here, slot_col, visual, slots, after):
    tokens, width = visual.shape
    return pl.pallas_call(
        pack_kernel,
        in_specs=[scalars()] + [whole()] * 2 + [anywhere()],
        out_specs=[whole()] * 2,
        out_shape=[shape((slots // 2, width), BF)] * 2,
        compiler_params=params(8),
        cost_estimate=FREE,
        name="pack",
    )(here, slot_col, visual, after)


def braid_kernel(stay_ref, crossed_ref, out_ref):
    count, _, rows, _ = out_ref.shape
    for c in range(count):
        at = slice(c * rows, (c + 1) * rows)
        out_ref[c, 0] = stay_ref[at, :]
        out_ref[c, 1] = crossed_ref[at, :]


def braid(stay, crossed, count):
    rows, width = stay.shape
    return pl.pallas_call(
        braid_kernel,
        in_specs=[whole()] * 2,
        out_specs=whole(),
        out_shape=shape((count, 2, rows // count, width), BF),
        compiler_params=params(6),
        cost_estimate=FREE,
        name="braid",
    )(stay, crossed)


def backward_kernel(full_width, chunks, here_ref, state_ref, cot_ref, ngain_ref, *refs):
    stats, stacks, refs = refs[:RING], refs[RING : 2 * RING], refs[2 * RING :]
    outs, (picked_ref, sums_ref, held_ref, sems) = refs[: 3 * chunks], refs[3 * chunks :]
    wait_weight = fetch(here_ref, stacks, held_ref, sems)
    tokens = state_ref.shape[0]
    rows = tokens // 2 // RING // chunks
    total = stats[0][...]
    for ref in stats[1:]:
        total = total + ref[...]
    sums_ref[...] = total.T
    far, img = here_ref[1], here_ref[2]
    gain = ngain_ref[...].astype(F32)
    for core in range(2):
        for away in range(RING):
            there = lax.rem(2 * far + img + away, RING)
            partner = lax.rem(there + img, 2)
            begin = partner * (tokens // 2) + core * (tokens // 4) + (there // 2) * (tokens // 8)
            at = pl.ds(pl.multiple_of(begin, tokens // 8), tokens // 8)
            sums = sums_ref[at, :]
            inv = lax.rsqrt(sums[:, 0:1] / full_width + 1e-06)
            inner = sums[:, 1:2] / full_width
            up = gain * cot_ref[at, :].astype(F32)
            grad = inv * up - state_ref[at, :] * (inv * inv * inv * inner)
            for chunk in range(chunks):
                to = ((core * chunks + chunk) * RING + away) * rows
                picked_ref[to : to + rows, :] = grad[chunk * rows : (chunk + 1) * rows].astype(BF)
    depth = outs[0].shape[1]
    wait_weight()
    block = depth // RING
    for step in range(RING):
        cols = slice(step * block, (step + 1) * block)
        both = lax.dot_general(
            picked_ref[...],
            held_ref[step].reshape(block, -1),
            (((1,), (1,)), ((), ())),
            preferred_element_type=F32,
        )
        for chunk in range(chunks):
            own, rest, other = outs[chunk], outs[chunks + chunk], outs[2 * chunks + chunk]
            start = chunk * RING * rows
            own[:, cols] = both[start : start + rows]
            rest[:, cols] = both[start + rows : start + RING * rows].astype(BF)
            start += tokens // 2
            other[:, cols] = both[start : start + RING * rows].astype(BF)


def backward(here, state, cot, ngain, stats, stacks, chunks, full_width):
    tokens, width = state.shape
    depth = RING * stacks[0].shape[0] * stacks[0].shape[1]
    rows = tokens // 2 // RING // chunks
    outs = (
        [shape((rows, depth), F32)] * chunks
        + [shape(((RING - 1) * rows, depth), BF)] * chunks
        + [shape((RING * rows, depth), BF)] * chunks
    )
    return pl.pallas_call(
        lambda *refs: backward_kernel(full_width, chunks, *refs),
        in_specs=[scalars()] + [whole()] * (3 + RING) + [anywhere()] * RING,
        out_specs=[whole()] * len(outs),
        out_shape=outs,
        scratch_shapes=[
            pltpu.VMEM((tokens, width), BF),
            pltpu.VMEM((tokens, 8), F32),
            pltpu.VMEM((RING,) + stacks[0].shape, BF),
            pltpu.SemaphoreType.DMA((RING,)),
        ],
        compiler_params=params(24),
        cost_estimate=FREE,
        name="backward",
    )(here, state, cot, ngain, *stats, *stacks)


def pair_kernel(rest_ref, got_ref, after_ref, *outs):
    rows = outs[0].shape[0]
    for away, out in enumerate(outs):
        at = slice(away * rows, (away + 1) * rows)
        got = slice((away + 1) * rows, (away + 2) * rows)
        out[...] = (rest_ref[at, :].astype(F32) + got_ref[got, :].astype(F32)).astype(BF)


def pair(rest, got, after):
    rows, depth = got.shape[0] // RING, got.shape[1]
    outs = [shape((rows, depth), BF)] * (RING - 1)
    return pl.pallas_call(
        pair_kernel,
        in_specs=[whole()] * 2 + [anywhere()],
        out_specs=[whole()] * (RING - 1),
        out_shape=outs,
        compiler_params=params(8),
        cost_estimate=FREE,
        name="pair",
    )(rest, got, after)


def finish_kernel(block_ref, own_ref, got_ref, *refs):
    came, (xw_ref, stat_ref, gain_ref, out_ref) = refs[: RING - 1], refs[RING - 1 :]
    window, tokens, width = xw_ref.shape
    full = window * width
    mean = stat_ref[:, 0:1]
    inv = stat_ref[:, 1:2]
    lifted = own_ref[...] + got_ref[...].astype(F32)
    for ref in came:
        lifted = lifted + ref[...].astype(F32)
    share = width // (RING * RING)
    scaled = []
    total = 0.0
    inner = 0.0
    for w in range(window):
        g = jnp.concatenate(
            [lifted[:, at : at + share] for at in range(w * share, full, window * share)], axis=1
        ) * gain_ref[w : w + 1].astype(F32)
        normed = (xw_ref[w].astype(F32) - mean) * inv
        total = total + jnp.sum(g, axis=1, keepdims=True)
        inner = inner + jnp.sum(g * normed, axis=1, keepdims=True)
        scaled.append((g, normed))
    total = total / full
    inner = inner / full
    rows = jnp.concatenate(
        [(inv * (g - total - normed * inner)).astype(BF) for g, normed in scaled], axis=0
    )
    out_ref[...] = jnp.dot(
        patch_major(tokens, window), rows, preferred_element_type=F32
    ).astype(BF)


def finish(block, own, got, came, xw, stat, gain):
    tokens, depth = own.shape
    window, width = gain.shape
    same = pl.BlockSpec((tokens, depth), lambda i, b: (0, 0))
    return pl.pallas_call(
        finish_kernel,
        grid_spec=pltpu.PrefetchScalarGridSpec(
            num_scalar_prefetch=1,
            grid=(1,),
            in_specs=[same] * (1 + RING)
            + [
                pl.BlockSpec((window, tokens, width), lambda i, b: (0, b[0], 0)),
                pl.BlockSpec((tokens, 128), lambda i, b: (b[0], 0)),
                pl.BlockSpec((window, width), lambda i, b: (0, 0)),
            ],
            out_specs=pl.BlockSpec((tokens * window, width), lambda i, b: (0, 0)),
        ),
        out_shape=shape((tokens * window, width), BF),
        compiler_params=params(12),
        cost_estimate=FREE,
        name="finish",
    )(block, own, got, *came, xw, stat, gain)


def place_kernel(here_ref, pos_ref, came_ref, stream_ref, out_ref):
    rows, width = stream_ref.shape
    cut = width // 2
    slots = pos_ref.shape[0]
    put = eq_hot((slots, rows), 1, pos_ref[...])
    for relative in range(2):
        start = pl.multiple_of((here_ref[2] ^ relative) * cut, cut)
        at = pl.ds(start, cut)
        out_ref[:, at] = (
            stream_ref[:, at].astype(F32)
            + lax.dot_general(
                put,
                came_ref[:, relative].reshape(slots, cut),
                (((0,), (0,)), ((), ())),
                preferred_element_type=F32,
            )
        ).astype(BF)


def place(here, pos, came, stream):
    rows, width = stream.shape
    return pl.pallas_call(
        place_kernel,
        in_specs=[scalars()] + [whole()] * 3,
        out_specs=whole(),
        out_shape=shape((rows, width), BF),
        compiler_params=params(12),
        cost_estimate=FREE,
        name="place",
    )(here, pos, came, stream)


def lay_kernel(chunks, at_ref, *refs):
    blocks, (out_ref, sems) = refs[:-2], refs[-2:]
    rows = blocks[0].shape[0]
    copies = []
    for index, ref in enumerate(blocks):
        quarter, chunk = index // chunks, index % chunks
        owner = 2 * (at_ref[0] ^ (quarter // 2)) + (at_ref[1] ^ (quarter % 2))
        start = pl.multiple_of((owner * chunks + chunk) * rows, rows)
        copies.append(pltpu.make_async_copy(ref, out_ref.at[pl.ds(start, rows)], sems.at[index]))
    for copy in copies:
        copy.start()
    for copy in copies:
        copy.wait()


def lay(at, blocks, chunks):
    rows, width = blocks[0].shape
    return pl.pallas_call(
        lambda *refs: lay_kernel(chunks, *refs),
        in_specs=[scalars()] + [whole()] * len(blocks),
        out_specs=anywhere(),
        out_shape=shape((len(blocks) * rows, width), BF),
        scratch_shapes=[pltpu.SemaphoreType.DMA((len(blocks),))],
        compiler_params=params(4),
        cost_estimate=FREE,
        name="lay",
    )(at, *blocks)


def shards(features, ln_gain, ln_bias, projection, stream, norm_gain, cotangent, slots):
    n_img = lax.axis_size("img")
    n_ctx = lax.axis_size("ctx")
    n_tp = lax.axis_size("tp")
    merged = slots.shape[0]
    tok_rows, width = stream.shape
    owners = n_img * n_ctx
    capacity = 2 * merged // owners
    slot_count = owners * capacity
    full_width = width * n_tp
    cut = width // n_img

    img = lax.axis_index("img").astype(jnp.int32)
    tp = lax.axis_index("tp").astype(jnp.int32)
    core, far_half = tp % 2, tp // 2
    z, y = lax.axis_index("ctx") // RING, lax.axis_index("ctx") % RING
    here = jnp.stack([core, far_half, img, z, y]).astype(jnp.int32)

    flip = [(i, 1 - i) for i in range(n_img)]
    core_pairs = [(t, t ^ 1) for t in range(n_tp)]
    far_pairs = [(t, t ^ 2) for t in range(n_tp)]

    def along_x(array, by):
        pairs = []
        for i in range(n_img):
            for t in range(n_tp):
                x = (2 * (t // 2) + i + by) % RING
                pairs.append((i * n_tp + t, (x % 2) * n_tp + 2 * (x // 2) + t % 2))
        return lax.ppermute(array, ("img", "tp"), pairs)

    def along_ctx(array, axis, by):
        pairs = []
        for c in range(n_ctx):
            for t in range(n_tp):
                z, y = c // RING, c % RING
                if t % 2 == axis:
                    y = (y + by) % RING
                else:
                    z = (z + by) % RING
                pairs.append((c * n_tp + t, (z * RING + y) * n_tp + t))
        return lax.ppermute(array, ("ctx", "tp"), pairs)

    moves = (1, -1, 2)
    columns = lax.dynamic_slice_in_dim(projection[0], img * cut, cut, axis=2).reshape(-1, cut)
    first = stack(here, [columns] + [along_ctx(columns, 0, by) for by in moves])

    slots = jnp.roll(slots, -core * (merged // 2))
    target = slots // tok_rows
    ids = jnp.arange(merged)
    earlier = (target[:, None] == target[None, :]) & (ids[:, None] < ids[None, :])
    rank = jnp.sum(earlier.astype(jnp.int32), axis=0)
    slot = target * capacity + rank
    local = slots - target * tok_rows
    packed = jnp.max(
        jnp.where(jnp.arange(slot_count)[:, None] == slot[None, :], local[None, :], -1), axis=1
    )
    asked = lax.all_to_all(
        packed.reshape(owners, capacity), ("img", "ctx"), split_axis=0, concat_axis=0, tiled=True
    )
    asked = asked.reshape(n_img, n_ctx, capacity).transpose(1, 0, 2)
    asked = asked.reshape(slot_count, 1)
    gain = ln_gain[0]
    lifted, lifted_other, xw, stat = layer_norm(here, features[0], gain, ln_bias[0])
    held = collect(asked, stream, cotangent[0], first, stat)
    came = lax.all_to_all(
        held.reshape(owners, n_img * capacity, width),
        ("img", "ctx"), split_axis=0, concat_axis=0, tiled=True,
    ).reshape(n_img * slot_count, width)
    paired = target * (n_img * capacity) + rank + img * capacity
    paired = jnp.concatenate([paired, lax.ppermute(paired, "img", flip)]).reshape(-1, 1)

    stacks = [first] + [along_ctx(first, 1, by) for by in moves]

    pairs = []
    for i in range(n_img):
        for t in range(n_tp):
            x = (2 * (t // 2) + i + (1 if t % 2 == 0 else -1)) % RING
            pairs.append((i * n_tp + t, (x % 2) * n_tp + 2 * (x // 2) + t % 2))
    next_mine = lax.ppermute(lifted, ("img", "tp"), pairs)
    next_other = lax.ppermute(next_mine, "tp", core_pairs)

    own_gain = lax.dynamic_slice_in_dim(norm_gain, img * cut, cut, axis=1)
    base, cot = unpack(paired, came)
    visual, state, sums = merge(here, base, cot, own_gain, stacks, [lifted, lifted_other, next_mine, next_other])

    near, turned = add(sums, lax.ppermute(sums, "tp", core_pairs))
    stats = [near] + [along_x(near if by == 2 else turned, by) for by in (1, 2, 3)]
    stay, cross = pack(here, paired, visual, n_img * slot_count, near)
    cross, stats = lax.optimization_barrier((cross, stats))
    crossed = lax.ppermute(cross, "img", flip)

    chunks = 1
    parts = backward(here, state, cot, own_gain, stats, stacks, chunks, full_width)
    parts, crossed = lax.optimization_barrier((parts, crossed))
    own, rest, other = (parts[i * chunks : (i + 1) * chunks] for i in range(3))
    got = [lax.ppermute(o, "tp", core_pairs) for o in other]
    sent = [pair(rest[c], got[c], crossed) for c in range(chunks)]
    came_back = [[along_x(sent[c][by - 1], by) for by in (1, 2, 3)] for c in range(chunks)]

    send = braid(stay, crossed, n_ctx)
    arrived = lax.all_to_all(send, "ctx", split_axis=0, concat_axis=0, tiled=True)
    new_stream = place(here, asked, arrived, stream)

    quarters = [[], [], [], []]
    for c in range(chunks):
        block = (far_half * chunks + c).reshape(1)
        out = finish(block, own[c], got[c], came_back[c], xw, stat, gain)
        beyond = lax.ppermute(out, "tp", far_pairs)
        beyond, new_stream = lax.optimization_barrier((beyond, new_stream))
        quarters[0].append(out)
        quarters[1].append(beyond)
        quarters[2].append(lax.ppermute(out, "tp", core_pairs))
        quarters[3].append(lax.ppermute(beyond, "tp", core_pairs))
    grad = lay(here, sum(quarters, []), chunks)
    return (new_stream, grad[None])


def solution(mesh):
    placed = (
        P(None, ("img", "ctx"), None),
        P(),
        P(),
        P(None, None, "ctx", "tp"),
        P(("img", "ctx"), "tp"),
        P(None, "tp"),
        P(None, ("img", "ctx"), "tp"),
        P(("img", "ctx")),
    )
    return jax.shard_map(
        shards,
        mesh=mesh,
        in_specs=placed,
        out_specs=(P(("img", "ctx"), "tp"), P(None, ("img", "ctx"), None)),
        check_vma=False,
    )
```

```python
import jax
import jax.numpy as jnp
from jax import lax
from jax.experimental import pallas as pl
from jax.experimental.pallas import tpu as pltpu
from jax.sharding import PartitionSpec as P


BF = jnp.bfloat16
F32 = jnp.float32
FREE = pl.CostEstimate(flops=0, bytes_accessed=0, transcendentals=0)
RING = 4
AWAY = (0, 3, 1, 2)


def params(mib):
    return pltpu.CompilerParams(vmem_limit_bytes=mib * 1024 * 1024)


def whole():
    return pl.BlockSpec(memory_space=pltpu.VMEM)


def shape(dims, kind):
    return jax.ShapeDtypeStruct(dims, kind)


def scalars():
    return pl.BlockSpec(memory_space=pltpu.SMEM)


def anywhere():
    return pl.BlockSpec(memory_space=pl.ANY)


def eq_hot(shape, dim, index):
    return (lax.broadcasted_iota(jnp.int32, shape, dim) == index).astype(BF)


def window_major(tokens, window):
    n = tokens * window
    row = lax.broadcasted_iota(jnp.int32, (n, n), 0)
    col = lax.broadcasted_iota(jnp.int32, (n, n), 1)
    return (col == (row % tokens) * window + row // tokens).astype(BF)


def patch_major(tokens, window):
    n = tokens * window
    row = lax.broadcasted_iota(jnp.int32, (n, n), 0)
    col = lax.broadcasted_iota(jnp.int32, (n, n), 1)
    return (col == (row % window) * tokens + row // window).astype(BF)


def norm_kernel(here_ref, x_ref, gain_ref, bias_ref, mine_ref, other_ref, xw_ref, stat_ref):
    window, width = gain_ref.shape
    tokens = x_ref.shape[0] // window
    full = window * width
    x = jnp.dot(window_major(tokens, window), x_ref[...], preferred_element_type=F32)
    parts = [x[w * tokens : (w + 1) * tokens] for w in range(window)]
    total = sum(jnp.sum(p, axis=1, keepdims=True) for p in parts)
    squares = sum(jnp.sum(p * p, axis=1, keepdims=True) for p in parts)
    mean = total / full
    inv = lax.rsqrt(squares / full - mean * mean + 1e-05)
    lifted = []
    for w, p in enumerate(parts):
        normed = (p - mean) * inv
        lifted.append(
            normed * gain_ref[w : w + 1].astype(F32) + bias_ref[w : w + 1].astype(F32)
        )
        xw_ref[w] = p.astype(BF)
    share = width // (RING * RING)
    lifted = jnp.concatenate(
        [p[:, at : at + share] for at in range(0, width, share) for p in lifted], axis=1
    ).astype(BF)
    half = pl.num_programs(0) // 2

    @pl.when(pl.program_id(0) < half)
    def _():
        mine_ref[...] = lifted

    @pl.when(pl.program_id(0) >= half)
    def _():
        other_ref[...] = lifted

    lane = lax.broadcasted_iota(jnp.int32, stat_ref.shape, 1)
    stat_ref[...] = jnp.where(lane == 0, mean, inv)


def layer_norm(here, features, gain, bias):
    rows, width = features.shape
    window = gain.shape[0]
    merged = rows // window
    block = 64
    steps = merged // block
    return pl.pallas_call(
        norm_kernel,
        grid_spec=pltpu.PrefetchScalarGridSpec(
            num_scalar_prefetch=1,
            grid=(steps,),
            in_specs=[
                pl.BlockSpec(
                    (block * window, width),
                    lambda i, c: (lax.rem(i + c[0] * (steps // 2), steps), 0),
                ),
                pl.BlockSpec((window, width), lambda i, c: (0, 0)),
                pl.BlockSpec((window, width), lambda i, c: (0, 0)),
            ],
            out_specs=[
                pl.BlockSpec((block, window * width), lambda i, c: (jnp.minimum(i, steps // 2 - 1), 0)),
                pl.BlockSpec((block, window * width), lambda i, c: (jnp.maximum(i - steps // 2, 0), 0)),
                pl.BlockSpec((window, block, width), lambda i, c: (0, i, 0)),
                pl.BlockSpec((block, 128), lambda i, c: (i, 0)),
            ],
        ),
        out_shape=[
            shape((merged // 2, window * width), BF),
            shape((merged // 2, window * width), BF),
            shape((window, merged, width), BF),
            shape((merged, 128), F32),
        ],
        compiler_params=params(16),
        cost_estimate=FREE,
        name="layer_norm",
    )(here, features, gain, bias)


def collect_kernel(pos_ref, stream_ref, cot_ref, after_ref, out_ref):
    slots = pos_ref.shape[0]
    rows, width = stream_ref.shape
    cut = width // 2
    pick = eq_hot((slots, rows), 1, pos_ref[...])
    for img in range(2):
        at = slice(img * cut, (img + 1) * cut)
        for place, ref in enumerate((stream_ref, cot_ref)):
            out_ref[img, :, place * cut : (place + 1) * cut] = jnp.dot(
                pick, ref[:, at], preferred_element_type=F32
            ).astype(BF)


def collect(pos, stream, cot, after):
    slots = pos.shape[0]
    rows, width = stream.shape
    out = shape((2, slots, width), BF)
    return pl.pallas_call(
        collect_kernel,
        in_specs=[whole()] * 3 + [anywhere()],
        out_specs=whole(),
        out_shape=out,
        compiler_params=params(20),
        cost_estimate=FREE,
        name="collect",
    )(pos, stream, cot, after)


def unpack_kernel(slot_ref, came_ref, base_ref, cot_ref):
    tokens, width = base_ref.shape
    slots = came_ref.shape[0]
    take = eq_hot((tokens, slots), 1, slot_ref[...])
    for start, out_ref in ((0, base_ref), (width, cot_ref)):
        out_ref[...] = jnp.dot(
            take, came_ref[:, start : start + width], preferred_element_type=F32
        ).astype(BF)


def unpack(slot_col, came):
    tokens = slot_col.shape[0]
    slots, both = came.shape
    width = both // 2
    outs = [shape((tokens, width), BF)] * 2
    return pl.pallas_call(
        unpack_kernel,
        in_specs=[whole()] * 2,
        out_specs=[whole()] * 2,
        out_shape=outs,
        compiler_params=params(12),
        cost_estimate=FREE,
        name="unpack",
    )(slot_col, came)


def stack_kernel(here_ref, *refs):
    first = jnp.where(here_ref[0] == 0, here_ref[4], here_ref[3])
    for away, ref in zip(AWAY, refs[:RING]):
        refs[RING][lax.rem(first + away, RING)] = ref[...]


def stack(here, blocks):
    rows, width = blocks[0].shape
    return pl.pallas_call(
        stack_kernel,
        in_specs=[scalars()] + [whole()] * RING,
        out_specs=whole(),
        out_shape=shape((RING, rows, width), BF),
        compiler_params=params(6),
        cost_estimate=FREE,
        name="stack",
    )(here, *blocks)


def fetch(here_ref, stacks, held_ref, sems):
    for index, (away, ref) in enumerate(zip(AWAY, stacks)):

        @pl.when(here_ref[0] == 0)
        def _():
            place = lax.rem(here_ref[3] + away, RING)
            pltpu.make_async_copy(ref, held_ref.at[place], sems.at[index]).start()

        @pl.when(here_ref[0] == 1)
        def _():
            place = lax.rem(here_ref[4] + away, RING)
            pltpu.make_async_copy(ref, held_ref.at[:, place], sems.at[index]).start()

    def wait():
        for index, ref in enumerate(stacks):
            pltpu.make_async_copy(ref, held_ref.at[0], sems.at[index]).wait()

    return wait


def merge_kernel(here_ref, ngain_ref, base_hbm, cot_hbm, *refs):
    stacks, refs = refs[:RING], refs[RING:]
    lifted, refs = refs[:-10], refs[-10:]
    visual_ref, state_ref, stat_ref, held_ref, left_ref, base_ref, cot_ref, w_sems, sems, row_sems = refs
    wait_weight = fetch(here_ref, stacks, held_ref, w_sems)
    depth = left_ref.shape[1]
    block = depth // RING
    steps = range(RING)
    copies = []
    for step in steps:
        at = pl.ds(step * block, block)
        start = 0
        group = []
        for index, ref in enumerate(lifted):
            rows = ref.shape[0]
            group.append(
                pltpu.make_async_copy(
                    ref.at[:, at], left_ref.at[pl.ds(start, rows), at], sems.at[step, index]
                )
            )
            group[-1].start()
            start += rows
        copies.append(group)
    row_copies = [
        pltpu.make_async_copy(a, b, row_sems.at[i])
        for i, (a, b) in enumerate(((base_hbm, base_ref), (cot_hbm, cot_ref)))
    ]
    for copy in row_copies:
        copy.start()
    wait_weight()
    total = None
    for step in steps:
        for copy in copies[step]:
            copy.wait()
        part = jnp.dot(
            left_ref[:, step * block : (step + 1) * block],
            held_ref[step].reshape(block, -1),
            preferred_element_type=F32,
        )
        total = part if total is None else total + part
    for copy in row_copies:
        copy.wait()
    visual = total.astype(BF)
    visual_ref[...] = visual
    state = base_ref[...].astype(F32) + visual.astype(F32)
    state_ref[...] = state
    up = ngain_ref[...].astype(F32) * cot_ref[...].astype(F32)
    lane = lax.broadcasted_iota(jnp.int32, (state.shape[0], 128), 1)
    sums = jnp.where(
        lane == 0,
        jnp.sum(state * state, axis=1, keepdims=True),
        jnp.sum(up * state, axis=1, keepdims=True),
    )
    stat_ref[...] = sums.T[: stat_ref.shape[0]]


def merge(here, base, cot, ngain, stacks, lifted):
    tokens, width = base.shape
    depth = lifted[0].shape[1]
    outs = [shape((tokens, width), BF), shape((tokens, width), F32), shape((8, tokens), F32)]
    return pl.pallas_call(
        merge_kernel,
        in_specs=[scalars(), whole()] + [anywhere()] * (2 + RING + len(lifted)),
        out_specs=[whole()] * 3,
        out_shape=outs,
        scratch_shapes=[
            pltpu.VMEM((RING,) + stacks[0].shape, BF),
            pltpu.VMEM((tokens, depth), BF),
            pltpu.VMEM((tokens, width), BF),
            pltpu.VMEM((tokens, width), BF),
            pltpu.SemaphoreType.DMA((RING,)),
            pltpu.SemaphoreType.DMA((RING, len(lifted))),
            pltpu.SemaphoreType.DMA((2,)),
        ],
        compiler_params=params(56),
        cost_estimate=FREE,
        name="merge",
    )(here, ngain, base, cot, *stacks, *lifted)


def add_kernel(sums_ref, got_ref, near_ref, turned_ref):
    count = sums_ref.shape[1] // 4
    cuts = [
        sums_ref[:, i * count : (i + 1) * count] + got_ref[:, (i ^ 1) * count : ((i ^ 1) + 1) * count]
        for i in range(4)
    ]
    near_ref[...] = jnp.concatenate(cuts, axis=1)
    turned_ref[...] = jnp.concatenate(cuts[2:] + cuts[:2], axis=1)


def add(sums, got):
    return pl.pallas_call(
        add_kernel,
        in_specs=[whole()] * 2,
        out_specs=[whole()] * 2,
        out_shape=[shape(sums.shape, F32)] * 2,
        compiler_params=params(4),
        cost_estimate=FREE,
        name="add",
    )(sums, got)


def pack_kernel(here_ref, slot_ref, visual_ref, after_ref, stay_ref, cross_ref):
    tokens = visual_ref.shape[0]
    slots = stay_ref.shape[0]
    for relative, out_ref in ((0, stay_ref), (1, cross_ref)):
        put = eq_hot((tokens, slots), 1, slot_ref[...] - (here_ref[2] ^ relative) * slots)
        out_ref[...] = lax.dot_general(
            put, visual_ref[...], (((0,), (0,)), ((), ())), preferred_element_type=F32
        ).astype(BF)


def pack(here, slot_col, visual, slots, after):
    tokens, width = visual.shape
    return pl.pallas_call(
        pack_kernel,
        in_specs=[scalars()] + [whole()] * 2 + [anywhere()],
        out_specs=[whole()] * 2,
        out_shape=[shape((slots // 2, width), BF)] * 2,
        compiler_params=params(8),
        cost_estimate=FREE,
        name="pack",
    )(here, slot_col, visual, after)


def braid_kernel(stay_ref, crossed_ref, out_ref):
    count, _, rows, _ = out_ref.shape
    for c in range(count):
        at = slice(c * rows, (c + 1) * rows)
        out_ref[c, 0] = stay_ref[at, :]
        out_ref[c, 1] = crossed_ref[at, :]


def braid(stay, crossed, count):
    rows, width = stay.shape
    return pl.pallas_call(
        braid_kernel,
        in_specs=[whole()] * 2,
        out_specs=whole(),
        out_shape=shape((count, 2, rows // count, width), BF),
        compiler_params=params(6),
        cost_estimate=FREE,
        name="braid",
    )(stay, crossed)


def backward_kernel(full_width, here_ref, ngain_ref, *refs):
    stats, stacks, refs = refs[:RING], refs[RING : 2 * RING], refs[2 * RING :]
    state_hbm, cot_hbm, own_ref, other_ref = refs[:4]
    picked_ref, sums_ref, state_ref, cot_ref, held_ref, row_sems, sems = refs[4:]
    row_copies = [
        pltpu.make_async_copy(a, b, row_sems.at[i])
        for i, (a, b) in enumerate(((state_hbm, state_ref), (cot_hbm, cot_ref)))
    ]
    for copy in row_copies:
        copy.start()
    wait_weight = fetch(here_ref, stacks, held_ref, sems)
    tokens = state_ref.shape[0]
    rows = tokens // 2 // RING
    total = stats[0][...]
    for ref in stats[1:]:
        total = total + ref[...]
    sums_ref[...] = total.T
    far, img = here_ref[1], here_ref[2]
    gain = ngain_ref[...].astype(F32)
    for copy in row_copies:
        copy.wait()
    for core in range(2):
        for away in range(RING):
            there = lax.rem(2 * far + img + away, RING)
            partner = lax.rem(there + img, 2)
            begin = partner * (tokens // 2) + core * (tokens // 4) + (there // 2) * (tokens // 8)
            at = pl.ds(pl.multiple_of(begin, rows), rows)
            sums = sums_ref[at, :]
            inv = lax.rsqrt(sums[:, 0:1] / full_width + 1e-06)
            inner = sums[:, 1:2] / full_width
            up = gain * cot_ref[at, :].astype(F32)
            grad = inv * up - state_ref[at, :] * (inv * inv * inv * inner)
            to = (core * RING + away) * rows
            picked_ref[to : to + rows, :] = grad.astype(BF)
    depth = own_ref.shape[1]
    wait_weight()
    block = depth // RING
    for step in range(RING):
        cols = slice(step * block, (step + 1) * block)
        both = lax.dot_general(
            picked_ref[...],
            held_ref[step].reshape(block, -1),
            (((1,), (1,)), ((), ())),
            preferred_element_type=F32,
        )
        own_ref[:, cols] = both[: tokens // 2].astype(BF)
        other_ref[:, cols] = both[tokens // 2 :].astype(BF)


def backward(here, state, cot, ngain, stats, stacks, full_width):
    tokens, width = state.shape
    depth = RING * stacks[0].shape[0] * stacks[0].shape[1]
    return pl.pallas_call(
        lambda *refs: backward_kernel(full_width, *refs),
        in_specs=[scalars()] + [whole()] * (1 + RING) + [anywhere()] * (RING + 2),
        out_specs=[whole()] * 2,
        out_shape=[shape((tokens // 2, depth), BF)] * 2,
        scratch_shapes=[
            pltpu.VMEM((tokens, width), BF),
            pltpu.VMEM((tokens, 8), F32),
            pltpu.VMEM((tokens, width), F32),
            pltpu.VMEM((tokens, width), BF),
            pltpu.VMEM((RING,) + stacks[0].shape, BF),
            pltpu.SemaphoreType.DMA((2,)),
            pltpu.SemaphoreType.DMA((RING,)),
        ],
        compiler_params=params(50),
        cost_estimate=FREE,
        name="backward",
    )(here, ngain, *stats, *stacks, state, cot)


def pair_kernel(own_ref, got_ref, after_ref, *outs):
    rows = outs[0].shape[0]
    for away, out in enumerate(outs):
        at = slice((away + 1) * rows, (away + 2) * rows)
        out[...] = (own_ref[at, :].astype(F32) + got_ref[at, :].astype(F32)).astype(BF)


def pair(own, got, after):
    rows, depth = got.shape[0] // RING, got.shape[1]
    outs = [shape((rows, depth), BF)] * (RING - 1)
    return pl.pallas_call(
        pair_kernel,
        in_specs=[whole()] * 2 + [anywhere()],
        out_specs=[whole()] * (RING - 1),
        out_shape=outs,
        compiler_params=params(8),
        cost_estimate=FREE,
        name="pair",
    )(own, got, after)


def finish_kernel(here_ref, own_ref, got_ref, *refs):
    came, (xw_ref, stat_ref, gain_ref, out_ref) = refs[: RING - 1], refs[RING - 1 :]
    window, tokens, width = xw_ref.shape
    full = window * width
    mean = stat_ref[:, 0:1]
    inv = stat_ref[:, 1:2]
    lifted = own_ref[...].astype(F32) + got_ref[...].astype(F32)
    for ref in came:
        lifted = lifted + ref[...].astype(F32)
    share = width // (RING * RING)
    scaled = []
    total = 0.0
    inner = 0.0
    for w in range(window):
        g = jnp.concatenate(
            [lifted[:, at : at + share] for at in range(w * share, full, window * share)], axis=1
        ) * gain_ref[w : w + 1].astype(F32)
        normed = (xw_ref[w].astype(F32) - mean) * inv
        total = total + jnp.sum(g, axis=1, keepdims=True)
        inner = inner + jnp.sum(g * normed, axis=1, keepdims=True)
        scaled.append((g, normed))
    total = total / full
    inner = inner / full
    rows = jnp.concatenate(
        [(inv * (g - total - normed * inner)).astype(BF) for g, normed in scaled], axis=0
    )
    out_ref[...] = jnp.dot(
        patch_major(tokens, window), rows, preferred_element_type=F32
    ).astype(BF)


def finish(here, own, got, came, xw, stat, gain):
    rows, depth = came[0].shape
    window, width = gain.shape
    steps = 2
    tokens = rows // steps
    same = pl.BlockSpec((tokens, depth), lambda i, h: (i, 0))
    return pl.pallas_call(
        finish_kernel,
        grid_spec=pltpu.PrefetchScalarGridSpec(
            num_scalar_prefetch=1,
            grid=(steps,),
            in_specs=[same] * (1 + RING)
            + [
                pl.BlockSpec((window, tokens, width), lambda i, h: (0, h[1] * steps + i, 0)),
                pl.BlockSpec((tokens, 128), lambda i, h: (h[1] * steps + i, 0)),
                pl.BlockSpec((window, width), lambda i, h: (0, 0)),
            ],
            out_specs=pl.BlockSpec((tokens * window, width), lambda i, h: (i, 0)),
        ),
        out_shape=shape((rows * window, width), BF),
        compiler_params=params(58),
        cost_estimate=FREE,
        name="finish",
    )(here, own, got, *came, xw, stat, gain)


def place_kernel(here_ref, pos_ref, came_ref, stream_ref, out_ref):
    rows, width = stream_ref.shape
    cut = width // 2
    slots = pos_ref.shape[0]
    put = eq_hot((slots, rows), 1, pos_ref[...])
    for relative in range(2):
        start = pl.multiple_of((here_ref[2] ^ relative) * cut, cut)
        at = pl.ds(start, cut)
        out_ref[:, at] = (
            stream_ref[:, at].astype(F32)
            + lax.dot_general(
                put,
                came_ref[:, relative].reshape(slots, cut),
                (((0,), (0,)), ((), ())),
                preferred_element_type=F32,
            )
        ).astype(BF)


def place(here, pos, came, stream):
    rows, width = stream.shape
    return pl.pallas_call(
        place_kernel,
        in_specs=[scalars()] + [whole()] * 3,
        out_specs=whole(),
        out_shape=shape((rows, width), BF),
        compiler_params=params(12),
        cost_estimate=FREE,
        name="place",
    )(here, pos, came, stream)


def lay_kernel(here_ref, *refs):
    blocks, (out_ref, sems) = refs[:-2], refs[-2:]
    rows = blocks[0].shape[0]
    copies = []
    for index, ref in enumerate(blocks):
        owner = 2 * (here_ref[0] ^ (index // 2)) + (here_ref[1] ^ (index % 2))
        start = pl.multiple_of(owner * rows, rows)
        copies.append(pltpu.make_async_copy(ref, out_ref.at[pl.ds(start, rows)], sems.at[index]))
    for copy in copies:
        copy.start()
    for copy in copies:
        copy.wait()


def lay(here, blocks):
    rows, width = blocks[0].shape
    return pl.pallas_call(
        lay_kernel,
        in_specs=[scalars()] + [whole()] * len(blocks),
        out_specs=anywhere(),
        out_shape=shape((len(blocks) * rows, width), BF),
        scratch_shapes=[pltpu.SemaphoreType.DMA((len(blocks),))],
        compiler_params=params(4),
        cost_estimate=FREE,
        name="lay",
    )(here, *blocks)


def shards(features, ln_gain, ln_bias, projection, stream, norm_gain, cotangent, slots):
    n_img = lax.axis_size("img")
    n_ctx = lax.axis_size("ctx")
    n_tp = lax.axis_size("tp")
    merged = slots.shape[0]
    tok_rows, width = stream.shape
    owners = n_img * n_ctx
    capacity = 2 * merged // owners
    slot_count = owners * capacity
    full_width = width * n_tp
    cut = width // n_img

    img = lax.axis_index("img").astype(jnp.int32)
    tp = lax.axis_index("tp").astype(jnp.int32)
    core, far_half = tp % 2, tp // 2
    z, y = lax.axis_index("ctx") // RING, lax.axis_index("ctx") % RING
    here = jnp.stack([core, far_half, img, z, y]).astype(jnp.int32)

    flip = [(i, 1 - i) for i in range(n_img)]
    core_pairs = [(t, t ^ 1) for t in range(n_tp)]
    far_pairs = [(t, t ^ 2) for t in range(n_tp)]

    def along_x(array, by):
        pairs = []
        for i in range(n_img):
            for t in range(n_tp):
                x = (2 * (t // 2) + i + by) % RING
                pairs.append((i * n_tp + t, (x % 2) * n_tp + 2 * (x // 2) + t % 2))
        return lax.ppermute(array, ("img", "tp"), pairs)

    def along_ctx(array, axis, by):
        pairs = []
        for c in range(n_ctx):
            for t in range(n_tp):
                z, y = c // RING, c % RING
                if t % 2 == axis:
                    y = (y + by) % RING
                else:
                    z = (z + by) % RING
                pairs.append((c * n_tp + t, (z * RING + y) * n_tp + t))
        return lax.ppermute(array, ("ctx", "tp"), pairs)

    slots = jnp.roll(slots, -core * (merged // 2))
    target = slots // tok_rows
    ids = jnp.arange(merged)
    earlier = (target[:, None] == target[None, :]) & (ids[:, None] < ids[None, :])
    rank = jnp.sum(earlier.astype(jnp.int32), axis=0)
    slot = target * capacity + rank
    local = slots - target * tok_rows
    packed = jnp.max(
        jnp.where(jnp.arange(slot_count)[:, None] == slot[None, :], local[None, :], -1), axis=1
    )
    asked = lax.all_to_all(
        packed.reshape(owners, capacity), ("img", "ctx"), split_axis=0, concat_axis=0, tiled=True
    )
    columns = lax.dynamic_slice_in_dim(projection[0], img * cut, cut, axis=2).reshape(-1, cut)
    gain = ln_gain[0]
    lifted, lifted_other, xw, stat = layer_norm(here, features[0], gain, ln_bias[0])
    columns, asked, lifted, stat = lax.optimization_barrier((columns, asked, lifted, stat))
    moves = (1, -1, 2)
    near_blocks = [along_ctx(columns, 0, by) for by in moves]

    asked = asked.reshape(n_img, n_ctx, capacity).transpose(1, 0, 2)
    asked = asked.reshape(slot_count, 1)
    first = stack(here, [columns] + near_blocks)
    held = collect(asked, stream, cotangent[0], first)
    came = lax.all_to_all(
        held.reshape(owners, n_img * capacity, width),
        ("img", "ctx"), split_axis=0, concat_axis=0, tiled=True,
    ).reshape(n_img * slot_count, width)
    paired = target * (n_img * capacity) + rank + img * capacity
    paired = jnp.concatenate([paired, lax.ppermute(paired, "img", flip)]).reshape(-1, 1)

    stacks = [first] + [along_ctx(first, 1, by) for by in moves]

    pairs = []
    for i in range(n_img):
        for t in range(n_tp):
            x = (2 * (t // 2) + i + (1 if t % 2 == 0 else -1)) % RING
            pairs.append((i * n_tp + t, (x % 2) * n_tp + 2 * (x // 2) + t % 2))
    next_mine = lax.ppermute(lifted, ("img", "tp"), pairs)
    next_other = lax.ppermute(next_mine, "tp", core_pairs)

    own_gain = lax.dynamic_slice_in_dim(norm_gain, img * cut, cut, axis=1)
    base, cot = unpack(paired, came)
    visual, state, sums = merge(here, base, cot, own_gain, stacks, [lifted, lifted_other, next_mine, next_other])

    near, turned = add(sums, lax.ppermute(sums, "tp", core_pairs))
    stats = [near] + [along_x(near if by == 2 else turned, by) for by in (1, 2, 3)]
    stay, cross = pack(here, paired, visual, n_img * slot_count, near)
    cross, stats = lax.optimization_barrier((cross, stats))
    crossed = lax.ppermute(cross, "img", flip)

    own, other = backward(here, state, cot, own_gain, stats, stacks, full_width)
    own, other, crossed = lax.optimization_barrier((own, other, crossed))
    got = lax.ppermute(other, "tp", core_pairs)
    sent = pair(own, got, crossed)
    came_back = [along_x(sent[by - 1], by) for by in (1, 2, 3)]

    send = braid(stay, crossed, n_ctx)
    arrived = lax.all_to_all(send, "ctx", split_axis=0, concat_axis=0, tiled=True)
    new_stream = place(here, asked, arrived, stream)

    out = finish(here, own, got, came_back, xw, stat, gain)
    beyond = lax.ppermute(out, "tp", far_pairs)
    beyond, new_stream = lax.optimization_barrier((beyond, new_stream))
    from_core = [lax.ppermute(x, "tp", core_pairs) for x in (out, beyond)]
    grad = lay(here, [out, beyond] + from_core)
    return (new_stream, grad[None])


def solution(mesh):
    placed = (
        P(None, ("img", "ctx"), None),
        P(),
        P(),
        P(None, None, "ctx", "tp"),
        P(("img", "ctx"), "tp"),
        P(None, "tp"),
        P(None, ("img", "ctx"), "tp"),
        P(("img", "ctx")),
    )
    return jax.shard_map(
        shards,
        mesh=mesh,
        in_specs=placed,
        out_specs=(P(("img", "ctx"), "tp"), P(None, ("img", "ctx"), None)),
        check_vma=False,
    )
```

```python
import jax
import jax.numpy as jnp
from jax import lax
from jax.experimental import pallas as pl
from jax.experimental.pallas import tpu as pltpu
from jax.sharding import PartitionSpec as P


BF = jnp.bfloat16
F32 = jnp.float32
FREE = pl.CostEstimate(flops=0, bytes_accessed=0, transcendentals=0)
RING = 4
AWAY = (0, 3, 1, 2)


def params(mib):
    return pltpu.CompilerParams(vmem_limit_bytes=mib * 1024 * 1024)


def whole():
    return pl.BlockSpec(memory_space=pltpu.VMEM)


def shape(dims, kind):
    return jax.ShapeDtypeStruct(dims, kind)


def scalars():
    return pl.BlockSpec(memory_space=pltpu.SMEM)


def in_hbm():
    return pl.BlockSpec(memory_space=pltpu.HBM)


def anywhere():
    return pl.BlockSpec(memory_space=pl.ANY)


def eq_hot(shape, dim, index):
    return (lax.broadcasted_iota(jnp.int32, shape, dim) == index).astype(BF)


def window_major(tokens, window):
    n = tokens * window
    row = lax.broadcasted_iota(jnp.int32, (n, n), 0)
    col = lax.broadcasted_iota(jnp.int32, (n, n), 1)
    return (col == (row % tokens) * window + row // tokens).astype(BF)


def patch_major(tokens, window):
    n = tokens * window
    row = lax.broadcasted_iota(jnp.int32, (n, n), 0)
    col = lax.broadcasted_iota(jnp.int32, (n, n), 1)
    return (col == (row % window) * tokens + row // window).astype(BF)


def norm_kernel(here_ref, x_ref, gain_ref, bias_ref, mine_ref, other_ref, xw_ref, stat_ref):
    window, width = gain_ref.shape
    tokens = x_ref.shape[0] // window
    full = window * width
    x = jnp.dot(window_major(tokens, window), x_ref[...], preferred_element_type=F32)
    parts = [x[w * tokens : (w + 1) * tokens] for w in range(window)]
    total = sum(jnp.sum(p, axis=1, keepdims=True) for p in parts)
    squares = sum(jnp.sum(p * p, axis=1, keepdims=True) for p in parts)
    mean = total / full
    inv = lax.rsqrt(squares / full - mean * mean + 1e-05)
    lifted = []
    for w, p in enumerate(parts):
        normed = (p - mean) * inv
        lifted.append(
            normed * gain_ref[w : w + 1].astype(F32) + bias_ref[w : w + 1].astype(F32)
        )
        xw_ref[w] = p.astype(BF)
    share = width // (RING * RING)
    lifted = jnp.concatenate(
        [p[:, at : at + share] for at in range(0, width, share) for p in lifted], axis=1
    ).astype(BF)
    half = pl.num_programs(0) // 2

    @pl.when(pl.program_id(0) < half)
    def _():
        mine_ref[...] = lifted

    @pl.when(pl.program_id(0) >= half)
    def _():
        other_ref[...] = lifted

    lane = lax.broadcasted_iota(jnp.int32, stat_ref.shape, 1)
    stat_ref[...] = jnp.where(lane == 0, mean, inv)


def layer_norm(here, features, gain, bias):
    rows, width = features.shape
    window = gain.shape[0]
    merged = rows // window
    block = 64
    steps = merged // block
    return pl.pallas_call(
        norm_kernel,
        grid_spec=pltpu.PrefetchScalarGridSpec(
            num_scalar_prefetch=1,
            grid=(steps,),
            in_specs=[
                pl.BlockSpec(
                    (block * window, width),
                    lambda i, c: (lax.rem(i + c[0] * (steps // 2), steps), 0),
                ),
                pl.BlockSpec((window, width), lambda i, c: (0, 0)),
                pl.BlockSpec((window, width), lambda i, c: (0, 0)),
            ],
            out_specs=[
                pl.BlockSpec((block, window * width), lambda i, c: (jnp.minimum(i, steps // 2 - 1), 0)),
                pl.BlockSpec((block, window * width), lambda i, c: (jnp.maximum(i - steps // 2, 0), 0)),
                pl.BlockSpec((window, block, width), lambda i, c: (0, i, 0)),
                pl.BlockSpec((block, 128), lambda i, c: (i, 0)),
            ],
        ),
        out_shape=[
            shape((merged // 2, window * width), BF),
            shape((merged // 2, window * width), BF),
            shape((window, merged, width), BF),
            shape((merged, 128), F32),
        ],
        compiler_params=params(16),
        cost_estimate=FREE,
        name="layer_norm",
    )(here, features, gain, bias)


def collect_kernel(pos_ref, stream_ref, cot_ref, after_ref, out_ref):
    slots = pos_ref.shape[0]
    rows, width = stream_ref.shape
    cut = width // 2
    pick = eq_hot((slots, rows), 1, pos_ref[...])
    for img in range(2):
        at = slice(img * cut, (img + 1) * cut)
        for place, ref in enumerate((stream_ref, cot_ref)):
            out_ref[img, :, place * cut : (place + 1) * cut] = jnp.dot(
                pick, ref[:, at], preferred_element_type=F32
            ).astype(BF)


def collect(pos, stream, cot, after):
    slots = pos.shape[0]
    rows, width = stream.shape
    return pl.pallas_call(
        collect_kernel,
        in_specs=[whole()] * 3 + [anywhere()],
        out_specs=whole(),
        out_shape=shape((2, slots, width), BF),
        compiler_params=params(20),
        cost_estimate=FREE,
        name="collect",
    )(pos, stream, cot, after)


def unpack_kernel(slot_ref, came_ref, base_ref, cot_ref):
    tokens, width = base_ref.shape
    slots = came_ref.shape[0]
    take = eq_hot((tokens, slots), 1, slot_ref[...])
    for start, out_ref in ((0, base_ref), (width, cot_ref)):
        out_ref[...] = jnp.dot(
            take, came_ref[:, start : start + width], preferred_element_type=F32
        ).astype(BF)


def unpack(slot_col, came):
    tokens = slot_col.shape[0]
    slots, both = came.shape
    width = both // 2
    outs = [shape((tokens, width), BF)] * 2
    return pl.pallas_call(
        unpack_kernel,
        in_specs=[whole()] * 2,
        out_specs=[whole()] * 2,
        out_shape=outs,
        compiler_params=params(12),
        cost_estimate=FREE,
        name="unpack",
    )(slot_col, came)


def stack_kernel(here_ref, *refs):
    out_ref, sems = refs[RING:]
    first = jnp.where(here_ref[0] == 0, here_ref[4], here_ref[3])
    copies = [
        pltpu.make_async_copy(ref, out_ref.at[lax.rem(first + away, RING)], sems.at[index])
        for index, (away, ref) in enumerate(zip(AWAY, refs[:RING]))
    ]
    for copy in copies:
        copy.start()
    for copy in copies:
        copy.wait()


def stack(here, blocks):
    rows, width = blocks[0].shape
    return pl.pallas_call(
        stack_kernel,
        in_specs=[scalars()] + [in_hbm()] * RING,
        out_specs=whole(),
        out_shape=shape((RING, rows, width), BF),
        scratch_shapes=[pltpu.SemaphoreType.DMA((RING,))],
        compiler_params=params(6),
        cost_estimate=FREE,
        name="stack",
    )(here, *blocks)


def fetch(here_ref, stacks, held_ref, sems):
    for index, (away, ref) in enumerate(zip(AWAY, stacks)):

        @pl.when(here_ref[0] == 0)
        def _():
            place = lax.rem(here_ref[3] + away, RING)
            pltpu.make_async_copy(ref, held_ref.at[place], sems.at[index]).start()

        @pl.when(here_ref[0] == 1)
        def _():
            place = lax.rem(here_ref[4] + away, RING)
            pltpu.make_async_copy(ref, held_ref.at[:, place], sems.at[index]).start()

    def wait():
        for index, ref in enumerate(stacks):
            pltpu.make_async_copy(ref, held_ref.at[0], sems.at[index]).wait()

    return wait


def merge_kernel(here_ref, ngain_ref, base_hbm, cot_hbm, *refs):
    stacks, refs = refs[:RING], refs[RING:]
    lifted, refs = refs[:-10], refs[-10:]
    visual_ref, state_ref, stat_ref, held_ref, left_ref, base_ref, cot_ref, w_sems, sems, row_sems = refs
    wait_weight = fetch(here_ref, stacks, held_ref, w_sems)
    depth = left_ref.shape[1]
    block = depth // RING
    steps = range(RING)
    copies = []
    for step in steps:
        at = pl.ds(step * block, block)
        start = 0
        group = []
        for index, ref in enumerate(lifted):
            rows = ref.shape[0]
            group.append(
                pltpu.make_async_copy(
                    ref.at[:, at], left_ref.at[pl.ds(start, rows), at], sems.at[step, index]
                )
            )
            group[-1].start()
            start += rows
        copies.append(group)
    row_copies = [
        pltpu.make_async_copy(a, b, row_sems.at[i])
        for i, (a, b) in enumerate(((base_hbm, base_ref), (cot_hbm, cot_ref)))
    ]
    for copy in row_copies:
        copy.start()
    wait_weight()
    total = None
    for step in steps:
        for copy in copies[step]:
            copy.wait()
        part = jnp.dot(
            left_ref[:, step * block : (step + 1) * block],
            held_ref[step].reshape(block, -1),
            preferred_element_type=F32,
        )
        total = part if total is None else total + part
    for copy in row_copies:
        copy.wait()
    visual = total.astype(BF)
    visual_ref[...] = visual
    state = base_ref[...].astype(F32) + visual.astype(F32)
    state_ref[...] = state
    up = ngain_ref[...].astype(F32) * cot_ref[...].astype(F32)
    lane = lax.broadcasted_iota(jnp.int32, (state.shape[0], 128), 1)
    sums = jnp.where(
        lane == 0,
        jnp.sum(state * state, axis=1, keepdims=True),
        jnp.sum(up * state, axis=1, keepdims=True),
    )
    stat_ref[...] = sums.T[: stat_ref.shape[0]]


def merge(here, base, cot, ngain, stacks, lifted):
    tokens, width = base.shape
    depth = lifted[0].shape[1]
    outs = [shape((tokens, width), BF), shape((tokens, width), F32), shape((8, tokens), F32)]
    return pl.pallas_call(
        merge_kernel,
        in_specs=[scalars(), whole()] + [in_hbm()] * (2 + RING + len(lifted)),
        out_specs=[whole()] * 3,
        out_shape=outs,
        scratch_shapes=[
            pltpu.VMEM((RING,) + stacks[0].shape, BF),
            pltpu.VMEM((tokens, depth), BF),
            pltpu.VMEM((tokens, width), BF),
            pltpu.VMEM((tokens, width), BF),
            pltpu.SemaphoreType.DMA((RING,)),
            pltpu.SemaphoreType.DMA((RING, len(lifted))),
            pltpu.SemaphoreType.DMA((2,)),
        ],
        compiler_params=params(56),
        cost_estimate=FREE,
        name="merge",
    )(here, ngain, base, cot, *stacks, *lifted)


def add_kernel(sums_ref, got_ref, near_ref, turned_ref):
    count = sums_ref.shape[1] // 4
    cuts = [
        sums_ref[:, i * count : (i + 1) * count] + got_ref[:, (i ^ 1) * count : ((i ^ 1) + 1) * count]
        for i in range(4)
    ]
    near_ref[...] = jnp.concatenate(cuts, axis=1)
    turned_ref[...] = jnp.concatenate(cuts[2:] + cuts[:2], axis=1)


def add(sums, got):
    return pl.pallas_call(
        add_kernel,
        in_specs=[whole()] * 2,
        out_specs=[whole()] * 2,
        out_shape=[shape(sums.shape, F32)] * 2,
        compiler_params=params(4),
        cost_estimate=FREE,
        name="add",
    )(sums, got)


def pack_kernel(here_ref, slot_ref, visual_ref, after_ref, stay_ref, cross_ref):
    tokens = visual_ref.shape[0]
    slots = stay_ref.shape[0]
    for relative, out_ref in ((0, stay_ref), (1, cross_ref)):
        put = eq_hot((tokens, slots), 1, slot_ref[...] - (here_ref[2] ^ relative) * slots)
        out_ref[...] = lax.dot_general(
            put, visual_ref[...], (((0,), (0,)), ((), ())), preferred_element_type=F32
        ).astype(BF)


def pack(here, slot_col, visual, slots, after):
    tokens, width = visual.shape
    return pl.pallas_call(
        pack_kernel,
        in_specs=[scalars()] + [whole()] * 2 + [anywhere()],
        out_specs=[whole()] * 2,
        out_shape=[shape((slots // 2, width), BF)] * 2,
        compiler_params=params(8),
        cost_estimate=FREE,
        name="pack",
    )(here, slot_col, visual, after)


def braid_kernel(stay_ref, crossed_ref, out_ref):
    count, _, rows, _ = out_ref.shape
    for c in range(count):
        at = slice(c * rows, (c + 1) * rows)
        out_ref[c, 0] = stay_ref[at, :]
        out_ref[c, 1] = crossed_ref[at, :]


def braid(stay, crossed, count):
    rows, width = stay.shape
    return pl.pallas_call(
        braid_kernel,
        in_specs=[whole()] * 2,
        out_specs=whole(),
        out_shape=shape((count, 2, rows // count, width), BF),
        compiler_params=params(6),
        cost_estimate=FREE,
        name="braid",
    )(stay, crossed)


def backward_kernel(full_width, here_ref, ngain_ref, *refs):
    stats, stacks, refs = refs[:RING], refs[RING : 2 * RING], refs[2 * RING :]
    state_hbm, cot_hbm, own_ref, other_ref = refs[:4]
    picked_ref, sums_ref, state_ref, cot_ref, held_ref, row_sems, sems = refs[4:]
    row_copies = [
        pltpu.make_async_copy(a, b, row_sems.at[i])
        for i, (a, b) in enumerate(((state_hbm, state_ref), (cot_hbm, cot_ref)))
    ]
    for copy in row_copies:
        copy.start()
    wait_weight = fetch(here_ref, stacks, held_ref, sems)
    tokens = state_ref.shape[0]
    rows = tokens // 2 // RING
    total = stats[0][...]
    for ref in stats[1:]:
        total = total + ref[...]
    sums_ref[...] = total.T
    far, img = here_ref[1], here_ref[2]
    gain = ngain_ref[...].astype(F32)
    for copy in row_copies:
        copy.wait()
    for core in range(2):
        for away in range(RING):
            there = lax.rem(2 * far + img + away, RING)
            partner = lax.rem(there + img, 2)
            begin = partner * (tokens // 2) + core * (tokens // 4) + (there // 2) * (tokens // 8)
            at = pl.ds(pl.multiple_of(begin, rows), rows)
            sums = sums_ref[at, :]
            inv = lax.rsqrt(sums[:, 0:1] / full_width + 1e-06)
            inner = sums[:, 1:2] / full_width
            up = gain * cot_ref[at, :].astype(F32)
            grad = inv * up - state_ref[at, :] * (inv * inv * inv * inner)
            to = (core * RING + away) * rows
            picked_ref[to : to + rows, :] = grad.astype(BF)
    depth = own_ref.shape[1]
    wait_weight()
    block = depth // RING
    for step in range(RING):
        cols = slice(step * block, (step + 1) * block)
        both = lax.dot_general(
            picked_ref[...],
            held_ref[step].reshape(block, -1),
            (((1,), (1,)), ((), ())),
            preferred_element_type=F32,
        )
        own_ref[:, cols] = both[: tokens // 2].astype(BF)
        other_ref[:, cols] = both[tokens // 2 :].astype(BF)


def backward(here, state, cot, ngain, stats, stacks, full_width):
    tokens, width = state.shape
    depth = RING * stacks[0].shape[0] * stacks[0].shape[1]
    return pl.pallas_call(
        lambda *refs: backward_kernel(full_width, *refs),
        in_specs=[scalars()] + [whole()] * (1 + RING) + [in_hbm()] * (RING + 2),
        out_specs=[whole()] * 2,
        out_shape=[shape((tokens // 2, depth), BF)] * 2,
        scratch_shapes=[
            pltpu.VMEM((tokens, width), BF),
            pltpu.VMEM((tokens, 8), F32),
            pltpu.VMEM((tokens, width), F32),
            pltpu.VMEM((tokens, width), BF),
            pltpu.VMEM((RING,) + stacks[0].shape, BF),
            pltpu.SemaphoreType.DMA((2,)),
            pltpu.SemaphoreType.DMA((RING,)),
        ],
        compiler_params=params(24),
        cost_estimate=FREE,
        name="backward",
    )(here, ngain, *stats, *stacks, state, cot)


def pair_kernel(own_ref, got_ref, after_ref, next_ref, last_ref, keep_ref):
    rows = own_ref.shape[0] // RING
    half = rows // 2

    def total(start):
        at = slice(start, start + half)
        return (own_ref[at, :].astype(F32) + got_ref[at, :].astype(F32)).astype(BF)

    next_ref[:half] = total(2 * rows)
    next_ref[half:] = total(rows + half)
    last_ref[:half] = total(2 * rows + half)
    last_ref[half:] = total(3 * rows)
    keep_ref[:half] = total(rows)
    keep_ref[half:] = total(3 * rows + half)


def pair(own, got, after):
    rows, depth = got.shape[0] // RING, got.shape[1]
    return pl.pallas_call(
        pair_kernel,
        in_specs=[whole()] * 2 + [anywhere()],
        out_specs=[whole()] * 3,
        out_shape=[shape((rows, depth), BF)] * 3,
        compiler_params=params(8),
        cost_estimate=FREE,
        name="pair",
    )(own, got, after)


def relay_kernel(keep_ref, from_last_ref, from_next_ref, next_ref, last_ref):
    half = next_ref.shape[0]
    for at, came_ref, out_ref in (
        (slice(0, half), from_last_ref, next_ref),
        (slice(half, 2 * half), from_next_ref, last_ref),
    ):
        out_ref[...] = (keep_ref[at, :].astype(F32) + came_ref[:half].astype(F32)).astype(BF)


def relay(keep, from_last, from_next):
    rows, depth = keep.shape
    return pl.pallas_call(
        relay_kernel,
        in_specs=[whole()] * 3,
        out_specs=[whole()] * 2,
        out_shape=[shape((rows // 2, depth), BF)] * 2,
        compiler_params=params(8),
        cost_estimate=FREE,
        name="relay",
    )(keep, from_last, from_next)


def finish_kernel(here_ref, own_ref, got_ref, from_last_ref, from_next_ref, late_last_ref, late_next_ref,
                  xw_ref, stat_ref, gain_ref, out_ref):
    window, tokens, width = xw_ref.shape
    full = window * width
    mean = stat_ref[:, 0:1]
    inv = stat_ref[:, 1:2]
    early = jnp.where(pl.program_id(0) == 0, from_next_ref[...], from_last_ref[...])
    late = jnp.where(pl.program_id(0) == 0, late_last_ref[...], late_next_ref[...])
    lifted = own_ref[...].astype(F32) + got_ref[...].astype(F32)
    lifted = lifted + early.astype(F32) + late.astype(F32)
    share = width // (RING * RING)
    scaled = []
    total = 0.0
    inner = 0.0
    for w in range(window):
        g = jnp.concatenate(
            [lifted[:, at : at + share] for at in range(w * share, full, window * share)], axis=1
        ) * gain_ref[w : w + 1].astype(F32)
        normed = (xw_ref[w].astype(F32) - mean) * inv
        total = total + jnp.sum(g, axis=1, keepdims=True)
        inner = inner + jnp.sum(g * normed, axis=1, keepdims=True)
        scaled.append((g, normed))
    total = total / full
    inner = inner / full
    rows = jnp.concatenate(
        [(inv * (g - total - normed * inner)).astype(BF) for g, normed in scaled], axis=0
    )
    out_ref[...] = jnp.dot(
        patch_major(tokens, window), rows, preferred_element_type=F32
    ).astype(BF)


def finish(here, own, got, early, late, xw, stat, gain):
    rows, depth = early[0].shape
    window, width = gain.shape
    steps = 2
    tokens = rows // steps
    same = pl.BlockSpec((tokens, depth), lambda i, h: (i, 0))
    second = pl.BlockSpec((tokens, depth), lambda i, h: (1, 0))
    only = pl.BlockSpec((tokens, depth), lambda i, h: (0, 0))
    return pl.pallas_call(
        finish_kernel,
        grid_spec=pltpu.PrefetchScalarGridSpec(
            num_scalar_prefetch=1,
            grid=(steps,),
            in_specs=[same, same, second, second, only, only]
            + [
                pl.BlockSpec((window, tokens, width), lambda i, h: (0, h[1] * steps + i, 0)),
                pl.BlockSpec((tokens, 128), lambda i, h: (h[1] * steps + i, 0)),
                pl.BlockSpec((window, width), lambda i, h: (0, 0)),
            ],
            out_specs=pl.BlockSpec((tokens * window, width), lambda i, h: (i, 0)),
        ),
        out_shape=shape((rows * window, width), BF),
        compiler_params=params(58),
        cost_estimate=FREE,
        name="finish",
    )(here, own, got, *early, *late, xw, stat, gain)


def place_kernel(here_ref, pos_ref, came_ref, stream_ref, out_ref):
    rows, width = stream_ref.shape
    cut = width // 2
    slots = pos_ref.shape[0]
    put = eq_hot((slots, rows), 1, pos_ref[...])
    for relative in range(2):
        start = pl.multiple_of((here_ref[2] ^ relative) * cut, cut)
        at = pl.ds(start, cut)
        out_ref[:, at] = (
            stream_ref[:, at].astype(F32)
            + lax.dot_general(
                put,
                came_ref[:, relative].reshape(slots, cut),
                (((0,), (0,)), ((), ())),
                preferred_element_type=F32,
            )
        ).astype(BF)


def place(here, pos, came, stream):
    rows, width = stream.shape
    return pl.pallas_call(
        place_kernel,
        in_specs=[scalars()] + [whole()] * 3,
        out_specs=whole(),
        out_shape=shape((rows, width), BF),
        compiler_params=params(12),
        cost_estimate=FREE,
        name="place",
    )(here, pos, came, stream)


def lay_kernel(here_ref, *refs):
    blocks, (out_ref, sems) = refs[:-2], refs[-2:]
    rows = blocks[0].shape[0]
    copies = []
    for index, ref in enumerate(blocks):
        owner = 2 * (here_ref[0] ^ (index // 2)) + (here_ref[1] ^ (index % 2))
        start = pl.multiple_of(owner * rows, rows)
        copies.append(pltpu.make_async_copy(ref, out_ref.at[pl.ds(start, rows)], sems.at[index]))
    for copy in copies:
        copy.start()
    for copy in copies:
        copy.wait()


def lay(here, blocks):
    rows, width = blocks[0].shape
    return pl.pallas_call(
        lay_kernel,
        in_specs=[scalars()] + [whole()] * len(blocks),
        out_specs=anywhere(),
        out_shape=shape((len(blocks) * rows, width), BF),
        scratch_shapes=[pltpu.SemaphoreType.DMA((len(blocks),))],
        compiler_params=params(4),
        cost_estimate=FREE,
        name="lay",
    )(here, *blocks)


def shards(features, ln_gain, ln_bias, projection, stream, norm_gain, cotangent, slots):
    n_img = lax.axis_size("img")
    n_ctx = lax.axis_size("ctx")
    n_tp = lax.axis_size("tp")
    merged = slots.shape[0]
    tok_rows, width = stream.shape
    owners = n_img * n_ctx
    capacity = 2 * merged // owners
    slot_count = owners * capacity
    full_width = width * n_tp
    cut = width // n_img

    img = lax.axis_index("img").astype(jnp.int32)
    tp = lax.axis_index("tp").astype(jnp.int32)
    core, far_half = tp % 2, tp // 2
    z, y = lax.axis_index("ctx") // RING, lax.axis_index("ctx") % RING
    here = jnp.stack([core, far_half, img, z, y]).astype(jnp.int32)

    flip = [(i, 1 - i) for i in range(n_img)]
    core_pairs = [(t, t ^ 1) for t in range(n_tp)]
    far_pairs = [(t, t ^ 2) for t in range(n_tp)]

    def along_x(array, by):
        pairs = []
        for i in range(n_img):
            for t in range(n_tp):
                x = (2 * (t // 2) + i + by) % RING
                pairs.append((i * n_tp + t, (x % 2) * n_tp + 2 * (x // 2) + t % 2))
        return lax.ppermute(array, ("img", "tp"), pairs)

    def along_ctx(array, axis, by):
        pairs = []
        for c in range(n_ctx):
            for t in range(n_tp):
                z, y = c // RING, c % RING
                if t % 2 == axis:
                    y = (y + by) % RING
                else:
                    z = (z + by) % RING
                pairs.append((c * n_tp + t, (z * RING + y) * n_tp + t))
        return lax.ppermute(array, ("ctx", "tp"), pairs)

    slots = jnp.roll(slots, -core * (merged // 2))
    target = slots // tok_rows
    ids = jnp.arange(merged)
    earlier = (target[:, None] == target[None, :]) & (ids[:, None] < ids[None, :])
    rank = jnp.sum(earlier.astype(jnp.int32), axis=0)
    slot = target * capacity + rank
    local = slots - target * tok_rows
    packed = jnp.max(
        jnp.where(jnp.arange(slot_count)[:, None] == slot[None, :], local[None, :], -1), axis=1
    )
    asked = lax.all_to_all(
        packed.reshape(owners, capacity), ("img", "ctx"), split_axis=0, concat_axis=0, tiled=True
    )
    columns = lax.dynamic_slice_in_dim(projection[0], img * cut, cut, axis=2).reshape(-1, cut)
    gain = ln_gain[0]
    lifted, lifted_other, xw, stat = layer_norm(here, features[0], gain, ln_bias[0])
    moves = (1, -1, 2)
    near_blocks = [along_ctx(columns, 0, by) for by in moves]
    asked, lifted, stat, near_blocks = lax.optimization_barrier((asked, lifted, stat, near_blocks))

    first = stack(here, [columns] + near_blocks)
    asked, first = lax.optimization_barrier((asked, first))

    asked = asked.reshape(n_img, n_ctx, capacity).transpose(1, 0, 2)
    asked = asked.reshape(slot_count, 1)
    held = collect(asked, stream, cotangent[0], first)
    paired = target * (n_img * capacity) + rank + img * capacity
    paired = jnp.concatenate([paired, lax.ppermute(paired, "img", flip)]).reshape(-1, 1)
    came = lax.all_to_all(
        held.reshape(owners, n_img * capacity, width),
        ("img", "ctx"), split_axis=0, concat_axis=0, tiled=True,
    ).reshape(n_img * slot_count, width)
    stacks = [first] + [along_ctx(first, 1, by) for by in moves]

    pairs = []
    for i in range(n_img):
        for t in range(n_tp):
            x = (2 * (t // 2) + i + (1 if t % 2 == 0 else -1)) % RING
            pairs.append((i * n_tp + t, (x % 2) * n_tp + 2 * (x // 2) + t % 2))
    next_mine = lax.ppermute(lifted, ("img", "tp"), pairs)
    next_other = lax.ppermute(next_mine, "tp", core_pairs)

    own_gain = lax.dynamic_slice_in_dim(norm_gain, img * cut, cut, axis=1)
    base, cot = unpack(paired, came)
    visual, state, sums = merge(here, base, cot, own_gain, stacks, [lifted, lifted_other, next_mine, next_other])

    near, turned = add(sums, lax.ppermute(sums, "tp", core_pairs))
    stats = [near] + [along_x(near if by == 2 else turned, by) for by in (1, 2, 3)]
    stay, cross = pack(here, paired, visual, n_img * slot_count, near)
    cross, stats = lax.optimization_barrier((cross, stats))
    crossed = lax.ppermute(cross, "img", flip)

    own, other = backward(here, state, cot, own_gain, stats, stacks, full_width)
    own, other, crossed = lax.optimization_barrier((own, other, crossed))
    got = lax.ppermute(other, "tp", core_pairs)
    to_next, to_last, keep = pair(own, got, crossed)
    from_last, from_next = along_x(to_next, 1), along_x(to_last, -1)
    to_next, to_last = relay(keep, from_last, from_next)
    late_last, late_next = along_x(to_next, 1), along_x(to_last, -1)

    send = braid(stay, crossed, n_ctx)
    arrived = lax.all_to_all(send, "ctx", split_axis=0, concat_axis=0, tiled=True)
    new_stream = place(here, asked, arrived, stream)

    out = finish(here, own, got, (from_last, from_next), (late_last, late_next), xw, stat, gain)
    beyond = lax.ppermute(out, "tp", far_pairs)
    beyond, new_stream = lax.optimization_barrier((beyond, new_stream))
    from_core = [lax.ppermute(x, "tp", core_pairs) for x in (out, beyond)]
    grad = lay(here, [out, beyond] + from_core)
    return (new_stream, grad[None])


def solution(mesh):
    placed = (
        P(None, ("img", "ctx"), None),
        P(),
        P(),
        P(None, None, "ctx", "tp"),
        P(("img", "ctx"), "tp"),
        P(None, "tp"),
        P(None, ("img", "ctx"), "tp"),
        P(("img", "ctx")),
    )
    return jax.shard_map(
        shards,
        mesh=mesh,
        in_specs=placed,
        out_specs=(P(("img", "ctx"), "tp"), P(None, ("img", "ctx"), None)),
        check_vma=False,
    )
```

```python
import jax
import jax.numpy as jnp
from jax import lax
from jax.experimental import pallas as pl
from jax.experimental.pallas import tpu as pltpu
from jax.sharding import PartitionSpec as P


BF = jnp.bfloat16
F32 = jnp.float32
FREE = pl.CostEstimate(flops=0, bytes_accessed=0, transcendentals=0)
RING = 4
AWAY = (0, 3, 1, 2)


def params(mib):
    return pltpu.CompilerParams(vmem_limit_bytes=mib * 1024 * 1024)


def whole():
    return pl.BlockSpec(memory_space=pltpu.VMEM)


def shape(dims, kind):
    return jax.ShapeDtypeStruct(dims, kind)


def scalars():
    return pl.BlockSpec(memory_space=pltpu.SMEM)


def in_hbm():
    return pl.BlockSpec(memory_space=pltpu.HBM)


def anywhere():
    return pl.BlockSpec(memory_space=pl.ANY)


def eq_hot(shape, dim, index):
    return (lax.broadcasted_iota(jnp.int32, shape, dim) == index).astype(BF)


def window_major(tokens, window):
    n = tokens * window
    row = lax.broadcasted_iota(jnp.int32, (n, n), 0)
    col = lax.broadcasted_iota(jnp.int32, (n, n), 1)
    return (col == (row % tokens) * window + row // tokens).astype(BF)


def patch_major(tokens, window):
    n = tokens * window
    row = lax.broadcasted_iota(jnp.int32, (n, n), 0)
    col = lax.broadcasted_iota(jnp.int32, (n, n), 1)
    return (col == (row % window) * tokens + row // window).astype(BF)


def norm_kernel(here_ref, x_ref, gain_ref, bias_ref, lifted_ref, xw_ref, stat_ref):
    window, width = gain_ref.shape
    tokens = x_ref.shape[0] // window
    full = window * width
    x = jnp.dot(window_major(tokens, window), x_ref[...], preferred_element_type=F32)
    parts = [x[w * tokens : (w + 1) * tokens] for w in range(window)]
    total = sum(jnp.sum(p, axis=1, keepdims=True) for p in parts)
    squares = sum(jnp.sum(p * p, axis=1, keepdims=True) for p in parts)
    mean = total / full
    inv = lax.rsqrt(squares / full - mean * mean + 1e-05)
    lifted = []
    for w, p in enumerate(parts):
        normed = (p - mean) * inv
        lifted.append(
            normed * gain_ref[w : w + 1].astype(F32) + bias_ref[w : w + 1].astype(F32)
        )
        xw_ref[w] = p.astype(BF)
    share = width // (RING * RING)
    for core in range(2):

        @pl.when(here_ref[0] == core)
        def _():
            blocks = [(a, b) for a in range(RING) for b in range(RING)]
            starts = [(a * RING + b if core == 0 else b * RING + a) * share for a, b in blocks]
            lifted_ref[...] = jnp.concatenate(
                [p[:, at : at + share] for at in starts for p in lifted], axis=1
            ).astype(BF)

    lane = lax.broadcasted_iota(jnp.int32, stat_ref.shape, 1)
    stat_ref[...] = jnp.where(lane == 0, mean, inv)


def layer_norm(here, features, gain, bias):
    rows, width = features.shape
    window = gain.shape[0]
    merged = rows // window
    block = 64
    steps = merged // block
    return pl.pallas_call(
        norm_kernel,
        grid_spec=pltpu.PrefetchScalarGridSpec(
            num_scalar_prefetch=1,
            grid=(steps,),
            in_specs=[
                pl.BlockSpec(
                    (block * window, width),
                    lambda i, c: (lax.rem(i + c[0] * (steps // 2), steps), 0),
                ),
                pl.BlockSpec((window, width), lambda i, c: (0, 0)),
                pl.BlockSpec((window, width), lambda i, c: (0, 0)),
            ],
            out_specs=[
                pl.BlockSpec((block, window * width), lambda i, c: (i, 0)),
                pl.BlockSpec((window, block, width), lambda i, c: (0, i, 0)),
                pl.BlockSpec((block, 128), lambda i, c: (i, 0)),
            ],
        ),
        out_shape=[
            shape((merged, window * width), BF),
            shape((window, merged, width), BF),
            shape((merged, 128), F32),
        ],
        compiler_params=params(58),
        cost_estimate=FREE,
        name="layer_norm",
    )(here, features, gain, bias)


def collect_kernel(pos_ref, stream_ref, cot_ref, after_ref, out_ref):
    slots = pos_ref.shape[0]
    rows, width = stream_ref.shape
    cut = width // 2
    pick = eq_hot((slots, rows), 1, pos_ref[...])
    for img in range(2):
        at = slice(img * cut, (img + 1) * cut)
        for place, ref in enumerate((stream_ref, cot_ref)):
            out_ref[img, :, place * cut : (place + 1) * cut] = jnp.dot(
                pick, ref[:, at], preferred_element_type=F32
            ).astype(BF)


def collect(pos, stream, cot, after):
    slots = pos.shape[0]
    rows, width = stream.shape
    return pl.pallas_call(
        collect_kernel,
        in_specs=[whole()] * 3 + [anywhere()],
        out_specs=whole(),
        out_shape=shape((2, slots, width), BF),
        compiler_params=params(20),
        cost_estimate=FREE,
        name="collect",
    )(pos, stream, cot, after)


def unpack_kernel(slot_ref, came_ref, base_ref, cot_ref):
    tokens, width = base_ref.shape
    slots = came_ref.shape[0]
    take = eq_hot((tokens, slots), 1, slot_ref[...])
    for start, out_ref in ((0, base_ref), (width, cot_ref)):
        out_ref[...] = jnp.dot(
            take, came_ref[:, start : start + width], preferred_element_type=F32
        ).astype(BF)


def unpack(slot_col, came):
    tokens = slot_col.shape[0]
    slots, both = came.shape
    width = both // 2
    outs = [shape((tokens, width), BF)] * 2
    return pl.pallas_call(
        unpack_kernel,
        in_specs=[whole()] * 2,
        out_specs=[whole()] * 2,
        out_shape=outs,
        compiler_params=params(12),
        cost_estimate=FREE,
        name="unpack",
    )(slot_col, came)


def stack_kernel(here_ref, *refs):
    out_ref, sems = refs[RING:]
    first = jnp.where(here_ref[0] == 0, here_ref[4], here_ref[3])
    copies = [
        pltpu.make_async_copy(ref, out_ref.at[lax.rem(first + away, RING)], sems.at[index])
        for index, (away, ref) in enumerate(zip(AWAY, refs[:RING]))
    ]
    for copy in copies:
        copy.start()
    for copy in copies:
        copy.wait()


def stack(here, blocks):
    rows, width = blocks[0].shape
    return pl.pallas_call(
        stack_kernel,
        in_specs=[scalars()] + [in_hbm()] * RING,
        out_specs=whole(),
        out_shape=shape((RING, rows, width), BF),
        scratch_shapes=[pltpu.SemaphoreType.DMA((RING,))],
        compiler_params=params(6),
        cost_estimate=FREE,
        name="stack",
    )(here, *blocks)


def fetch(here_ref, stacks, held_ref, sems):
    for index, (away, ref) in enumerate(zip(AWAY, stacks)):

        @pl.when(here_ref[0] == 0)
        def _():
            place = lax.rem(here_ref[3] + away, RING)
            pltpu.make_async_copy(ref, held_ref.at[place], sems.at[index]).start()

        @pl.when(here_ref[0] == 1)
        def _():
            place = lax.rem(here_ref[4] + away, RING)
            pltpu.make_async_copy(ref, held_ref.at[:, place], sems.at[index]).start()

    def wait():
        for index, ref in enumerate(stacks):
            pltpu.make_async_copy(ref, held_ref.at[0], sems.at[index]).wait()

    return wait


def product(here_ref, away, stacks, lifted, held_ref, left_ref, sems):
    second = jnp.where(here_ref[0] == 0, here_ref[3], here_ref[4])
    block = left_ref.shape[2]
    rows = lifted[0].shape[0]
    copies = []
    for index, ref in enumerate(stacks):
        place = lax.rem(second + away[index], RING)
        at = pl.ds(pl.multiple_of(place * block, block), block)
        group = [pltpu.make_async_copy(ref, held_ref.at[index], sems.at[index, 0])]
        for i, part in enumerate(lifted):
            to = left_ref.at[index, pl.ds(i * rows, rows)]
            group.append(pltpu.make_async_copy(part.at[:, at], to, sems.at[index, 1 + i]))
        for copy in group:
            copy.start()
        copies.append(group)

    def run(total):
        for index, group in enumerate(copies):
            for copy in group:
                copy.wait()
            part = jnp.dot(
                left_ref[index], held_ref[index].reshape(block, -1), preferred_element_type=F32
            )
            total = part if total is None else total + part
        return total

    return run


def product_scratch(stacks, lifted):
    count = len(stacks)
    rows, depth = lifted[0].shape
    return [
        pltpu.VMEM((count,) + stacks[0].shape, BF),
        pltpu.VMEM((count, len(lifted) * rows, depth // RING), BF),
        pltpu.SemaphoreType.DMA((count, 1 + len(lifted))),
    ]


def multiply_kernel(here_ref, *refs):
    stacks, lifted, (out_ref, *scratch) = refs[: RING - 1], refs[RING - 1 : RING + 1], refs[RING + 1 :]
    out_ref[...] = product(here_ref, AWAY[: RING - 1], stacks, lifted, *scratch)(None)


def multiply(here, stacks, lifted):
    tokens, width = 2 * lifted[0].shape[0], stacks[0].shape[2]
    return pl.pallas_call(
        multiply_kernel,
        in_specs=[scalars()] + [in_hbm()] * (len(stacks) + len(lifted)),
        out_specs=whole(),
        out_shape=shape((tokens, width), F32),
        scratch_shapes=product_scratch(stacks, lifted),
        compiler_params=params(40),
        cost_estimate=FREE,
        name="multiply",
    )(here, *stacks, *lifted)


def merge_kernel(here_ref, ngain_ref, acc_hbm, base_hbm, cot_hbm, stack_ref, *refs):
    lifted, refs = refs[:2], refs[2:]
    visual_ref, state_ref, stat_ref, acc_ref, base_ref, cot_ref, row_sems, *scratch = refs
    run = product(here_ref, AWAY[RING - 1 :], (stack_ref,), lifted, *scratch)
    copies = [
        pltpu.make_async_copy(a, b, row_sems.at[i])
        for i, (a, b) in enumerate(((acc_hbm, acc_ref), (base_hbm, base_ref), (cot_hbm, cot_ref)))
    ]
    for copy in copies:
        copy.start()
    total = run(None)
    for copy in copies:
        copy.wait()
    visual = (acc_ref[...] + total).astype(BF)
    visual_ref[...] = visual
    state = base_ref[...].astype(F32) + visual.astype(F32)
    state_ref[...] = state
    up = ngain_ref[...].astype(F32) * cot_ref[...].astype(F32)
    lane = lax.broadcasted_iota(jnp.int32, (state.shape[0], 128), 1)
    sums = jnp.where(
        lane == 0,
        jnp.sum(state * state, axis=1, keepdims=True),
        jnp.sum(up * state, axis=1, keepdims=True),
    )
    stat_ref[...] = sums.T[: stat_ref.shape[0]]


def merge(here, ngain, acc, base, cot, stack, lifted):
    tokens, width = base.shape
    outs = [shape((tokens, width), BF), shape((tokens, width), F32), shape((8, tokens), F32)]
    return pl.pallas_call(
        merge_kernel,
        in_specs=[scalars(), whole()] + [in_hbm()] * 6,
        out_specs=[whole()] * 3,
        out_shape=outs,
        scratch_shapes=[
            pltpu.VMEM((tokens, width), F32),
            pltpu.VMEM((tokens, width), BF),
            pltpu.VMEM((tokens, width), BF),
            pltpu.SemaphoreType.DMA((3,)),
        ]
        + product_scratch((stack,), lifted),
        compiler_params=params(24),
        cost_estimate=FREE,
        name="merge",
    )(here, ngain, acc, base, cot, stack, *lifted)


def add_kernel(sums_ref, got_ref, near_ref, turned_ref):
    count = sums_ref.shape[1] // 4
    cuts = [
        sums_ref[:, i * count : (i + 1) * count] + got_ref[:, (i ^ 1) * count : ((i ^ 1) + 1) * count]
        for i in range(4)
    ]
    near_ref[...] = jnp.concatenate(cuts, axis=1)
    turned_ref[...] = jnp.concatenate(cuts[2:] + cuts[:2], axis=1)


def add(sums, got):
    return pl.pallas_call(
        add_kernel,
        in_specs=[whole()] * 2,
        out_specs=[whole()] * 2,
        out_shape=[shape(sums.shape, F32)] * 2,
        compiler_params=params(4),
        cost_estimate=FREE,
        name="add",
    )(sums, got)


def pack_kernel(here_ref, slot_ref, visual_ref, after_ref, stay_ref, cross_ref):
    tokens = visual_ref.shape[0]
    slots = stay_ref.shape[0]
    for relative, out_ref in ((0, stay_ref), (1, cross_ref)):
        put = eq_hot((tokens, slots), 1, slot_ref[...] - (here_ref[2] ^ relative) * slots)
        out_ref[...] = lax.dot_general(
            put, visual_ref[...], (((0,), (0,)), ((), ())), preferred_element_type=F32
        ).astype(BF)


def pack(here, slot_col, visual, slots, after):
    tokens, width = visual.shape
    return pl.pallas_call(
        pack_kernel,
        in_specs=[scalars()] + [whole()] * 2 + [anywhere()],
        out_specs=[whole()] * 2,
        out_shape=[shape((slots // 2, width), BF)] * 2,
        compiler_params=params(8),
        cost_estimate=FREE,
        name="pack",
    )(here, slot_col, visual, after)


def braid_kernel(stay_ref, crossed_ref, out_ref):
    count, _, rows, _ = out_ref.shape
    for c in range(count):
        at = slice(c * rows, (c + 1) * rows)
        out_ref[c, 0] = stay_ref[at, :]
        out_ref[c, 1] = crossed_ref[at, :]


def braid(stay, crossed, count):
    rows, width = stay.shape
    return pl.pallas_call(
        braid_kernel,
        in_specs=[whole()] * 2,
        out_specs=whole(),
        out_shape=shape((count, 2, rows // count, width), BF),
        compiler_params=params(6),
        cost_estimate=FREE,
        name="braid",
    )(stay, crossed)


def backward_kernel(full_width, here_ref, ngain_ref, *refs):
    stats, stacks, refs = refs[:RING], refs[RING : 2 * RING], refs[2 * RING :]
    state_hbm, cot_hbm, own_ref, other_ref = refs[:4]
    picked_ref, sums_ref, state_ref, cot_ref, held_ref, row_sems, sems = refs[4:]
    row_copies = [
        pltpu.make_async_copy(a, b, row_sems.at[i])
        for i, (a, b) in enumerate(((state_hbm, state_ref), (cot_hbm, cot_ref)))
    ]
    for copy in row_copies:
        copy.start()
    wait_weight = fetch(here_ref, stacks, held_ref, sems)
    tokens = state_ref.shape[0]
    rows = tokens // 2 // RING
    total = stats[0][...]
    for ref in stats[1:]:
        total = total + ref[...]
    sums_ref[...] = total.T
    far, img = here_ref[1], here_ref[2]
    gain = ngain_ref[...].astype(F32)
    for copy in row_copies:
        copy.wait()
    for core in range(2):
        for away in range(RING):
            there = lax.rem(2 * far + img + away, RING)
            partner = lax.rem(there + img, 2)
            begin = partner * (tokens // 2) + core * (tokens // 4) + (there // 2) * (tokens // 8)
            at = pl.ds(pl.multiple_of(begin, rows), rows)
            sums = sums_ref[at, :]
            inv = lax.rsqrt(sums[:, 0:1] / full_width + 1e-06)
            inner = sums[:, 1:2] / full_width
            up = gain * cot_ref[at, :].astype(F32)
            grad = inv * up - state_ref[at, :] * (inv * inv * inv * inner)
            to = (core * RING + away) * rows
            picked_ref[to : to + rows, :] = grad.astype(BF)
    depth = own_ref.shape[1]
    wait_weight()
    block = depth // RING
    for step in range(RING):
        cols = slice(step * block, (step + 1) * block)
        both = lax.dot_general(
            picked_ref[...],
            held_ref[step].reshape(block, -1),
            (((1,), (1,)), ((), ())),
            preferred_element_type=F32,
        )
        own_ref[:, cols] = both[: tokens // 2].astype(BF)
        other_ref[:, cols] = both[tokens // 2 :].astype(BF)


def backward(here, state, cot, ngain, stats, stacks, full_width):
    tokens, width = state.shape
    depth = RING * stacks[0].shape[0] * stacks[0].shape[1]
    return pl.pallas_call(
        lambda *refs: backward_kernel(full_width, *refs),
        in_specs=[scalars()] + [whole()] * (1 + RING) + [in_hbm()] * (RING + 2),
        out_specs=[whole()] * 2,
        out_shape=[shape((tokens // 2, depth), BF)] * 2,
        scratch_shapes=[
            pltpu.VMEM((tokens, width), BF),
            pltpu.VMEM((tokens, 8), F32),
            pltpu.VMEM((tokens, width), F32),
            pltpu.VMEM((tokens, width), BF),
            pltpu.VMEM((RING,) + stacks[0].shape, BF),
            pltpu.SemaphoreType.DMA((2,)),
            pltpu.SemaphoreType.DMA((RING,)),
        ],
        compiler_params=params(24),
        cost_estimate=FREE,
        name="backward",
    )(here, ngain, *stats, *stacks, state, cot)


def pair_kernel(own_ref, got_ref, after_ref, next_ref, last_ref, keep_ref):
    rows = own_ref.shape[0] // RING
    half = rows // 2

    def total(start):
        at = slice(start, start + half)
        return (own_ref[at, :].astype(F32) + got_ref[at, :].astype(F32)).astype(BF)

    next_ref[:half] = total(2 * rows)
    next_ref[half:] = total(rows + half)
    last_ref[:half] = total(2 * rows + half)
    last_ref[half:] = total(3 * rows)
    keep_ref[:half] = total(rows)
    keep_ref[half:] = total(3 * rows + half)


def pair(own, got, after):
    rows, depth = got.shape[0] // RING, got.shape[1]
    return pl.pallas_call(
        pair_kernel,
        in_specs=[whole()] * 2 + [anywhere()],
        out_specs=[whole()] * 3,
        out_shape=[shape((rows, depth), BF)] * 3,
        compiler_params=params(8),
        cost_estimate=FREE,
        name="pair",
    )(own, got, after)


def relay_kernel(keep_ref, from_last_ref, from_next_ref, next_ref, last_ref):
    half = next_ref.shape[0]
    for at, came_ref, out_ref in (
        (slice(0, half), from_last_ref, next_ref),
        (slice(half, 2 * half), from_next_ref, last_ref),
    ):
        out_ref[...] = (keep_ref[at, :].astype(F32) + came_ref[:half].astype(F32)).astype(BF)


def relay(keep, from_last, from_next):
    rows, depth = keep.shape
    return pl.pallas_call(
        relay_kernel,
        in_specs=[whole()] * 3,
        out_specs=[whole()] * 2,
        out_shape=[shape((rows // 2, depth), BF)] * 2,
        compiler_params=params(8),
        cost_estimate=FREE,
        name="relay",
    )(keep, from_last, from_next)


def finish_kernel(here_ref, own_ref, got_ref, from_last_ref, from_next_ref, late_last_ref, late_next_ref,
                  xw_ref, stat_ref, gain_ref, out_ref):
    window, tokens, width = xw_ref.shape
    full = window * width
    mean = stat_ref[:, 0:1]
    inv = stat_ref[:, 1:2]
    early = jnp.where(pl.program_id(0) == 0, from_next_ref[...], from_last_ref[...])
    late = jnp.where(pl.program_id(0) == 0, late_last_ref[...], late_next_ref[...])
    lifted = own_ref[...].astype(F32) + got_ref[...].astype(F32)
    lifted = lifted + early.astype(F32) + late.astype(F32)
    share = width // (RING * RING)
    scaled = []
    total = 0.0
    inner = 0.0
    for w in range(window):
        g = jnp.concatenate(
            [lifted[:, at : at + share] for at in range(w * share, full, window * share)], axis=1
        ) * gain_ref[w : w + 1].astype(F32)
        normed = (xw_ref[w].astype(F32) - mean) * inv
        total = total + jnp.sum(g, axis=1, keepdims=True)
        inner = inner + jnp.sum(g * normed, axis=1, keepdims=True)
        scaled.append((g, normed))
    total = total / full
    inner = inner / full
    rows = jnp.concatenate(
        [(inv * (g - total - normed * inner)).astype(BF) for g, normed in scaled], axis=0
    )
    out_ref[...] = jnp.dot(
        patch_major(tokens, window), rows, preferred_element_type=F32
    ).astype(BF)


def finish(here, own, got, early, late, xw, stat, gain):
    rows, depth = early[0].shape
    window, width = gain.shape
    steps = 2
    tokens = rows // steps
    same = pl.BlockSpec((tokens, depth), lambda i, h: (i, 0))
    second = pl.BlockSpec((tokens, depth), lambda i, h: (1, 0))
    only = pl.BlockSpec((tokens, depth), lambda i, h: (0, 0))
    return pl.pallas_call(
        finish_kernel,
        grid_spec=pltpu.PrefetchScalarGridSpec(
            num_scalar_prefetch=1,
            grid=(steps,),
            in_specs=[same, same, second, second, only, only]
            + [
                pl.BlockSpec((window, tokens, width), lambda i, h: (0, h[1] * steps + i, 0)),
                pl.BlockSpec((tokens, 128), lambda i, h: (h[1] * steps + i, 0)),
                pl.BlockSpec((window, width), lambda i, h: (0, 0)),
            ],
            out_specs=pl.BlockSpec((tokens * window, width), lambda i, h: (i, 0)),
        ),
        out_shape=shape((rows * window, width), BF),
        compiler_params=params(58),
        cost_estimate=FREE,
        name="finish",
    )(here, own, got, *early, *late, xw, stat, gain)


def place_kernel(here_ref, pos_ref, came_ref, stream_ref, out_ref):
    rows, width = stream_ref.shape
    cut = width // 2
    slots = pos_ref.shape[0]
    put = eq_hot((slots, rows), 1, pos_ref[...])
    for relative in range(2):
        start = pl.multiple_of((here_ref[2] ^ relative) * cut, cut)
        at = pl.ds(start, cut)
        out_ref[:, at] = (
            stream_ref[:, at].astype(F32)
            + lax.dot_general(
                put,
                came_ref[:, relative].reshape(slots, cut),
                (((0,), (0,)), ((), ())),
                preferred_element_type=F32,
            )
        ).astype(BF)


def place(here, pos, came, stream):
    rows, width = stream.shape
    return pl.pallas_call(
        place_kernel,
        in_specs=[scalars()] + [whole()] * 3,
        out_specs=whole(),
        out_shape=shape((rows, width), BF),
        compiler_params=params(12),
        cost_estimate=FREE,
        name="place",
    )(here, pos, came, stream)


def lay_kernel(here_ref, *refs):
    blocks, (out_ref, sems) = refs[:-2], refs[-2:]
    rows = blocks[0].shape[0]
    copies = []
    for index, ref in enumerate(blocks):
        owner = 2 * (here_ref[0] ^ (index // 2)) + (here_ref[1] ^ (index % 2))
        start = pl.multiple_of(owner * rows, rows)
        copies.append(pltpu.make_async_copy(ref, out_ref.at[pl.ds(start, rows)], sems.at[index]))
    for copy in copies:
        copy.start()
    for copy in copies:
        copy.wait()


def lay(here, blocks):
    rows, width = blocks[0].shape
    return pl.pallas_call(
        lay_kernel,
        in_specs=[scalars()] + [whole()] * len(blocks),
        out_specs=anywhere(),
        out_shape=shape((len(blocks) * rows, width), BF),
        scratch_shapes=[pltpu.SemaphoreType.DMA((len(blocks),))],
        compiler_params=params(4),
        cost_estimate=FREE,
        name="lay",
    )(here, *blocks)


def shards(features, ln_gain, ln_bias, projection, stream, norm_gain, cotangent, slots):
    n_img = lax.axis_size("img")
    n_ctx = lax.axis_size("ctx")
    n_tp = lax.axis_size("tp")
    merged = slots.shape[0]
    tok_rows, width = stream.shape
    owners = n_img * n_ctx
    capacity = 2 * merged // owners
    slot_count = owners * capacity
    full_width = width * n_tp
    cut = width // n_img

    img = lax.axis_index("img").astype(jnp.int32)
    tp = lax.axis_index("tp").astype(jnp.int32)
    core, far_half = tp % 2, tp // 2
    z, y = lax.axis_index("ctx") // RING, lax.axis_index("ctx") % RING
    here = jnp.stack([core, far_half, img, z, y]).astype(jnp.int32)

    flip = [(i, 1 - i) for i in range(n_img)]
    core_pairs = [(t, t ^ 1) for t in range(n_tp)]
    far_pairs = [(t, t ^ 2) for t in range(n_tp)]

    def along_x(array, by):
        pairs = []
        for i in range(n_img):
            for t in range(n_tp):
                x = (2 * (t // 2) + i + by) % RING
                pairs.append((i * n_tp + t, (x % 2) * n_tp + 2 * (x // 2) + t % 2))
        return lax.ppermute(array, ("img", "tp"), pairs)

    def along_ctx(array, axis, by):
        pairs = []
        for c in range(n_ctx):
            for t in range(n_tp):
                z, y = c // RING, c % RING
                if t % 2 == axis:
                    y = (y + by) % RING
                else:
                    z = (z + by) % RING
                pairs.append((c * n_tp + t, (z * RING + y) * n_tp + t))
        return lax.ppermute(array, ("ctx", "tp"), pairs)

    slots = jnp.roll(slots, -core * (merged // 2))
    target = slots // tok_rows
    ids = jnp.arange(merged)
    earlier = (target[:, None] == target[None, :]) & (ids[:, None] < ids[None, :])
    rank = jnp.sum(earlier.astype(jnp.int32), axis=0)
    slot = target * capacity + rank
    local = slots - target * tok_rows
    packed = jnp.max(
        jnp.where(jnp.arange(slot_count)[:, None] == slot[None, :], local[None, :], -1), axis=1
    )
    asked = lax.all_to_all(
        packed.reshape(owners, capacity), ("img", "ctx"), split_axis=0, concat_axis=0, tiled=True
    )
    columns = lax.dynamic_slice_in_dim(projection[0], img * cut, cut, axis=2).reshape(-1, cut)
    moves = (1, -1, 2)
    near_blocks = [along_ctx(columns, 0, by) for by in moves]
    paired = target * (n_img * capacity) + rank + img * capacity
    partner = lax.ppermute(paired, "img", flip)
    gain = ln_gain[0]
    lifted, xw, stat = layer_norm(here, features[0], gain, ln_bias[0])
    asked, lifted, stat, near_blocks, partner = lax.optimization_barrier(
        (asked, lifted, stat, near_blocks, partner)
    )
    paired = jnp.concatenate([paired, partner]).reshape(-1, 1)

    first = stack(here, [columns] + near_blocks)
    asked, first = lax.optimization_barrier((asked, first))

    asked = asked.reshape(n_img, n_ctx, capacity).transpose(1, 0, 2)
    asked = asked.reshape(slot_count, 1)
    held = collect(asked, stream, cotangent[0], first)
    came = lax.all_to_all(
        held.reshape(owners, n_img * capacity, width),
        ("img", "ctx"), split_axis=0, concat_axis=0, tiled=True,
    ).reshape(n_img * slot_count, width)

    stacks = [first] + [along_ctx(first, 1, by) for by in moves[:2]]
    stacks.append(along_ctx(stacks[1], 1, 1))

    pairs = []
    for i in range(n_img):
        for t in range(n_tp):
            x = (2 * (t // 2) + i + (1 if t % 2 == 0 else -1)) % RING
            pairs.append((i * n_tp + t, (x % 2) * n_tp + 2 * (x // 2) + t % 2))
    lifted = [lifted, lax.ppermute(lifted, ("img", "tp"), pairs)]

    own_gain = lax.dynamic_slice_in_dim(norm_gain, img * cut, cut, axis=1)
    base, cot = unpack(paired, came)
    acc = multiply(here, stacks[: RING - 1], lifted)
    visual, state, sums = merge(here, own_gain, acc, base, cot, stacks[RING - 1], lifted)

    near, turned = add(sums, lax.ppermute(sums, "tp", core_pairs))
    stats = [near] + [along_x(near if by == 2 else turned, by) for by in (1, 2, 3)]
    stay, cross = pack(here, paired, visual, n_img * slot_count, near)
    cross, stats = lax.optimization_barrier((cross, stats))
    crossed = lax.ppermute(cross, "img", flip)

    own, other = backward(here, state, cot, own_gain, stats, stacks, full_width)
    own, other, crossed = lax.optimization_barrier((own, other, crossed))
    got = lax.ppermute(other, "tp", core_pairs)
    to_next, to_last, keep = pair(own, got, crossed)
    from_last, from_next = along_x(to_next, 1), along_x(to_last, -1)
    to_next, to_last = relay(keep, from_last, from_next)
    late_last, late_next = along_x(to_next, 1), along_x(to_last, -1)

    send = braid(stay, crossed, n_ctx)
    arrived = lax.all_to_all(send, "ctx", split_axis=0, concat_axis=0, tiled=True)
    new_stream = place(here, asked, arrived, stream)

    out = finish(here, own, got, (from_last, from_next), (late_last, late_next), xw, stat, gain)
    beyond = lax.ppermute(out, "tp", far_pairs)
    beyond, new_stream = lax.optimization_barrier((beyond, new_stream))
    from_core = [lax.ppermute(x, "tp", core_pairs) for x in (out, beyond)]
    grad = lay(here, [out, beyond] + from_core)
    return (new_stream, grad[None])


def solution(mesh):
    placed = (
        P(None, ("img", "ctx"), None),
        P(),
        P(),
        P(None, None, "ctx", "tp"),
        P(("img", "ctx"), "tp"),
        P(None, "tp"),
        P(None, ("img", "ctx"), "tp"),
        P(("img", "ctx")),
    )
    return jax.shard_map(
        shards,
        mesh=mesh,
        in_specs=placed,
        out_specs=(P(("img", "ctx"), "tp"), P(None, ("img", "ctx"), None)),
        check_vma=False,
    )
```

```python
import jax
import jax.numpy as jnp
from jax import lax
from jax.experimental import pallas as pl
from jax.experimental.pallas import tpu as pltpu
from jax.sharding import PartitionSpec as P


BF = jnp.bfloat16
F32 = jnp.float32
FREE = pl.CostEstimate(flops=0, bytes_accessed=0, transcendentals=0)
RING = 4
AWAY = (0, 3, 1, 2)


def params(mib):
    return pltpu.CompilerParams(vmem_limit_bytes=mib * 1024 * 1024)


def whole():
    return pl.BlockSpec(memory_space=pltpu.VMEM)


def shape(dims, kind):
    return jax.ShapeDtypeStruct(dims, kind)


def scalars():
    return pl.BlockSpec(memory_space=pltpu.SMEM)


def in_hbm():
    return pl.BlockSpec(memory_space=pltpu.HBM)


def anywhere():
    return pl.BlockSpec(memory_space=pl.ANY)


def eq_hot(shape, dim, index):
    return (lax.broadcasted_iota(jnp.int32, shape, dim) == index).astype(BF)


def window_major(tokens, window):
    n = tokens * window
    row = lax.broadcasted_iota(jnp.int32, (n, n), 0)
    col = lax.broadcasted_iota(jnp.int32, (n, n), 1)
    return (col == (row % tokens) * window + row // tokens).astype(BF)


def patch_major(tokens, window):
    n = tokens * window
    row = lax.broadcasted_iota(jnp.int32, (n, n), 0)
    col = lax.broadcasted_iota(jnp.int32, (n, n), 1)
    return (col == (row % window) * tokens + row // window).astype(BF)


def norm_kernel(here_ref, x_ref, gain_ref, bias_ref, first_ref, second_ref, xw_ref, stat_ref):
    window, width = gain_ref.shape
    tokens = x_ref.shape[0] // window
    full = window * width
    x = jnp.dot(window_major(tokens, window), x_ref[...], preferred_element_type=F32)
    parts = [x[w * tokens : (w + 1) * tokens] for w in range(window)]
    total = sum(jnp.sum(p, axis=1, keepdims=True) for p in parts)
    squares = sum(jnp.sum(p * p, axis=1, keepdims=True) for p in parts)
    mean = total / full
    inv = lax.rsqrt(squares / full - mean * mean + 1e-05)
    lifted = []
    for w, p in enumerate(parts):
        normed = (p - mean) * inv
        lifted.append(
            normed * gain_ref[w : w + 1].astype(F32) + bias_ref[w : w + 1].astype(F32)
        )
        xw_ref[w] = p.astype(BF)
    share = width // (RING * RING)
    for core in range(2):

        @pl.when(here_ref[0] == core)
        def _():
            blocks = [(a, b) for a in range(RING) for b in range(RING)]
            starts = [(a * RING + b if core == 0 else b * RING + a) * share for a, b in blocks]
            ordered = jnp.concatenate(
                [p[:, at : at + share] for at in starts for p in lifted], axis=1
            ).astype(BF)
            half = pl.num_programs(0) // 2

            @pl.when(pl.program_id(0) < half)
            def _():
                first_ref[...] = ordered

            @pl.when(pl.program_id(0) >= half)
            def _():
                second_ref[...] = ordered


    lane = lax.broadcasted_iota(jnp.int32, stat_ref.shape, 1)
    stat_ref[...] = jnp.where(lane == 0, mean, inv)


def layer_norm(here, features, gain, bias):
    rows, width = features.shape
    window = gain.shape[0]
    merged = rows // window
    block = 64
    steps = merged // block
    return pl.pallas_call(
        norm_kernel,
        grid_spec=pltpu.PrefetchScalarGridSpec(
            num_scalar_prefetch=1,
            grid=(steps,),
            in_specs=[
                pl.BlockSpec(
                    (block * window, width),
                    lambda i, c: (lax.rem(i + c[0] * (steps // 2), steps), 0),
                ),
                pl.BlockSpec((window, width), lambda i, c: (0, 0)),
                pl.BlockSpec((window, width), lambda i, c: (0, 0)),
            ],
            out_specs=[
                pl.BlockSpec((block, window * width), lambda i, c: (jnp.minimum(i, steps // 2 - 1), 0)),
                pl.BlockSpec((block, window * width), lambda i, c: (jnp.maximum(i - steps // 2, 0), 0)),
                pl.BlockSpec((window, block, width), lambda i, c: (0, i, 0)),
                pl.BlockSpec((block, 128), lambda i, c: (i, 0)),
            ],
        ),
        out_shape=[
            shape((merged // 2, window * width), BF),
            shape((merged // 2, window * width), BF),
            shape((window, merged, width), BF),
            shape((merged, 128), F32),
        ],
        compiler_params=params(58),
        cost_estimate=FREE,
        name="layer_norm",
    )(here, features, gain, bias)


def collect_kernel(pos_ref, stream_ref, cot_ref, out_ref):
    slots = pos_ref.shape[0]
    rows, width = stream_ref.shape
    cut = width // 2
    pick = eq_hot((slots, rows), 1, pos_ref[...])
    for img in range(2):
        at = slice(img * cut, (img + 1) * cut)
        for place, ref in enumerate((stream_ref, cot_ref)):
            out_ref[img, :, place * cut : (place + 1) * cut] = jnp.dot(
                pick, ref[:, at], preferred_element_type=F32
            ).astype(BF)


def collect(pos, stream, cot):
    slots = pos.shape[0]
    rows, width = stream.shape
    return pl.pallas_call(
        collect_kernel,
        in_specs=[whole()] * 3,
        out_specs=whole(),
        out_shape=shape((2, slots, width), BF),
        compiler_params=params(20),
        cost_estimate=FREE,
        name="collect",
    )(pos, stream, cot)


def unpack_kernel(slot_ref, came_ref, base_ref, cot_ref):
    tokens, width = base_ref.shape
    slots = came_ref.shape[0]
    take = eq_hot((tokens, slots), 1, slot_ref[...])
    for start, out_ref in ((0, base_ref), (width, cot_ref)):
        out_ref[...] = jnp.dot(
            take, came_ref[:, start : start + width], preferred_element_type=F32
        ).astype(BF)


def unpack(slot_col, came):
    tokens = slot_col.shape[0]
    slots, both = came.shape
    width = both // 2
    outs = [shape((tokens, width), BF)] * 2
    return pl.pallas_call(
        unpack_kernel,
        in_specs=[whole()] * 2,
        out_specs=[whole()] * 2,
        out_shape=outs,
        compiler_params=params(12),
        cost_estimate=FREE,
        name="unpack",
    )(slot_col, came)


def stack_kernel(here_ref, *refs):
    out_ref, sems = refs[RING:]
    first = jnp.where(here_ref[0] == 0, here_ref[4], here_ref[3])
    copies = [
        pltpu.make_async_copy(ref, out_ref.at[lax.rem(first + away, RING)], sems.at[index])
        for index, (away, ref) in enumerate(zip(AWAY, refs[:RING]))
    ]
    for copy in copies:
        copy.start()
    for copy in copies:
        copy.wait()


def stack(here, blocks):
    rows, width = blocks[0].shape
    return pl.pallas_call(
        stack_kernel,
        in_specs=[scalars()] + [in_hbm()] * RING,
        out_specs=whole(),
        out_shape=shape((RING, rows, width), BF),
        scratch_shapes=[pltpu.SemaphoreType.DMA((RING,))],
        compiler_params=params(6),
        cost_estimate=FREE,
        name="stack",
    )(here, *blocks)


def fetch(here_ref, stacks, held_ref, sems):
    for index, (away, ref) in enumerate(zip(AWAY, stacks)):

        @pl.when(here_ref[0] == 0)
        def _():
            place = lax.rem(here_ref[3] + away, RING)
            pltpu.make_async_copy(ref, held_ref.at[place], sems.at[index]).start()

        @pl.when(here_ref[0] == 1)
        def _():
            place = lax.rem(here_ref[4] + away, RING)
            pltpu.make_async_copy(ref, held_ref.at[:, place], sems.at[index]).start()

    def wait():
        for index, ref in enumerate(stacks):
            pltpu.make_async_copy(ref, held_ref.at[0], sems.at[index]).wait()

    return wait


def product(here_ref, away, stacks, lifted, held_ref, left_ref, sems):
    second = jnp.where(here_ref[0] == 0, here_ref[3], here_ref[4])
    block = left_ref.shape[2]
    rows = lifted[0].shape[0]
    copies = []
    for index, ref in enumerate(stacks):
        place = lax.rem(second + away[index], RING)
        at = pl.ds(pl.multiple_of(place * block, block), block)
        group = [pltpu.make_async_copy(ref, held_ref.at[index], sems.at[index, 0])]
        for i, part in enumerate(lifted):
            to = left_ref.at[index, pl.ds(i * rows, rows)]
            group.append(pltpu.make_async_copy(part.at[:, at], to, sems.at[index, 1 + i]))
        for copy in group:
            copy.start()
        copies.append(group)

    def run(total):
        for index, group in enumerate(copies):
            for copy in group:
                copy.wait()
            part = jnp.dot(
                left_ref[index], held_ref[index].reshape(block, -1), preferred_element_type=F32
            )
            total = part if total is None else total + part
        return total

    return run


def product_scratch(stacks, lifted):
    count = len(stacks)
    rows, depth = lifted[0].shape
    return [
        pltpu.VMEM((count,) + stacks[0].shape, BF),
        pltpu.VMEM((count, len(lifted) * rows, depth // RING), BF),
        pltpu.SemaphoreType.DMA((count, 1 + len(lifted))),
    ]


def multiply_kernel(here_ref, *refs):
    stacks, lifted, (out_ref, *scratch) = refs[: RING - 1], refs[RING - 1 : RING + 3], refs[RING + 3 :]
    out_ref[...] = product(here_ref, AWAY[: RING - 1], stacks, lifted, *scratch)(None)


def multiply(here, stacks, lifted):
    tokens, width = len(lifted) * lifted[0].shape[0], stacks[0].shape[2]
    return pl.pallas_call(
        multiply_kernel,
        in_specs=[scalars()] + [in_hbm()] * (len(stacks) + len(lifted)),
        out_specs=whole(),
        out_shape=shape((tokens, width), F32),
        scratch_shapes=product_scratch(stacks, lifted),
        compiler_params=params(40),
        cost_estimate=FREE,
        name="multiply",
    )(here, *stacks, *lifted)


def merge_kernel(here_ref, ngain_ref, acc_hbm, base_hbm, cot_hbm, stack_ref, *refs):
    lifted, refs = refs[:4], refs[4:]
    visual_ref, state_ref, stat_ref, acc_ref, base_ref, cot_ref, row_sems, *scratch = refs
    run = product(here_ref, AWAY[RING - 1 :], (stack_ref,), lifted, *scratch)
    copies = [
        pltpu.make_async_copy(a, b, row_sems.at[i])
        for i, (a, b) in enumerate(((acc_hbm, acc_ref), (base_hbm, base_ref), (cot_hbm, cot_ref)))
    ]
    for copy in copies:
        copy.start()
    total = run(None)
    for copy in copies:
        copy.wait()
    visual = (acc_ref[...] + total).astype(BF)
    visual_ref[...] = visual
    state = base_ref[...].astype(F32) + visual.astype(F32)
    state_ref[...] = state
    up = ngain_ref[...].astype(F32) * cot_ref[...].astype(F32)
    lane = lax.broadcasted_iota(jnp.int32, (state.shape[0], 128), 1)
    sums = jnp.where(
        lane == 0,
        jnp.sum(state * state, axis=1, keepdims=True),
        jnp.sum(up * state, axis=1, keepdims=True),
    )
    stat_ref[...] = sums.T[: stat_ref.shape[0]]


def merge(here, ngain, acc, base, cot, stack, lifted):
    tokens, width = base.shape
    outs = [shape((tokens, width), BF), shape((tokens, width), F32), shape((8, tokens), F32)]
    return pl.pallas_call(
        merge_kernel,
        in_specs=[scalars(), whole()] + [in_hbm()] * (4 + len(lifted)),
        out_specs=[whole()] * 3,
        out_shape=outs,
        scratch_shapes=[
            pltpu.VMEM((tokens, width), F32),
            pltpu.VMEM((tokens, width), BF),
            pltpu.VMEM((tokens, width), BF),
            pltpu.SemaphoreType.DMA((3,)),
        ]
        + product_scratch((stack,), lifted),
        compiler_params=params(24),
        cost_estimate=FREE,
        name="merge",
    )(here, ngain, acc, base, cot, stack, *lifted)


def add_kernel(sums_ref, got_ref, near_ref, turned_ref):
    count = sums_ref.shape[1] // 4
    cuts = [
        sums_ref[:, i * count : (i + 1) * count] + got_ref[:, (i ^ 1) * count : ((i ^ 1) + 1) * count]
        for i in range(4)
    ]
    near_ref[...] = jnp.concatenate(cuts, axis=1)
    turned_ref[...] = jnp.concatenate(cuts[2:] + cuts[:2], axis=1)


def add(sums, got):
    return pl.pallas_call(
        add_kernel,
        in_specs=[whole()] * 2,
        out_specs=[whole()] * 2,
        out_shape=[shape(sums.shape, F32)] * 2,
        compiler_params=params(4),
        cost_estimate=FREE,
        name="add",
    )(sums, got)


def pack_kernel(here_ref, slot_ref, visual_ref, after_ref, stay_ref, cross_ref):
    tokens = visual_ref.shape[0]
    slots = stay_ref.shape[0]
    for relative, out_ref in ((0, stay_ref), (1, cross_ref)):
        put = eq_hot((tokens, slots), 1, slot_ref[...] - (here_ref[2] ^ relative) * slots)
        out_ref[...] = lax.dot_general(
            put, visual_ref[...], (((0,), (0,)), ((), ())), preferred_element_type=F32
        ).astype(BF)


def pack(here, slot_col, visual, slots, after):
    tokens, width = visual.shape
    return pl.pallas_call(
        pack_kernel,
        in_specs=[scalars()] + [whole()] * 2 + [anywhere()],
        out_specs=[whole()] * 2,
        out_shape=[shape((slots // 2, width), BF)] * 2,
        compiler_params=params(8),
        cost_estimate=FREE,
        name="pack",
    )(here, slot_col, visual, after)


def braid_kernel(stay_ref, crossed_ref, out_ref):
    count, _, rows, _ = out_ref.shape
    for c in range(count):
        at = slice(c * rows, (c + 1) * rows)
        out_ref[c, 0] = stay_ref[at, :]
        out_ref[c, 1] = crossed_ref[at, :]


def braid(stay, crossed, count):
    rows, width = stay.shape
    return pl.pallas_call(
        braid_kernel,
        in_specs=[whole()] * 2,
        out_specs=whole(),
        out_shape=shape((count, 2, rows // count, width), BF),
        compiler_params=params(6),
        cost_estimate=FREE,
        name="braid",
    )(stay, crossed)


def backward_kernel(full_width, here_ref, ngain_ref, *refs):
    stats, stacks, refs = refs[:RING], refs[RING : 2 * RING], refs[2 * RING :]
    state_hbm, cot_hbm, own_ref, other_ref = refs[:4]
    picked_ref, sums_ref, state_ref, cot_ref, held_ref, row_sems, sems = refs[4:]
    row_copies = [
        pltpu.make_async_copy(a, b, row_sems.at[i])
        for i, (a, b) in enumerate(((state_hbm, state_ref), (cot_hbm, cot_ref)))
    ]
    for copy in row_copies:
        copy.start()
    wait_weight = fetch(here_ref, stacks, held_ref, sems)
    tokens = state_ref.shape[0]
    rows = tokens // 2 // RING
    total = stats[0][...]
    for ref in stats[1:]:
        total = total + ref[...]
    sums_ref[...] = total.T
    far, img = here_ref[1], here_ref[2]
    gain = ngain_ref[...].astype(F32)
    for copy in row_copies:
        copy.wait()
    for core in range(2):
        for away in range(RING):
            there = lax.rem(2 * far + img + away, RING)
            partner = lax.rem(there + img, 2)
            begin = partner * (tokens // 2) + core * (tokens // 4) + (there // 2) * (tokens // 8)
            at = pl.ds(pl.multiple_of(begin, rows), rows)
            sums = sums_ref[at, :]
            inv = lax.rsqrt(sums[:, 0:1] / full_width + 1e-06)
            inner = sums[:, 1:2] / full_width
            up = gain * cot_ref[at, :].astype(F32)
            grad = inv * up - state_ref[at, :] * (inv * inv * inv * inner)
            to = (core * RING + away) * rows
            picked_ref[to : to + rows, :] = grad.astype(BF)
    depth = own_ref.shape[1]
    wait_weight()
    block = depth // RING
    for step in range(RING):
        cols = slice(step * block, (step + 1) * block)
        both = lax.dot_general(
            picked_ref[...],
            held_ref[step].reshape(block, -1),
            (((1,), (1,)), ((), ())),
            preferred_element_type=F32,
        )
        own_ref[:, cols] = both[: tokens // 2].astype(BF)
        other_ref[:, cols] = both[tokens // 2 :].astype(BF)


def backward(here, state, cot, ngain, stats, stacks, full_width):
    tokens, width = state.shape
    depth = RING * stacks[0].shape[0] * stacks[0].shape[1]
    return pl.pallas_call(
        lambda *refs: backward_kernel(full_width, *refs),
        in_specs=[scalars()] + [whole()] * (1 + RING) + [in_hbm()] * (RING + 2),
        out_specs=[whole()] * 2,
        out_shape=[shape((tokens // 2, depth), BF)] * 2,
        scratch_shapes=[
            pltpu.VMEM((tokens, width), BF),
            pltpu.VMEM((tokens, 8), F32),
            pltpu.VMEM((tokens, width), F32),
            pltpu.VMEM((tokens, width), BF),
            pltpu.VMEM((RING,) + stacks[0].shape, BF),
            pltpu.SemaphoreType.DMA((2,)),
            pltpu.SemaphoreType.DMA((RING,)),
        ],
        compiler_params=params(24),
        cost_estimate=FREE,
        name="backward",
    )(here, ngain, *stats, *stacks, state, cot)


def pair_kernel(own_ref, got_ref, after_ref, next_ref, last_ref, keep_ref):
    rows = own_ref.shape[0] // RING
    half = rows // 2

    def total(start):
        at = slice(start, start + half)
        return (own_ref[at, :].astype(F32) + got_ref[at, :].astype(F32)).astype(BF)

    next_ref[:half] = total(2 * rows)
    next_ref[half:] = total(rows + half)
    last_ref[:half] = total(2 * rows + half)
    last_ref[half:] = total(3 * rows)
    keep_ref[:half] = total(rows)
    keep_ref[half:] = total(3 * rows + half)


def pair(own, got, after):
    rows, depth = got.shape[0] // RING, got.shape[1]
    return pl.pallas_call(
        pair_kernel,
        in_specs=[whole()] * 2 + [anywhere()],
        out_specs=[whole()] * 3,
        out_shape=[shape((rows, depth), BF)] * 3,
        compiler_params=params(8),
        cost_estimate=FREE,
        name="pair",
    )(own, got, after)


def relay_kernel(keep_ref, from_last_ref, from_next_ref, next_ref, last_ref):
    half = next_ref.shape[0]
    for at, came_ref, out_ref in (
        (slice(0, half), from_last_ref, next_ref),
        (slice(half, 2 * half), from_next_ref, last_ref),
    ):
        out_ref[...] = (keep_ref[at, :].astype(F32) + came_ref[:half].astype(F32)).astype(BF)


def relay(keep, from_last, from_next):
    rows, depth = keep.shape
    return pl.pallas_call(
        relay_kernel,
        in_specs=[whole()] * 3,
        out_specs=[whole()] * 2,
        out_shape=[shape((rows // 2, depth), BF)] * 2,
        compiler_params=params(8),
        cost_estimate=FREE,
        name="relay",
    )(keep, from_last, from_next)


def finish_kernel(here_ref, own_ref, got_ref, from_last_ref, from_next_ref, late_last_ref, late_next_ref,
                  xw_ref, stat_ref, gain_ref, out_ref):
    window, tokens, width = xw_ref.shape
    full = window * width
    mean = stat_ref[:, 0:1]
    inv = stat_ref[:, 1:2]
    early = jnp.where(pl.program_id(0) == 0, from_next_ref[...], from_last_ref[...])
    late = jnp.where(pl.program_id(0) == 0, late_last_ref[...], late_next_ref[...])
    lifted = own_ref[...].astype(F32) + got_ref[...].astype(F32)
    lifted = lifted + early.astype(F32) + late.astype(F32)
    share = width // (RING * RING)
    scaled = []
    total = 0.0
    inner = 0.0
    for w in range(window):
        g = jnp.concatenate(
            [lifted[:, at : at + share] for at in range(w * share, full, window * share)], axis=1
        ) * gain_ref[w : w + 1].astype(F32)
        normed = (xw_ref[w].astype(F32) - mean) * inv
        total = total + jnp.sum(g, axis=1, keepdims=True)
        inner = inner + jnp.sum(g * normed, axis=1, keepdims=True)
        scaled.append((g, normed))
    total = total / full
    inner = inner / full
    rows = jnp.concatenate(
        [(inv * (g - total - normed * inner)).astype(BF) for g, normed in scaled], axis=0
    )
    out_ref[...] = jnp.dot(
        patch_major(tokens, window), rows, preferred_element_type=F32
    ).astype(BF)


def finish(here, own, got, early, late, xw, stat, gain):
    rows, depth = early[0].shape
    window, width = gain.shape
    steps = 2
    tokens = rows // steps
    same = pl.BlockSpec((tokens, depth), lambda i, h: (i, 0))
    second = pl.BlockSpec((tokens, depth), lambda i, h: (1, 0))
    only = pl.BlockSpec((tokens, depth), lambda i, h: (0, 0))
    return pl.pallas_call(
        finish_kernel,
        grid_spec=pltpu.PrefetchScalarGridSpec(
            num_scalar_prefetch=1,
            grid=(steps,),
            in_specs=[same, same, second, second, only, only]
            + [
                pl.BlockSpec((window, tokens, width), lambda i, h: (0, h[1] * steps + i, 0)),
                pl.BlockSpec((tokens, 128), lambda i, h: (h[1] * steps + i, 0)),
                pl.BlockSpec((window, width), lambda i, h: (0, 0)),
            ],
            out_specs=pl.BlockSpec((tokens * window, width), lambda i, h: (i, 0)),
        ),
        out_shape=shape((rows * window, width), BF),
        compiler_params=params(58),
        cost_estimate=FREE,
        name="finish",
    )(here, own, got, *early, *late, xw, stat, gain)


def place_kernel(here_ref, pos_ref, came_ref, stream_ref, out_ref):
    rows, width = stream_ref.shape
    cut = width // 2
    slots = pos_ref.shape[0]
    put = eq_hot((slots, rows), 1, pos_ref[...])
    for relative in range(2):
        start = pl.multiple_of((here_ref[2] ^ relative) * cut, cut)
        at = pl.ds(start, cut)
        out_ref[:, at] = (
            stream_ref[:, at].astype(F32)
            + lax.dot_general(
                put,
                came_ref[:, relative].reshape(slots, cut),
                (((0,), (0,)), ((), ())),
                preferred_element_type=F32,
            )
        ).astype(BF)


def place(here, pos, came, stream):
    rows, width = stream.shape
    return pl.pallas_call(
        place_kernel,
        in_specs=[scalars()] + [whole()] * 3,
        out_specs=whole(),
        out_shape=shape((rows, width), BF),
        compiler_params=params(12),
        cost_estimate=FREE,
        name="place",
    )(here, pos, came, stream)


def lay_kernel(here_ref, *refs):
    blocks, (out_ref, sems) = refs[:-2], refs[-2:]
    rows = blocks[0].shape[0]
    copies = []
    for index, ref in enumerate(blocks):
        owner = 2 * (here_ref[0] ^ (index // 2)) + (here_ref[1] ^ (index % 2))
        start = pl.multiple_of(owner * rows, rows)
        copies.append(pltpu.make_async_copy(ref, out_ref.at[pl.ds(start, rows)], sems.at[index]))
    for copy in copies:
        copy.start()
    for copy in copies:
        copy.wait()


def lay(here, blocks):
    rows, width = blocks[0].shape
    return pl.pallas_call(
        lay_kernel,
        in_specs=[scalars()] + [whole()] * len(blocks),
        out_specs=anywhere(),
        out_shape=shape((len(blocks) * rows, width), BF),
        scratch_shapes=[pltpu.SemaphoreType.DMA((len(blocks),))],
        compiler_params=params(4),
        cost_estimate=FREE,
        name="lay",
    )(here, *blocks)


def shards(features, ln_gain, ln_bias, projection, stream, norm_gain, cotangent, slots):
    n_img = lax.axis_size("img")
    n_ctx = lax.axis_size("ctx")
    n_tp = lax.axis_size("tp")
    merged = slots.shape[0]
    tok_rows, width = stream.shape
    owners = n_img * n_ctx
    capacity = 2 * merged // owners
    slot_count = owners * capacity
    full_width = width * n_tp
    cut = width // n_img

    img = lax.axis_index("img").astype(jnp.int32)
    tp = lax.axis_index("tp").astype(jnp.int32)
    core, far_half = tp % 2, tp // 2
    z, y = lax.axis_index("ctx") // RING, lax.axis_index("ctx") % RING
    here = jnp.stack([core, far_half, img, z, y]).astype(jnp.int32)

    flip = [(i, 1 - i) for i in range(n_img)]
    core_pairs = [(t, t ^ 1) for t in range(n_tp)]
    far_pairs = [(t, t ^ 2) for t in range(n_tp)]

    def along_x(array, by):
        pairs = []
        for i in range(n_img):
            for t in range(n_tp):
                x = (2 * (t // 2) + i + by) % RING
                pairs.append((i * n_tp + t, (x % 2) * n_tp + 2 * (x // 2) + t % 2))
        return lax.ppermute(array, ("img", "tp"), pairs)

    def along_ctx(array, axis, by):
        pairs = []
        for c in range(n_ctx):
            for t in range(n_tp):
                z, y = c // RING, c % RING
                if t % 2 == axis:
                    y = (y + by) % RING
                else:
                    z = (z + by) % RING
                pairs.append((c * n_tp + t, (z * RING + y) * n_tp + t))
        return lax.ppermute(array, ("ctx", "tp"), pairs)

    slots = jnp.roll(slots, -core * (merged // 2))
    target = slots // tok_rows
    ids = jnp.arange(merged)
    earlier = (target[:, None] == target[None, :]) & (ids[:, None] < ids[None, :])
    rank = jnp.sum(earlier.astype(jnp.int32), axis=0)
    slot = target * capacity + rank
    local = slots - target * tok_rows
    packed = jnp.max(
        jnp.where(jnp.arange(slot_count)[:, None] == slot[None, :], local[None, :], -1), axis=1
    )
    asked = lax.all_to_all(
        packed.reshape(owners, capacity), ("img", "ctx"), split_axis=0, concat_axis=0, tiled=True
    )
    columns = lax.dynamic_slice_in_dim(projection[0], img * cut, cut, axis=2).reshape(-1, cut)
    paired = target * (n_img * capacity) + rank + img * capacity
    partner = lax.ppermute(paired, "img", flip)
    columns, asked, partner = lax.optimization_barrier((columns, asked, partner))
    paired = jnp.concatenate([paired, partner]).reshape(-1, 1)
    moves = (1, -1, 2)
    near_blocks = [along_ctx(columns, 0, by) for by in moves]

    first = stack(here, [columns] + near_blocks)

    asked = asked.reshape(n_img, n_ctx, capacity).transpose(1, 0, 2)
    asked = asked.reshape(slot_count, 1)
    held = collect(asked, stream, cotangent[0])
    came = lax.all_to_all(
        held.reshape(owners, n_img * capacity, width),
        ("img", "ctx"), split_axis=0, concat_axis=0, tiled=True,
    ).reshape(n_img * slot_count, width)

    stacks = [first] + [along_ctx(first, 1, by) for by in moves[:2]]
    stacks.append(along_ctx(stacks[1], 1, 1))

    gain = ln_gain[0]
    *lifted, xw, stat = layer_norm(here, features[0], gain, ln_bias[0])
    for part in range(2):
        pairs = []
        for i in range(n_img):
            for t in range(n_tp):
                in_pair = part == 0 and t % 2 == 1
                x = (2 * (t // 2) + i + (1 if in_pair == (i == 0) else -1)) % RING
                pairs.append((i * n_tp + t, (x % 2) * n_tp + 2 * (x // 2) + t % 2))
        lifted.append(lax.ppermute(lifted[part], ("img", "tp"), pairs))

    own_gain = lax.dynamic_slice_in_dim(norm_gain, img * cut, cut, axis=1)
    base, cot = unpack(paired, came)
    acc = multiply(here, stacks[: RING - 1], lifted)
    visual, state, sums = merge(here, own_gain, acc, base, cot, stacks[RING - 1], lifted)

    near, turned = add(sums, lax.ppermute(sums, "tp", core_pairs))
    stats = [near] + [along_x(near if by == 2 else turned, by) for by in (1, 2, 3)]
    stay, cross = pack(here, paired, visual, n_img * slot_count, near)
    cross, stats = lax.optimization_barrier((cross, stats))
    crossed = lax.ppermute(cross, "img", flip)

    own, other = backward(here, state, cot, own_gain, stats, stacks, full_width)
    own, other, crossed = lax.optimization_barrier((own, other, crossed))
    got = lax.ppermute(other, "tp", core_pairs)
    to_next, to_last, keep = pair(own, got, crossed)
    from_last, from_next = along_x(to_next, 1), along_x(to_last, -1)
    to_next, to_last = relay(keep, from_last, from_next)
    late_last, late_next = along_x(to_next, 1), along_x(to_last, -1)

    send = braid(stay, crossed, n_ctx)
    arrived = lax.all_to_all(send, "ctx", split_axis=0, concat_axis=0, tiled=True)
    new_stream = place(here, asked, arrived, stream)

    out = finish(here, own, got, (from_last, from_next), (late_last, late_next), xw, stat, gain)
    beyond = lax.ppermute(out, "tp", far_pairs)
    beyond, new_stream = lax.optimization_barrier((beyond, new_stream))
    from_core = [lax.ppermute(x, "tp", core_pairs) for x in (out, beyond)]
    grad = lay(here, [out, beyond] + from_core)
    return (new_stream, grad[None])


def solution(mesh):
    placed = (
        P(None, ("img", "ctx"), None),
        P(),
        P(),
        P(None, None, "ctx", "tp"),
        P(("img", "ctx"), "tp"),
        P(None, "tp"),
        P(None, ("img", "ctx"), "tp"),
        P(("img", "ctx")),
    )
    return jax.shard_map(
        shards,
        mesh=mesh,
        in_specs=placed,
        out_specs=(P(("img", "ctx"), "tp"), P(None, ("img", "ctx"), None)),
        check_vma=False,
    )
```

```python
import jax
import jax.numpy as jnp
from jax import lax
from jax.experimental import pallas as pl
from jax.experimental.pallas import tpu as pltpu
from jax.sharding import PartitionSpec as P


BF = jnp.bfloat16
F32 = jnp.float32
FREE = pl.CostEstimate(flops=0, bytes_accessed=0, transcendentals=0)
RING = 4
AWAY = (0, 3, 1, 2)


def params(mib):
    return pltpu.CompilerParams(vmem_limit_bytes=mib * 1024 * 1024)


def whole():
    return pl.BlockSpec(memory_space=pltpu.VMEM)


def shape(dims, kind):
    return jax.ShapeDtypeStruct(dims, kind)


def scalars():
    return pl.BlockSpec(memory_space=pltpu.SMEM)


def in_hbm():
    return pl.BlockSpec(memory_space=pltpu.HBM)


def anywhere():
    return pl.BlockSpec(memory_space=pl.ANY)


def eq_hot(shape, dim, index):
    return (lax.broadcasted_iota(jnp.int32, shape, dim) == index).astype(BF)


def window_major(tokens, window):
    n = tokens * window
    row = lax.broadcasted_iota(jnp.int32, (n, n), 0)
    col = lax.broadcasted_iota(jnp.int32, (n, n), 1)
    return (col == (row % tokens) * window + row // tokens).astype(BF)


def patch_major(tokens, window):
    n = tokens * window
    row = lax.broadcasted_iota(jnp.int32, (n, n), 0)
    col = lax.broadcasted_iota(jnp.int32, (n, n), 1)
    return (col == (row % window) * tokens + row // window).astype(BF)


def norm_kernel(here_ref, x_ref, gain_ref, bias_ref, lifted_ref, xw_ref, stat_ref):
    window, width = gain_ref.shape
    tokens = x_ref.shape[0] // window
    full = window * width
    x = jnp.dot(window_major(tokens, window), x_ref[...], preferred_element_type=F32)
    parts = [x[w * tokens : (w + 1) * tokens] for w in range(window)]
    total = sum(jnp.sum(p, axis=1, keepdims=True) for p in parts)
    squares = sum(jnp.sum(p * p, axis=1, keepdims=True) for p in parts)
    mean = total / full
    inv = lax.rsqrt(squares / full - mean * mean + 1e-05)
    lifted = []
    for w, p in enumerate(parts):
        normed = (p - mean) * inv
        lifted.append(
            normed * gain_ref[w : w + 1].astype(F32) + bias_ref[w : w + 1].astype(F32)
        )
        xw_ref[w] = p.astype(BF)
    share = width // (RING * RING)
    for core in range(2):

        @pl.when(here_ref[0] == core)
        def _():
            blocks = [(a, b) for a in range(RING) for b in range(RING)]
            starts = [(a * RING + b if core == 0 else b * RING + a) * share for a, b in blocks]
            lifted_ref[...] = jnp.concatenate(
                [p[:, at : at + share] for at in starts for p in lifted], axis=1
            ).astype(BF)

    lane = lax.broadcasted_iota(jnp.int32, stat_ref.shape, 1)
    stat_ref[...] = jnp.where(lane == 0, mean, inv)


def layer_norm(here, features, gain, bias):
    rows, width = features.shape
    window = gain.shape[0]
    merged = rows // window
    block = 64
    steps = merged // block
    return pl.pallas_call(
        norm_kernel,
        grid_spec=pltpu.PrefetchScalarGridSpec(
            num_scalar_prefetch=1,
            grid=(steps,),
            in_specs=[
                pl.BlockSpec(
                    (block * window, width),
                    lambda i, c: (lax.rem(i + c[0] * (steps // 2), steps), 0),
                ),
                pl.BlockSpec((window, width), lambda i, c: (0, 0)),
                pl.BlockSpec((window, width), lambda i, c: (0, 0)),
            ],
            out_specs=[
                pl.BlockSpec((block, window * width), lambda i, c: (i, 0)),
                pl.BlockSpec((window, block, width), lambda i, c: (0, i, 0)),
                pl.BlockSpec((block, 128), lambda i, c: (i, 0)),
            ],
        ),
        out_shape=[
            shape((merged, window * width), BF),
            shape((window, merged, width), BF),
            shape((merged, 128), F32),
        ],
        compiler_params=params(58),
        cost_estimate=FREE,
        name="layer_norm",
    )(here, features, gain, bias)


def collect_kernel(pos_ref, stream_ref, cot_ref, after_ref, out_ref):
    slots = pos_ref.shape[0]
    rows, width = stream_ref.shape
    cut = width // 2
    pick = eq_hot((slots, rows), 1, pos_ref[...])
    for img in range(2):
        at = slice(img * cut, (img + 1) * cut)
        for place, ref in enumerate((stream_ref, cot_ref)):
            out_ref[img, :, place * cut : (place + 1) * cut] = jnp.dot(
                pick, ref[:, at], preferred_element_type=F32
            ).astype(BF)


def collect(pos, stream, cot, after):
    slots = pos.shape[0]
    rows, width = stream.shape
    return pl.pallas_call(
        collect_kernel,
        in_specs=[whole()] * 3 + [anywhere()],
        out_specs=whole(),
        out_shape=shape((2, slots, width), BF),
        compiler_params=params(20),
        cost_estimate=FREE,
        name="collect",
    )(pos, stream, cot, after)


def unpack_kernel(slot_ref, came_ref, after_ref, base_ref, cot_ref):
    tokens, width = base_ref.shape
    slots = came_ref.shape[0]
    take = eq_hot((tokens, slots), 1, slot_ref[...])
    for start, out_ref in ((0, base_ref), (width, cot_ref)):
        out_ref[...] = jnp.dot(
            take, came_ref[:, start : start + width], preferred_element_type=F32
        ).astype(BF)


def unpack(slot_col, came, after):
    tokens = slot_col.shape[0]
    slots, both = came.shape
    width = both // 2
    outs = [shape((tokens, width), BF)] * 2
    return pl.pallas_call(
        unpack_kernel,
        in_specs=[whole()] * 2 + [anywhere()],
        out_specs=[whole()] * 2,
        out_shape=outs,
        compiler_params=params(12),
        cost_estimate=FREE,
        name="unpack",
    )(slot_col, came, after)


def stack_kernel(here_ref, *refs):
    out_ref, sems = refs[RING:]
    first = jnp.where(here_ref[0] == 0, here_ref[4], here_ref[3])
    copies = [
        pltpu.make_async_copy(ref, out_ref.at[lax.rem(first + away, RING)], sems.at[index])
        for index, (away, ref) in enumerate(zip(AWAY, refs[:RING]))
    ]
    for copy in copies:
        copy.start()
    for copy in copies:
        copy.wait()


def stack(here, blocks):
    rows, width = blocks[0].shape
    return pl.pallas_call(
        stack_kernel,
        in_specs=[scalars()] + [in_hbm()] * RING,
        out_specs=whole(),
        out_shape=shape((RING, rows, width), BF),
        scratch_shapes=[pltpu.SemaphoreType.DMA((RING,))],
        compiler_params=params(6),
        cost_estimate=FREE,
        name="stack",
    )(here, *blocks)


def fetch(here_ref, stacks, held_ref, sems):
    for index, (away, ref) in enumerate(zip(AWAY, stacks)):

        @pl.when(here_ref[0] == 0)
        def _():
            place = lax.rem(here_ref[3] + away, RING)
            pltpu.make_async_copy(ref, held_ref.at[place], sems.at[index]).start()

        @pl.when(here_ref[0] == 1)
        def _():
            place = lax.rem(here_ref[4] + away, RING)
            pltpu.make_async_copy(ref, held_ref.at[:, place], sems.at[index]).start()

    def wait():
        for index, ref in enumerate(stacks):
            pltpu.make_async_copy(ref, held_ref.at[0], sems.at[index]).wait()

    return wait


def product(here_ref, away, stacks, lifted, held_ref, left_ref, sems):
    second = jnp.where(here_ref[0] == 0, here_ref[3], here_ref[4])
    block = left_ref.shape[2]
    rows = lifted[0].shape[0]
    copies = []
    for index, ref in enumerate(stacks):
        place = lax.rem(second + away[index], RING)
        at = pl.ds(pl.multiple_of(place * block, block), block)
        group = [pltpu.make_async_copy(ref, held_ref.at[index], sems.at[index, 0])]
        for i, part in enumerate(lifted):
            to = left_ref.at[index, pl.ds(i * rows, rows)]
            group.append(pltpu.make_async_copy(part.at[:, at], to, sems.at[index, 1 + i]))
        for copy in group:
            copy.start()
        copies.append(group)

    def run(total):
        for index, group in enumerate(copies):
            for copy in group:
                copy.wait()
            part = jnp.dot(
                left_ref[index], held_ref[index].reshape(block, -1), preferred_element_type=F32
            )
            total = part if total is None else total + part
        return total

    return run


def product_scratch(stacks, lifted):
    count = len(stacks)
    rows, depth = lifted[0].shape
    return [
        pltpu.VMEM((count,) + stacks[0].shape, BF),
        pltpu.VMEM((count, len(lifted) * rows, depth // RING), BF),
        pltpu.SemaphoreType.DMA((count, 1 + len(lifted))),
    ]


def multiply_kernel(here_ref, *refs):
    stacks, lifted, (out_ref, *scratch) = refs[: RING - 1], refs[RING - 1 : RING + 1], refs[RING + 1 :]
    out_ref[...] = product(here_ref, AWAY[: RING - 1], stacks, lifted, *scratch)(None)


def multiply(here, stacks, lifted):
    tokens, width = 2 * lifted[0].shape[0], stacks[0].shape[2]
    return pl.pallas_call(
        multiply_kernel,
        in_specs=[scalars()] + [in_hbm()] * (len(stacks) + len(lifted)),
        out_specs=whole(),
        out_shape=shape((tokens, width), F32),
        scratch_shapes=product_scratch(stacks, lifted),
        compiler_params=params(40),
        cost_estimate=FREE,
        name="multiply",
    )(here, *stacks, *lifted)


def merge_kernel(here_ref, ngain_ref, acc_hbm, base_hbm, cot_hbm, stack_ref, *refs):
    lifted, refs = refs[:2], refs[2:]
    visual_ref, state_ref, stat_ref, acc_ref, base_ref, cot_ref, row_sems, *scratch = refs
    run = product(here_ref, AWAY[RING - 1 :], (stack_ref,), lifted, *scratch)
    copies = [
        pltpu.make_async_copy(a, b, row_sems.at[i])
        for i, (a, b) in enumerate(((acc_hbm, acc_ref), (base_hbm, base_ref), (cot_hbm, cot_ref)))
    ]
    for copy in copies:
        copy.start()
    total = run(None)
    for copy in copies:
        copy.wait()
    visual = (acc_ref[...] + total).astype(BF)
    visual_ref[...] = visual
    state = base_ref[...].astype(F32) + visual.astype(F32)
    state_ref[...] = state
    up = ngain_ref[...].astype(F32) * cot_ref[...].astype(F32)
    lane = lax.broadcasted_iota(jnp.int32, (state.shape[0], 128), 1)
    sums = jnp.where(
        lane == 0,
        jnp.sum(state * state, axis=1, keepdims=True),
        jnp.sum(up * state, axis=1, keepdims=True),
    )
    stat_ref[...] = sums.T[: stat_ref.shape[0]]


def merge(here, ngain, acc, base, cot, stack, lifted):
    tokens, width = base.shape
    outs = [shape((tokens, width), BF), shape((tokens, width), F32), shape((8, tokens), F32)]
    return pl.pallas_call(
        merge_kernel,
        in_specs=[scalars(), whole()] + [in_hbm()] * 6,
        out_specs=[whole()] * 3,
        out_shape=outs,
        scratch_shapes=[
            pltpu.VMEM((tokens, width), F32),
            pltpu.VMEM((tokens, width), BF),
            pltpu.VMEM((tokens, width), BF),
            pltpu.SemaphoreType.DMA((3,)),
        ]
        + product_scratch((stack,), lifted),
        compiler_params=params(24),
        cost_estimate=FREE,
        name="merge",
    )(here, ngain, acc, base, cot, stack, *lifted)


def add_kernel(sums_ref, got_ref, near_ref, turned_ref):
    count = sums_ref.shape[1] // 4
    cuts = [
        sums_ref[:, i * count : (i + 1) * count] + got_ref[:, (i ^ 1) * count : ((i ^ 1) + 1) * count]
        for i in range(4)
    ]
    near_ref[...] = jnp.concatenate(cuts, axis=1)
    turned_ref[...] = jnp.concatenate(cuts[2:] + cuts[:2], axis=1)


def add(sums, got):
    return pl.pallas_call(
        add_kernel,
        in_specs=[whole()] * 2,
        out_specs=[whole()] * 2,
        out_shape=[shape(sums.shape, F32)] * 2,
        compiler_params=params(4),
        cost_estimate=FREE,
        name="add",
    )(sums, got)


def pack_kernel(here_ref, slot_ref, visual_ref, after_ref, stay_ref, cross_ref):
    tokens = visual_ref.shape[0]
    slots = stay_ref.shape[0]
    for relative, out_ref in ((0, stay_ref), (1, cross_ref)):
        put = eq_hot((tokens, slots), 1, slot_ref[...] - (here_ref[2] ^ relative) * slots)
        out_ref[...] = lax.dot_general(
            put, visual_ref[...], (((0,), (0,)), ((), ())), preferred_element_type=F32
        ).astype(BF)


def pack(here, slot_col, visual, slots, after):
    tokens, width = visual.shape
    return pl.pallas_call(
        pack_kernel,
        in_specs=[scalars()] + [whole()] * 2 + [anywhere()],
        out_specs=[whole()] * 2,
        out_shape=[shape((slots // 2, width), BF)] * 2,
        compiler_params=params(8),
        cost_estimate=FREE,
        name="pack",
    )(here, slot_col, visual, after)


def braid_kernel(stay_ref, crossed_ref, out_ref):
    count, _, rows, _ = out_ref.shape
    for c in range(count):
        at = slice(c * rows, (c + 1) * rows)
        out_ref[c, 0] = stay_ref[at, :]
        out_ref[c, 1] = crossed_ref[at, :]


def braid(stay, crossed, count):
    rows, width = stay.shape
    return pl.pallas_call(
        braid_kernel,
        in_specs=[whole()] * 2,
        out_specs=whole(),
        out_shape=shape((count, 2, rows // count, width), BF),
        compiler_params=params(6),
        cost_estimate=FREE,
        name="braid",
    )(stay, crossed)


def backward_kernel(full_width, here_ref, ngain_ref, *refs):
    stats, stacks, refs = refs[:RING], refs[RING : 2 * RING], refs[2 * RING :]
    state_hbm, cot_hbm, own_ref, other_ref = refs[:4]
    picked_ref, sums_ref, state_ref, cot_ref, held_ref, row_sems, sems = refs[4:]
    row_copies = [
        pltpu.make_async_copy(a, b, row_sems.at[i])
        for i, (a, b) in enumerate(((state_hbm, state_ref), (cot_hbm, cot_ref)))
    ]
    for copy in row_copies:
        copy.start()
    wait_weight = fetch(here_ref, stacks, held_ref, sems)
    tokens = state_ref.shape[0]
    rows = tokens // 2 // RING
    total = stats[0][...]
    for ref in stats[1:]:
        total = total + ref[...]
    sums_ref[...] = total.T
    far, img = here_ref[1], here_ref[2]
    gain = ngain_ref[...].astype(F32)
    for copy in row_copies:
        copy.wait()
    for core in range(2):
        for away in range(RING):
            there = lax.rem(2 * far + img + away, RING)
            partner = lax.rem(there + img, 2)
            begin = partner * (tokens // 2) + core * (tokens // 4) + (there // 2) * (tokens // 8)
            at = pl.ds(pl.multiple_of(begin, rows), rows)
            sums = sums_ref[at, :]
            inv = lax.rsqrt(sums[:, 0:1] / full_width + 1e-06)
            inner = sums[:, 1:2] / full_width
            up = gain * cot_ref[at, :].astype(F32)
            grad = inv * up - state_ref[at, :] * (inv * inv * inv * inner)
            to = (core * RING + away) * rows
            picked_ref[to : to + rows, :] = grad.astype(BF)
    depth = own_ref.shape[1]
    wait_weight()
    block = depth // RING
    for step in range(RING):
        cols = slice(step * block, (step + 1) * block)
        both = lax.dot_general(
            picked_ref[...],
            held_ref[step].reshape(block, -1),
            (((1,), (1,)), ((), ())),
            preferred_element_type=F32,
        )
        own_ref[:, cols] = both[: tokens // 2].astype(BF)
        other_ref[:, cols] = both[tokens // 2 :].astype(BF)


def backward(here, state, cot, ngain, stats, stacks, full_width):
    tokens, width = state.shape
    depth = RING * stacks[0].shape[0] * stacks[0].shape[1]
    return pl.pallas_call(
        lambda *refs: backward_kernel(full_width, *refs),
        in_specs=[scalars()] + [whole()] * (1 + RING) + [in_hbm()] * (RING + 2),
        out_specs=[whole()] * 2,
        out_shape=[shape((tokens // 2, depth), BF)] * 2,
        scratch_shapes=[
            pltpu.VMEM((tokens, width), BF),
            pltpu.VMEM((tokens, 8), F32),
            pltpu.VMEM((tokens, width), F32),
            pltpu.VMEM((tokens, width), BF),
            pltpu.VMEM((RING,) + stacks[0].shape, BF),
            pltpu.SemaphoreType.DMA((2,)),
            pltpu.SemaphoreType.DMA((RING,)),
        ],
        compiler_params=params(24),
        cost_estimate=FREE,
        name="backward",
    )(here, ngain, *stats, *stacks, state, cot)


def pair_kernel(own_ref, got_ref, after_ref, next_ref, last_ref, keep_ref):
    rows = own_ref.shape[0] // RING
    half = rows // 2

    def total(start):
        at = slice(start, start + half)
        return (own_ref[at, :].astype(F32) + got_ref[at, :].astype(F32)).astype(BF)

    next_ref[:half] = total(2 * rows)
    next_ref[half:] = total(rows + half)
    last_ref[:half] = total(2 * rows + half)
    last_ref[half:] = total(3 * rows)
    keep_ref[:half] = total(rows)
    keep_ref[half:] = total(3 * rows + half)


def pair(own, got, after):
    rows, depth = got.shape[0] // RING, got.shape[1]
    return pl.pallas_call(
        pair_kernel,
        in_specs=[whole()] * 2 + [anywhere()],
        out_specs=[whole()] * 3,
        out_shape=[shape((rows, depth), BF)] * 3,
        compiler_params=params(8),
        cost_estimate=FREE,
        name="pair",
    )(own, got, after)


def relay_kernel(keep_ref, from_last_ref, from_next_ref, next_ref, last_ref):
    half = next_ref.shape[0]
    for at, came_ref, out_ref in (
        (slice(0, half), from_last_ref, next_ref),
        (slice(half, 2 * half), from_next_ref, last_ref),
    ):
        out_ref[...] = (keep_ref[at, :].astype(F32) + came_ref[:half].astype(F32)).astype(BF)


def relay(keep, from_last, from_next):
    rows, depth = keep.shape
    return pl.pallas_call(
        relay_kernel,
        in_specs=[whole()] * 3,
        out_specs=[whole()] * 2,
        out_shape=[shape((rows // 2, depth), BF)] * 2,
        compiler_params=params(8),
        cost_estimate=FREE,
        name="relay",
    )(keep, from_last, from_next)


def finish_kernel(here_ref, own_ref, got_ref, from_last_ref, from_next_ref, late_last_ref, late_next_ref,
                  xw_ref, stat_ref, gain_ref, out_ref):
    window, tokens, width = xw_ref.shape
    full = window * width
    mean = stat_ref[:, 0:1]
    inv = stat_ref[:, 1:2]
    early = jnp.where(pl.program_id(0) == 0, from_next_ref[...], from_last_ref[...])
    late = jnp.where(pl.program_id(0) == 0, late_last_ref[...], late_next_ref[...])
    lifted = own_ref[...].astype(F32) + got_ref[...].astype(F32)
    lifted = lifted + early.astype(F32) + late.astype(F32)
    share = width // (RING * RING)
    scaled = []
    total = 0.0
    inner = 0.0
    for w in range(window):
        g = jnp.concatenate(
            [lifted[:, at : at + share] for at in range(w * share, full, window * share)], axis=1
        ) * gain_ref[w : w + 1].astype(F32)
        normed = (xw_ref[w].astype(F32) - mean) * inv
        total = total + jnp.sum(g, axis=1, keepdims=True)
        inner = inner + jnp.sum(g * normed, axis=1, keepdims=True)
        scaled.append((g, normed))
    total = total / full
    inner = inner / full
    rows = jnp.concatenate(
        [(inv * (g - total - normed * inner)).astype(BF) for g, normed in scaled], axis=0
    )
    out_ref[...] = jnp.dot(
        patch_major(tokens, window), rows, preferred_element_type=F32
    ).astype(BF)


def finish(here, own, got, early, late, xw, stat, gain):
    rows, depth = early[0].shape
    window, width = gain.shape
    steps = 2
    tokens = rows // steps
    same = pl.BlockSpec((tokens, depth), lambda i, h: (i, 0))
    second = pl.BlockSpec((tokens, depth), lambda i, h: (1, 0))
    only = pl.BlockSpec((tokens, depth), lambda i, h: (0, 0))
    return pl.pallas_call(
        finish_kernel,
        grid_spec=pltpu.PrefetchScalarGridSpec(
            num_scalar_prefetch=1,
            grid=(steps,),
            in_specs=[same, same, second, second, only, only]
            + [
                pl.BlockSpec((window, tokens, width), lambda i, h: (0, h[1] * steps + i, 0)),
                pl.BlockSpec((tokens, 128), lambda i, h: (h[1] * steps + i, 0)),
                pl.BlockSpec((window, width), lambda i, h: (0, 0)),
            ],
            out_specs=pl.BlockSpec((tokens * window, width), lambda i, h: (i, 0)),
        ),
        out_shape=shape((rows * window, width), BF),
        compiler_params=params(58),
        cost_estimate=FREE,
        name="finish",
    )(here, own, got, *early, *late, xw, stat, gain)


def place_kernel(here_ref, pos_ref, came_ref, stream_ref, out_ref):
    rows, width = stream_ref.shape
    cut = width // 2
    slots = pos_ref.shape[0]
    put = eq_hot((slots, rows), 1, pos_ref[...])
    for relative in range(2):
        start = pl.multiple_of((here_ref[2] ^ relative) * cut, cut)
        at = pl.ds(start, cut)
        out_ref[:, at] = (
            stream_ref[:, at].astype(F32)
            + lax.dot_general(
                put,
                came_ref[:, relative].reshape(slots, cut),
                (((0,), (0,)), ((), ())),
                preferred_element_type=F32,
            )
        ).astype(BF)


def place(here, pos, came, stream):
    rows, width = stream.shape
    return pl.pallas_call(
        place_kernel,
        in_specs=[scalars()] + [whole()] * 3,
        out_specs=whole(),
        out_shape=shape((rows, width), BF),
        compiler_params=params(12),
        cost_estimate=FREE,
        name="place",
    )(here, pos, came, stream)


def lay_kernel(here_ref, *refs):
    blocks, (out_ref, sems) = refs[:-2], refs[-2:]
    rows = blocks[0].shape[0]
    copies = []
    for index, ref in enumerate(blocks):
        owner = 2 * (here_ref[0] ^ (index // 2)) + (here_ref[1] ^ (index % 2))
        start = pl.multiple_of(owner * rows, rows)
        copies.append(pltpu.make_async_copy(ref, out_ref.at[pl.ds(start, rows)], sems.at[index]))
    for copy in copies:
        copy.start()
    for copy in copies:
        copy.wait()


def lay(here, blocks):
    rows, width = blocks[0].shape
    return pl.pallas_call(
        lay_kernel,
        in_specs=[scalars()] + [whole()] * len(blocks),
        out_specs=anywhere(),
        out_shape=shape((len(blocks) * rows, width), BF),
        scratch_shapes=[pltpu.SemaphoreType.DMA((len(blocks),))],
        compiler_params=params(4),
        cost_estimate=FREE,
        name="lay",
    )(here, *blocks)


def shards(features, ln_gain, ln_bias, projection, stream, norm_gain, cotangent, slots):
    n_img = lax.axis_size("img")
    n_ctx = lax.axis_size("ctx")
    n_tp = lax.axis_size("tp")
    merged = slots.shape[0]
    tok_rows, width = stream.shape
    owners = n_img * n_ctx
    capacity = 2 * merged // owners
    slot_count = owners * capacity
    full_width = width * n_tp
    cut = width // n_img

    img = lax.axis_index("img").astype(jnp.int32)
    tp = lax.axis_index("tp").astype(jnp.int32)
    core, far_half = tp % 2, tp // 2
    z, y = lax.axis_index("ctx") // RING, lax.axis_index("ctx") % RING
    here = jnp.stack([core, far_half, img, z, y]).astype(jnp.int32)

    flip = [(i, 1 - i) for i in range(n_img)]
    core_pairs = [(t, t ^ 1) for t in range(n_tp)]
    far_pairs = [(t, t ^ 2) for t in range(n_tp)]

    def along_x(array, by):
        pairs = []
        for i in range(n_img):
            for t in range(n_tp):
                x = (2 * (t // 2) + i + by) % RING
                pairs.append((i * n_tp + t, (x % 2) * n_tp + 2 * (x // 2) + t % 2))
        return lax.ppermute(array, ("img", "tp"), pairs)

    def along_ctx(array, axis, by):
        pairs = []
        for c in range(n_ctx):
            for t in range(n_tp):
                z, y = c // RING, c % RING
                if t % 2 == axis:
                    y = (y + by) % RING
                else:
                    z = (z + by) % RING
                pairs.append((c * n_tp + t, (z * RING + y) * n_tp + t))
        return lax.ppermute(array, ("ctx", "tp"), pairs)

    slots = jnp.roll(slots, -core * (merged // 2))
    target = slots // tok_rows
    ids = jnp.arange(merged)
    earlier = (target[:, None] == target[None, :]) & (ids[:, None] < ids[None, :])
    rank = jnp.sum(earlier.astype(jnp.int32), axis=0)
    slot = target * capacity + rank
    local = slots - target * tok_rows
    packed = jnp.max(
        jnp.where(jnp.arange(slot_count)[:, None] == slot[None, :], local[None, :], -1), axis=1
    )
    asked = lax.all_to_all(
        packed.reshape(owners, capacity), ("img", "ctx"), split_axis=0, concat_axis=0, tiled=True
    )
    columns = lax.dynamic_slice_in_dim(projection[0], img * cut, cut, axis=2).reshape(-1, cut)
    moves = (1, -1, 2)
    near_blocks = [along_ctx(columns, 0, by) for by in moves]
    paired = target * (n_img * capacity) + rank + img * capacity
    partner = lax.ppermute(paired, "img", flip)
    gain = ln_gain[0]
    lifted, xw, stat = layer_norm(here, features[0], gain, ln_bias[0])
    asked, lifted, stat, near_blocks, partner = lax.optimization_barrier(
        (asked, lifted, stat, near_blocks, partner)
    )
    paired = jnp.concatenate([paired, partner]).reshape(-1, 1)

    first = stack(here, [columns] + near_blocks)
    asked, first = lax.optimization_barrier((asked, first))

    asked = asked.reshape(n_img, n_ctx, capacity).transpose(1, 0, 2)
    asked = asked.reshape(slot_count, 1)
    held = collect(asked, stream, cotangent[0], first)
    came = lax.all_to_all(
        held.reshape(owners, n_img * capacity, width),
        ("img", "ctx"), split_axis=0, concat_axis=0, tiled=True,
    ).reshape(n_img * slot_count, width)

    stacks = [first] + [along_ctx(first, 1, by) for by in moves[:2]]
    stacks.append(along_ctx(stacks[1], 1, 1))

    pairs = []
    for i in range(n_img):
        for t in range(n_tp):
            x = (2 * (t // 2) + i + (1 if i == 1 else -1)) % RING
            pairs.append((i * n_tp + t, (x % 2) * n_tp + 2 * (x // 2) + t % 2))
    lifted = [lifted, lax.ppermute(lifted, ("img", "tp"), pairs)]

    own_gain = lax.dynamic_slice_in_dim(norm_gain, img * cut, cut, axis=1)
    acc = multiply(here, stacks[: RING - 1], lifted)
    base, cot = unpack(paired, came, acc)
    visual, state, sums = merge(here, own_gain, acc, base, cot, stacks[RING - 1], lifted)

    near, turned = add(sums, lax.ppermute(sums, "tp", core_pairs))
    stats = [near] + [along_x(near if by == 2 else turned, by) for by in (1, 2, 3)]
    stay, cross = pack(here, paired, visual, n_img * slot_count, near)
    cross, stats = lax.optimization_barrier((cross, stats))
    crossed = lax.ppermute(cross, "img", flip)

    own, other = backward(here, state, cot, own_gain, stats, stacks, full_width)
    own, other, crossed = lax.optimization_barrier((own, other, crossed))
    got = lax.ppermute(other, "tp", core_pairs)
    to_next, to_last, keep = pair(own, got, crossed)
    from_last, from_next = along_x(to_next, 1), along_x(to_last, -1)
    to_next, to_last = relay(keep, from_last, from_next)
    late_last, late_next = along_x(to_next, 1), along_x(to_last, -1)

    send = braid(stay, crossed, n_ctx)
    arrived = lax.all_to_all(send, "ctx", split_axis=0, concat_axis=0, tiled=True)
    new_stream = place(here, asked, arrived, stream)

    out = finish(here, own, got, (from_last, from_next), (late_last, late_next), xw, stat, gain)
    beyond = lax.ppermute(out, "tp", far_pairs)
    beyond, new_stream = lax.optimization_barrier((beyond, new_stream))
    from_core = [lax.ppermute(x, "tp", core_pairs) for x in (out, beyond)]
    grad = lay(here, [out, beyond] + from_core)
    return (new_stream, grad[None])


def solution(mesh):
    placed = (
        P(None, ("img", "ctx"), None),
        P(),
        P(),
        P(None, None, "ctx", "tp"),
        P(("img", "ctx"), "tp"),
        P(None, "tp"),
        P(None, ("img", "ctx"), "tp"),
        P(("img", "ctx")),
    )
    return jax.shard_map(
        shards,
        mesh=mesh,
        in_specs=placed,
        out_specs=(P(("img", "ctx"), "tp"), P(None, ("img", "ctx"), None)),
        check_vma=False,
    )
```

```python
import jax
import jax.numpy as jnp
from jax import lax
from jax.experimental import pallas as pl
from jax.experimental.pallas import tpu as pltpu
from jax.sharding import PartitionSpec as P


BF = jnp.bfloat16
F32 = jnp.float32
FREE = pl.CostEstimate(flops=0, bytes_accessed=0, transcendentals=0)
RING = 4
AWAY = (0, 3, 1, 2)


def params(mib):
    return pltpu.CompilerParams(vmem_limit_bytes=mib * 1024 * 1024)


def whole():
    return pl.BlockSpec(memory_space=pltpu.VMEM)


def shape(dims, kind):
    return jax.ShapeDtypeStruct(dims, kind)


def scalars():
    return pl.BlockSpec(memory_space=pltpu.SMEM)


def in_hbm():
    return pl.BlockSpec(memory_space=pltpu.HBM)


def anywhere():
    return pl.BlockSpec(memory_space=pl.ANY)


def eq_hot(shape, dim, index):
    return (lax.broadcasted_iota(jnp.int32, shape, dim) == index).astype(BF)


def window_major(tokens, window):
    n = tokens * window
    row = lax.broadcasted_iota(jnp.int32, (n, n), 0)
    col = lax.broadcasted_iota(jnp.int32, (n, n), 1)
    return (col == (row % tokens) * window + row // tokens).astype(BF)


def patch_major(tokens, window):
    n = tokens * window
    row = lax.broadcasted_iota(jnp.int32, (n, n), 0)
    col = lax.broadcasted_iota(jnp.int32, (n, n), 1)
    return (col == (row % window) * tokens + row // window).astype(BF)


def norm_kernel(here_ref, x_ref, gain_ref, bias_ref, lifted_ref, xw_ref, stat_ref):
    window, width = gain_ref.shape
    tokens = x_ref.shape[0] // window
    full = window * width
    x = jnp.dot(window_major(tokens, window), x_ref[...], preferred_element_type=F32)
    parts = [x[w * tokens : (w + 1) * tokens] for w in range(window)]
    total = sum(jnp.sum(p, axis=1, keepdims=True) for p in parts)
    squares = sum(jnp.sum(p * p, axis=1, keepdims=True) for p in parts)
    mean = total / full
    inv = lax.rsqrt(squares / full - mean * mean + 1e-05)
    lifted = []
    for w, p in enumerate(parts):
        normed = (p - mean) * inv
        lifted.append(
            normed * gain_ref[w : w + 1].astype(F32) + bias_ref[w : w + 1].astype(F32)
        )
        xw_ref[w] = p.astype(BF)
    share = width // (RING * RING)
    for core in range(2):

        @pl.when(here_ref[0] == core)
        def _():
            blocks = [(a, b) for a in range(RING) for b in range(RING)]
            starts = [(a * RING + b if core == 0 else b * RING + a) * share for a, b in blocks]
            lifted_ref[...] = jnp.concatenate(
                [p[:, at : at + share] for at in starts for p in lifted], axis=1
            ).astype(BF)

    lane = lax.broadcasted_iota(jnp.int32, stat_ref.shape, 1)
    stat_ref[...] = jnp.where(lane == 0, mean, inv)


def layer_norm(here, features, gain, bias):
    rows, width = features.shape
    window = gain.shape[0]
    merged = rows // window
    block = 64
    steps = merged // block
    return pl.pallas_call(
        norm_kernel,
        grid_spec=pltpu.PrefetchScalarGridSpec(
            num_scalar_prefetch=1,
            grid=(steps,),
            in_specs=[
                pl.BlockSpec(
                    (block * window, width),
                    lambda i, c: (lax.rem(i + c[0] * (steps // 2), steps), 0),
                ),
                pl.BlockSpec((window, width), lambda i, c: (0, 0)),
                pl.BlockSpec((window, width), lambda i, c: (0, 0)),
            ],
            out_specs=[
                pl.BlockSpec((block, window * width), lambda i, c: (i, 0)),
                pl.BlockSpec((window, block, width), lambda i, c: (0, i, 0)),
                pl.BlockSpec((block, 128), lambda i, c: (i, 0)),
            ],
        ),
        out_shape=[
            shape((merged, window * width), BF),
            shape((window, merged, width), BF),
            shape((merged, 128), F32),
        ],
        compiler_params=params(58),
        cost_estimate=FREE,
        name="layer_norm",
    )(here, features, gain, bias)


def collect_kernel(pos_ref, stream_ref, cot_ref, after_ref, out_ref):
    slots = pos_ref.shape[0]
    rows, width = stream_ref.shape
    cut = width // 2
    pick = eq_hot((slots, rows), 1, pos_ref[...])
    for img in range(2):
        at = slice(img * cut, (img + 1) * cut)
        for place, ref in enumerate((stream_ref, cot_ref)):
            out_ref[img, :, place * cut : (place + 1) * cut] = jnp.dot(
                pick, ref[:, at], preferred_element_type=F32
            ).astype(BF)


def collect(pos, stream, cot, after):
    slots = pos.shape[0]
    rows, width = stream.shape
    return pl.pallas_call(
        collect_kernel,
        in_specs=[whole()] * 3 + [anywhere()],
        out_specs=whole(),
        out_shape=shape((2, slots, width), BF),
        compiler_params=params(20),
        cost_estimate=FREE,
        name="collect",
    )(pos, stream, cot, after)


def unpack_kernel(slot_ref, came_ref, after_ref, base_ref, cot_ref):
    tokens, width = base_ref.shape
    slots = came_ref.shape[0]
    take = eq_hot((tokens, slots), 1, slot_ref[...])
    for start, out_ref in ((0, base_ref), (width, cot_ref)):
        out_ref[...] = jnp.dot(
            take, came_ref[:, start : start + width], preferred_element_type=F32
        ).astype(BF)


def unpack(slot_col, came, after):
    tokens = slot_col.shape[0]
    slots, both = came.shape
    width = both // 2
    outs = [shape((tokens, width), BF)] * 2
    return pl.pallas_call(
        unpack_kernel,
        in_specs=[whole()] * 2 + [anywhere()],
        out_specs=[whole()] * 2,
        out_shape=outs,
        compiler_params=params(12),
        cost_estimate=FREE,
        name="unpack",
    )(slot_col, came, after)


def stack_kernel(here_ref, *refs):
    halves, sems = refs[RING : RING + 2], refs[RING + 2]
    first = jnp.where(here_ref[0] == 0, here_ref[4], here_ref[3])
    for index, (away, ref) in enumerate(zip(AWAY, refs[:RING])):
        place = lax.rem(first + away, RING)
        for side, half in enumerate(halves):

            @pl.when(place // 2 == side)
            def _():
                pltpu.make_async_copy(ref, half.at[lax.rem(place, 2)], sems.at[index]).start()

    for index, ref in enumerate(refs[:RING]):
        pltpu.make_async_copy(ref, halves[0].at[0], sems.at[index]).wait()


def stack(here, blocks):
    rows, width = blocks[0].shape
    return pl.pallas_call(
        stack_kernel,
        in_specs=[scalars()] + [in_hbm()] * RING,
        out_specs=[whole()] * 2,
        out_shape=[shape((2, rows, width), BF)] * 2,
        scratch_shapes=[pltpu.SemaphoreType.DMA((RING,))],
        compiler_params=params(6),
        cost_estimate=FREE,
        name="stack",
    )(here, *blocks)


def fetch(here_ref, stacks, held_ref, sems):
    for index, ref in enumerate(stacks):
        away, side = AWAY[index // 2], pl.ds(2 * (index % 2), 2)

        @pl.when(here_ref[0] == 0)
        def _():
            place = lax.rem(here_ref[3] + away, RING)
            pltpu.make_async_copy(ref, held_ref.at[place, side], sems.at[index]).start()

        @pl.when(here_ref[0] == 1)
        def _():
            place = lax.rem(here_ref[4] + away, RING)
            pltpu.make_async_copy(ref, held_ref.at[side, place], sems.at[index]).start()

    def wait():
        for index, ref in enumerate(stacks):
            pltpu.make_async_copy(ref, held_ref.at[0, pl.ds(0, 2)], sems.at[index]).wait()

    return wait


def product(here_ref, away, stacks, lifted, held_ref, left_ref, sems):
    second = jnp.where(here_ref[0] == 0, here_ref[3], here_ref[4])
    block = left_ref.shape[2]
    rows = lifted[0].shape[0]
    copies = []
    for index in range(len(stacks) // 2):
        place = lax.rem(second + away[index], RING)
        at = pl.ds(pl.multiple_of(place * block, block), block)
        group = [
            pltpu.make_async_copy(
                stacks[2 * index + side], held_ref.at[index, pl.ds(2 * side, 2)], sems.at[index, side]
            )
            for side in range(2)
        ]
        for i, part in enumerate(lifted):
            to = left_ref.at[index, pl.ds(i * rows, rows)]
            group.append(pltpu.make_async_copy(part.at[:, at], to, sems.at[index, 2 + i]))
        for copy in group:
            copy.start()
        copies.append(group)

    def run(total):
        for index, group in enumerate(copies):
            for copy in group:
                copy.wait()
            part = jnp.dot(
                left_ref[index], held_ref[index].reshape(block, -1), preferred_element_type=F32
            )
            total = part if total is None else total + part
        return total

    return run


def product_scratch(stacks, lifted):
    count = len(stacks) // 2
    rows, depth = lifted[0].shape
    _, block_rows, width = stacks[0].shape
    return [
        pltpu.VMEM((count, RING, block_rows, width), BF),
        pltpu.VMEM((count, len(lifted) * rows, depth // RING), BF),
        pltpu.SemaphoreType.DMA((count, 2 + len(lifted))),
    ]


def multiply_kernel(here_ref, *refs):
    count = 2 * (RING - 1)
    stacks, lifted, (out_ref, *scratch) = refs[:count], refs[count : count + 2], refs[count + 2 :]
    out_ref[...] = product(here_ref, AWAY[: RING - 1], stacks, lifted, *scratch)(None)


def multiply(here, stacks, lifted):
    tokens, width = 2 * lifted[0].shape[0], stacks[0].shape[2]
    return pl.pallas_call(
        multiply_kernel,
        in_specs=[scalars()] + [in_hbm()] * (len(stacks) + len(lifted)),
        out_specs=whole(),
        out_shape=shape((tokens, width), F32),
        scratch_shapes=product_scratch(stacks, lifted),
        compiler_params=params(40),
        cost_estimate=FREE,
        name="multiply",
    )(here, *stacks, *lifted)


def merge_kernel(here_ref, ngain_ref, acc_hbm, base_hbm, cot_hbm, *refs):
    stacks, lifted, refs = refs[:2], refs[2:4], refs[4:]
    visual_ref, state_ref, stat_ref, acc_ref, base_ref, cot_ref, row_sems, *scratch = refs
    run = product(here_ref, AWAY[RING - 1 :], stacks, lifted, *scratch)
    copies = [
        pltpu.make_async_copy(a, b, row_sems.at[i])
        for i, (a, b) in enumerate(((acc_hbm, acc_ref), (base_hbm, base_ref), (cot_hbm, cot_ref)))
    ]
    for copy in copies:
        copy.start()
    total = run(None)
    for copy in copies:
        copy.wait()
    visual = (acc_ref[...] + total).astype(BF)
    visual_ref[...] = visual
    state = base_ref[...].astype(F32) + visual.astype(F32)
    state_ref[...] = state
    up = ngain_ref[...].astype(F32) * cot_ref[...].astype(F32)
    lane = lax.broadcasted_iota(jnp.int32, (state.shape[0], 128), 1)
    sums = jnp.where(
        lane == 0,
        jnp.sum(state * state, axis=1, keepdims=True),
        jnp.sum(up * state, axis=1, keepdims=True),
    )
    stat_ref[...] = sums.T[: stat_ref.shape[0]]


def merge(here, ngain, acc, base, cot, stacks, lifted):
    tokens, width = base.shape
    outs = [shape((tokens, width), BF), shape((tokens, width), F32), shape((8, tokens), F32)]
    return pl.pallas_call(
        merge_kernel,
        in_specs=[scalars(), whole()] + [in_hbm()] * 7,
        out_specs=[whole()] * 3,
        out_shape=outs,
        scratch_shapes=[
            pltpu.VMEM((tokens, width), F32),
            pltpu.VMEM((tokens, width), BF),
            pltpu.VMEM((tokens, width), BF),
            pltpu.SemaphoreType.DMA((3,)),
        ]
        + product_scratch(stacks, lifted),
        compiler_params=params(24),
        cost_estimate=FREE,
        name="merge",
    )(here, ngain, acc, base, cot, *stacks, *lifted)


def add_kernel(sums_ref, got_ref, near_ref, turned_ref):
    count = sums_ref.shape[1] // 4
    cuts = [
        sums_ref[:, i * count : (i + 1) * count] + got_ref[:, (i ^ 1) * count : ((i ^ 1) + 1) * count]
        for i in range(4)
    ]
    near_ref[...] = jnp.concatenate(cuts, axis=1)
    turned_ref[...] = jnp.concatenate(cuts[2:] + cuts[:2], axis=1)


def add(sums, got):
    return pl.pallas_call(
        add_kernel,
        in_specs=[whole()] * 2,
        out_specs=[whole()] * 2,
        out_shape=[shape(sums.shape, F32)] * 2,
        compiler_params=params(4),
        cost_estimate=FREE,
        name="add",
    )(sums, got)


def pack_kernel(here_ref, slot_ref, visual_ref, after_ref, stay_ref, cross_ref):
    tokens = visual_ref.shape[0]
    slots = stay_ref.shape[0]
    for relative, out_ref in ((0, stay_ref), (1, cross_ref)):
        put = eq_hot((tokens, slots), 1, slot_ref[...] - (here_ref[2] ^ relative) * slots)
        out_ref[...] = lax.dot_general(
            put, visual_ref[...], (((0,), (0,)), ((), ())), preferred_element_type=F32
        ).astype(BF)


def pack(here, slot_col, visual, slots, after):
    tokens, width = visual.shape
    return pl.pallas_call(
        pack_kernel,
        in_specs=[scalars()] + [whole()] * 2 + [anywhere()],
        out_specs=[whole()] * 2,
        out_shape=[shape((slots // 2, width), BF)] * 2,
        compiler_params=params(8),
        cost_estimate=FREE,
        name="pack",
    )(here, slot_col, visual, after)


def braid_kernel(stay_ref, crossed_ref, out_ref):
    count, _, rows, _ = out_ref.shape
    for c in range(count):
        at = slice(c * rows, (c + 1) * rows)
        out_ref[c, 0] = stay_ref[at, :]
        out_ref[c, 1] = crossed_ref[at, :]


def braid(stay, crossed, count):
    rows, width = stay.shape
    return pl.pallas_call(
        braid_kernel,
        in_specs=[whole()] * 2,
        out_specs=whole(),
        out_shape=shape((count, 2, rows // count, width), BF),
        compiler_params=params(6),
        cost_estimate=FREE,
        name="braid",
    )(stay, crossed)


def backward_kernel(full_width, here_ref, ngain_ref, *refs):
    stats, stacks, refs = refs[:RING], refs[RING : 3 * RING], refs[3 * RING :]
    state_hbm, cot_hbm, own_ref, other_ref = refs[:4]
    picked_ref, sums_ref, state_ref, cot_ref, held_ref, row_sems, sems = refs[4:]
    row_copies = [
        pltpu.make_async_copy(a, b, row_sems.at[i])
        for i, (a, b) in enumerate(((state_hbm, state_ref), (cot_hbm, cot_ref)))
    ]
    for copy in row_copies:
        copy.start()
    wait_weight = fetch(here_ref, stacks, held_ref, sems)
    tokens = state_ref.shape[0]
    rows = tokens // 2 // RING
    total = stats[0][...]
    for ref in stats[1:]:
        total = total + ref[...]
    sums_ref[...] = total.T
    far, img = here_ref[1], here_ref[2]
    gain = ngain_ref[...].astype(F32)
    for copy in row_copies:
        copy.wait()
    for core in range(2):
        for away in range(RING):
            there = lax.rem(2 * far + img + away, RING)
            partner = lax.rem(there + img, 2)
            begin = partner * (tokens // 2) + core * (tokens // 4) + (there // 2) * (tokens // 8)
            at = pl.ds(pl.multiple_of(begin, rows), rows)
            sums = sums_ref[at, :]
            inv = lax.rsqrt(sums[:, 0:1] / full_width + 1e-06)
            inner = sums[:, 1:2] / full_width
            up = gain * cot_ref[at, :].astype(F32)
            grad = inv * up - state_ref[at, :] * (inv * inv * inv * inner)
            to = (core * RING + away) * rows
            picked_ref[to : to + rows, :] = grad.astype(BF)
    depth = own_ref.shape[1]
    wait_weight()
    block = depth // RING
    for step in range(RING):
        cols = slice(step * block, (step + 1) * block)
        both = lax.dot_general(
            picked_ref[...],
            held_ref[step].reshape(block, -1),
            (((1,), (1,)), ((), ())),
            preferred_element_type=F32,
        )
        own_ref[:, cols] = both[: tokens // 2].astype(BF)
        other_ref[:, cols] = both[tokens // 2 :].astype(BF)


def backward(here, state, cot, ngain, stats, stacks, full_width):
    tokens, width = state.shape
    _, block_rows, _ = stacks[0].shape
    depth = RING * RING * block_rows
    return pl.pallas_call(
        lambda *refs: backward_kernel(full_width, *refs),
        in_specs=[scalars()] + [whole()] * (1 + RING) + [in_hbm()] * (2 * RING + 2),
        out_specs=[whole()] * 2,
        out_shape=[shape((tokens // 2, depth), BF)] * 2,
        scratch_shapes=[
            pltpu.VMEM((tokens, width), BF),
            pltpu.VMEM((tokens, 8), F32),
            pltpu.VMEM((tokens, width), F32),
            pltpu.VMEM((tokens, width), BF),
            pltpu.VMEM((RING, RING, block_rows, width), BF),
            pltpu.SemaphoreType.DMA((2,)),
            pltpu.SemaphoreType.DMA((2 * RING,)),
        ],
        compiler_params=params(24),
        cost_estimate=FREE,
        name="backward",
    )(here, ngain, *stats, *stacks, state, cot)


def pair_kernel(own_ref, got_ref, after_ref, next_ref, last_ref, keep_ref):
    rows = own_ref.shape[0] // RING
    half = rows // 2

    def total(start):
        at = slice(start, start + half)
        return (own_ref[at, :].astype(F32) + got_ref[at, :].astype(F32)).astype(BF)

    next_ref[:half] = total(2 * rows)
    next_ref[half:] = total(rows + half)
    last_ref[:half] = total(2 * rows + half)
    last_ref[half:] = total(3 * rows)
    keep_ref[:half] = total(rows)
    keep_ref[half:] = total(3 * rows + half)


def pair(own, got, after):
    rows, depth = got.shape[0] // RING, got.shape[1]
    return pl.pallas_call(
        pair_kernel,
        in_specs=[whole()] * 2 + [anywhere()],
        out_specs=[whole()] * 3,
        out_shape=[shape((rows, depth), BF)] * 3,
        compiler_params=params(8),
        cost_estimate=FREE,
        name="pair",
    )(own, got, after)


def relay_kernel(keep_ref, from_last_ref, from_next_ref, next_ref, last_ref):
    half = next_ref.shape[0]
    for at, came_ref, out_ref in (
        (slice(0, half), from_last_ref, next_ref),
        (slice(half, 2 * half), from_next_ref, last_ref),
    ):
        out_ref[...] = (keep_ref[at, :].astype(F32) + came_ref[:half].astype(F32)).astype(BF)


def relay(keep, from_last, from_next):
    rows, depth = keep.shape
    return pl.pallas_call(
        relay_kernel,
        in_specs=[whole()] * 3,
        out_specs=[whole()] * 2,
        out_shape=[shape((rows // 2, depth), BF)] * 2,
        compiler_params=params(8),
        cost_estimate=FREE,
        name="relay",
    )(keep, from_last, from_next)


def finish_kernel(here_ref, own_ref, got_ref, from_last_ref, from_next_ref, late_last_ref, late_next_ref,
                  xw_ref, stat_ref, gain_ref, out_ref):
    window, tokens, width = xw_ref.shape
    full = window * width
    mean = stat_ref[:, 0:1]
    inv = stat_ref[:, 1:2]
    early = jnp.where(pl.program_id(0) == 0, from_next_ref[...], from_last_ref[...])
    late = jnp.where(pl.program_id(0) == 0, late_last_ref[...], late_next_ref[...])
    lifted = own_ref[...].astype(F32) + got_ref[...].astype(F32)
    lifted = lifted + early.astype(F32) + late.astype(F32)
    share = width // (RING * RING)
    scaled = []
    total = 0.0
    inner = 0.0
    for w in range(window):
        g = jnp.concatenate(
            [lifted[:, at : at + share] for at in range(w * share, full, window * share)], axis=1
        ) * gain_ref[w : w + 1].astype(F32)
        normed = (xw_ref[w].astype(F32) - mean) * inv
        total = total + jnp.sum(g, axis=1, keepdims=True)
        inner = inner + jnp.sum(g * normed, axis=1, keepdims=True)
        scaled.append((g, normed))
    total = total / full
    inner = inner / full
    rows = jnp.concatenate(
        [(inv * (g - total - normed * inner)).astype(BF) for g, normed in scaled], axis=0
    )
    out_ref[...] = jnp.dot(
        patch_major(tokens, window), rows, preferred_element_type=F32
    ).astype(BF)


def finish(here, own, got, early, late, xw, stat, gain):
    rows, depth = early[0].shape
    window, width = gain.shape
    steps = 2
    tokens = rows // steps
    same = pl.BlockSpec((tokens, depth), lambda i, h: (i, 0))
    second = pl.BlockSpec((tokens, depth), lambda i, h: (1, 0))
    only = pl.BlockSpec((tokens, depth), lambda i, h: (0, 0))
    return pl.pallas_call(
        finish_kernel,
        grid_spec=pltpu.PrefetchScalarGridSpec(
            num_scalar_prefetch=1,
            grid=(steps,),
            in_specs=[same, same, second, second, only, only]
            + [
                pl.BlockSpec((window, tokens, width), lambda i, h: (0, h[1] * steps + i, 0)),
                pl.BlockSpec((tokens, 128), lambda i, h: (h[1] * steps + i, 0)),
                pl.BlockSpec((window, width), lambda i, h: (0, 0)),
            ],
            out_specs=pl.BlockSpec((tokens * window, width), lambda i, h: (i, 0)),
        ),
        out_shape=shape((rows * window, width), BF),
        compiler_params=params(58),
        cost_estimate=FREE,
        name="finish",
    )(here, own, got, *early, *late, xw, stat, gain)


def place_kernel(here_ref, pos_ref, came_ref, stream_ref, out_ref):
    rows, width = stream_ref.shape
    cut = width // 2
    slots = pos_ref.shape[0]
    put = eq_hot((slots, rows), 1, pos_ref[...])
    for relative in range(2):
        start = pl.multiple_of((here_ref[2] ^ relative) * cut, cut)
        at = pl.ds(start, cut)
        out_ref[:, at] = (
            stream_ref[:, at].astype(F32)
            + lax.dot_general(
                put,
                came_ref[:, relative].reshape(slots, cut),
                (((0,), (0,)), ((), ())),
                preferred_element_type=F32,
            )
        ).astype(BF)


def place(here, pos, came, stream):
    rows, width = stream.shape
    return pl.pallas_call(
        place_kernel,
        in_specs=[scalars()] + [whole()] * 3,
        out_specs=whole(),
        out_shape=shape((rows, width), BF),
        compiler_params=params(12),
        cost_estimate=FREE,
        name="place",
    )(here, pos, came, stream)


def lay_kernel(here_ref, *refs):
    blocks, (out_ref, sems) = refs[:-2], refs[-2:]
    rows = blocks[0].shape[0]
    copies = []
    for index, ref in enumerate(blocks):
        owner = 2 * (here_ref[0] ^ (index // 2)) + (here_ref[1] ^ (index % 2))
        start = pl.multiple_of(owner * rows, rows)
        copies.append(pltpu.make_async_copy(ref, out_ref.at[pl.ds(start, rows)], sems.at[index]))
    for copy in copies:
        copy.start()
    for copy in copies:
        copy.wait()


def lay(here, blocks):
    rows, width = blocks[0].shape
    return pl.pallas_call(
        lay_kernel,
        in_specs=[scalars()] + [whole()] * len(blocks),
        out_specs=anywhere(),
        out_shape=shape((len(blocks) * rows, width), BF),
        scratch_shapes=[pltpu.SemaphoreType.DMA((len(blocks),))],
        compiler_params=params(4),
        cost_estimate=FREE,
        name="lay",
    )(here, *blocks)


def shards(features, ln_gain, ln_bias, projection, stream, norm_gain, cotangent, slots):
    n_img = lax.axis_size("img")
    n_ctx = lax.axis_size("ctx")
    n_tp = lax.axis_size("tp")
    merged = slots.shape[0]
    tok_rows, width = stream.shape
    owners = n_img * n_ctx
    capacity = 2 * merged // owners
    slot_count = owners * capacity
    full_width = width * n_tp
    cut = width // n_img

    img = lax.axis_index("img").astype(jnp.int32)
    tp = lax.axis_index("tp").astype(jnp.int32)
    core, far_half = tp % 2, tp // 2
    z, y = lax.axis_index("ctx") // RING, lax.axis_index("ctx") % RING
    here = jnp.stack([core, far_half, img, z, y]).astype(jnp.int32)

    flip = [(i, 1 - i) for i in range(n_img)]
    core_pairs = [(t, t ^ 1) for t in range(n_tp)]
    far_pairs = [(t, t ^ 2) for t in range(n_tp)]

    def along_x(array, by):
        pairs = []
        for i in range(n_img):
            for t in range(n_tp):
                x = (2 * (t // 2) + i + by) % RING
                pairs.append((i * n_tp + t, (x % 2) * n_tp + 2 * (x // 2) + t % 2))
        return lax.ppermute(array, ("img", "tp"), pairs)

    def along_ctx(array, axis, by):
        pairs = []
        for c in range(n_ctx):
            for t in range(n_tp):
                z, y = c // RING, c % RING
                if t % 2 == axis:
                    y = (y + by) % RING
                else:
                    z = (z + by) % RING
                pairs.append((c * n_tp + t, (z * RING + y) * n_tp + t))
        return lax.ppermute(array, ("ctx", "tp"), pairs)

    slots = jnp.roll(slots, -core * (merged // 2))
    target = slots // tok_rows
    ids = jnp.arange(merged)
    earlier = (target[:, None] == target[None, :]) & (ids[:, None] < ids[None, :])
    rank = jnp.sum(earlier.astype(jnp.int32), axis=0)
    slot = target * capacity + rank
    local = slots - target * tok_rows
    packed = jnp.max(
        jnp.where(jnp.arange(slot_count)[:, None] == slot[None, :], local[None, :], -1), axis=1
    )
    asked = lax.all_to_all(
        packed.reshape(owners, capacity), ("img", "ctx"), split_axis=0, concat_axis=0, tiled=True
    )
    columns = lax.dynamic_slice_in_dim(projection[0], img * cut, cut, axis=2).reshape(-1, cut)
    moves = (1, -1, 2)
    near_blocks = [along_ctx(columns, 0, by) for by in moves]
    paired = target * (n_img * capacity) + rank + img * capacity
    partner = lax.ppermute(paired, "img", flip)
    gain = ln_gain[0]
    lifted, xw, stat = layer_norm(here, features[0], gain, ln_bias[0])
    asked, lifted, stat, near_blocks, partner = lax.optimization_barrier(
        (asked, lifted, stat, near_blocks, partner)
    )
    paired = jnp.concatenate([paired, partner]).reshape(-1, 1)

    first = stack(here, [columns] + near_blocks)
    asked, first = lax.optimization_barrier((asked, first))

    asked = asked.reshape(n_img, n_ctx, capacity).transpose(1, 0, 2)
    asked = asked.reshape(slot_count, 1)
    held = collect(asked, stream, cotangent[0], first[0])
    came = lax.all_to_all(
        held.reshape(owners, n_img * capacity, width),
        ("img", "ctx"), split_axis=0, concat_axis=0, tiled=True,
    ).reshape(n_img * slot_count, width)

    before = [along_ctx(half, 1, 1) for half in first]
    after = [along_ctx(half, 1, -1) for half in first]
    far = [along_ctx(before[0], 1, 1), along_ctx(after[1], 1, -1)]

    pairs = []
    for i in range(n_img):
        for t in range(n_tp):
            x = (2 * (t // 2) + i + (1 if t % 2 == 0 else -1)) % RING
            pairs.append((i * n_tp + t, (x % 2) * n_tp + 2 * (x // 2) + t % 2))
    lifted = [lifted, lax.ppermute(lifted, ("img", "tp"), pairs)]

    own_gain = lax.dynamic_slice_in_dim(norm_gain, img * cut, cut, axis=1)
    acc = multiply(here, [*first, *before, *after], lifted)
    base, cot = unpack(paired, came, acc)
    visual, state, sums = merge(here, own_gain, acc, base, cot, far, lifted)

    near, turned = add(sums, lax.ppermute(sums, "tp", core_pairs))
    stats = [near] + [along_x(near if by == 2 else turned, by) for by in (1, 2, 3)]
    stay, cross = pack(here, paired, visual, n_img * slot_count, near)
    cross, stats = lax.optimization_barrier((cross, stats))
    crossed = lax.ppermute(cross, "img", flip)

    own, other = backward(
        here, state, cot, own_gain, stats, [*first, *before, *after, *far], full_width
    )
    own, other, crossed = lax.optimization_barrier((own, other, crossed))
    got = lax.ppermute(other, "tp", core_pairs)
    to_next, to_last, keep = pair(own, got, crossed)
    from_last, from_next = along_x(to_next, 1), along_x(to_last, -1)
    to_next, to_last = relay(keep, from_last, from_next)
    late_last, late_next = along_x(to_next, 1), along_x(to_last, -1)

    send = braid(stay, crossed, n_ctx)
    arrived = lax.all_to_all(send, "ctx", split_axis=0, concat_axis=0, tiled=True)
    new_stream = place(here, asked, arrived, stream)

    out = finish(here, own, got, (from_last, from_next), (late_last, late_next), xw, stat, gain)
    beyond = lax.ppermute(out, "tp", far_pairs)
    beyond, new_stream = lax.optimization_barrier((beyond, new_stream))
    from_core = [lax.ppermute(x, "tp", core_pairs) for x in (out, beyond)]
    grad = lay(here, [out, beyond] + from_core)
    return (new_stream, grad[None])


def solution(mesh):
    placed = (
        P(None, ("img", "ctx"), None),
        P(),
        P(),
        P(None, None, "ctx", "tp"),
        P(("img", "ctx"), "tp"),
        P(None, "tp"),
        P(None, ("img", "ctx"), "tp"),
        P(("img", "ctx")),
    )
    return jax.shard_map(
        shards,
        mesh=mesh,
        in_specs=placed,
        out_specs=(P(("img", "ctx"), "tp"), P(None, ("img", "ctx"), None)),
        check_vma=False,
    )
```

```python
import jax
import jax.numpy as jnp
from jax import lax
from jax.experimental import pallas as pl
from jax.experimental.pallas import tpu as pltpu
from jax.sharding import PartitionSpec as P


BF = jnp.bfloat16
F32 = jnp.float32
FREE = pl.CostEstimate(flops=0, bytes_accessed=0, transcendentals=0)
RING = 4
AWAY = (0, 3, 1, 2)


def params(mib):
    return pltpu.CompilerParams(vmem_limit_bytes=mib * 1024 * 1024)


def whole():
    return pl.BlockSpec(memory_space=pltpu.VMEM)


def shape(dims, kind):
    return jax.ShapeDtypeStruct(dims, kind)


def scalars():
    return pl.BlockSpec(memory_space=pltpu.SMEM)


def in_hbm():
    return pl.BlockSpec(memory_space=pltpu.HBM)


def anywhere():
    return pl.BlockSpec(memory_space=pl.ANY)


def eq_hot(shape, dim, index):
    return (lax.broadcasted_iota(jnp.int32, shape, dim) == index).astype(BF)


def window_major(tokens, window):
    n = tokens * window
    row = lax.broadcasted_iota(jnp.int32, (n, n), 0)
    col = lax.broadcasted_iota(jnp.int32, (n, n), 1)
    return (col == (row % tokens) * window + row // tokens).astype(BF)


def patch_major(tokens, window):
    n = tokens * window
    row = lax.broadcasted_iota(jnp.int32, (n, n), 0)
    col = lax.broadcasted_iota(jnp.int32, (n, n), 1)
    return (col == (row % window) * tokens + row // window).astype(BF)


def norm_kernel(here_ref, x_ref, gain_ref, bias_ref, lifted_ref, xw_ref, stat_ref):
    window, width = gain_ref.shape
    tokens = x_ref.shape[0] // window
    full = window * width
    x = jnp.dot(window_major(tokens, window), x_ref[...], preferred_element_type=F32)
    parts = [x[w * tokens : (w + 1) * tokens] for w in range(window)]
    total = sum(jnp.sum(p, axis=1, keepdims=True) for p in parts)
    squares = sum(jnp.sum(p * p, axis=1, keepdims=True) for p in parts)
    mean = total / full
    inv = lax.rsqrt(squares / full - mean * mean + 1e-05)
    lifted = []
    for w, p in enumerate(parts):
        normed = (p - mean) * inv
        lifted.append(
            normed * gain_ref[w : w + 1].astype(F32) + bias_ref[w : w + 1].astype(F32)
        )
        xw_ref[w] = p.astype(BF)
    share = width // (RING * RING)
    for core in range(2):

        @pl.when(here_ref[0] == core)
        def _():
            blocks = [(a, b) for a in range(RING) for b in range(RING)]
            starts = [(a * RING + b if core == 0 else b * RING + a) * share for a, b in blocks]
            lifted_ref[...] = jnp.concatenate(
                [p[:, at : at + share] for at in starts for p in lifted], axis=1
            ).astype(BF)

    lane = lax.broadcasted_iota(jnp.int32, stat_ref.shape, 1)
    stat_ref[...] = jnp.where(lane == 0, mean, inv)


def layer_norm(here, features, gain, bias):
    rows, width = features.shape
    window = gain.shape[0]
    merged = rows // window
    block = 64
    steps = merged // block
    return pl.pallas_call(
        norm_kernel,
        grid_spec=pltpu.PrefetchScalarGridSpec(
            num_scalar_prefetch=1,
            grid=(steps,),
            in_specs=[
                pl.BlockSpec(
                    (block * window, width),
                    lambda i, c: (lax.rem(i + c[0] * (steps // 2), steps), 0),
                ),
                pl.BlockSpec((window, width), lambda i, c: (0, 0)),
                pl.BlockSpec((window, width), lambda i, c: (0, 0)),
            ],
            out_specs=[
                pl.BlockSpec((block, window * width), lambda i, c: (i, 0)),
                pl.BlockSpec((window, block, width), lambda i, c: (0, i, 0)),
                pl.BlockSpec((block, 128), lambda i, c: (i, 0)),
            ],
        ),
        out_shape=[
            shape((merged, window * width), BF),
            shape((window, merged, width), BF),
            shape((merged, 128), F32),
        ],
        compiler_params=params(58),
        cost_estimate=FREE,
        name="layer_norm",
    )(here, features, gain, bias)


def collect_kernel(pos_ref, stream_ref, cot_ref, after_ref, out_ref):
    slots = pos_ref.shape[0]
    rows, width = stream_ref.shape
    cut = width // 2
    pick = eq_hot((slots, rows), 1, pos_ref[...])
    for img in range(2):
        at = slice(img * cut, (img + 1) * cut)
        for place, ref in enumerate((stream_ref, cot_ref)):
            out_ref[img, :, place * cut : (place + 1) * cut] = jnp.dot(
                pick, ref[:, at], preferred_element_type=F32
            ).astype(BF)


def collect(pos, stream, cot, after):
    slots = pos.shape[0]
    rows, width = stream.shape
    return pl.pallas_call(
        collect_kernel,
        in_specs=[whole()] * 3 + [anywhere()],
        out_specs=whole(),
        out_shape=shape((2, slots, width), BF),
        compiler_params=params(20),
        cost_estimate=FREE,
        name="collect",
    )(pos, stream, cot, after)


def unpack_kernel(slot_ref, came_ref, after_ref, base_ref, cot_ref):
    tokens, width = base_ref.shape
    slots = came_ref.shape[0]
    take = eq_hot((tokens, slots), 1, slot_ref[...])
    for start, out_ref in ((0, base_ref), (width, cot_ref)):
        out_ref[...] = jnp.dot(
            take, came_ref[:, start : start + width], preferred_element_type=F32
        ).astype(BF)


def unpack(slot_col, came, after):
    tokens = slot_col.shape[0]
    slots, both = came.shape
    width = both // 2
    outs = [shape((tokens, width), BF)] * 2
    return pl.pallas_call(
        unpack_kernel,
        in_specs=[whole()] * 2 + [anywhere()],
        out_specs=[whole()] * 2,
        out_shape=outs,
        compiler_params=params(12),
        cost_estimate=FREE,
        name="unpack",
    )(slot_col, came, after)


def stack_kernel(here_ref, *refs):
    out_ref, sems = refs[RING:]
    first = jnp.where(here_ref[0] == 0, here_ref[4], here_ref[3])
    copies = [
        pltpu.make_async_copy(ref, out_ref.at[lax.rem(first + away, RING)], sems.at[index])
        for index, (away, ref) in enumerate(zip(AWAY, refs[:RING]))
    ]
    for copy in copies:
        copy.start()
    for copy in copies:
        copy.wait()


def stack(here, blocks):
    rows, width = blocks[0].shape
    return pl.pallas_call(
        stack_kernel,
        in_specs=[scalars()] + [in_hbm()] * RING,
        out_specs=whole(),
        out_shape=shape((RING, rows, width), BF),
        scratch_shapes=[pltpu.SemaphoreType.DMA((RING,))],
        compiler_params=params(6),
        cost_estimate=FREE,
        name="stack",
    )(here, *blocks)


def fetch(here_ref, stacks, held_ref, sems):
    for index, (away, ref) in enumerate(zip(AWAY, stacks)):

        @pl.when(here_ref[0] == 0)
        def _():
            place = lax.rem(here_ref[3] + away, RING)
            pltpu.make_async_copy(ref, held_ref.at[place], sems.at[index]).start()

        @pl.when(here_ref[0] == 1)
        def _():
            place = lax.rem(here_ref[4] + away, RING)
            pltpu.make_async_copy(ref, held_ref.at[:, place], sems.at[index]).start()

    def wait():
        for index, ref in enumerate(stacks):
            pltpu.make_async_copy(ref, held_ref.at[0], sems.at[index]).wait()

    return wait


def product(here_ref, away, stacks, lifted, held_ref, left_ref, sems):
    second = jnp.where(here_ref[0] == 0, here_ref[3], here_ref[4])
    block = left_ref.shape[2]
    rows = lifted[0].shape[0]
    copies = []
    for index, ref in enumerate(stacks):
        place = lax.rem(second + away[index], RING)
        at = pl.ds(pl.multiple_of(place * block, block), block)
        group = [pltpu.make_async_copy(ref, held_ref.at[index], sems.at[index, 0])]
        for i, part in enumerate(lifted):
            to = left_ref.at[index, pl.ds(i * rows, rows)]
            group.append(pltpu.make_async_copy(part.at[:, at], to, sems.at[index, 1 + i]))
        for copy in group:
            copy.start()
        copies.append(group)

    def run(total):
        for index, group in enumerate(copies):
            for copy in group:
                copy.wait()
            part = jnp.dot(
                left_ref[index], held_ref[index].reshape(block, -1), preferred_element_type=F32
            )
            total = part if total is None else total + part
        return total

    return run


def product_scratch(stacks, lifted):
    count = len(stacks)
    rows, depth = lifted[0].shape
    return [
        pltpu.VMEM((count,) + stacks[0].shape, BF),
        pltpu.VMEM((count, len(lifted) * rows, depth // RING), BF),
        pltpu.SemaphoreType.DMA((count, 1 + len(lifted))),
    ]


def multiply_kernel(here_ref, *refs):
    stacks, lifted, (out_ref, *scratch) = refs[: RING - 1], refs[RING - 1 : RING + 1], refs[RING + 1 :]
    out_ref[...] = product(here_ref, AWAY[: RING - 1], stacks, lifted, *scratch)(None)


def multiply(here, stacks, lifted):
    tokens, width = 2 * lifted[0].shape[0], stacks[0].shape[2]
    return pl.pallas_call(
        multiply_kernel,
        in_specs=[scalars()] + [in_hbm()] * (len(stacks) + len(lifted)),
        out_specs=whole(),
        out_shape=shape((tokens, width), F32),
        scratch_shapes=product_scratch(stacks, lifted),
        compiler_params=params(60),
        cost_estimate=FREE,
        name="multiply",
    )(here, *stacks, *lifted)


def merge_kernel(here_ref, ngain_ref, acc_hbm, base_hbm, cot_hbm, stack_ref, *refs):
    lifted, refs = refs[:2], refs[2:]
    visual_ref, state_ref, stat_ref, acc_ref, base_ref, cot_ref, row_sems, *scratch = refs
    run = product(here_ref, AWAY[RING - 1 :], (stack_ref,), lifted, *scratch)
    copies = [
        pltpu.make_async_copy(a, b, row_sems.at[i])
        for i, (a, b) in enumerate(((acc_hbm, acc_ref), (base_hbm, base_ref), (cot_hbm, cot_ref)))
    ]
    for copy in copies:
        copy.start()
    total = run(None)
    for copy in copies:
        copy.wait()
    visual = (acc_ref[...] + total).astype(BF)
    visual_ref[...] = visual
    state = base_ref[...].astype(F32) + visual.astype(F32)
    state_ref[...] = state
    up = ngain_ref[...].astype(F32) * cot_ref[...].astype(F32)
    lane = lax.broadcasted_iota(jnp.int32, (state.shape[0], 128), 1)
    sums = jnp.where(
        lane == 0,
        jnp.sum(state * state, axis=1, keepdims=True),
        jnp.sum(up * state, axis=1, keepdims=True),
    )
    stat_ref[...] = sums.T[: stat_ref.shape[0]]


def merge(here, ngain, acc, base, cot, stack, lifted):
    tokens, width = base.shape
    outs = [shape((tokens, width), BF), shape((tokens, width), F32), shape((8, tokens), F32)]
    return pl.pallas_call(
        merge_kernel,
        in_specs=[scalars(), whole()] + [in_hbm()] * 6,
        out_specs=[whole()] * 3,
        out_shape=outs,
        scratch_shapes=[
            pltpu.VMEM((tokens, width), F32),
            pltpu.VMEM((tokens, width), BF),
            pltpu.VMEM((tokens, width), BF),
            pltpu.SemaphoreType.DMA((3,)),
        ]
        + product_scratch((stack,), lifted),
        compiler_params=params(24),
        cost_estimate=FREE,
        name="merge",
    )(here, ngain, acc, base, cot, stack, *lifted)


def add_kernel(sums_ref, got_ref, near_ref, turned_ref):
    count = sums_ref.shape[1] // 4
    cuts = [
        sums_ref[:, i * count : (i + 1) * count] + got_ref[:, (i ^ 1) * count : ((i ^ 1) + 1) * count]
        for i in range(4)
    ]
    near_ref[...] = jnp.concatenate(cuts, axis=1)
    turned_ref[...] = jnp.concatenate(cuts[2:] + cuts[:2], axis=1)


def add(sums, got):
    return pl.pallas_call(
        add_kernel,
        in_specs=[whole()] * 2,
        out_specs=[whole()] * 2,
        out_shape=[shape(sums.shape, F32)] * 2,
        compiler_params=params(4),
        cost_estimate=FREE,
        name="add",
    )(sums, got)


def pack_kernel(here_ref, slot_ref, visual_ref, after_ref, stay_ref, cross_ref):
    tokens = visual_ref.shape[0]
    slots = stay_ref.shape[0]
    for relative, out_ref in ((0, stay_ref), (1, cross_ref)):
        put = eq_hot((tokens, slots), 1, slot_ref[...] - (here_ref[2] ^ relative) * slots)
        out_ref[...] = lax.dot_general(
            put, visual_ref[...], (((0,), (0,)), ((), ())), preferred_element_type=F32
        ).astype(BF)


def pack(here, slot_col, visual, slots, after):
    tokens, width = visual.shape
    return pl.pallas_call(
        pack_kernel,
        in_specs=[scalars()] + [whole()] * 2 + [anywhere()],
        out_specs=[whole()] * 2,
        out_shape=[shape((slots // 2, width), BF)] * 2,
        compiler_params=params(8),
        cost_estimate=FREE,
        name="pack",
    )(here, slot_col, visual, after)


def braid_kernel(stay_ref, crossed_ref, out_ref):
    count, _, rows, _ = out_ref.shape
    for c in range(count):
        at = slice(c * rows, (c + 1) * rows)
        out_ref[c, 0] = stay_ref[at, :]
        out_ref[c, 1] = crossed_ref[at, :]


def braid(stay, crossed, count):
    rows, width = stay.shape
    return pl.pallas_call(
        braid_kernel,
        in_specs=[whole()] * 2,
        out_specs=whole(),
        out_shape=shape((count, 2, rows // count, width), BF),
        compiler_params=params(6),
        cost_estimate=FREE,
        name="braid",
    )(stay, crossed)


def backward_kernel(full_width, here_ref, ngain_ref, *refs):
    stats, stacks, refs = refs[:RING], refs[RING : 2 * RING], refs[2 * RING :]
    state_hbm, cot_hbm, own_ref, other_ref = refs[:4]
    picked_ref, sums_ref, state_ref, cot_ref, held_ref, row_sems, sems = refs[4:]
    row_copies = [
        pltpu.make_async_copy(a, b, row_sems.at[i])
        for i, (a, b) in enumerate(((state_hbm, state_ref), (cot_hbm, cot_ref)))
    ]
    for copy in row_copies:
        copy.start()
    wait_weight = fetch(here_ref, stacks, held_ref, sems)
    tokens = state_ref.shape[0]
    rows = tokens // 2 // RING
    total = stats[0][...]
    for ref in stats[1:]:
        total = total + ref[...]
    sums_ref[...] = total.T
    far, img = here_ref[1], here_ref[2]
    gain = ngain_ref[...].astype(F32)
    for copy in row_copies:
        copy.wait()
    for core in range(2):
        for away in range(RING):
            there = lax.rem(2 * far + img + away, RING)
            partner = lax.rem(there + img, 2)
            begin = partner * (tokens // 2) + core * (tokens // 4) + (there // 2) * (tokens // 8)
            at = pl.ds(pl.multiple_of(begin, rows), rows)
            sums = sums_ref[at, :]
            inv = lax.rsqrt(sums[:, 0:1] / full_width + 1e-06)
            inner = sums[:, 1:2] / full_width
            up = gain * cot_ref[at, :].astype(F32)
            grad = inv * up - state_ref[at, :] * (inv * inv * inv * inner)
            to = (core * RING + away) * rows
            picked_ref[to : to + rows, :] = grad.astype(BF)
    depth = own_ref.shape[1]
    wait_weight()
    block = depth // RING
    for step in range(RING):
        cols = slice(step * block, (step + 1) * block)
        both = lax.dot_general(
            picked_ref[...],
            held_ref[step].reshape(block, -1),
            (((1,), (1,)), ((), ())),
            preferred_element_type=F32,
        )
        own_ref[:, cols] = both[: tokens // 2].astype(BF)
        other_ref[:, cols] = both[tokens // 2 :].astype(BF)


def backward(here, state, cot, ngain, stats, stacks, full_width):
    tokens, width = state.shape
    depth = RING * stacks[0].shape[0] * stacks[0].shape[1]
    return pl.pallas_call(
        lambda *refs: backward_kernel(full_width, *refs),
        in_specs=[scalars()] + [whole()] * (1 + RING) + [in_hbm()] * (RING + 2),
        out_specs=[whole()] * 2,
        out_shape=[shape((tokens // 2, depth), BF)] * 2,
        scratch_shapes=[
            pltpu.VMEM((tokens, width), BF),
            pltpu.VMEM((tokens, 8), F32),
            pltpu.VMEM((tokens, width), F32),
            pltpu.VMEM((tokens, width), BF),
            pltpu.VMEM((RING,) + stacks[0].shape, BF),
            pltpu.SemaphoreType.DMA((2,)),
            pltpu.SemaphoreType.DMA((RING,)),
        ],
        compiler_params=params(24),
        cost_estimate=FREE,
        name="backward",
    )(here, ngain, *stats, *stacks, state, cot)


def pair_kernel(own_ref, got_ref, after_ref, next_ref, last_ref, keep_ref):
    rows = own_ref.shape[0] // RING
    half = rows // 2

    def total(start):
        at = slice(start, start + half)
        return (own_ref[at, :].astype(F32) + got_ref[at, :].astype(F32)).astype(BF)

    next_ref[:half] = total(2 * rows)
    next_ref[half:] = total(rows + half)
    last_ref[:half] = total(2 * rows + half)
    last_ref[half:] = total(3 * rows)
    keep_ref[:half] = total(rows)
    keep_ref[half:] = total(3 * rows + half)


def pair(own, got, after):
    rows, depth = got.shape[0] // RING, got.shape[1]
    return pl.pallas_call(
        pair_kernel,
        in_specs=[whole()] * 2 + [anywhere()],
        out_specs=[whole()] * 3,
        out_shape=[shape((rows, depth), BF)] * 3,
        compiler_params=params(8),
        cost_estimate=FREE,
        name="pair",
    )(own, got, after)


def relay_kernel(keep_ref, from_last_ref, from_next_ref, next_ref, last_ref):
    half = next_ref.shape[0]
    for at, came_ref, out_ref in (
        (slice(0, half), from_last_ref, next_ref),
        (slice(half, 2 * half), from_next_ref, last_ref),
    ):
        out_ref[...] = (keep_ref[at, :].astype(F32) + came_ref[:half].astype(F32)).astype(BF)


def relay(keep, from_last, from_next):
    rows, depth = keep.shape
    return pl.pallas_call(
        relay_kernel,
        in_specs=[whole()] * 3,
        out_specs=[whole()] * 2,
        out_shape=[shape((rows // 2, depth), BF)] * 2,
        compiler_params=params(8),
        cost_estimate=FREE,
        name="relay",
    )(keep, from_last, from_next)


def finish_kernel(here_ref, own_ref, got_ref, from_last_ref, from_next_ref, late_last_ref, late_next_ref,
                  xw_ref, stat_ref, gain_ref, out_ref):
    window, tokens, width = xw_ref.shape
    full = window * width
    mean = stat_ref[:, 0:1]
    inv = stat_ref[:, 1:2]
    early = jnp.where(pl.program_id(0) == 0, from_next_ref[...], from_last_ref[...])
    late = jnp.where(pl.program_id(0) == 0, late_last_ref[...], late_next_ref[...])
    lifted = own_ref[...].astype(F32) + got_ref[...].astype(F32)
    lifted = lifted + early.astype(F32) + late.astype(F32)
    share = width // (RING * RING)
    scaled = []
    total = 0.0
    inner = 0.0
    for w in range(window):
        g = jnp.concatenate(
            [lifted[:, at : at + share] for at in range(w * share, full, window * share)], axis=1
        ) * gain_ref[w : w + 1].astype(F32)
        normed = (xw_ref[w].astype(F32) - mean) * inv
        total = total + jnp.sum(g, axis=1, keepdims=True)
        inner = inner + jnp.sum(g * normed, axis=1, keepdims=True)
        scaled.append((g, normed))
    total = total / full
    inner = inner / full
    rows = jnp.concatenate(
        [(inv * (g - total - normed * inner)).astype(BF) for g, normed in scaled], axis=0
    )
    out_ref[...] = jnp.dot(
        patch_major(tokens, window), rows, preferred_element_type=F32
    ).astype(BF)


def finish(here, own, got, early, late, xw, stat, gain):
    rows, depth = early[0].shape
    window, width = gain.shape
    steps = 2
    tokens = rows // steps
    same = pl.BlockSpec((tokens, depth), lambda i, h: (i, 0))
    second = pl.BlockSpec((tokens, depth), lambda i, h: (1, 0))
    only = pl.BlockSpec((tokens, depth), lambda i, h: (0, 0))
    return pl.pallas_call(
        finish_kernel,
        grid_spec=pltpu.PrefetchScalarGridSpec(
            num_scalar_prefetch=1,
            grid=(steps,),
            in_specs=[same, same, second, second, only, only]
            + [
                pl.BlockSpec((window, tokens, width), lambda i, h: (0, h[1] * steps + i, 0)),
                pl.BlockSpec((tokens, 128), lambda i, h: (h[1] * steps + i, 0)),
                pl.BlockSpec((window, width), lambda i, h: (0, 0)),
            ],
            out_specs=pl.BlockSpec((tokens * window, width), lambda i, h: (i, 0)),
        ),
        out_shape=shape((rows * window, width), BF),
        compiler_params=params(58),
        cost_estimate=FREE,
        name="finish",
    )(here, own, got, *early, *late, xw, stat, gain)


def place_kernel(here_ref, pos_ref, came_ref, stream_ref, out_ref):
    rows, width = stream_ref.shape
    cut = width // 2
    slots = pos_ref.shape[0]
    put = eq_hot((slots, rows), 1, pos_ref[...])
    for relative in range(2):
        start = pl.multiple_of((here_ref[2] ^ relative) * cut, cut)
        at = pl.ds(start, cut)
        out_ref[:, at] = (
            stream_ref[:, at].astype(F32)
            + lax.dot_general(
                put,
                came_ref[:, relative].reshape(slots, cut),
                (((0,), (0,)), ((), ())),
                preferred_element_type=F32,
            )
        ).astype(BF)


def place(here, pos, came, stream):
    rows, width = stream.shape
    return pl.pallas_call(
        place_kernel,
        in_specs=[scalars()] + [whole()] * 3,
        out_specs=whole(),
        out_shape=shape((rows, width), BF),
        compiler_params=params(12),
        cost_estimate=FREE,
        name="place",
    )(here, pos, came, stream)


def lay_kernel(here_ref, *refs):
    blocks, (out_ref, sems) = refs[:-2], refs[-2:]
    rows = blocks[0].shape[0]
    copies = []
    for index, ref in enumerate(blocks):
        owner = 2 * (here_ref[0] ^ (index // 2)) + (here_ref[1] ^ (index % 2))
        start = pl.multiple_of(owner * rows, rows)
        copies.append(pltpu.make_async_copy(ref, out_ref.at[pl.ds(start, rows)], sems.at[index]))
    for copy in copies:
        copy.start()
    for copy in copies:
        copy.wait()


def lay(here, blocks):
    rows, width = blocks[0].shape
    return pl.pallas_call(
        lay_kernel,
        in_specs=[scalars()] + [whole()] * len(blocks),
        out_specs=anywhere(),
        out_shape=shape((len(blocks) * rows, width), BF),
        scratch_shapes=[pltpu.SemaphoreType.DMA((len(blocks),))],
        compiler_params=params(4),
        cost_estimate=FREE,
        name="lay",
    )(here, *blocks)


def shards(features, ln_gain, ln_bias, projection, stream, norm_gain, cotangent, slots):
    n_img = lax.axis_size("img")
    n_ctx = lax.axis_size("ctx")
    n_tp = lax.axis_size("tp")
    merged = slots.shape[0]
    tok_rows, width = stream.shape
    owners = n_img * n_ctx
    capacity = 2 * merged // owners
    slot_count = owners * capacity
    full_width = width * n_tp
    cut = width // n_img

    img = lax.axis_index("img").astype(jnp.int32)
    tp = lax.axis_index("tp").astype(jnp.int32)
    core, far_half = tp % 2, tp // 2
    z, y = lax.axis_index("ctx") // RING, lax.axis_index("ctx") % RING
    here = jnp.stack([core, far_half, img, z, y]).astype(jnp.int32)

    flip = [(i, 1 - i) for i in range(n_img)]
    core_pairs = [(t, t ^ 1) for t in range(n_tp)]
    far_pairs = [(t, t ^ 2) for t in range(n_tp)]

    def along_x(array, by):
        pairs = []
        for i in range(n_img):
            for t in range(n_tp):
                x = (2 * (t // 2) + i + by) % RING
                pairs.append((i * n_tp + t, (x % 2) * n_tp + 2 * (x // 2) + t % 2))
        return lax.ppermute(array, ("img", "tp"), pairs)

    def along_ctx(array, axis, by):
        pairs = []
        for c in range(n_ctx):
            for t in range(n_tp):
                z, y = c // RING, c % RING
                if t % 2 == axis:
                    y = (y + by) % RING
                else:
                    z = (z + by) % RING
                pairs.append((c * n_tp + t, (z * RING + y) * n_tp + t))
        return lax.ppermute(array, ("ctx", "tp"), pairs)

    slots = jnp.roll(slots, -core * (merged // 2))
    target = slots // tok_rows
    ids = jnp.arange(merged)
    earlier = (target[:, None] == target[None, :]) & (ids[:, None] < ids[None, :])
    rank = jnp.sum(earlier.astype(jnp.int32), axis=0)
    slot = target * capacity + rank
    local = slots - target * tok_rows
    packed = jnp.max(
        jnp.where(jnp.arange(slot_count)[:, None] == slot[None, :], local[None, :], -1), axis=1
    )
    asked = lax.all_to_all(
        packed.reshape(owners, capacity), ("img", "ctx"), split_axis=0, concat_axis=0, tiled=True
    )
    columns = lax.dynamic_slice_in_dim(projection[0], img * cut, cut, axis=2).reshape(-1, cut)
    moves = (1, -1, 2)
    near_blocks = [along_ctx(columns, 0, by) for by in moves]
    paired = target * (n_img * capacity) + rank + img * capacity
    partner = lax.ppermute(paired, "img", flip)
    gain = ln_gain[0]
    lifted, xw, stat = layer_norm(here, features[0], gain, ln_bias[0])
    asked, lifted, stat, near_blocks, partner = lax.optimization_barrier(
        (asked, lifted, stat, near_blocks, partner)
    )
    paired = jnp.concatenate([paired, partner]).reshape(-1, 1)

    first = stack(here, [columns] + near_blocks)
    asked, first, lifted = lax.optimization_barrier((asked, first, lifted))

    asked = asked.reshape(n_img, n_ctx, capacity).transpose(1, 0, 2)
    asked = asked.reshape(slot_count, 1)
    held = collect(asked, stream, cotangent[0], first)
    came = lax.all_to_all(
        held.reshape(owners, n_img * capacity, width),
        ("img", "ctx"), split_axis=0, concat_axis=0, tiled=True,
    ).reshape(n_img * slot_count, width)

    stacks = [first] + [along_ctx(first, 1, by) for by in moves[:2]]
    stacks.append(along_ctx(stacks[1], 1, 1))

    pairs = []
    for i in range(n_img):
        for t in range(n_tp):
            x = (2 * (t // 2) + i + (1 if t % 2 == 0 else -1)) % RING
            pairs.append((i * n_tp + t, (x % 2) * n_tp + 2 * (x // 2) + t % 2))
    lifted = [lifted, lax.ppermute(lifted, ("img", "tp"), pairs)]

    own_gain = lax.dynamic_slice_in_dim(norm_gain, img * cut, cut, axis=1)
    acc = multiply(here, stacks[: RING - 1], lifted)
    base, cot = unpack(paired, came, acc)
    visual, state, sums = merge(here, own_gain, acc, base, cot, stacks[RING - 1], lifted)

    near, turned = add(sums, lax.ppermute(sums, "tp", core_pairs))
    stats = [near] + [along_x(near if by == 2 else turned, by) for by in (1, 2, 3)]
    stay, cross = pack(here, paired, visual, n_img * slot_count, near)
    cross, stats = lax.optimization_barrier((cross, stats))
    crossed = lax.ppermute(cross, "img", flip)

    own, other = backward(here, state, cot, own_gain, stats, stacks, full_width)
    own, other, crossed = lax.optimization_barrier((own, other, crossed))
    got = lax.ppermute(other, "tp", core_pairs)
    to_next, to_last, keep = pair(own, got, crossed)
    from_last, from_next = along_x(to_next, 1), along_x(to_last, -1)
    to_next, to_last = relay(keep, from_last, from_next)
    late_last, late_next = along_x(to_next, 1), along_x(to_last, -1)

    send = braid(stay, crossed, n_ctx)
    arrived = lax.all_to_all(send, "ctx", split_axis=0, concat_axis=0, tiled=True)
    new_stream = place(here, asked, arrived, stream)

    out = finish(here, own, got, (from_last, from_next), (late_last, late_next), xw, stat, gain)
    beyond = lax.ppermute(out, "tp", far_pairs)
    beyond, new_stream = lax.optimization_barrier((beyond, new_stream))
    from_core = [lax.ppermute(x, "tp", core_pairs) for x in (out, beyond)]
    grad = lay(here, [out, beyond] + from_core)
    return (new_stream, grad[None])


def solution(mesh):
    placed = (
        P(None, ("img", "ctx"), None),
        P(),
        P(),
        P(None, None, "ctx", "tp"),
        P(("img", "ctx"), "tp"),
        P(None, "tp"),
        P(None, ("img", "ctx"), "tp"),
        P(("img", "ctx")),
    )
    return jax.shard_map(
        shards,
        mesh=mesh,
        in_specs=placed,
        out_specs=(P(("img", "ctx"), "tp"), P(None, ("img", "ctx"), None)),
        check_vma=False,
    )
```

```python
import jax
import jax.numpy as jnp
from jax import lax
from jax.experimental import pallas as pl
from jax.experimental.pallas import tpu as pltpu
from jax.sharding import PartitionSpec as P


BF = jnp.bfloat16
F32 = jnp.float32
FREE = pl.CostEstimate(flops=0, bytes_accessed=0, transcendentals=0)
RING = 4
AWAY = (0, 3, 1, 2)
EARLY = 2


def params(mib):
    return pltpu.CompilerParams(vmem_limit_bytes=mib * 1024 * 1024)


def whole():
    return pl.BlockSpec(memory_space=pltpu.VMEM)


def shape(dims, kind):
    return jax.ShapeDtypeStruct(dims, kind)


def scalars():
    return pl.BlockSpec(memory_space=pltpu.SMEM)


def in_hbm():
    return pl.BlockSpec(memory_space=pltpu.HBM)


def anywhere():
    return pl.BlockSpec(memory_space=pl.ANY)


def eq_hot(shape, dim, index):
    return (lax.broadcasted_iota(jnp.int32, shape, dim) == index).astype(BF)


def window_major(tokens, window):
    n = tokens * window
    row = lax.broadcasted_iota(jnp.int32, (n, n), 0)
    col = lax.broadcasted_iota(jnp.int32, (n, n), 1)
    return (col == (row % tokens) * window + row // tokens).astype(BF)


def patch_major(tokens, window):
    n = tokens * window
    row = lax.broadcasted_iota(jnp.int32, (n, n), 0)
    col = lax.broadcasted_iota(jnp.int32, (n, n), 1)
    return (col == (row % window) * tokens + row // window).astype(BF)


def norm_kernel(here_ref, x_ref, gain_ref, bias_ref, lifted_ref, xw_ref, stat_ref):
    window, width = gain_ref.shape
    tokens = x_ref.shape[0] // window
    full = window * width
    x = jnp.dot(window_major(tokens, window), x_ref[...], preferred_element_type=F32)
    parts = [x[w * tokens : (w + 1) * tokens] for w in range(window)]
    total = sum(jnp.sum(p, axis=1, keepdims=True) for p in parts)
    squares = sum(jnp.sum(p * p, axis=1, keepdims=True) for p in parts)
    mean = total / full
    inv = lax.rsqrt(squares / full - mean * mean + 1e-05)
    lifted = []
    for w, p in enumerate(parts):
        normed = (p - mean) * inv
        lifted.append(
            normed * gain_ref[w : w + 1].astype(F32) + bias_ref[w : w + 1].astype(F32)
        )
        xw_ref[w] = p.astype(BF)
    share = width // (RING * RING)
    for core in range(2):

        @pl.when(here_ref[0] == core)
        def _():
            blocks = [(a, b) for a in range(RING) for b in range(RING)]
            starts = [(a * RING + b if core == 0 else b * RING + a) * share for a, b in blocks]
            lifted_ref[...] = jnp.concatenate(
                [p[:, at : at + share] for at in starts for p in lifted], axis=1
            ).astype(BF)

    lane = lax.broadcasted_iota(jnp.int32, stat_ref.shape, 1)
    stat_ref[...] = jnp.where(lane == 0, mean, inv)


def layer_norm(here, features, gain, bias):
    rows, width = features.shape
    window = gain.shape[0]
    merged = rows // window
    block = 64
    steps = merged // block
    return pl.pallas_call(
        norm_kernel,
        grid_spec=pltpu.PrefetchScalarGridSpec(
            num_scalar_prefetch=1,
            grid=(steps,),
            in_specs=[
                pl.BlockSpec(
                    (block * window, width),
                    lambda i, c: (lax.rem(i + c[0] * (steps // 2), steps), 0),
                ),
                pl.BlockSpec((window, width), lambda i, c: (0, 0)),
                pl.BlockSpec((window, width), lambda i, c: (0, 0)),
            ],
            out_specs=[
                pl.BlockSpec((block, window * width), lambda i, c: (i, 0)),
                pl.BlockSpec((window, block, width), lambda i, c: (0, i, 0)),
                pl.BlockSpec((block, 128), lambda i, c: (i, 0)),
            ],
        ),
        out_shape=[
            shape((merged, window * width), BF),
            shape((window, merged, width), BF),
            shape((merged, 128), F32),
        ],
        compiler_params=params(58),
        cost_estimate=FREE,
        name="layer_norm",
    )(here, features, gain, bias)


def collect_kernel(pos_ref, stream_ref, cot_ref, after_ref, out_ref):
    slots = pos_ref.shape[0]
    rows, width = stream_ref.shape
    cut = width // 2
    pick = eq_hot((slots, rows), 1, pos_ref[...])
    for img in range(2):
        at = slice(img * cut, (img + 1) * cut)
        for place, ref in enumerate((stream_ref, cot_ref)):
            out_ref[img, :, place * cut : (place + 1) * cut] = jnp.dot(
                pick, ref[:, at], preferred_element_type=F32
            ).astype(BF)


def collect(pos, stream, cot, after):
    slots = pos.shape[0]
    rows, width = stream.shape
    return pl.pallas_call(
        collect_kernel,
        in_specs=[whole()] * 3 + [anywhere()],
        out_specs=whole(),
        out_shape=shape((2, slots, width), BF),
        compiler_params=params(20),
        cost_estimate=FREE,
        name="collect",
    )(pos, stream, cot, after)


def unpack_kernel(slot_ref, came_ref, after_ref, base_ref, cot_ref):
    tokens, width = base_ref.shape
    slots = came_ref.shape[0]
    take = eq_hot((tokens, slots), 1, slot_ref[...])
    for start, out_ref in ((0, base_ref), (width, cot_ref)):
        out_ref[...] = jnp.dot(
            take, came_ref[:, start : start + width], preferred_element_type=F32
        ).astype(BF)


def unpack(slot_col, came, after):
    tokens = slot_col.shape[0]
    slots, both = came.shape
    width = both // 2
    outs = [shape((tokens, width), BF)] * 2
    return pl.pallas_call(
        unpack_kernel,
        in_specs=[whole()] * 2 + [anywhere()],
        out_specs=[whole()] * 2,
        out_shape=outs,
        compiler_params=params(12),
        cost_estimate=FREE,
        name="unpack",
    )(slot_col, came, after)


def stack_kernel(here_ref, *refs):
    out_ref, sems = refs[RING:]
    first = jnp.where(here_ref[0] == 0, here_ref[4], here_ref[3])
    copies = [
        pltpu.make_async_copy(ref, out_ref.at[lax.rem(first + away, RING)], sems.at[index])
        for index, (away, ref) in enumerate(zip(AWAY, refs[:RING]))
    ]
    for copy in copies:
        copy.start()
    for copy in copies:
        copy.wait()


def stack(here, blocks):
    rows, width = blocks[0].shape
    return pl.pallas_call(
        stack_kernel,
        in_specs=[scalars()] + [in_hbm()] * RING,
        out_specs=whole(),
        out_shape=shape((RING, rows, width), BF),
        scratch_shapes=[pltpu.SemaphoreType.DMA((RING,))],
        compiler_params=params(6),
        cost_estimate=FREE,
        name="stack",
    )(here, *blocks)


def fetch(here_ref, stacks, held_ref, sems):
    for index, (away, ref) in enumerate(zip(AWAY, stacks)):

        @pl.when(here_ref[0] == 0)
        def _():
            place = lax.rem(here_ref[3] + away, RING)
            pltpu.make_async_copy(ref, held_ref.at[place], sems.at[index]).start()

        @pl.when(here_ref[0] == 1)
        def _():
            place = lax.rem(here_ref[4] + away, RING)
            pltpu.make_async_copy(ref, held_ref.at[:, place], sems.at[index]).start()

    def wait():
        for index, ref in enumerate(stacks):
            pltpu.make_async_copy(ref, held_ref.at[0], sems.at[index]).wait()

    return wait


def product(here_ref, away, stacks, lifted, held_ref, left_ref, sems):
    second = jnp.where(here_ref[0] == 0, here_ref[3], here_ref[4])
    block = left_ref.shape[2]
    rows = lifted[0].shape[0]
    copies = []
    for index, ref in enumerate(stacks):
        place = lax.rem(second + away[index], RING)
        at = pl.ds(pl.multiple_of(place * block, block), block)
        group = [pltpu.make_async_copy(ref, held_ref.at[index], sems.at[index, 0])]
        for i, part in enumerate(lifted):
            to = left_ref.at[index, pl.ds(i * rows, rows)]
            group.append(pltpu.make_async_copy(part.at[:, at], to, sems.at[index, 1 + i]))
        for copy in group:
            copy.start()
        copies.append(group)

    def run(total):
        for index, group in enumerate(copies):
            for copy in group:
                copy.wait()
            part = jnp.dot(
                left_ref[index], held_ref[index].reshape(block, -1), preferred_element_type=F32
            )
            total = part if total is None else total + part
        return total

    return run


def product_scratch(stacks, lifted):
    count = len(stacks)
    rows, depth = lifted[0].shape
    return [
        pltpu.VMEM((count,) + stacks[0].shape, BF),
        pltpu.VMEM((count, len(lifted) * rows, depth // RING), BF),
        pltpu.SemaphoreType.DMA((count, 1 + len(lifted))),
    ]


def multiply_kernel(here_ref, *refs):
    stacks, lifted, (out_ref, *scratch) = refs[:EARLY], refs[EARLY : EARLY + 2], refs[EARLY + 2 :]
    out_ref[...] = product(here_ref, AWAY[:EARLY], stacks, lifted, *scratch)(None)


def multiply(here, stacks, lifted):
    tokens, width = 2 * lifted[0].shape[0], stacks[0].shape[2]
    return pl.pallas_call(
        multiply_kernel,
        in_specs=[scalars()] + [in_hbm()] * (len(stacks) + len(lifted)),
        out_specs=whole(),
        out_shape=shape((tokens, width), F32),
        scratch_shapes=product_scratch(stacks, lifted),
        compiler_params=params(60),
        cost_estimate=FREE,
        name="multiply",
    )(here, *stacks, *lifted)


def merge_kernel(here_ref, ngain_ref, acc_hbm, base_hbm, cot_hbm, *refs):
    stacks, lifted, refs = refs[: RING - EARLY], refs[RING - EARLY : RING - EARLY + 2], refs[RING - EARLY + 2 :]
    visual_ref, state_ref, stat_ref, acc_ref, base_ref, cot_ref, row_sems, *scratch = refs
    run = product(here_ref, AWAY[EARLY:], stacks, lifted, *scratch)
    copies = [
        pltpu.make_async_copy(a, b, row_sems.at[i])
        for i, (a, b) in enumerate(((acc_hbm, acc_ref), (base_hbm, base_ref), (cot_hbm, cot_ref)))
    ]
    for copy in copies:
        copy.start()
    total = run(None)
    for copy in copies:
        copy.wait()
    visual = (acc_ref[...] + total).astype(BF)
    visual_ref[...] = visual
    state = base_ref[...].astype(F32) + visual.astype(F32)
    state_ref[...] = state
    up = ngain_ref[...].astype(F32) * cot_ref[...].astype(F32)
    lane = lax.broadcasted_iota(jnp.int32, (state.shape[0], 128), 1)
    sums = jnp.where(
        lane == 0,
        jnp.sum(state * state, axis=1, keepdims=True),
        jnp.sum(up * state, axis=1, keepdims=True),
    )
    stat_ref[...] = sums.T[: stat_ref.shape[0]]


def merge(here, ngain, acc, base, cot, stacks, lifted):
    tokens, width = base.shape
    outs = [shape((tokens, width), BF), shape((tokens, width), F32), shape((8, tokens), F32)]
    return pl.pallas_call(
        merge_kernel,
        in_specs=[scalars(), whole()] + [in_hbm()] * (3 + len(stacks) + len(lifted)),
        out_specs=[whole()] * 3,
        out_shape=outs,
        scratch_shapes=[
            pltpu.VMEM((tokens, width), F32),
            pltpu.VMEM((tokens, width), BF),
            pltpu.VMEM((tokens, width), BF),
            pltpu.SemaphoreType.DMA((3,)),
        ]
        + product_scratch(stacks, lifted),
        compiler_params=params(24),
        cost_estimate=FREE,
        name="merge",
    )(here, ngain, acc, base, cot, *stacks, *lifted)


def add_kernel(sums_ref, got_ref, near_ref, turned_ref):
    count = sums_ref.shape[1] // 4
    cuts = [
        sums_ref[:, i * count : (i + 1) * count] + got_ref[:, (i ^ 1) * count : ((i ^ 1) + 1) * count]
        for i in range(4)
    ]
    near_ref[...] = jnp.concatenate(cuts, axis=1)
    turned_ref[...] = jnp.concatenate(cuts[2:] + cuts[:2], axis=1)


def add(sums, got):
    return pl.pallas_call(
        add_kernel,
        in_specs=[whole()] * 2,
        out_specs=[whole()] * 2,
        out_shape=[shape(sums.shape, F32)] * 2,
        compiler_params=params(4),
        cost_estimate=FREE,
        name="add",
    )(sums, got)


def pack_kernel(here_ref, slot_ref, visual_ref, after_ref, stay_ref, cross_ref):
    tokens = visual_ref.shape[0]
    slots = stay_ref.shape[0]
    for relative, out_ref in ((0, stay_ref), (1, cross_ref)):
        put = eq_hot((tokens, slots), 1, slot_ref[...] - (here_ref[2] ^ relative) * slots)
        out_ref[...] = lax.dot_general(
            put, visual_ref[...], (((0,), (0,)), ((), ())), preferred_element_type=F32
        ).astype(BF)


def pack(here, slot_col, visual, slots, after):
    tokens, width = visual.shape
    return pl.pallas_call(
        pack_kernel,
        in_specs=[scalars()] + [whole()] * 2 + [anywhere()],
        out_specs=[whole()] * 2,
        out_shape=[shape((slots // 2, width), BF)] * 2,
        compiler_params=params(8),
        cost_estimate=FREE,
        name="pack",
    )(here, slot_col, visual, after)


def braid_kernel(stay_ref, crossed_ref, out_ref):
    count, _, rows, _ = out_ref.shape
    for c in range(count):
        at = slice(c * rows, (c + 1) * rows)
        out_ref[c, 0] = stay_ref[at, :]
        out_ref[c, 1] = crossed_ref[at, :]


def braid(stay, crossed, count):
    rows, width = stay.shape
    return pl.pallas_call(
        braid_kernel,
        in_specs=[whole()] * 2,
        out_specs=whole(),
        out_shape=shape((count, 2, rows // count, width), BF),
        compiler_params=params(6),
        cost_estimate=FREE,
        name="braid",
    )(stay, crossed)


def backward_kernel(full_width, here_ref, ngain_ref, *refs):
    stats, stacks, refs = refs[:RING], refs[RING : 2 * RING], refs[2 * RING :]
    state_hbm, cot_hbm, own_ref, other_ref = refs[:4]
    picked_ref, sums_ref, state_ref, cot_ref, held_ref, row_sems, sems = refs[4:]
    row_copies = [
        pltpu.make_async_copy(a, b, row_sems.at[i])
        for i, (a, b) in enumerate(((state_hbm, state_ref), (cot_hbm, cot_ref)))
    ]
    for copy in row_copies:
        copy.start()
    wait_weight = fetch(here_ref, stacks, held_ref, sems)
    tokens = state_ref.shape[0]
    rows = tokens // 2 // RING
    total = stats[0][...]
    for ref in stats[1:]:
        total = total + ref[...]
    sums_ref[...] = total.T
    far, img = here_ref[1], here_ref[2]
    gain = ngain_ref[...].astype(F32)
    for copy in row_copies:
        copy.wait()
    for core in range(2):
        for away in range(RING):
            there = lax.rem(2 * far + img + away, RING)
            partner = lax.rem(there + img, 2)
            begin = partner * (tokens // 2) + core * (tokens // 4) + (there // 2) * (tokens // 8)
            at = pl.ds(pl.multiple_of(begin, rows), rows)
            sums = sums_ref[at, :]
            inv = lax.rsqrt(sums[:, 0:1] / full_width + 1e-06)
            inner = sums[:, 1:2] / full_width
            up = gain * cot_ref[at, :].astype(F32)
            grad = inv * up - state_ref[at, :] * (inv * inv * inv * inner)
            to = (core * RING + away) * rows
            picked_ref[to : to + rows, :] = grad.astype(BF)
    depth = own_ref.shape[1]
    wait_weight()
    block = depth // RING
    for step in range(RING):
        cols = slice(step * block, (step + 1) * block)
        both = lax.dot_general(
            picked_ref[...],
            held_ref[step].reshape(block, -1),
            (((1,), (1,)), ((), ())),
            preferred_element_type=F32,
        )
        own_ref[:, cols] = both[: tokens // 2].astype(BF)
        other_ref[:, cols] = both[tokens // 2 :].astype(BF)


def backward(here, state, cot, ngain, stats, stacks, full_width):
    tokens, width = state.shape
    depth = RING * stacks[0].shape[0] * stacks[0].shape[1]
    return pl.pallas_call(
        lambda *refs: backward_kernel(full_width, *refs),
        in_specs=[scalars()] + [whole()] * (1 + RING) + [in_hbm()] * (RING + 2),
        out_specs=[whole()] * 2,
        out_shape=[shape((tokens // 2, depth), BF)] * 2,
        scratch_shapes=[
            pltpu.VMEM((tokens, width), BF),
            pltpu.VMEM((tokens, 8), F32),
            pltpu.VMEM((tokens, width), F32),
            pltpu.VMEM((tokens, width), BF),
            pltpu.VMEM((RING,) + stacks[0].shape, BF),
            pltpu.SemaphoreType.DMA((2,)),
            pltpu.SemaphoreType.DMA((RING,)),
        ],
        compiler_params=params(24),
        cost_estimate=FREE,
        name="backward",
    )(here, ngain, *stats, *stacks, state, cot)


def pair_kernel(own_ref, got_ref, after_ref, next_ref, last_ref, keep_hbm, keep_ref, sem):
    rows = own_ref.shape[0] // RING
    half = rows // 2

    def total(start):
        at = slice(start, start + half)
        return (own_ref[at, :].astype(F32) + got_ref[at, :].astype(F32)).astype(BF)

    keep_ref[:half] = total(rows)
    keep_ref[half:] = total(3 * rows + half)
    copy = pltpu.make_async_copy(keep_ref, keep_hbm, sem)
    copy.start()
    next_ref[:half] = total(2 * rows)
    next_ref[half:] = total(rows + half)
    last_ref[:half] = total(2 * rows + half)
    last_ref[half:] = total(3 * rows)
    copy.wait()


def pair(own, got, after):
    rows, depth = got.shape[0] // RING, got.shape[1]
    return pl.pallas_call(
        pair_kernel,
        in_specs=[whole()] * 2 + [anywhere()],
        out_specs=[whole()] * 2 + [anywhere()],
        out_shape=[shape((rows, depth), BF)] * 3,
        scratch_shapes=[pltpu.VMEM((rows, depth), BF), pltpu.SemaphoreType.DMA],
        compiler_params=params(8),
        cost_estimate=FREE,
        name="pair",
    )(own, got, after)


def relay_kernel(keep_hbm, from_last_ref, from_next_ref, next_ref, last_ref, keep_ref, sem):
    copy = pltpu.make_async_copy(keep_hbm, keep_ref, sem)
    copy.start()
    copy.wait()
    half = next_ref.shape[0]
    for at, came_ref, out_ref in (
        (slice(0, half), from_last_ref, next_ref),
        (slice(half, 2 * half), from_next_ref, last_ref),
    ):
        out_ref[...] = (keep_ref[at, :].astype(F32) + came_ref[:half].astype(F32)).astype(BF)


def relay(keep, from_last, from_next):
    rows, depth = keep.shape
    return pl.pallas_call(
        relay_kernel,
        in_specs=[in_hbm()] + [whole()] * 2,
        out_specs=[whole()] * 2,
        out_shape=[shape((rows // 2, depth), BF)] * 2,
        scratch_shapes=[pltpu.VMEM((rows, depth), BF), pltpu.SemaphoreType.DMA],
        compiler_params=params(8),
        cost_estimate=FREE,
        name="relay",
    )(keep, from_last, from_next)


def finish_kernel(here_ref, own_ref, got_ref, early_ref, late_ref, xw_ref, stat_ref, gain_ref, out_ref):
    window, tokens, width = xw_ref.shape
    full = window * width
    mean = stat_ref[:, 0:1]
    inv = stat_ref[:, 1:2]
    lifted = own_ref[...].astype(F32) + got_ref[...].astype(F32)
    lifted = lifted + early_ref[...].astype(F32) + late_ref[...].astype(F32)
    share = width // (RING * RING)
    scaled = []
    total = 0.0
    inner = 0.0
    for w in range(window):
        g = jnp.concatenate(
            [lifted[:, at : at + share] for at in range(w * share, full, window * share)], axis=1
        ) * gain_ref[w : w + 1].astype(F32)
        normed = (xw_ref[w].astype(F32) - mean) * inv
        total = total + jnp.sum(g, axis=1, keepdims=True)
        inner = inner + jnp.sum(g * normed, axis=1, keepdims=True)
        scaled.append((g, normed))
    total = total / full
    inner = inner / full
    rows = jnp.concatenate(
        [(inv * (g - total - normed * inner)).astype(BF) for g, normed in scaled], axis=0
    )
    out_ref[...] = jnp.dot(
        patch_major(tokens, window), rows, preferred_element_type=F32
    ).astype(BF)


def finish(here, step, own, got, early, late, xw, stat, gain):
    tokens, depth = late.shape
    window, width = gain.shape
    same = pl.BlockSpec((tokens, depth), lambda i, h: (step, 0))
    second = pl.BlockSpec((tokens, depth), lambda i, h: (1, 0))
    only = pl.BlockSpec((tokens, depth), lambda i, h: (0, 0))
    return pl.pallas_call(
        finish_kernel,
        grid_spec=pltpu.PrefetchScalarGridSpec(
            num_scalar_prefetch=1,
            grid=(1,),
            in_specs=[same, same, second, only]
            + [
                pl.BlockSpec((window, tokens, width), lambda i, h: (0, h[1] * 2 + step, 0)),
                pl.BlockSpec((tokens, 128), lambda i, h: (h[1] * 2 + step, 0)),
                pl.BlockSpec((window, width), lambda i, h: (0, 0)),
            ],
            out_specs=pl.BlockSpec((tokens * window, width), lambda i, h: (0, 0)),
        ),
        out_shape=shape((tokens * window, width), BF),
        compiler_params=params(58),
        cost_estimate=FREE,
        name="finish",
    )(here, own, got, early, late, xw, stat, gain)


def place_kernel(here_ref, pos_ref, came_ref, stream_ref, out_ref):
    rows, width = stream_ref.shape
    cut = width // 2
    slots = pos_ref.shape[0]
    put = eq_hot((slots, rows), 1, pos_ref[...])
    for relative in range(2):
        start = pl.multiple_of((here_ref[2] ^ relative) * cut, cut)
        at = pl.ds(start, cut)
        out_ref[:, at] = (
            stream_ref[:, at].astype(F32)
            + lax.dot_general(
                put,
                came_ref[:, relative].reshape(slots, cut),
                (((0,), (0,)), ((), ())),
                preferred_element_type=F32,
            )
        ).astype(BF)


def place(here, pos, came, stream):
    rows, width = stream.shape
    return pl.pallas_call(
        place_kernel,
        in_specs=[scalars()] + [whole()] * 3,
        out_specs=whole(),
        out_shape=shape((rows, width), BF),
        compiler_params=params(12),
        cost_estimate=FREE,
        name="place",
    )(here, pos, came, stream)


def lay_kernel(here_ref, *refs):
    blocks, (out_ref, sems) = refs[:-2], refs[-2:]
    rows = blocks[0].shape[0]
    copies = []
    for index, ref in enumerate(blocks):
        quarter, step = index // 2, index % 2
        owner = 2 * (here_ref[0] ^ (quarter // 2)) + (here_ref[1] ^ (quarter % 2))
        start = pl.multiple_of((2 * owner + step) * rows, rows)
        copies.append(pltpu.make_async_copy(ref, out_ref.at[pl.ds(start, rows)], sems.at[index]))
    for copy in copies:
        copy.start()
    for copy in copies:
        copy.wait()


def lay(here, blocks):
    rows, width = blocks[0].shape
    return pl.pallas_call(
        lay_kernel,
        in_specs=[scalars()] + [whole()] * len(blocks),
        out_specs=anywhere(),
        out_shape=shape((len(blocks) * rows, width), BF),
        scratch_shapes=[pltpu.SemaphoreType.DMA((len(blocks),))],
        compiler_params=params(4),
        cost_estimate=FREE,
        name="lay",
    )(here, *blocks)


def shards(features, ln_gain, ln_bias, projection, stream, norm_gain, cotangent, slots):
    n_img = lax.axis_size("img")
    n_ctx = lax.axis_size("ctx")
    n_tp = lax.axis_size("tp")
    merged = slots.shape[0]
    tok_rows, width = stream.shape
    owners = n_img * n_ctx
    capacity = 2 * merged // owners
    slot_count = owners * capacity
    full_width = width * n_tp
    cut = width // n_img

    img = lax.axis_index("img").astype(jnp.int32)
    tp = lax.axis_index("tp").astype(jnp.int32)
    core, far_half = tp % 2, tp // 2
    z, y = lax.axis_index("ctx") // RING, lax.axis_index("ctx") % RING
    here = jnp.stack([core, far_half, img, z, y]).astype(jnp.int32)

    flip = [(i, 1 - i) for i in range(n_img)]
    core_pairs = [(t, t ^ 1) for t in range(n_tp)]
    far_pairs = [(t, t ^ 2) for t in range(n_tp)]

    def along_x(array, by):
        pairs = []
        for i in range(n_img):
            for t in range(n_tp):
                x = (2 * (t // 2) + i + by) % RING
                pairs.append((i * n_tp + t, (x % 2) * n_tp + 2 * (x // 2) + t % 2))
        return lax.ppermute(array, ("img", "tp"), pairs)

    def along_ctx(array, axis, by):
        pairs = []
        for c in range(n_ctx):
            for t in range(n_tp):
                z, y = c // RING, c % RING
                if t % 2 == axis:
                    y = (y + by) % RING
                else:
                    z = (z + by) % RING
                pairs.append((c * n_tp + t, (z * RING + y) * n_tp + t))
        return lax.ppermute(array, ("ctx", "tp"), pairs)

    slots = jnp.roll(slots, -core * (merged // 2))
    target = slots // tok_rows
    ids = jnp.arange(merged)
    earlier = (target[:, None] == target[None, :]) & (ids[:, None] < ids[None, :])
    rank = jnp.sum(earlier.astype(jnp.int32), axis=0)
    slot = target * capacity + rank
    local = slots - target * tok_rows
    packed = jnp.max(
        jnp.where(jnp.arange(slot_count)[:, None] == slot[None, :], local[None, :], -1), axis=1
    )
    asked = lax.all_to_all(
        packed.reshape(owners, capacity), ("img", "ctx"), split_axis=0, concat_axis=0, tiled=True
    )
    columns = lax.dynamic_slice_in_dim(projection[0], img * cut, cut, axis=2).reshape(-1, cut)
    moves = (1, -1, 2)
    near_blocks = [along_ctx(columns, 0, by) for by in moves]
    paired = target * (n_img * capacity) + rank + img * capacity
    partner = lax.ppermute(paired, "img", flip)
    gain = ln_gain[0]
    lifted, xw, stat = layer_norm(here, features[0], gain, ln_bias[0])
    asked, lifted, stat, near_blocks, partner = lax.optimization_barrier(
        (asked, lifted, stat, near_blocks, partner)
    )
    paired = jnp.concatenate([paired, partner]).reshape(-1, 1)

    first = stack(here, [columns] + near_blocks)
    asked, first, lifted = lax.optimization_barrier((asked, first, lifted))

    asked = asked.reshape(n_img, n_ctx, capacity).transpose(1, 0, 2)
    asked = asked.reshape(slot_count, 1)
    held = collect(asked, stream, cotangent[0], first)
    came = lax.all_to_all(
        held.reshape(owners, n_img * capacity, width),
        ("img", "ctx"), split_axis=0, concat_axis=0, tiled=True,
    ).reshape(n_img * slot_count, width)

    stacks = [first] + [along_ctx(first, 1, by) for by in moves[:2]]
    stacks.append(along_ctx(stacks[1], 1, 1))

    pairs = []
    for i in range(n_img):
        for t in range(n_tp):
            x = (2 * (t // 2) + i + (1 if t % 2 == 0 else -1)) % RING
            pairs.append((i * n_tp + t, (x % 2) * n_tp + 2 * (x // 2) + t % 2))
    lifted = [lifted, lax.ppermute(lifted, ("img", "tp"), pairs)]

    own_gain = lax.dynamic_slice_in_dim(norm_gain, img * cut, cut, axis=1)
    acc = multiply(here, stacks[:EARLY], lifted)
    base, cot = unpack(paired, came, acc)
    visual, state, sums = merge(here, own_gain, acc, base, cot, stacks[EARLY:], lifted)

    near, turned = add(sums, lax.ppermute(sums, "tp", core_pairs))
    stats = [near] + [along_x(near if by == 2 else turned, by) for by in (1, 2, 3)]
    stay, cross = pack(here, paired, visual, n_img * slot_count, near)
    cross, stats = lax.optimization_barrier((cross, stats))
    crossed = lax.ppermute(cross, "img", flip)

    own, other = backward(here, state, cot, own_gain, stats, stacks, full_width)
    own, other, crossed = lax.optimization_barrier((own, other, crossed))
    got = lax.ppermute(other, "tp", core_pairs)
    to_next, to_last, keep = pair(own, got, crossed)
    from_last, from_next = along_x(to_next, 1), along_x(to_last, -1)
    to_next, to_last = relay(keep, from_last, from_next)
    late_last, late_next = along_x(to_next, 1), along_x(to_last, -1)

    send = braid(stay, crossed, n_ctx)
    arrived = lax.all_to_all(send, "ctx", split_axis=0, concat_axis=0, tiled=True)
    new_stream = place(here, asked, arrived, stream)

    out = [
        finish(here, step, own, got, early, late, xw, stat, gain)
        for step, (early, late) in enumerate(((from_next, late_last), (from_last, late_next)))
    ]
    beyond = [lax.ppermute(x, "tp", far_pairs) for x in out]
    beyond[1], new_stream = lax.optimization_barrier((beyond[1], new_stream))
    from_core = [lax.ppermute(x, "tp", core_pairs) for x in out + beyond]
    grad = lay(here, out + beyond + from_core)
    return (new_stream, grad[None])


def solution(mesh):
    placed = (
        P(None, ("img", "ctx"), None),
        P(),
        P(),
        P(None, None, "ctx", "tp"),
        P(("img", "ctx"), "tp"),
        P(None, "tp"),
        P(None, ("img", "ctx"), "tp"),
        P(("img", "ctx")),
    )
    return jax.shard_map(
        shards,
        mesh=mesh,
        in_specs=placed,
        out_specs=(P(("img", "ctx"), "tp"), P(None, ("img", "ctx"), None)),
        check_vma=False,
    )
```

```python
import jax
import jax.numpy as jnp
from jax import lax
from jax.experimental import pallas as pl
from jax.experimental.pallas import tpu as pltpu
from jax.sharding import PartitionSpec as P


BF = jnp.bfloat16
F32 = jnp.float32
FREE = pl.CostEstimate(flops=0, bytes_accessed=0, transcendentals=0)
RING = 4
AWAY = (0, 3, 1, 2)
EARLY = 2


def params(mib):
    return pltpu.CompilerParams(vmem_limit_bytes=mib * 1024 * 1024)


def whole():
    return pl.BlockSpec(memory_space=pltpu.VMEM)


def shape(dims, kind):
    return jax.ShapeDtypeStruct(dims, kind)


def scalars():
    return pl.BlockSpec(memory_space=pltpu.SMEM)


def in_hbm():
    return pl.BlockSpec(memory_space=pltpu.HBM)


def anywhere():
    return pl.BlockSpec(memory_space=pl.ANY)


def eq_hot(shape, dim, index):
    return (lax.broadcasted_iota(jnp.int32, shape, dim) == index).astype(BF)


def window_major(tokens, window):
    n = tokens * window
    row = lax.broadcasted_iota(jnp.int32, (n, n), 0)
    col = lax.broadcasted_iota(jnp.int32, (n, n), 1)
    return (col == (row % tokens) * window + row // tokens).astype(BF)


def patch_major(tokens, window):
    n = tokens * window
    row = lax.broadcasted_iota(jnp.int32, (n, n), 0)
    col = lax.broadcasted_iota(jnp.int32, (n, n), 1)
    return (col == (row % window) * tokens + row // window).astype(BF)


def norm_kernel(here_ref, x_ref, gain_ref, bias_ref, lifted_ref, xw_ref, stat_ref):
    window, width = gain_ref.shape
    tokens = x_ref.shape[0] // window
    full = window * width
    x = jnp.dot(window_major(tokens, window), x_ref[...], preferred_element_type=F32)
    parts = [x[w * tokens : (w + 1) * tokens] for w in range(window)]
    total = sum(jnp.sum(p, axis=1, keepdims=True) for p in parts)
    squares = sum(jnp.sum(p * p, axis=1, keepdims=True) for p in parts)
    mean = total / full
    inv = lax.rsqrt(squares / full - mean * mean + 1e-05)
    lifted = []
    for w, p in enumerate(parts):
        normed = (p - mean) * inv
        lifted.append(
            normed * gain_ref[w : w + 1].astype(F32) + bias_ref[w : w + 1].astype(F32)
        )
        xw_ref[w] = p.astype(BF)
    share = width // (RING * RING)
    for core in range(2):

        @pl.when(here_ref[0] == core)
        def _():
            blocks = [(a, b) for a in range(RING) for b in range(RING)]
            starts = [(a * RING + b if core == 0 else b * RING + a) * share for a, b in blocks]
            lifted_ref[...] = jnp.concatenate(
                [p[:, at : at + share] for at in starts for p in lifted], axis=1
            ).astype(BF)

    lane = lax.broadcasted_iota(jnp.int32, stat_ref.shape, 1)
    stat_ref[...] = jnp.where(lane == 0, mean, inv)


def layer_norm(here, features, gain, bias):
    rows, width = features.shape
    window = gain.shape[0]
    merged = rows // window
    block = 64
    steps = merged // block
    return pl.pallas_call(
        norm_kernel,
        grid_spec=pltpu.PrefetchScalarGridSpec(
            num_scalar_prefetch=1,
            grid=(steps,),
            in_specs=[
                pl.BlockSpec(
                    (block * window, width),
                    lambda i, c: (lax.rem(i + c[0] * (steps // 2), steps), 0),
                ),
                pl.BlockSpec((window, width), lambda i, c: (0, 0)),
                pl.BlockSpec((window, width), lambda i, c: (0, 0)),
            ],
            out_specs=[
                pl.BlockSpec((block, window * width), lambda i, c: (i, 0)),
                pl.BlockSpec((window, block, width), lambda i, c: (0, i, 0)),
                pl.BlockSpec((block, 128), lambda i, c: (i, 0)),
            ],
        ),
        out_shape=[
            shape((merged, window * width), BF),
            shape((window, merged, width), BF),
            shape((merged, 128), F32),
        ],
        compiler_params=params(58),
        cost_estimate=FREE,
        name="layer_norm",
    )(here, features, gain, bias)


def collect_kernel(pos_ref, stream_hbm, cot_hbm, after_ref, out_hbm, stream_ref, cot_ref, out_ref, sems):
    slots = pos_ref.shape[0]
    rows, width = stream_ref.shape
    cut = width // 2
    fetches = [
        pltpu.make_async_copy(a, b, sems.at[i])
        for i, (a, b) in enumerate(((stream_hbm, stream_ref), (cot_hbm, cot_ref)))
    ]
    for copy in fetches:
        copy.start()
    pick = eq_hot((slots, rows), 1, pos_ref[...])
    for copy in fetches:
        copy.wait()
    stores = []
    for img in range(2):
        at = slice(img * cut, (img + 1) * cut)
        for place, ref in enumerate((stream_ref, cot_ref)):
            out_ref[img, :, place * cut : (place + 1) * cut] = jnp.dot(
                pick, ref[:, at], preferred_element_type=F32
            ).astype(BF)
        stores.append(pltpu.make_async_copy(out_ref.at[img], out_hbm.at[img], sems.at[2 + img]))
        stores[img].start()
    for copy in stores:
        copy.wait()


def collect(pos, stream, cot, after):
    slots = pos.shape[0]
    rows, width = stream.shape
    return pl.pallas_call(
        collect_kernel,
        in_specs=[whole()] + [anywhere()] * 3,
        out_specs=anywhere(),
        out_shape=shape((2, slots, width), BF),
        scratch_shapes=[pltpu.VMEM((rows, width), BF)] * 2
        + [pltpu.VMEM((2, slots, width), BF), pltpu.SemaphoreType.DMA((4,))],
        compiler_params=params(58),
        cost_estimate=FREE,
        name="collect",
    )(pos, stream, cot, after)


def unpack_kernel(slot_ref, came_ref, after_ref, base_ref, cot_ref):
    tokens, width = base_ref.shape
    slots = came_ref.shape[0]
    take = eq_hot((tokens, slots), 1, slot_ref[...])
    for start, out_ref in ((0, base_ref), (width, cot_ref)):
        out_ref[...] = jnp.dot(
            take, came_ref[:, start : start + width], preferred_element_type=F32
        ).astype(BF)


def unpack(slot_col, came, after):
    tokens = slot_col.shape[0]
    slots, both = came.shape
    width = both // 2
    outs = [shape((tokens, width), BF)] * 2
    return pl.pallas_call(
        unpack_kernel,
        in_specs=[whole()] * 2 + [anywhere()],
        out_specs=[whole()] * 2,
        out_shape=outs,
        compiler_params=params(12),
        cost_estimate=FREE,
        name="unpack",
    )(slot_col, came, after)


def stack_kernel(here_ref, *refs):
    out_ref, sems = refs[RING:]
    first = jnp.where(here_ref[0] == 0, here_ref[4], here_ref[3])
    copies = [
        pltpu.make_async_copy(ref, out_ref.at[lax.rem(first + away, RING)], sems.at[index])
        for index, (away, ref) in enumerate(zip(AWAY, refs[:RING]))
    ]
    for copy in copies:
        copy.start()
    for copy in copies:
        copy.wait()


def stack(here, blocks):
    rows, width = blocks[0].shape
    return pl.pallas_call(
        stack_kernel,
        in_specs=[scalars()] + [in_hbm()] * RING,
        out_specs=whole(),
        out_shape=shape((RING, rows, width), BF),
        scratch_shapes=[pltpu.SemaphoreType.DMA((RING,))],
        compiler_params=params(6),
        cost_estimate=FREE,
        name="stack",
    )(here, *blocks)


def fetch(here_ref, stacks, held_ref, sems):
    for index, (away, ref) in enumerate(zip(AWAY, stacks)):

        @pl.when(here_ref[0] == 0)
        def _():
            place = lax.rem(here_ref[3] + away, RING)
            pltpu.make_async_copy(ref, held_ref.at[place], sems.at[index]).start()

        @pl.when(here_ref[0] == 1)
        def _():
            place = lax.rem(here_ref[4] + away, RING)
            pltpu.make_async_copy(ref, held_ref.at[:, place], sems.at[index]).start()

    def wait():
        for index, ref in enumerate(stacks):
            pltpu.make_async_copy(ref, held_ref.at[0], sems.at[index]).wait()

    return wait


def product(here_ref, away, stacks, lifted, held_ref, left_ref, sems):
    second = jnp.where(here_ref[0] == 0, here_ref[3], here_ref[4])
    block = left_ref.shape[2]
    rows = lifted[0].shape[0]
    copies = []
    for index, ref in enumerate(stacks):
        place = lax.rem(second + away[index], RING)
        at = pl.ds(pl.multiple_of(place * block, block), block)
        group = [pltpu.make_async_copy(ref, held_ref.at[index], sems.at[index, 0])]
        for i, part in enumerate(lifted):
            to = left_ref.at[index, pl.ds(i * rows, rows)]
            group.append(pltpu.make_async_copy(part.at[:, at], to, sems.at[index, 1 + i]))
        for copy in group:
            copy.start()
        copies.append(group)

    def run(total):
        for index, group in enumerate(copies):
            for copy in group:
                copy.wait()
            part = jnp.dot(
                left_ref[index], held_ref[index].reshape(block, -1), preferred_element_type=F32
            )
            total = part if total is None else total + part
        return total

    return run


def product_scratch(stacks, lifted):
    count = len(stacks)
    rows, depth = lifted[0].shape
    return [
        pltpu.VMEM((count,) + stacks[0].shape, BF),
        pltpu.VMEM((count, len(lifted) * rows, depth // RING), BF),
        pltpu.SemaphoreType.DMA((count, 1 + len(lifted))),
    ]


def multiply_kernel(here_ref, *refs):
    stacks, lifted, refs = refs[:EARLY], refs[EARLY : EARLY + 2], refs[EARLY + 2 :]
    out_ref, done_ref, *scratch = refs
    done_ref[...] = jnp.zeros_like(done_ref)
    out_ref[...] = product(here_ref, AWAY[:EARLY], stacks, lifted, *scratch)(None)


def multiply(here, stacks, lifted):
    tokens, width = 2 * lifted[0].shape[0], stacks[0].shape[2]
    return pl.pallas_call(
        multiply_kernel,
        in_specs=[scalars()] + [in_hbm()] * (len(stacks) + len(lifted)),
        out_specs=[whole()] * 2,
        out_shape=[shape((tokens, width), F32), shape((8, 128), F32)],
        scratch_shapes=product_scratch(stacks, lifted),
        compiler_params=params(60),
        cost_estimate=FREE,
        name="multiply",
    )(here, *stacks, *lifted)


def merge_kernel(here_ref, ngain_ref, acc_hbm, base_hbm, cot_hbm, *refs):
    stacks, lifted, refs = refs[: RING - EARLY], refs[RING - EARLY : RING - EARLY + 2], refs[RING - EARLY + 2 :]
    visual_ref, state_ref, stat_ref, acc_ref, base_ref, cot_ref, row_sems, *scratch = refs
    run = product(here_ref, AWAY[EARLY:], stacks, lifted, *scratch)
    copies = [
        pltpu.make_async_copy(a, b, row_sems.at[i])
        for i, (a, b) in enumerate(((acc_hbm, acc_ref), (base_hbm, base_ref), (cot_hbm, cot_ref)))
    ]
    for copy in copies:
        copy.start()
    total = run(None)
    for copy in copies:
        copy.wait()
    visual = (acc_ref[...] + total).astype(BF)
    visual_ref[...] = visual
    state = base_ref[...].astype(F32) + visual.astype(F32)
    state_ref[...] = state
    up = ngain_ref[...].astype(F32) * cot_ref[...].astype(F32)
    lane = lax.broadcasted_iota(jnp.int32, (state.shape[0], 128), 1)
    sums = jnp.where(
        lane == 0,
        jnp.sum(state * state, axis=1, keepdims=True),
        jnp.sum(up * state, axis=1, keepdims=True),
    )
    stat_ref[...] = sums.T[: stat_ref.shape[0]]


def merge(here, ngain, acc, base, cot, stacks, lifted):
    tokens, width = base.shape
    outs = [shape((tokens, width), BF), shape((tokens, width), F32), shape((8, tokens), F32)]
    return pl.pallas_call(
        merge_kernel,
        in_specs=[scalars(), whole()] + [in_hbm()] * (3 + len(stacks) + len(lifted)),
        out_specs=[whole()] * 3,
        out_shape=outs,
        scratch_shapes=[
            pltpu.VMEM((tokens, width), F32),
            pltpu.VMEM((tokens, width), BF),
            pltpu.VMEM((tokens, width), BF),
            pltpu.SemaphoreType.DMA((3,)),
        ]
        + product_scratch(stacks, lifted),
        compiler_params=params(24),
        cost_estimate=FREE,
        name="merge",
    )(here, ngain, acc, base, cot, *stacks, *lifted)


def add_kernel(sums_ref, got_ref, near_ref, turned_ref):
    count = sums_ref.shape[1] // 4
    cuts = [
        sums_ref[:, i * count : (i + 1) * count] + got_ref[:, (i ^ 1) * count : ((i ^ 1) + 1) * count]
        for i in range(4)
    ]
    near_ref[...] = jnp.concatenate(cuts, axis=1)
    turned_ref[...] = jnp.concatenate(cuts[2:] + cuts[:2], axis=1)


def add(sums, got):
    return pl.pallas_call(
        add_kernel,
        in_specs=[whole()] * 2,
        out_specs=[whole()] * 2,
        out_shape=[shape(sums.shape, F32)] * 2,
        compiler_params=params(4),
        cost_estimate=FREE,
        name="add",
    )(sums, got)


def pack_kernel(here_ref, slot_ref, visual_ref, after_ref, stay_ref, cross_ref):
    tokens = visual_ref.shape[0]
    slots = stay_ref.shape[0]
    for relative, out_ref in ((0, stay_ref), (1, cross_ref)):
        put = eq_hot((tokens, slots), 1, slot_ref[...] - (here_ref[2] ^ relative) * slots)
        out_ref[...] = lax.dot_general(
            put, visual_ref[...], (((0,), (0,)), ((), ())), preferred_element_type=F32
        ).astype(BF)


def pack(here, slot_col, visual, slots, after):
    tokens, width = visual.shape
    return pl.pallas_call(
        pack_kernel,
        in_specs=[scalars()] + [whole()] * 2 + [anywhere()],
        out_specs=[whole()] * 2,
        out_shape=[shape((slots // 2, width), BF)] * 2,
        compiler_params=params(8),
        cost_estimate=FREE,
        name="pack",
    )(here, slot_col, visual, after)


def braid_kernel(stay_ref, crossed_ref, out_ref):
    count, _, rows, _ = out_ref.shape
    for c in range(count):
        at = slice(c * rows, (c + 1) * rows)
        out_ref[c, 0] = stay_ref[at, :]
        out_ref[c, 1] = crossed_ref[at, :]


def braid(stay, crossed, count):
    rows, width = stay.shape
    return pl.pallas_call(
        braid_kernel,
        in_specs=[whole()] * 2,
        out_specs=whole(),
        out_shape=shape((count, 2, rows // count, width), BF),
        compiler_params=params(6),
        cost_estimate=FREE,
        name="braid",
    )(stay, crossed)


def backward_kernel(full_width, here_ref, ngain_ref, *refs):
    stats, stacks, refs = refs[:RING], refs[RING : 2 * RING], refs[2 * RING :]
    state_hbm, cot_hbm, own_ref, other_ref = refs[:4]
    picked_ref, sums_ref, state_ref, cot_ref, held_ref, row_sems, sems = refs[4:]
    row_copies = [
        pltpu.make_async_copy(a, b, row_sems.at[i])
        for i, (a, b) in enumerate(((state_hbm, state_ref), (cot_hbm, cot_ref)))
    ]
    for copy in row_copies:
        copy.start()
    wait_weight = fetch(here_ref, stacks, held_ref, sems)
    tokens = state_ref.shape[0]
    rows = tokens // 2 // RING
    total = stats[0][...]
    for ref in stats[1:]:
        total = total + ref[...]
    sums_ref[...] = total.T
    far, img = here_ref[1], here_ref[2]
    gain = ngain_ref[...].astype(F32)
    for copy in row_copies:
        copy.wait()
    for core in range(2):
        for away in range(RING):
            there = lax.rem(2 * far + img + away, RING)
            partner = lax.rem(there + img, 2)
            begin = partner * (tokens // 2) + core * (tokens // 4) + (there // 2) * (tokens // 8)
            at = pl.ds(pl.multiple_of(begin, rows), rows)
            sums = sums_ref[at, :]
            inv = lax.rsqrt(sums[:, 0:1] / full_width + 1e-06)
            inner = sums[:, 1:2] / full_width
            up = gain * cot_ref[at, :].astype(F32)
            grad = inv * up - state_ref[at, :] * (inv * inv * inv * inner)
            to = (core * RING + away) * rows
            picked_ref[to : to + rows, :] = grad.astype(BF)
    depth = own_ref.shape[1]
    wait_weight()
    block = depth // RING
    for step in range(RING):
        cols = slice(step * block, (step + 1) * block)
        both = lax.dot_general(
            picked_ref[...],
            held_ref[step].reshape(block, -1),
            (((1,), (1,)), ((), ())),
            preferred_element_type=F32,
        )
        own_ref[:, cols] = both[: tokens // 2].astype(BF)
        other_ref[:, cols] = both[tokens // 2 :].astype(BF)


def backward(here, state, cot, ngain, stats, stacks, full_width):
    tokens, width = state.shape
    depth = RING * stacks[0].shape[0] * stacks[0].shape[1]
    return pl.pallas_call(
        lambda *refs: backward_kernel(full_width, *refs),
        in_specs=[scalars()] + [whole()] * (1 + RING) + [in_hbm()] * (RING + 2),
        out_specs=[whole()] * 2,
        out_shape=[shape((tokens // 2, depth), BF)] * 2,
        scratch_shapes=[
            pltpu.VMEM((tokens, width), BF),
            pltpu.VMEM((tokens, 8), F32),
            pltpu.VMEM((tokens, width), F32),
            pltpu.VMEM((tokens, width), BF),
            pltpu.VMEM((RING,) + stacks[0].shape, BF),
            pltpu.SemaphoreType.DMA((2,)),
            pltpu.SemaphoreType.DMA((RING,)),
        ],
        compiler_params=params(24),
        cost_estimate=FREE,
        name="backward",
    )(here, ngain, *stats, *stacks, state, cot)


def pair_kernel(own_ref, got_ref, after_ref, next_ref, last_ref):
    rows = own_ref.shape[0] // RING
    half = rows // 2

    def total(start):
        at = slice(start, start + half)
        return (own_ref[at, :].astype(F32) + got_ref[at, :].astype(F32)).astype(BF)

    next_ref[:half] = total(2 * rows)
    next_ref[half:] = total(rows + half)
    last_ref[:half] = total(2 * rows + half)
    last_ref[half:] = total(3 * rows)


def pair(own, got, after):
    rows, depth = got.shape[0] // RING, got.shape[1]
    return pl.pallas_call(
        pair_kernel,
        in_specs=[whole()] * 2 + [anywhere()],
        out_specs=[whole()] * 2,
        out_shape=[shape((rows, depth), BF)] * 2,
        compiler_params=params(8),
        cost_estimate=FREE,
        name="pair",
    )(own, got, after)


def relay_kernel(own_hbm, got_hbm, from_last_ref, from_next_ref, next_ref, last_ref, kept_ref, sems):
    half = next_ref.shape[0]
    rows = 2 * half
    copies = []
    for place, start in enumerate((rows, 3 * rows + half)):
        for core, ref in enumerate((own_hbm, got_hbm)):
            copies.append(
                pltpu.make_async_copy(
                    ref.at[pl.ds(start, half)], kept_ref.at[place, core], sems.at[place, core]
                )
            )
            copies[-1].start()
    for copy in copies:
        copy.wait()
    for place, (came_ref, out_ref) in enumerate(((from_last_ref, next_ref), (from_next_ref, last_ref))):
        kept = (kept_ref[place, 0].astype(F32) + kept_ref[place, 1].astype(F32)).astype(BF)
        out_ref[...] = (kept.astype(F32) + came_ref[:half].astype(F32)).astype(BF)


def relay(own, got, from_last, from_next):
    rows, depth = from_last.shape
    half = rows // 2
    return pl.pallas_call(
        relay_kernel,
        in_specs=[anywhere()] * 2 + [whole()] * 2,
        out_specs=[whole()] * 2,
        out_shape=[shape((half, depth), BF)] * 2,
        scratch_shapes=[pltpu.VMEM((2, 2, half, depth), BF), pltpu.SemaphoreType.DMA((2, 2))],
        compiler_params=params(60),
        cost_estimate=FREE,
        name="relay",
    )(own, got, from_last, from_next)


def finish_kernel(here_ref, own_ref, got_ref, early_ref, late_ref, xw_ref, stat_ref, gain_ref, out_ref):
    window, tokens, width = xw_ref.shape
    full = window * width
    mean = stat_ref[:, 0:1]
    inv = stat_ref[:, 1:2]
    lifted = own_ref[...].astype(F32) + got_ref[...].astype(F32)
    lifted = lifted + early_ref[...].astype(F32) + late_ref[...].astype(F32)
    share = width // (RING * RING)
    scaled = []
    total = 0.0
    inner = 0.0
    for w in range(window):
        g = jnp.concatenate(
            [lifted[:, at : at + share] for at in range(w * share, full, window * share)], axis=1
        ) * gain_ref[w : w + 1].astype(F32)
        normed = (xw_ref[w].astype(F32) - mean) * inv
        total = total + jnp.sum(g, axis=1, keepdims=True)
        inner = inner + jnp.sum(g * normed, axis=1, keepdims=True)
        scaled.append((g, normed))
    total = total / full
    inner = inner / full
    rows = jnp.concatenate(
        [(inv * (g - total - normed * inner)).astype(BF) for g, normed in scaled], axis=0
    )
    out_ref[...] = jnp.dot(
        patch_major(tokens, window), rows, preferred_element_type=F32
    ).astype(BF)


def finish(here, step, own, got, early, late, xw, stat, gain):
    tokens, depth = late.shape
    window, width = gain.shape
    same = pl.BlockSpec((tokens, depth), lambda i, h: (step, 0))
    second = pl.BlockSpec((tokens, depth), lambda i, h: (1, 0))
    only = pl.BlockSpec((tokens, depth), lambda i, h: (0, 0))
    return pl.pallas_call(
        finish_kernel,
        grid_spec=pltpu.PrefetchScalarGridSpec(
            num_scalar_prefetch=1,
            grid=(1,),
            in_specs=[same, same, second, only]
            + [
                pl.BlockSpec((window, tokens, width), lambda i, h: (0, h[1] * 2 + step, 0)),
                pl.BlockSpec((tokens, 128), lambda i, h: (h[1] * 2 + step, 0)),
                pl.BlockSpec((window, width), lambda i, h: (0, 0)),
            ],
            out_specs=pl.BlockSpec((tokens * window, width), lambda i, h: (0, 0)),
        ),
        out_shape=shape((tokens * window, width), BF),
        compiler_params=params(58),
        cost_estimate=FREE,
        name="finish",
    )(here, own, got, early, late, xw, stat, gain)


def place_kernel(here_ref, pos_ref, came_ref, stream_ref, out_ref):
    rows, width = stream_ref.shape
    cut = width // 2
    slots = pos_ref.shape[0]
    put = eq_hot((slots, rows), 1, pos_ref[...])
    for relative in range(2):
        start = pl.multiple_of((here_ref[2] ^ relative) * cut, cut)
        at = pl.ds(start, cut)
        out_ref[:, at] = (
            stream_ref[:, at].astype(F32)
            + lax.dot_general(
                put,
                came_ref[:, relative].reshape(slots, cut),
                (((0,), (0,)), ((), ())),
                preferred_element_type=F32,
            )
        ).astype(BF)


def place(here, pos, came, stream):
    rows, width = stream.shape
    return pl.pallas_call(
        place_kernel,
        in_specs=[scalars()] + [whole()] * 3,
        out_specs=whole(),
        out_shape=shape((rows, width), BF),
        compiler_params=params(12),
        cost_estimate=FREE,
        name="place",
    )(here, pos, came, stream)


def lay_kernel(here_ref, *refs):
    blocks, (out_ref, sems) = refs[:-2], refs[-2:]
    rows = blocks[0].shape[0]
    copies = []
    for index, ref in enumerate(blocks):
        quarter, step = index // 2, index % 2
        owner = 2 * (here_ref[0] ^ (quarter // 2)) + (here_ref[1] ^ (quarter % 2))
        start = pl.multiple_of((2 * owner + step) * rows, rows)
        copies.append(pltpu.make_async_copy(ref, out_ref.at[pl.ds(start, rows)], sems.at[index]))
    for copy in copies:
        copy.start()
    for copy in copies:
        copy.wait()


def lay(here, blocks):
    rows, width = blocks[0].shape
    return pl.pallas_call(
        lay_kernel,
        in_specs=[scalars()] + [whole()] * len(blocks),
        out_specs=anywhere(),
        out_shape=shape((len(blocks) * rows, width), BF),
        scratch_shapes=[pltpu.SemaphoreType.DMA((len(blocks),))],
        compiler_params=params(4),
        cost_estimate=FREE,
        name="lay",
    )(here, *blocks)


def shards(features, ln_gain, ln_bias, projection, stream, norm_gain, cotangent, slots):
    n_img = lax.axis_size("img")
    n_ctx = lax.axis_size("ctx")
    n_tp = lax.axis_size("tp")
    merged = slots.shape[0]
    tok_rows, width = stream.shape
    owners = n_img * n_ctx
    capacity = 2 * merged // owners
    slot_count = owners * capacity
    full_width = width * n_tp
    cut = width // n_img

    img = lax.axis_index("img").astype(jnp.int32)
    tp = lax.axis_index("tp").astype(jnp.int32)
    core, far_half = tp % 2, tp // 2
    z, y = lax.axis_index("ctx") // RING, lax.axis_index("ctx") % RING
    here = jnp.stack([core, far_half, img, z, y]).astype(jnp.int32)

    flip = [(i, 1 - i) for i in range(n_img)]
    core_pairs = [(t, t ^ 1) for t in range(n_tp)]
    far_pairs = [(t, t ^ 2) for t in range(n_tp)]

    def along_x(array, by):
        pairs = []
        for i in range(n_img):
            for t in range(n_tp):
                x = (2 * (t // 2) + i + by) % RING
                pairs.append((i * n_tp + t, (x % 2) * n_tp + 2 * (x // 2) + t % 2))
        return lax.ppermute(array, ("img", "tp"), pairs)

    def along_ctx(array, axis, by):
        pairs = []
        for c in range(n_ctx):
            for t in range(n_tp):
                z, y = c // RING, c % RING
                if t % 2 == axis:
                    y = (y + by) % RING
                else:
                    z = (z + by) % RING
                pairs.append((c * n_tp + t, (z * RING + y) * n_tp + t))
        return lax.ppermute(array, ("ctx", "tp"), pairs)

    slots = jnp.roll(slots, -core * (merged // 2))
    target = slots // tok_rows
    ids = jnp.arange(merged)
    earlier = (target[:, None] == target[None, :]) & (ids[:, None] < ids[None, :])
    rank = jnp.sum(earlier.astype(jnp.int32), axis=0)
    slot = target * capacity + rank
    local = slots - target * tok_rows
    packed = jnp.max(
        jnp.where(jnp.arange(slot_count)[:, None] == slot[None, :], local[None, :], -1), axis=1
    )
    asked = lax.all_to_all(
        packed.reshape(owners, capacity), ("img", "ctx"), split_axis=0, concat_axis=0, tiled=True
    )
    columns = lax.dynamic_slice_in_dim(projection[0], img * cut, cut, axis=2).reshape(-1, cut)
    moves = (1, -1, 2)
    near_blocks = [along_ctx(columns, 0, by) for by in moves]
    paired = target * (n_img * capacity) + rank + img * capacity
    partner = lax.ppermute(paired, "img", flip)
    gain = ln_gain[0]
    lifted, xw, stat = layer_norm(here, features[0], gain, ln_bias[0])
    asked, lifted, stat, near_blocks, partner = lax.optimization_barrier(
        (asked, lifted, stat, near_blocks, partner)
    )
    paired = jnp.concatenate([paired, partner]).reshape(-1, 1)

    first = stack(here, [columns] + near_blocks)
    asked, first, lifted = lax.optimization_barrier((asked, first, lifted))

    asked = asked.reshape(n_img, n_ctx, capacity).transpose(1, 0, 2)
    asked = asked.reshape(slot_count, 1)
    held = collect(asked, stream, cotangent[0], first)
    came = lax.all_to_all(
        held.reshape(owners, n_img * capacity, width),
        ("img", "ctx"), split_axis=0, concat_axis=0, tiled=True,
    ).reshape(n_img * slot_count, width)

    stacks = [first] + [along_ctx(first, 1, by) for by in moves[:2]]
    stacks.append(along_ctx(stacks[1], 1, 1))

    pairs = []
    for i in range(n_img):
        for t in range(n_tp):
            x = (2 * (t // 2) + i + (1 if t % 2 == 0 else -1)) % RING
            pairs.append((i * n_tp + t, (x % 2) * n_tp + 2 * (x // 2) + t % 2))
    lifted = [lifted, lax.ppermute(lifted, ("img", "tp"), pairs)]

    own_gain = lax.dynamic_slice_in_dim(norm_gain, img * cut, cut, axis=1)
    acc, done = multiply(here, stacks[:EARLY], lifted)
    base, cot = unpack(paired, came, done)
    visual, state, sums = merge(here, own_gain, acc, base, cot, stacks[EARLY:], lifted)

    near, turned = add(sums, lax.ppermute(sums, "tp", core_pairs))
    stats = [near] + [along_x(near if by == 2 else turned, by) for by in (1, 2, 3)]
    stay, cross = pack(here, paired, visual, n_img * slot_count, near)
    cross, stats = lax.optimization_barrier((cross, stats))
    crossed = lax.ppermute(cross, "img", flip)

    own, other = backward(here, state, cot, own_gain, stats, stacks, full_width)
    own, other, crossed = lax.optimization_barrier((own, other, crossed))
    got = lax.ppermute(other, "tp", core_pairs)
    to_next, to_last = pair(own, got, crossed)
    from_last, from_next = along_x(to_next, 1), along_x(to_last, -1)
    to_next, to_last = relay(own, got, from_last, from_next)
    late_last, late_next = along_x(to_next, 1), along_x(to_last, -1)

    send = braid(stay, crossed, n_ctx)
    arrived = lax.all_to_all(send, "ctx", split_axis=0, concat_axis=0, tiled=True)
    new_stream = place(here, asked, arrived, stream)

    out = [
        finish(here, step, own, got, early, late, xw, stat, gain)
        for step, (early, late) in enumerate(((from_next, late_last), (from_last, late_next)))
    ]
    beyond = [lax.ppermute(x, "tp", far_pairs) for x in out]
    beyond[1], new_stream = lax.optimization_barrier((beyond[1], new_stream))
    from_core = [lax.ppermute(x, "tp", core_pairs) for x in out + beyond]
    grad = lay(here, out + beyond + from_core)
    return (new_stream, grad[None])


def solution(mesh):
    placed = (
        P(None, ("img", "ctx"), None),
        P(),
        P(),
        P(None, None, "ctx", "tp"),
        P(("img", "ctx"), "tp"),
        P(None, "tp"),
        P(None, ("img", "ctx"), "tp"),
        P(("img", "ctx")),
    )
    return jax.shard_map(
        shards,
        mesh=mesh,
        in_specs=placed,
        out_specs=(P(("img", "ctx"), "tp"), P(None, ("img", "ctx"), None)),
        check_vma=False,
    )
```

```python
import jax
import jax.numpy as jnp
from jax import lax
from jax.experimental import pallas as pl
from jax.experimental.pallas import tpu as pltpu
from jax.sharding import PartitionSpec as P


BF = jnp.bfloat16
F32 = jnp.float32
FREE = pl.CostEstimate(flops=0, bytes_accessed=0, transcendentals=0)
RING = 4
AWAY = (0, 3, 1, 2)
EARLY = 2


def params(mib):
    return pltpu.CompilerParams(vmem_limit_bytes=mib * 1024 * 1024)


def whole():
    return pl.BlockSpec(memory_space=pltpu.VMEM)


def shape(dims, kind):
    return jax.ShapeDtypeStruct(dims, kind)


def scalars():
    return pl.BlockSpec(memory_space=pltpu.SMEM)


def in_hbm():
    return pl.BlockSpec(memory_space=pltpu.HBM)


def anywhere():
    return pl.BlockSpec(memory_space=pl.ANY)


def eq_hot(shape, dim, index):
    return (lax.broadcasted_iota(jnp.int32, shape, dim) == index).astype(BF)


def window_major(tokens, window):
    n = tokens * window
    row = lax.broadcasted_iota(jnp.int32, (n, n), 0)
    col = lax.broadcasted_iota(jnp.int32, (n, n), 1)
    return (col == (row % tokens) * window + row // tokens).astype(BF)


def patch_major(tokens, window):
    n = tokens * window
    row = lax.broadcasted_iota(jnp.int32, (n, n), 0)
    col = lax.broadcasted_iota(jnp.int32, (n, n), 1)
    return (col == (row % window) * tokens + row // window).astype(BF)


def norm_kernel(here_ref, x_ref, gain_ref, bias_ref, lifted_ref, xw_ref, stat_ref):
    window, width = gain_ref.shape
    tokens = x_ref.shape[0] // window
    full = window * width
    x = jnp.dot(window_major(tokens, window), x_ref[...], preferred_element_type=F32)
    parts = [x[w * tokens : (w + 1) * tokens] for w in range(window)]
    total = sum(jnp.sum(p, axis=1, keepdims=True) for p in parts)
    squares = sum(jnp.sum(p * p, axis=1, keepdims=True) for p in parts)
    mean = total / full
    inv = lax.rsqrt(squares / full - mean * mean + 1e-05)
    lifted = []
    for w, p in enumerate(parts):
        normed = (p - mean) * inv
        lifted.append(
            normed * gain_ref[w : w + 1].astype(F32) + bias_ref[w : w + 1].astype(F32)
        )
        xw_ref[w] = p.astype(BF)
    share = width // (RING * RING)
    for core in range(2):

        @pl.when(here_ref[0] == core)
        def _():
            blocks = [(a, b) for a in range(RING) for b in range(RING)]
            starts = [(a * RING + b if core == 0 else b * RING + a) * share for a, b in blocks]
            lifted_ref[...] = jnp.concatenate(
                [p[:, at : at + share] for at in starts for p in lifted], axis=1
            ).astype(BF)

    lane = lax.broadcasted_iota(jnp.int32, stat_ref.shape, 1)
    stat_ref[...] = jnp.where(lane == 0, mean, inv)


def layer_norm(here, features, gain, bias):
    rows, width = features.shape
    window = gain.shape[0]
    merged = rows // window
    block = 64
    steps = merged // block
    return pl.pallas_call(
        norm_kernel,
        grid_spec=pltpu.PrefetchScalarGridSpec(
            num_scalar_prefetch=1,
            grid=(steps,),
            in_specs=[
                pl.BlockSpec(
                    (block * window, width),
                    lambda i, c: (lax.rem(i + c[0] * (steps // 2), steps), 0),
                ),
                pl.BlockSpec((window, width), lambda i, c: (0, 0)),
                pl.BlockSpec((window, width), lambda i, c: (0, 0)),
            ],
            out_specs=[
                pl.BlockSpec((block, window * width), lambda i, c: (i, 0)),
                pl.BlockSpec((window, block, width), lambda i, c: (0, i, 0)),
                pl.BlockSpec((block, 128), lambda i, c: (i, 0)),
            ],
        ),
        out_shape=[
            shape((merged, window * width), BF),
            shape((window, merged, width), BF),
            shape((merged, 128), F32),
        ],
        compiler_params=params(58),
        cost_estimate=FREE,
        name="layer_norm",
    )(here, features, gain, bias)


def collect_kernel(pos_ref, stream_ref, cot_ref, after_ref, out_ref):
    slots = pos_ref.shape[0]
    rows, width = stream_ref.shape
    cut = width // 2
    pick = eq_hot((slots, rows), 1, pos_ref[...])
    for img in range(2):
        at = slice(img * cut, (img + 1) * cut)
        for place, ref in enumerate((stream_ref, cot_ref)):
            out_ref[img, :, place * cut : (place + 1) * cut] = jnp.dot(
                pick, ref[:, at], preferred_element_type=F32
            ).astype(BF)


def collect(pos, stream, cot, after):
    slots = pos.shape[0]
    rows, width = stream.shape
    return pl.pallas_call(
        collect_kernel,
        in_specs=[whole()] * 3 + [anywhere()],
        out_specs=whole(),
        out_shape=shape((2, slots, width), BF),
        compiler_params=params(20),
        cost_estimate=FREE,
        name="collect",
    )(pos, stream, cot, after)


def unpack_kernel(slot_ref, came_ref, after_ref, base_ref, cot_ref):
    tokens, width = base_ref.shape
    slots = came_ref.shape[0]
    take = eq_hot((tokens, slots), 1, slot_ref[...])
    for start, out_ref in ((0, base_ref), (width, cot_ref)):
        out_ref[...] = jnp.dot(
            take, came_ref[:, start : start + width], preferred_element_type=F32
        ).astype(BF)


def unpack(slot_col, came, after):
    tokens = slot_col.shape[0]
    slots, both = came.shape
    width = both // 2
    outs = [shape((tokens, width), BF)] * 2
    return pl.pallas_call(
        unpack_kernel,
        in_specs=[whole()] * 2 + [anywhere()],
        out_specs=[whole()] * 2,
        out_shape=outs,
        compiler_params=params(12),
        cost_estimate=FREE,
        name="unpack",
    )(slot_col, came, after)


def stack_kernel(here_ref, *refs):
    out_ref, sems = refs[RING:]
    first = jnp.where(here_ref[0] == 0, here_ref[4], here_ref[3])
    copies = [
        pltpu.make_async_copy(ref, out_ref.at[lax.rem(first + away, RING)], sems.at[index])
        for index, (away, ref) in enumerate(zip(AWAY, refs[:RING]))
    ]
    for copy in copies:
        copy.start()
    for copy in copies:
        copy.wait()


def stack(here, blocks):
    rows, width = blocks[0].shape
    return pl.pallas_call(
        stack_kernel,
        in_specs=[scalars()] + [in_hbm()] * RING,
        out_specs=whole(),
        out_shape=shape((RING, rows, width), BF),
        scratch_shapes=[pltpu.SemaphoreType.DMA((RING,))],
        compiler_params=params(6),
        cost_estimate=FREE,
        name="stack",
    )(here, *blocks)


def fetch(here_ref, stacks, held_ref, sems):
    for index, (away, ref) in enumerate(zip(AWAY, stacks)):

        @pl.when(here_ref[0] == 0)
        def _():
            place = lax.rem(here_ref[3] + away, RING)
            pltpu.make_async_copy(ref, held_ref.at[place], sems.at[index]).start()

        @pl.when(here_ref[0] == 1)
        def _():
            place = lax.rem(here_ref[4] + away, RING)
            pltpu.make_async_copy(ref, held_ref.at[:, place], sems.at[index]).start()

    def wait():
        for index, ref in enumerate(stacks):
            pltpu.make_async_copy(ref, held_ref.at[0], sems.at[index]).wait()

    return wait


def product(here_ref, away, stacks, lifted, held_ref, left_ref, sems):
    second = jnp.where(here_ref[0] == 0, here_ref[3], here_ref[4])
    block = left_ref.shape[2]
    rows = lifted[0].shape[0]
    copies = []
    for index, ref in enumerate(stacks):
        place = lax.rem(second + away[index], RING)
        at = pl.ds(pl.multiple_of(place * block, block), block)
        group = [pltpu.make_async_copy(ref, held_ref.at[index], sems.at[index, 0])]
        for i, part in enumerate(lifted):
            to = left_ref.at[index, pl.ds(i * rows, rows)]
            group.append(pltpu.make_async_copy(part.at[:, at], to, sems.at[index, 1 + i]))
        for copy in group:
            copy.start()
        copies.append(group)

    def run(total):
        for index, group in enumerate(copies):
            for copy in group:
                copy.wait()
            part = jnp.dot(
                left_ref[index], held_ref[index].reshape(block, -1), preferred_element_type=F32
            )
            total = part if total is None else total + part
        return total

    return run


def product_scratch(stacks, lifted):
    count = len(stacks)
    rows, depth = lifted[0].shape
    return [
        pltpu.VMEM((count,) + stacks[0].shape, BF),
        pltpu.VMEM((count, len(lifted) * rows, depth // RING), BF),
        pltpu.SemaphoreType.DMA((count, 1 + len(lifted))),
    ]


def multiply_kernel(here_ref, *refs):
    stacks, lifted, (out_ref, *scratch) = refs[:EARLY], refs[EARLY : EARLY + 2], refs[EARLY + 2 :]
    out_ref[...] = product(here_ref, AWAY[:EARLY], stacks, lifted, *scratch)(None)


def multiply(here, stacks, lifted):
    tokens, width = 2 * lifted[0].shape[0], stacks[0].shape[2]
    return pl.pallas_call(
        multiply_kernel,
        in_specs=[scalars()] + [in_hbm()] * (len(stacks) + len(lifted)),
        out_specs=whole(),
        out_shape=shape((tokens, width), F32),
        scratch_shapes=product_scratch(stacks, lifted),
        compiler_params=params(60),
        cost_estimate=FREE,
        name="multiply",
    )(here, *stacks, *lifted)


def merge_kernel(here_ref, ngain_ref, acc_hbm, base_hbm, cot_hbm, *refs):
    stacks, lifted, refs = refs[: RING - EARLY], refs[RING - EARLY : RING - EARLY + 2], refs[RING - EARLY + 2 :]
    visual_ref, state_ref, stat_ref, acc_ref, base_ref, cot_ref, row_sems, *scratch = refs
    run = product(here_ref, AWAY[EARLY:], stacks, lifted, *scratch)
    copies = [
        pltpu.make_async_copy(a, b, row_sems.at[i])
        for i, (a, b) in enumerate(((acc_hbm, acc_ref), (base_hbm, base_ref), (cot_hbm, cot_ref)))
    ]
    for copy in copies:
        copy.start()
    total = run(None)
    for copy in copies:
        copy.wait()
    visual = (acc_ref[...] + total).astype(BF)
    visual_ref[...] = visual
    state = base_ref[...].astype(F32) + visual.astype(F32)
    state_ref[...] = state
    up = ngain_ref[...].astype(F32) * cot_ref[...].astype(F32)
    lane = lax.broadcasted_iota(jnp.int32, (state.shape[0], 128), 1)
    sums = jnp.where(
        lane == 0,
        jnp.sum(state * state, axis=1, keepdims=True),
        jnp.sum(up * state, axis=1, keepdims=True),
    )
    stat_ref[...] = sums.T[: stat_ref.shape[0]]


def merge(here, ngain, acc, base, cot, stacks, lifted):
    tokens, width = base.shape
    outs = [shape((tokens, width), BF), shape((tokens, width), F32), shape((8, tokens), F32)]
    return pl.pallas_call(
        merge_kernel,
        in_specs=[scalars(), whole()] + [in_hbm()] * (3 + len(stacks) + len(lifted)),
        out_specs=[whole()] * 3,
        out_shape=outs,
        scratch_shapes=[
            pltpu.VMEM((tokens, width), F32),
            pltpu.VMEM((tokens, width), BF),
            pltpu.VMEM((tokens, width), BF),
            pltpu.SemaphoreType.DMA((3,)),
        ]
        + product_scratch(stacks, lifted),
        compiler_params=params(24),
        cost_estimate=FREE,
        name="merge",
    )(here, ngain, acc, base, cot, *stacks, *lifted)


def add_kernel(sums_ref, got_ref, near_ref, turned_ref):
    count = sums_ref.shape[1] // 4
    cuts = [
        sums_ref[:, i * count : (i + 1) * count] + got_ref[:, (i ^ 1) * count : ((i ^ 1) + 1) * count]
        for i in range(4)
    ]
    near_ref[...] = jnp.concatenate(cuts, axis=1)
    turned_ref[...] = jnp.concatenate(cuts[2:] + cuts[:2], axis=1)


def add(sums, got):
    return pl.pallas_call(
        add_kernel,
        in_specs=[whole()] * 2,
        out_specs=[whole()] * 2,
        out_shape=[shape(sums.shape, F32)] * 2,
        compiler_params=params(4),
        cost_estimate=FREE,
        name="add",
    )(sums, got)


def pack_kernel(here_ref, slot_ref, visual_ref, after_ref, stay_ref, cross_ref):
    tokens = visual_ref.shape[0]
    slots = stay_ref.shape[0]
    for relative, out_ref in ((0, stay_ref), (1, cross_ref)):
        put = eq_hot((tokens, slots), 1, slot_ref[...] - (here_ref[2] ^ relative) * slots)
        out_ref[...] = lax.dot_general(
            put, visual_ref[...], (((0,), (0,)), ((), ())), preferred_element_type=F32
        ).astype(BF)


def pack(here, slot_col, visual, slots, after):
    tokens, width = visual.shape
    return pl.pallas_call(
        pack_kernel,
        in_specs=[scalars()] + [whole()] * 2 + [anywhere()],
        out_specs=[whole()] * 2,
        out_shape=[shape((slots // 2, width), BF)] * 2,
        compiler_params=params(8),
        cost_estimate=FREE,
        name="pack",
    )(here, slot_col, visual, after)


def braid_kernel(stay_ref, crossed_ref, out_ref):
    count, _, rows, _ = out_ref.shape
    for c in range(count):
        at = slice(c * rows, (c + 1) * rows)
        out_ref[c, 0] = stay_ref[at, :]
        out_ref[c, 1] = crossed_ref[at, :]


def braid(stay, crossed, count):
    rows, width = stay.shape
    return pl.pallas_call(
        braid_kernel,
        in_specs=[whole()] * 2,
        out_specs=whole(),
        out_shape=shape((count, 2, rows // count, width), BF),
        compiler_params=params(6),
        cost_estimate=FREE,
        name="braid",
    )(stay, crossed)


def backward_kernel(full_width, here_ref, ngain_ref, *refs):
    stats, stacks, refs = refs[:RING], refs[RING : 2 * RING], refs[2 * RING :]
    state_hbm, cot_hbm, own_ref, other_ref = refs[:4]
    picked_ref, sums_ref, state_ref, cot_ref, held_ref, row_sems, sems = refs[4:]
    row_copies = [
        pltpu.make_async_copy(a, b, row_sems.at[i])
        for i, (a, b) in enumerate(((state_hbm, state_ref), (cot_hbm, cot_ref)))
    ]
    for copy in row_copies:
        copy.start()
    wait_weight = fetch(here_ref, stacks, held_ref, sems)
    tokens = state_ref.shape[0]
    rows = tokens // 2 // RING
    total = stats[0][...]
    for ref in stats[1:]:
        total = total + ref[...]
    sums_ref[...] = total.T
    far, img = here_ref[1], here_ref[2]
    gain = ngain_ref[...].astype(F32)
    for copy in row_copies:
        copy.wait()
    for core in range(2):
        for away in range(RING):
            there = lax.rem(2 * far + img + away, RING)
            partner = lax.rem(there + img, 2)
            begin = partner * (tokens // 2) + core * (tokens // 4) + (there // 2) * (tokens // 8)
            at = pl.ds(pl.multiple_of(begin, rows), rows)
            sums = sums_ref[at, :]
            inv = lax.rsqrt(sums[:, 0:1] / full_width + 1e-06)
            inner = sums[:, 1:2] / full_width
            up = gain * cot_ref[at, :].astype(F32)
            grad = inv * up - state_ref[at, :] * (inv * inv * inv * inner)
            to = (core * RING + away) * rows
            picked_ref[to : to + rows, :] = grad.astype(BF)
    depth = own_ref.shape[1]
    wait_weight()
    block = depth // RING
    for step in range(RING):
        cols = slice(step * block, (step + 1) * block)
        both = lax.dot_general(
            picked_ref[...],
            held_ref[step].reshape(block, -1),
            (((1,), (1,)), ((), ())),
            preferred_element_type=F32,
        )
        own_ref[:, cols] = both[: tokens // 2].astype(BF)
        other_ref[:, cols] = both[tokens // 2 :].astype(BF)


def backward(here, state, cot, ngain, stats, stacks, full_width):
    tokens, width = state.shape
    depth = RING * stacks[0].shape[0] * stacks[0].shape[1]
    return pl.pallas_call(
        lambda *refs: backward_kernel(full_width, *refs),
        in_specs=[scalars()] + [whole()] * (1 + RING) + [in_hbm()] * (RING + 2),
        out_specs=[whole()] * 2,
        out_shape=[shape((tokens // 2, depth), BF)] * 2,
        scratch_shapes=[
            pltpu.VMEM((tokens, width), BF),
            pltpu.VMEM((tokens, 8), F32),
            pltpu.VMEM((tokens, width), F32),
            pltpu.VMEM((tokens, width), BF),
            pltpu.VMEM((RING,) + stacks[0].shape, BF),
            pltpu.SemaphoreType.DMA((2,)),
            pltpu.SemaphoreType.DMA((RING,)),
        ],
        compiler_params=params(24),
        cost_estimate=FREE,
        name="backward",
    )(here, ngain, *stats, *stacks, state, cot)


def both(own_ref, got_ref, start, count):
    at = slice(start, start + count)
    return (own_ref[at, :].astype(F32) + got_ref[at, :].astype(F32)).astype(BF)


def pair_kernel(own_ref, got_ref, after_ref, next_ref, last_ref):
    rows = own_ref.shape[0] // RING
    half = rows // 2
    next_ref[:half] = both(own_ref, got_ref, 2 * rows, half)
    next_ref[half:] = both(own_ref, got_ref, rows + half, half)
    last_ref[:half] = both(own_ref, got_ref, 2 * rows + half, half)
    last_ref[half:] = both(own_ref, got_ref, 3 * rows, half)


def pair(own, got, after):
    rows, depth = got.shape[0] // RING, got.shape[1]
    return pl.pallas_call(
        pair_kernel,
        in_specs=[whole()] * 2 + [anywhere()],
        out_specs=[whole()] * 2,
        out_shape=[shape((rows, depth), BF)] * 2,
        compiler_params=params(8),
        cost_estimate=FREE,
        name="pair",
    )(own, got, after)


def relay_kernel(own_ref, got_ref, from_last_ref, from_next_ref, next_ref, last_ref):
    half = next_ref.shape[0]
    rows = 2 * half
    for start, came_ref, out_ref in (
        (rows, from_last_ref, next_ref),
        (3 * rows + half, from_next_ref, last_ref),
    ):
        kept = both(own_ref, got_ref, start, half).astype(F32)
        out_ref[...] = (kept + came_ref[:half].astype(F32)).astype(BF)


def relay(own, got, from_last, from_next):
    rows, depth = from_last.shape
    return pl.pallas_call(
        relay_kernel,
        in_specs=[whole()] * 4,
        out_specs=[whole()] * 2,
        out_shape=[shape((rows // 2, depth), BF)] * 2,
        compiler_params=params(8),
        cost_estimate=FREE,
        name="relay",
    )(own, got, from_last, from_next)


def finish_kernel(here_ref, own_ref, got_ref, early_ref, late_ref, xw_ref, stat_ref, gain_ref, out_ref):
    window, tokens, width = xw_ref.shape
    full = window * width
    mean = stat_ref[:, 0:1]
    inv = stat_ref[:, 1:2]
    lifted = own_ref[...].astype(F32) + got_ref[...].astype(F32)
    lifted = lifted + early_ref[...].astype(F32) + late_ref[...].astype(F32)
    share = width // (RING * RING)
    scaled = []
    total = 0.0
    inner = 0.0
    for w in range(window):
        g = jnp.concatenate(
            [lifted[:, at : at + share] for at in range(w * share, full, window * share)], axis=1
        ) * gain_ref[w : w + 1].astype(F32)
        normed = (xw_ref[w].astype(F32) - mean) * inv
        total = total + jnp.sum(g, axis=1, keepdims=True)
        inner = inner + jnp.sum(g * normed, axis=1, keepdims=True)
        scaled.append((g, normed))
    total = total / full
    inner = inner / full
    rows = jnp.concatenate(
        [(inv * (g - total - normed * inner)).astype(BF) for g, normed in scaled], axis=0
    )
    out_ref[...] = jnp.dot(
        patch_major(tokens, window), rows, preferred_element_type=F32
    ).astype(BF)


def finish(here, step, own, got, early, late, xw, stat, gain):
    tokens, depth = late.shape
    window, width = gain.shape
    same = pl.BlockSpec((tokens, depth), lambda i, h: (step, 0))
    second = pl.BlockSpec((tokens, depth), lambda i, h: (1, 0))
    only = pl.BlockSpec((tokens, depth), lambda i, h: (0, 0))
    return pl.pallas_call(
        finish_kernel,
        grid_spec=pltpu.PrefetchScalarGridSpec(
            num_scalar_prefetch=1,
            grid=(1,),
            in_specs=[same, same, second, only]
            + [
                pl.BlockSpec((window, tokens, width), lambda i, h: (0, h[1] * 2 + step, 0)),
                pl.BlockSpec((tokens, 128), lambda i, h: (h[1] * 2 + step, 0)),
                pl.BlockSpec((window, width), lambda i, h: (0, 0)),
            ],
            out_specs=pl.BlockSpec((tokens * window, width), lambda i, h: (0, 0)),
        ),
        out_shape=shape((tokens * window, width), BF),
        compiler_params=params(12),
        cost_estimate=FREE,
        name="finish",
    )(here, own, got, early, late, xw, stat, gain)


def place_kernel(here_ref, pos_ref, came_ref, stream_ref, out_ref):
    rows, width = stream_ref.shape
    cut = width // 2
    slots = pos_ref.shape[0]
    put = eq_hot((slots, rows), 1, pos_ref[...])
    for relative in range(2):
        start = pl.multiple_of((here_ref[2] ^ relative) * cut, cut)
        at = pl.ds(start, cut)
        out_ref[:, at] = (
            stream_ref[:, at].astype(F32)
            + lax.dot_general(
                put,
                came_ref[:, relative].reshape(slots, cut),
                (((0,), (0,)), ((), ())),
                preferred_element_type=F32,
            )
        ).astype(BF)


def place(here, pos, came, stream):
    rows, width = stream.shape
    return pl.pallas_call(
        place_kernel,
        in_specs=[scalars()] + [whole()] * 3,
        out_specs=whole(),
        out_shape=shape((rows, width), BF),
        compiler_params=params(12),
        cost_estimate=FREE,
        name="place",
    )(here, pos, came, stream)


def lay_kernel(here_ref, *refs):
    blocks, (out_ref, sems) = refs[:-2], refs[-2:]
    rows = blocks[0].shape[0]
    copies = []
    for index, ref in enumerate(blocks):
        quarter, step = index // 2, index % 2
        owner = 2 * (here_ref[0] ^ (quarter // 2)) + (here_ref[1] ^ (quarter % 2))
        start = pl.multiple_of((2 * owner + step) * rows, rows)
        copies.append(pltpu.make_async_copy(ref, out_ref.at[pl.ds(start, rows)], sems.at[index]))
    for copy in copies:
        copy.start()
    for copy in copies:
        copy.wait()


def lay(here, blocks):
    rows, width = blocks[0].shape
    return pl.pallas_call(
        lay_kernel,
        in_specs=[scalars()] + [whole()] * len(blocks),
        out_specs=anywhere(),
        out_shape=shape((len(blocks) * rows, width), BF),
        scratch_shapes=[pltpu.SemaphoreType.DMA((len(blocks),))],
        compiler_params=params(4),
        cost_estimate=FREE,
        name="lay",
    )(here, *blocks)


def shards(features, ln_gain, ln_bias, projection, stream, norm_gain, cotangent, slots):
    n_img = lax.axis_size("img")
    n_ctx = lax.axis_size("ctx")
    n_tp = lax.axis_size("tp")
    merged = slots.shape[0]
    tok_rows, width = stream.shape
    owners = n_img * n_ctx
    capacity = 2 * merged // owners
    slot_count = owners * capacity
    full_width = width * n_tp
    cut = width // n_img

    img = lax.axis_index("img").astype(jnp.int32)
    tp = lax.axis_index("tp").astype(jnp.int32)
    core, far_half = tp % 2, tp // 2
    z, y = lax.axis_index("ctx") // RING, lax.axis_index("ctx") % RING
    here = jnp.stack([core, far_half, img, z, y]).astype(jnp.int32)

    flip = [(i, 1 - i) for i in range(n_img)]
    core_pairs = [(t, t ^ 1) for t in range(n_tp)]
    far_pairs = [(t, t ^ 2) for t in range(n_tp)]

    def along_x(array, by):
        pairs = []
        for i in range(n_img):
            for t in range(n_tp):
                x = (2 * (t // 2) + i + by) % RING
                pairs.append((i * n_tp + t, (x % 2) * n_tp + 2 * (x // 2) + t % 2))
        return lax.ppermute(array, ("img", "tp"), pairs)

    def along_ctx(array, axis, by):
        pairs = []
        for c in range(n_ctx):
            for t in range(n_tp):
                z, y = c // RING, c % RING
                if t % 2 == axis:
                    y = (y + by) % RING
                else:
                    z = (z + by) % RING
                pairs.append((c * n_tp + t, (z * RING + y) * n_tp + t))
        return lax.ppermute(array, ("ctx", "tp"), pairs)

    slots = jnp.roll(slots, -core * (merged // 2))
    target = slots // tok_rows
    ids = jnp.arange(merged)
    earlier = (target[:, None] == target[None, :]) & (ids[:, None] < ids[None, :])
    rank = jnp.sum(earlier.astype(jnp.int32), axis=0)
    slot = target * capacity + rank
    local = slots - target * tok_rows
    packed = jnp.max(
        jnp.where(jnp.arange(slot_count)[:, None] == slot[None, :], local[None, :], -1), axis=1
    )
    asked = lax.all_to_all(
        packed.reshape(owners, capacity), ("img", "ctx"), split_axis=0, concat_axis=0, tiled=True
    )
    columns = lax.dynamic_slice_in_dim(projection[0], img * cut, cut, axis=2).reshape(-1, cut)
    moves = (1, -1, 2)
    near_blocks = [along_ctx(columns, 0, by) for by in moves]
    paired = target * (n_img * capacity) + rank + img * capacity
    partner = lax.ppermute(paired, "img", flip)
    gain = ln_gain[0]
    lifted, xw, stat = layer_norm(here, features[0], gain, ln_bias[0])
    asked, lifted, stat, near_blocks, partner = lax.optimization_barrier(
        (asked, lifted, stat, near_blocks, partner)
    )
    paired = jnp.concatenate([paired, partner]).reshape(-1, 1)

    first = stack(here, [columns] + near_blocks)
    asked, first, lifted = lax.optimization_barrier((asked, first, lifted))

    asked = asked.reshape(n_img, n_ctx, capacity).transpose(1, 0, 2)
    asked = asked.reshape(slot_count, 1)
    held = collect(asked, stream, cotangent[0], first)
    came = lax.all_to_all(
        held.reshape(owners, n_img * capacity, width),
        ("img", "ctx"), split_axis=0, concat_axis=0, tiled=True,
    ).reshape(n_img * slot_count, width)

    stacks = [first] + [along_ctx(first, 1, by) for by in moves[:2]]
    stacks.append(along_ctx(stacks[1], 1, 1))

    pairs = []
    for i in range(n_img):
        for t in range(n_tp):
            x = (2 * (t // 2) + i + (1 if t % 2 == 0 else -1)) % RING
            pairs.append((i * n_tp + t, (x % 2) * n_tp + 2 * (x // 2) + t % 2))
    lifted = [lifted, lax.ppermute(lifted, ("img", "tp"), pairs)]

    own_gain = lax.dynamic_slice_in_dim(norm_gain, img * cut, cut, axis=1)
    acc = multiply(here, stacks[:EARLY], lifted)
    base, cot = unpack(paired, came, acc)
    visual, state, sums = merge(here, own_gain, acc, base, cot, stacks[EARLY:], lifted)

    near, turned = add(sums, lax.ppermute(sums, "tp", core_pairs))
    stats = [near] + [along_x(near if by == 2 else turned, by) for by in (1, 2, 3)]
    stay, cross = pack(here, paired, visual, n_img * slot_count, near)
    cross, stats = lax.optimization_barrier((cross, stats))
    crossed = lax.ppermute(cross, "img", flip)

    own, other = backward(here, state, cot, own_gain, stats, stacks, full_width)
    own, other, crossed = lax.optimization_barrier((own, other, crossed))
    got = lax.ppermute(other, "tp", core_pairs)
    to_next, to_last = pair(own, got, crossed)
    from_last, from_next = along_x(to_next, 1), along_x(to_last, -1)
    to_next, to_last = relay(own, got, from_last, from_next)
    late_last, late_next = along_x(to_next, 1), along_x(to_last, -1)

    send = braid(stay, crossed, n_ctx)
    arrived = lax.all_to_all(send, "ctx", split_axis=0, concat_axis=0, tiled=True)
    new_stream = place(here, asked, arrived, stream)

    out = [
        finish(here, step, own, got, early, late, xw, stat, gain)
        for step, (early, late) in enumerate(((from_next, late_last), (from_last, late_next)))
    ]
    beyond = [lax.ppermute(x, "tp", far_pairs) for x in out]
    beyond[1], new_stream = lax.optimization_barrier((beyond[1], new_stream))
    from_core = [lax.ppermute(x, "tp", core_pairs) for x in out + beyond]
    grad = lay(here, out + beyond + from_core)
    return (new_stream, grad[None])


def solution(mesh):
    placed = (
        P(None, ("img", "ctx"), None),
        P(),
        P(),
        P(None, None, "ctx", "tp"),
        P(("img", "ctx"), "tp"),
        P(None, "tp"),
        P(None, ("img", "ctx"), "tp"),
        P(("img", "ctx")),
    )
    return jax.shard_map(
        shards,
        mesh=mesh,
        in_specs=placed,
        out_specs=(P(("img", "ctx"), "tp"), P(None, ("img", "ctx"), None)),
        check_vma=False,
    )
```

```python
import jax
import jax.numpy as jnp
from jax import lax
from jax.experimental import pallas as pl
from jax.experimental.pallas import tpu as pltpu
from jax.sharding import PartitionSpec as P


BF = jnp.bfloat16
F32 = jnp.float32
FREE = pl.CostEstimate(flops=0, bytes_accessed=0, transcendentals=0)
RING = 4
AWAY = (0, 3, 1, 2)
EARLY = 2


def params(mib):
    return pltpu.CompilerParams(vmem_limit_bytes=mib * 1024 * 1024)


def whole():
    return pl.BlockSpec(memory_space=pltpu.VMEM)


def shape(dims, kind):
    return jax.ShapeDtypeStruct(dims, kind)


def scalars():
    return pl.BlockSpec(memory_space=pltpu.SMEM)


def in_hbm():
    return pl.BlockSpec(memory_space=pltpu.HBM)


def anywhere():
    return pl.BlockSpec(memory_space=pl.ANY)


def eq_hot(shape, dim, index):
    return (lax.broadcasted_iota(jnp.int32, shape, dim) == index).astype(BF)


def window_major(tokens, window):
    n = tokens * window
    row = lax.broadcasted_iota(jnp.int32, (n, n), 0)
    col = lax.broadcasted_iota(jnp.int32, (n, n), 1)
    return (col == (row % tokens) * window + row // tokens).astype(BF)


def patch_major(tokens, window):
    n = tokens * window
    row = lax.broadcasted_iota(jnp.int32, (n, n), 0)
    col = lax.broadcasted_iota(jnp.int32, (n, n), 1)
    return (col == (row % window) * tokens + row // window).astype(BF)


def norm_kernel(here_ref, x_ref, gain_ref, bias_ref, lifted_ref, xw_ref, stat_ref):
    window, width = gain_ref.shape
    tokens = x_ref.shape[0] // window
    full = window * width
    x = jnp.dot(window_major(tokens, window), x_ref[...], preferred_element_type=F32)
    parts = [x[w * tokens : (w + 1) * tokens] for w in range(window)]
    total = sum(jnp.sum(p, axis=1, keepdims=True) for p in parts)
    squares = sum(jnp.sum(p * p, axis=1, keepdims=True) for p in parts)
    mean = total / full
    inv = lax.rsqrt(squares / full - mean * mean + 1e-05)
    lifted = []
    for w, p in enumerate(parts):
        normed = (p - mean) * inv
        lifted.append(
            normed * gain_ref[w : w + 1].astype(F32) + bias_ref[w : w + 1].astype(F32)
        )
        xw_ref[w] = p.astype(BF)
    share = width // (RING * RING)
    for core in range(2):

        @pl.when(here_ref[0] == core)
        def _():
            blocks = [(a, b) for a in range(RING) for b in range(RING)]
            starts = [(a * RING + b if core == 0 else b * RING + a) * share for a, b in blocks]
            lifted_ref[...] = jnp.concatenate(
                [p[:, at : at + share] for at in starts for p in lifted], axis=1
            ).astype(BF)

    lane = lax.broadcasted_iota(jnp.int32, stat_ref.shape, 1)
    stat_ref[...] = jnp.where(lane == 0, mean, inv)


def layer_norm(here, features, gain, bias):
    rows, width = features.shape
    window = gain.shape[0]
    merged = rows // window
    block = 64
    steps = merged // block
    return pl.pallas_call(
        norm_kernel,
        grid_spec=pltpu.PrefetchScalarGridSpec(
            num_scalar_prefetch=1,
            grid=(steps,),
            in_specs=[
                pl.BlockSpec(
                    (block * window, width),
                    lambda i, c: (lax.rem(i + c[0] * (steps // 2), steps), 0),
                ),
                pl.BlockSpec((window, width), lambda i, c: (0, 0)),
                pl.BlockSpec((window, width), lambda i, c: (0, 0)),
            ],
            out_specs=[
                pl.BlockSpec((block, window * width), lambda i, c: (i, 0)),
                pl.BlockSpec((window, block, width), lambda i, c: (0, i, 0)),
                pl.BlockSpec((block, 128), lambda i, c: (i, 0)),
            ],
        ),
        out_shape=[
            shape((merged, window * width), BF),
            shape((window, merged, width), BF),
            shape((merged, 128), F32),
        ],
        compiler_params=params(58),
        cost_estimate=FREE,
        name="layer_norm",
    )(here, features, gain, bias)


def collect_kernel(pos_ref, stream_ref, cot_ref, after_ref, out_ref):
    slots = pos_ref.shape[0]
    rows, width = stream_ref.shape
    cut = width // 2
    pick = eq_hot((slots, rows), 1, pos_ref[...])
    for img in range(2):
        at = slice(img * cut, (img + 1) * cut)
        for place, ref in enumerate((stream_ref, cot_ref)):
            out_ref[img, :, place * cut : (place + 1) * cut] = jnp.dot(
                pick, ref[:, at], preferred_element_type=F32
            ).astype(BF)


def collect(pos, stream, cot, after):
    slots = pos.shape[0]
    rows, width = stream.shape
    return pl.pallas_call(
        collect_kernel,
        in_specs=[whole()] * 3 + [anywhere()],
        out_specs=whole(),
        out_shape=shape((2, slots, width), BF),
        compiler_params=params(20),
        cost_estimate=FREE,
        name="collect",
    )(pos, stream, cot, after)


def stack_kernel(here_ref, *refs):
    out_ref, sems = refs[RING:]
    first = jnp.where(here_ref[0] == 0, here_ref[4], here_ref[3])
    copies = [
        pltpu.make_async_copy(ref, out_ref.at[lax.rem(first + away, RING)], sems.at[index])
        for index, (away, ref) in enumerate(zip(AWAY, refs[:RING]))
    ]
    for copy in copies:
        copy.start()
    for copy in copies:
        copy.wait()


def stack(here, blocks):
    rows, width = blocks[0].shape
    return pl.pallas_call(
        stack_kernel,
        in_specs=[scalars()] + [in_hbm()] * RING,
        out_specs=whole(),
        out_shape=shape((RING, rows, width), BF),
        scratch_shapes=[pltpu.SemaphoreType.DMA((RING,))],
        compiler_params=params(60),
        cost_estimate=FREE,
        name="stack",
    )(here, *blocks)


def fetch(here_ref, stacks, held_ref, sems):
    for index, (away, ref) in enumerate(zip(AWAY, stacks)):

        @pl.when(here_ref[0] == 0)
        def _():
            place = lax.rem(here_ref[3] + away, RING)
            pltpu.make_async_copy(ref, held_ref.at[place], sems.at[index]).start()

        @pl.when(here_ref[0] == 1)
        def _():
            place = lax.rem(here_ref[4] + away, RING)
            pltpu.make_async_copy(ref, held_ref.at[:, place], sems.at[index]).start()

    def wait():
        for index, ref in enumerate(stacks):
            pltpu.make_async_copy(ref, held_ref.at[0], sems.at[index]).wait()

    return wait


def product(here_ref, away, stacks, lifted, held_ref, left_ref, sems):
    second = jnp.where(here_ref[0] == 0, here_ref[3], here_ref[4])
    block = left_ref.shape[2]
    rows = lifted[0].shape[0]
    copies = []
    for index, ref in enumerate(stacks):
        place = lax.rem(second + away[index], RING)
        at = pl.ds(pl.multiple_of(place * block, block), block)
        group = [pltpu.make_async_copy(ref, held_ref.at[index], sems.at[index, 0])]
        for i, part in enumerate(lifted):
            to = left_ref.at[index, pl.ds(i * rows, rows)]
            group.append(pltpu.make_async_copy(part.at[:, at], to, sems.at[index, 1 + i]))
        for copy in group:
            copy.start()
        copies.append(group)

    def run(total):
        for index, group in enumerate(copies):
            for copy in group:
                copy.wait()
            part = jnp.dot(
                left_ref[index], held_ref[index].reshape(block, -1), preferred_element_type=F32
            )
            total = part if total is None else total + part
        return total

    return run


def product_scratch(stacks, lifted):
    count = len(stacks)
    rows, depth = lifted[0].shape
    return [
        pltpu.VMEM((count,) + stacks[0].shape, BF),
        pltpu.VMEM((count, len(lifted) * rows, depth // RING), BF),
        pltpu.SemaphoreType.DMA((count, 1 + len(lifted))),
    ]


def multiply_kernel(here_ref, *refs):
    stacks, lifted, (out_ref, *scratch) = refs[:EARLY], refs[EARLY : EARLY + 2], refs[EARLY + 2 :]
    out_ref[...] = product(here_ref, AWAY[:EARLY], stacks, lifted, *scratch)(None)


def multiply(here, stacks, lifted):
    tokens, width = 2 * lifted[0].shape[0], stacks[0].shape[2]
    return pl.pallas_call(
        multiply_kernel,
        in_specs=[scalars()] + [in_hbm()] * (len(stacks) + len(lifted)),
        out_specs=whole(),
        out_shape=shape((tokens, width), F32),
        scratch_shapes=product_scratch(stacks, lifted),
        compiler_params=params(60),
        cost_estimate=FREE,
        name="multiply",
    )(here, *stacks, *lifted)


def merge_kernel(here_ref, ngain_ref, slot_ref, acc_hbm, came_hbm, *refs):
    stacks, lifted, refs = refs[: RING - EARLY], refs[RING - EARLY : RING - EARLY + 2], refs[RING - EARLY + 2 :]
    visual_ref, state_ref, cot_ref, stat_ref, acc_ref, came_ref, row_sems, *scratch = refs
    run = product(here_ref, AWAY[EARLY:], stacks, lifted, *scratch)
    copies = [
        pltpu.make_async_copy(a, b, row_sems.at[i])
        for i, (a, b) in enumerate(((came_hbm, came_ref), (acc_hbm, acc_ref)))
    ]
    for copy in copies:
        copy.start()
    tokens, width = cot_ref.shape
    take = eq_hot((tokens, came_ref.shape[0]), 1, slot_ref[...])
    total = run(None)
    for copy in copies:
        copy.wait()
    base = jnp.dot(take, came_ref[:, :width], preferred_element_type=F32)
    cot = jnp.dot(take, came_ref[:, width:], preferred_element_type=F32)
    cot_ref[...] = cot.astype(BF)
    visual = (acc_ref[...] + total).astype(BF)
    visual_ref[...] = visual
    state = base + visual.astype(F32)
    state_ref[...] = state
    up = ngain_ref[...].astype(F32) * cot
    lane = lax.broadcasted_iota(jnp.int32, (state.shape[0], 128), 1)
    sums = jnp.where(
        lane == 0,
        jnp.sum(state * state, axis=1, keepdims=True),
        jnp.sum(up * state, axis=1, keepdims=True),
    )
    stat_ref[...] = sums.T[: stat_ref.shape[0]]


def merge(here, ngain, slot_col, acc, came, stacks, lifted):
    tokens, width = acc.shape
    outs = [
        shape((tokens, width), BF),
        shape((tokens, width), F32),
        shape((tokens, width), BF),
        shape((8, tokens), F32),
    ]
    return pl.pallas_call(
        merge_kernel,
        in_specs=[scalars()] + [whole()] * 2 + [in_hbm()] * (2 + len(stacks) + len(lifted)),
        out_specs=[whole()] * 4,
        out_shape=outs,
        scratch_shapes=[
            pltpu.VMEM((tokens, width), F32),
            pltpu.VMEM(came.shape, BF),
            pltpu.SemaphoreType.DMA((2,)),
        ]
        + product_scratch(stacks, lifted),
        compiler_params=params(28),
        cost_estimate=FREE,
        name="merge",
    )(here, ngain, slot_col, acc, came, *stacks, *lifted)


def add_kernel(sums_ref, got_ref, near_ref, turned_ref):
    count = sums_ref.shape[1] // 4
    cuts = [
        sums_ref[:, i * count : (i + 1) * count] + got_ref[:, (i ^ 1) * count : ((i ^ 1) + 1) * count]
        for i in range(4)
    ]
    near_ref[...] = jnp.concatenate(cuts, axis=1)
    turned_ref[...] = jnp.concatenate(cuts[2:] + cuts[:2], axis=1)


def add(sums, got):
    return pl.pallas_call(
        add_kernel,
        in_specs=[whole()] * 2,
        out_specs=[whole()] * 2,
        out_shape=[shape(sums.shape, F32)] * 2,
        compiler_params=params(4),
        cost_estimate=FREE,
        name="add",
    )(sums, got)


def pack_kernel(here_ref, slot_ref, visual_ref, after_ref, stay_ref, cross_ref):
    tokens = visual_ref.shape[0]
    slots = stay_ref.shape[0]
    for relative, out_ref in ((0, stay_ref), (1, cross_ref)):
        put = eq_hot((tokens, slots), 1, slot_ref[...] - (here_ref[2] ^ relative) * slots)
        out_ref[...] = lax.dot_general(
            put, visual_ref[...], (((0,), (0,)), ((), ())), preferred_element_type=F32
        ).astype(BF)


def pack(here, slot_col, visual, slots, after):
    tokens, width = visual.shape
    return pl.pallas_call(
        pack_kernel,
        in_specs=[scalars()] + [whole()] * 2 + [anywhere()],
        out_specs=[whole()] * 2,
        out_shape=[shape((slots // 2, width), BF)] * 2,
        compiler_params=params(8),
        cost_estimate=FREE,
        name="pack",
    )(here, slot_col, visual, after)


def braid_kernel(stay_ref, crossed_ref, out_ref):
    count, _, rows, _ = out_ref.shape
    for c in range(count):
        at = slice(c * rows, (c + 1) * rows)
        out_ref[c, 0] = stay_ref[at, :]
        out_ref[c, 1] = crossed_ref[at, :]


def braid(stay, crossed, count):
    rows, width = stay.shape
    return pl.pallas_call(
        braid_kernel,
        in_specs=[whole()] * 2,
        out_specs=whole(),
        out_shape=shape((count, 2, rows // count, width), BF),
        compiler_params=params(6),
        cost_estimate=FREE,
        name="braid",
    )(stay, crossed)


def backward_kernel(full_width, here_ref, ngain_ref, *refs):
    stats, stacks, refs = refs[:RING], refs[RING : 2 * RING], refs[2 * RING :]
    state_hbm, cot_hbm, own_ref, other_ref = refs[:4]
    picked_ref, sums_ref, state_ref, cot_ref, held_ref, row_sems, sems = refs[4:]
    row_copies = [
        pltpu.make_async_copy(a, b, row_sems.at[i])
        for i, (a, b) in enumerate(((state_hbm, state_ref), (cot_hbm, cot_ref)))
    ]
    for copy in row_copies:
        copy.start()
    wait_weight = fetch(here_ref, stacks, held_ref, sems)
    tokens = state_ref.shape[0]
    rows = tokens // 2 // RING
    total = stats[0][...]
    for ref in stats[1:]:
        total = total + ref[...]
    sums_ref[...] = total.T
    far, img = here_ref[1], here_ref[2]
    gain = ngain_ref[...].astype(F32)
    for copy in row_copies:
        copy.wait()
    for core in range(2):
        for away in range(RING):
            there = lax.rem(2 * far + img + away, RING)
            partner = lax.rem(there + img, 2)
            begin = partner * (tokens // 2) + core * (tokens // 4) + (there // 2) * (tokens // 8)
            at = pl.ds(pl.multiple_of(begin, rows), rows)
            sums = sums_ref[at, :]
            inv = lax.rsqrt(sums[:, 0:1] / full_width + 1e-06)
            inner = sums[:, 1:2] / full_width
            up = gain * cot_ref[at, :].astype(F32)
            grad = inv * up - state_ref[at, :] * (inv * inv * inv * inner)
            to = (core * RING + away) * rows
            picked_ref[to : to + rows, :] = grad.astype(BF)
    depth = own_ref.shape[1]
    wait_weight()
    block = depth // RING
    for step in range(RING):
        cols = slice(step * block, (step + 1) * block)
        both = lax.dot_general(
            picked_ref[...],
            held_ref[step].reshape(block, -1),
            (((1,), (1,)), ((), ())),
            preferred_element_type=F32,
        )
        own_ref[:, cols] = both[: tokens // 2].astype(BF)
        other_ref[:, cols] = both[tokens // 2 :].astype(BF)


def backward(here, state, cot, ngain, stats, stacks, full_width):
    tokens, width = state.shape
    depth = RING * stacks[0].shape[0] * stacks[0].shape[1]
    return pl.pallas_call(
        lambda *refs: backward_kernel(full_width, *refs),
        in_specs=[scalars()] + [whole()] * (1 + RING) + [in_hbm()] * (RING + 2),
        out_specs=[whole()] * 2,
        out_shape=[shape((tokens // 2, depth), BF)] * 2,
        scratch_shapes=[
            pltpu.VMEM((tokens, width), BF),
            pltpu.VMEM((tokens, 8), F32),
            pltpu.VMEM((tokens, width), F32),
            pltpu.VMEM((tokens, width), BF),
            pltpu.VMEM((RING,) + stacks[0].shape, BF),
            pltpu.SemaphoreType.DMA((2,)),
            pltpu.SemaphoreType.DMA((RING,)),
        ],
        compiler_params=params(24),
        cost_estimate=FREE,
        name="backward",
    )(here, ngain, *stats, *stacks, state, cot)


def both(own_ref, got_ref, start, count):
    at = slice(start, start + count)
    return (own_ref[at, :].astype(F32) + got_ref[at, :].astype(F32)).astype(BF)


def pair_kernel(own_ref, got_ref, after_ref, next_ref, last_ref):
    rows = own_ref.shape[0] // RING
    half = rows // 2
    next_ref[:half] = both(own_ref, got_ref, 2 * rows, half)
    next_ref[half:] = both(own_ref, got_ref, rows + half, half)
    last_ref[:half] = both(own_ref, got_ref, 2 * rows + half, half)
    last_ref[half:] = both(own_ref, got_ref, 3 * rows, half)


def pair(own, got, after):
    rows, depth = got.shape[0] // RING, got.shape[1]
    return pl.pallas_call(
        pair_kernel,
        in_specs=[whole()] * 2 + [anywhere()],
        out_specs=[whole()] * 2,
        out_shape=[shape((rows, depth), BF)] * 2,
        compiler_params=params(8),
        cost_estimate=FREE,
        name="pair",
    )(own, got, after)


def relay_kernel(own_ref, got_ref, from_last_ref, from_next_ref, next_ref, last_ref):
    half = next_ref.shape[0]
    rows = 2 * half
    for start, came_ref, out_ref in (
        (rows, from_last_ref, next_ref),
        (3 * rows + half, from_next_ref, last_ref),
    ):
        kept = both(own_ref, got_ref, start, half).astype(F32)
        out_ref[...] = (kept + came_ref[:half].astype(F32)).astype(BF)


def relay(own, got, from_last, from_next):
    rows, depth = from_last.shape
    return pl.pallas_call(
        relay_kernel,
        in_specs=[whole()] * 4,
        out_specs=[whole()] * 2,
        out_shape=[shape((rows // 2, depth), BF)] * 2,
        compiler_params=params(8),
        cost_estimate=FREE,
        name="relay",
    )(own, got, from_last, from_next)


def finish_kernel(here_ref, own_ref, got_ref, early_ref, late_ref, xw_ref, stat_ref, gain_ref, out_ref):
    window, tokens, width = xw_ref.shape
    full = window * width
    mean = stat_ref[:, 0:1]
    inv = stat_ref[:, 1:2]
    lifted = own_ref[...].astype(F32) + got_ref[...].astype(F32)
    lifted = lifted + early_ref[...].astype(F32) + late_ref[...].astype(F32)
    share = width // (RING * RING)
    scaled = []
    total = 0.0
    inner = 0.0
    for w in range(window):
        g = jnp.concatenate(
            [lifted[:, at : at + share] for at in range(w * share, full, window * share)], axis=1
        ) * gain_ref[w : w + 1].astype(F32)
        normed = (xw_ref[w].astype(F32) - mean) * inv
        total = total + jnp.sum(g, axis=1, keepdims=True)
        inner = inner + jnp.sum(g * normed, axis=1, keepdims=True)
        scaled.append((g, normed))
    total = total / full
    inner = inner / full
    rows = jnp.concatenate(
        [(inv * (g - total - normed * inner)).astype(BF) for g, normed in scaled], axis=0
    )
    out_ref[...] = jnp.dot(
        patch_major(tokens, window), rows, preferred_element_type=F32
    ).astype(BF)


def finish(here, step, own, got, early, late, xw, stat, gain):
    tokens, depth = late.shape
    window, width = gain.shape
    same = pl.BlockSpec((tokens, depth), lambda i, h: (step, 0))
    second = pl.BlockSpec((tokens, depth), lambda i, h: (1, 0))
    only = pl.BlockSpec((tokens, depth), lambda i, h: (0, 0))
    return pl.pallas_call(
        finish_kernel,
        grid_spec=pltpu.PrefetchScalarGridSpec(
            num_scalar_prefetch=1,
            grid=(1,),
            in_specs=[same, same, second, only]
            + [
                pl.BlockSpec((window, tokens, width), lambda i, h: (0, h[1] * 2 + step, 0)),
                pl.BlockSpec((tokens, 128), lambda i, h: (h[1] * 2 + step, 0)),
                pl.BlockSpec((window, width), lambda i, h: (0, 0)),
            ],
            out_specs=pl.BlockSpec((tokens * window, width), lambda i, h: (0, 0)),
        ),
        out_shape=shape((tokens * window, width), BF),
        compiler_params=params(12),
        cost_estimate=FREE,
        name="finish",
    )(here, own, got, early, late, xw, stat, gain)


def place_kernel(here_ref, pos_ref, came_ref, stream_ref, out_ref):
    rows, width = stream_ref.shape
    cut = width // 2
    slots = pos_ref.shape[0]
    put = eq_hot((slots, rows), 1, pos_ref[...])
    for relative in range(2):
        start = pl.multiple_of((here_ref[2] ^ relative) * cut, cut)
        at = pl.ds(start, cut)
        out_ref[:, at] = (
            stream_ref[:, at].astype(F32)
            + lax.dot_general(
                put,
                came_ref[:, relative].reshape(slots, cut),
                (((0,), (0,)), ((), ())),
                preferred_element_type=F32,
            )
        ).astype(BF)


def place(here, pos, came, stream):
    rows, width = stream.shape
    return pl.pallas_call(
        place_kernel,
        in_specs=[scalars()] + [whole()] * 3,
        out_specs=whole(),
        out_shape=shape((rows, width), BF),
        compiler_params=params(12),
        cost_estimate=FREE,
        name="place",
    )(here, pos, came, stream)


def lay_kernel(here_ref, *refs):
    blocks, (out_ref, sems) = refs[:-2], refs[-2:]
    rows = blocks[0].shape[0]
    copies = []
    for index, ref in enumerate(blocks):
        quarter, step = index // 2, index % 2
        owner = 2 * (here_ref[0] ^ (quarter // 2)) + (here_ref[1] ^ (quarter % 2))
        start = pl.multiple_of((2 * owner + step) * rows, rows)
        copies.append(pltpu.make_async_copy(ref, out_ref.at[pl.ds(start, rows)], sems.at[index]))
    for copy in copies:
        copy.start()
    for copy in copies:
        copy.wait()


def lay(here, blocks):
    rows, width = blocks[0].shape
    return pl.pallas_call(
        lay_kernel,
        in_specs=[scalars()] + [whole()] * len(blocks),
        out_specs=anywhere(),
        out_shape=shape((len(blocks) * rows, width), BF),
        scratch_shapes=[pltpu.SemaphoreType.DMA((len(blocks),))],
        compiler_params=params(4),
        cost_estimate=FREE,
        name="lay",
    )(here, *blocks)


def shards(features, ln_gain, ln_bias, projection, stream, norm_gain, cotangent, slots):
    n_img = lax.axis_size("img")
    n_ctx = lax.axis_size("ctx")
    n_tp = lax.axis_size("tp")
    merged = slots.shape[0]
    tok_rows, width = stream.shape
    owners = n_img * n_ctx
    capacity = 2 * merged // owners
    slot_count = owners * capacity
    full_width = width * n_tp
    cut = width // n_img

    img = lax.axis_index("img").astype(jnp.int32)
    tp = lax.axis_index("tp").astype(jnp.int32)
    core, far_half = tp % 2, tp // 2
    z, y = lax.axis_index("ctx") // RING, lax.axis_index("ctx") % RING
    here = jnp.stack([core, far_half, img, z, y]).astype(jnp.int32)

    flip = [(i, 1 - i) for i in range(n_img)]
    core_pairs = [(t, t ^ 1) for t in range(n_tp)]
    far_pairs = [(t, t ^ 2) for t in range(n_tp)]

    def along_x(array, by):
        pairs = []
        for i in range(n_img):
            for t in range(n_tp):
                x = (2 * (t // 2) + i + by) % RING
                pairs.append((i * n_tp + t, (x % 2) * n_tp + 2 * (x // 2) + t % 2))
        return lax.ppermute(array, ("img", "tp"), pairs)

    def along_ctx(array, axis, by):
        pairs = []
        for c in range(n_ctx):
            for t in range(n_tp):
                z, y = c // RING, c % RING
                if t % 2 == axis:
                    y = (y + by) % RING
                else:
                    z = (z + by) % RING
                pairs.append((c * n_tp + t, (z * RING + y) * n_tp + t))
        return lax.ppermute(array, ("ctx", "tp"), pairs)

    slots = jnp.roll(slots, -core * (merged // 2))
    target = slots // tok_rows
    ids = jnp.arange(merged)
    earlier = (target[:, None] == target[None, :]) & (ids[:, None] < ids[None, :])
    rank = jnp.sum(earlier.astype(jnp.int32), axis=0)
    slot = target * capacity + rank
    local = slots - target * tok_rows
    packed = jnp.max(
        jnp.where(jnp.arange(slot_count)[:, None] == slot[None, :], local[None, :], -1), axis=1
    )
    asked = lax.all_to_all(
        packed.reshape(owners, capacity), ("img", "ctx"), split_axis=0, concat_axis=0, tiled=True
    )
    columns = lax.dynamic_slice_in_dim(projection[0], img * cut, cut, axis=2).reshape(-1, cut)
    moves = (1, -1, 2)
    near_blocks = [along_ctx(columns, 0, by) for by in moves]
    paired = target * (n_img * capacity) + rank + img * capacity
    partner = lax.ppermute(paired, "img", flip)
    gain = ln_gain[0]
    lifted, xw, stat = layer_norm(here, features[0], gain, ln_bias[0])
    asked, lifted, stat, near_blocks, partner = lax.optimization_barrier(
        (asked, lifted, stat, near_blocks, partner)
    )
    paired = jnp.concatenate([paired, partner]).reshape(-1, 1)

    first = stack(here, [columns] + near_blocks)
    asked, first, lifted = lax.optimization_barrier((asked, first, lifted))

    asked = asked.reshape(n_img, n_ctx, capacity).transpose(1, 0, 2)
    asked = asked.reshape(slot_count, 1)
    held = collect(asked, stream, cotangent[0], first)
    came = lax.all_to_all(
        held.reshape(owners, n_img * capacity, width),
        ("img", "ctx"), split_axis=0, concat_axis=0, tiled=True,
    ).reshape(n_img * slot_count, width)

    stacks = [first] + [along_ctx(first, 1, by) for by in moves[:2]]
    stacks.append(along_ctx(stacks[1], 1, 1))

    pairs = []
    for i in range(n_img):
        for t in range(n_tp):
            x = (2 * (t // 2) + i + (1 if t % 2 == 0 else -1)) % RING
            pairs.append((i * n_tp + t, (x % 2) * n_tp + 2 * (x // 2) + t % 2))
    lifted = [lifted, lax.ppermute(lifted, ("img", "tp"), pairs)]

    own_gain = lax.dynamic_slice_in_dim(norm_gain, img * cut, cut, axis=1)
    acc = multiply(here, stacks[:EARLY], lifted)
    visual, state, cot, sums = merge(here, own_gain, paired, acc, came, stacks[EARLY:], lifted)

    near, turned = add(sums, lax.ppermute(sums, "tp", core_pairs))
    stats = [near] + [along_x(near if by == 2 else turned, by) for by in (1, 2, 3)]
    stay, cross = pack(here, paired, visual, n_img * slot_count, near)
    cross, stats = lax.optimization_barrier((cross, stats))
    crossed = lax.ppermute(cross, "img", flip)

    own, other = backward(here, state, cot, own_gain, stats, stacks, full_width)
    own, other, crossed = lax.optimization_barrier((own, other, crossed))
    got = lax.ppermute(other, "tp", core_pairs)
    to_next, to_last = pair(own, got, crossed)
    from_last, from_next = along_x(to_next, 1), along_x(to_last, -1)
    to_next, to_last = relay(own, got, from_last, from_next)
    late_last, late_next = along_x(to_next, 1), along_x(to_last, -1)

    send = braid(stay, crossed, n_ctx)
    arrived = lax.all_to_all(send, "ctx", split_axis=0, concat_axis=0, tiled=True)
    new_stream = place(here, asked, arrived, stream)

    out = [
        finish(here, step, own, got, early, late, xw, stat, gain)
        for step, (early, late) in enumerate(((from_next, late_last), (from_last, late_next)))
    ]
    beyond = [lax.ppermute(x, "tp", far_pairs) for x in out]
    beyond[1], new_stream = lax.optimization_barrier((beyond[1], new_stream))
    from_core = [lax.ppermute(x, "tp", core_pairs) for x in out + beyond]
    grad = lay(here, out + beyond + from_core)
    return (new_stream, grad[None])


def solution(mesh):
    placed = (
        P(None, ("img", "ctx"), None),
        P(),
        P(),
        P(None, None, "ctx", "tp"),
        P(("img", "ctx"), "tp"),
        P(None, "tp"),
        P(None, ("img", "ctx"), "tp"),
        P(("img", "ctx")),
    )
    return jax.shard_map(
        shards,
        mesh=mesh,
        in_specs=placed,
        out_specs=(P(("img", "ctx"), "tp"), P(None, ("img", "ctx"), None)),
        check_vma=False,
    )
```

```python
import jax
import jax.numpy as jnp
from jax import lax
from jax.experimental import pallas as pl
from jax.experimental.pallas import tpu as pltpu
from jax.sharding import PartitionSpec as P


BF = jnp.bfloat16
F32 = jnp.float32
FREE = pl.CostEstimate(flops=0, bytes_accessed=0, transcendentals=0)
RING = 4
AWAY = (0, 3, 1, 2)
EARLY = 2


def params(mib):
    return pltpu.CompilerParams(vmem_limit_bytes=mib * 1024 * 1024)


def whole():
    return pl.BlockSpec(memory_space=pltpu.VMEM)


def shape(dims, kind):
    return jax.ShapeDtypeStruct(dims, kind)


def scalars():
    return pl.BlockSpec(memory_space=pltpu.SMEM)


def in_hbm():
    return pl.BlockSpec(memory_space=pltpu.HBM)


def anywhere():
    return pl.BlockSpec(memory_space=pl.ANY)


def eq_hot(shape, dim, index):
    return (lax.broadcasted_iota(jnp.int32, shape, dim) == index).astype(BF)


def window_major(tokens, window):
    n = tokens * window
    row = lax.broadcasted_iota(jnp.int32, (n, n), 0)
    col = lax.broadcasted_iota(jnp.int32, (n, n), 1)
    return (col == (row % tokens) * window + row // tokens).astype(BF)


def patch_major(tokens, window):
    n = tokens * window
    row = lax.broadcasted_iota(jnp.int32, (n, n), 0)
    col = lax.broadcasted_iota(jnp.int32, (n, n), 1)
    return (col == (row % window) * tokens + row // window).astype(BF)


def norm_kernel(here_ref, x_ref, gain_ref, bias_ref, lifted_ref, xw_ref, stat_ref):
    window, width = gain_ref.shape
    tokens = x_ref.shape[0] // window
    full = window * width
    x = jnp.dot(window_major(tokens, window), x_ref[...], preferred_element_type=F32)
    parts = [x[w * tokens : (w + 1) * tokens] for w in range(window)]
    total = sum(jnp.sum(p, axis=1, keepdims=True) for p in parts)
    squares = sum(jnp.sum(p * p, axis=1, keepdims=True) for p in parts)
    mean = total / full
    inv = lax.rsqrt(squares / full - mean * mean + 1e-05)
    lifted = []
    for w, p in enumerate(parts):
        normed = (p - mean) * inv
        lifted.append(
            normed * gain_ref[w : w + 1].astype(F32) + bias_ref[w : w + 1].astype(F32)
        )
        xw_ref[w] = p.astype(BF)
    share = width // (RING * RING)
    for core in range(2):

        @pl.when(here_ref[0] == core)
        def _():
            blocks = [(a, b) for a in range(RING) for b in range(RING)]
            starts = [(a * RING + b if core == 0 else b * RING + a) * share for a, b in blocks]
            lifted_ref[...] = jnp.concatenate(
                [p[:, at : at + share] for at in starts for p in lifted], axis=1
            ).astype(BF)

    lane = lax.broadcasted_iota(jnp.int32, stat_ref.shape, 1)
    stat_ref[...] = jnp.where(lane == 0, mean, inv)


def layer_norm(here, features, gain, bias):
    rows, width = features.shape
    window = gain.shape[0]
    merged = rows // window
    block = 64
    steps = merged // block
    return pl.pallas_call(
        norm_kernel,
        grid_spec=pltpu.PrefetchScalarGridSpec(
            num_scalar_prefetch=1,
            grid=(steps,),
            in_specs=[
                pl.BlockSpec(
                    (block * window, width),
                    lambda i, c: (lax.rem(i + c[0] * (steps // 2), steps), 0),
                ),
                pl.BlockSpec((window, width), lambda i, c: (0, 0)),
                pl.BlockSpec((window, width), lambda i, c: (0, 0)),
            ],
            out_specs=[
                pl.BlockSpec((block, window * width), lambda i, c: (i, 0)),
                pl.BlockSpec((window, block, width), lambda i, c: (0, i, 0)),
                pl.BlockSpec((block, 128), lambda i, c: (i, 0)),
            ],
        ),
        out_shape=[
            shape((merged, window * width), BF),
            shape((window, merged, width), BF),
            shape((merged, 128), F32),
        ],
        compiler_params=params(58),
        cost_estimate=FREE,
        name="layer_norm",
    )(here, features, gain, bias)


def collect_kernel(pos_ref, stream_ref, cot_ref, after_ref, out_ref):
    slots = pos_ref.shape[0]
    rows, width = stream_ref.shape
    cut = width // 2
    pick = eq_hot((slots, rows), 1, pos_ref[...])
    for img in range(2):
        at = slice(img * cut, (img + 1) * cut)
        for place, ref in enumerate((stream_ref, cot_ref)):
            out_ref[img, :, place * cut : (place + 1) * cut] = jnp.dot(
                pick, ref[:, at], preferred_element_type=F32
            ).astype(BF)


def collect(pos, stream, cot, after):
    slots = pos.shape[0]
    rows, width = stream.shape
    return pl.pallas_call(
        collect_kernel,
        in_specs=[whole()] * 3 + [anywhere()],
        out_specs=whole(),
        out_shape=shape((2, slots, width), BF),
        compiler_params=params(20),
        cost_estimate=FREE,
        name="collect",
    )(pos, stream, cot, after)


def unpack_kernel(slot_ref, came_ref, after_ref, base_ref, cot_ref):
    tokens, width = base_ref.shape
    slots = came_ref.shape[0]
    take = eq_hot((tokens, slots), 1, slot_ref[...])
    for start, out_ref in ((0, base_ref), (width, cot_ref)):
        out_ref[...] = jnp.dot(
            take, came_ref[:, start : start + width], preferred_element_type=F32
        ).astype(BF)


def unpack(slot_col, came, after):
    tokens = slot_col.shape[0]
    slots, both = came.shape
    width = both // 2
    outs = [shape((tokens, width), BF)] * 2
    return pl.pallas_call(
        unpack_kernel,
        in_specs=[whole()] * 2 + [anywhere()],
        out_specs=[whole()] * 2,
        out_shape=outs,
        compiler_params=params(12),
        cost_estimate=FREE,
        name="unpack",
    )(slot_col, came, after)


def stack_kernel(here_ref, *refs):
    out_ref, sems = refs[RING:]
    first = jnp.where(here_ref[0] == 0, here_ref[4], here_ref[3])
    copies = [
        pltpu.make_async_copy(ref, out_ref.at[lax.rem(first + away, RING)], sems.at[index])
        for index, (away, ref) in enumerate(zip(AWAY, refs[:RING]))
    ]
    for copy in copies:
        copy.start()
    for copy in copies:
        copy.wait()


def stack(here, blocks):
    rows, width = blocks[0].shape
    return pl.pallas_call(
        stack_kernel,
        in_specs=[scalars()] + [in_hbm()] * RING,
        out_specs=whole(),
        out_shape=shape((RING, rows, width), BF),
        scratch_shapes=[pltpu.SemaphoreType.DMA((RING,))],
        compiler_params=params(6),
        cost_estimate=FREE,
        name="stack",
    )(here, *blocks)


def fetch(here_ref, stacks, held_ref, sems):
    for index, (away, ref) in enumerate(zip(AWAY, stacks)):

        @pl.when(here_ref[0] == 0)
        def _():
            place = lax.rem(here_ref[3] + away, RING)
            pltpu.make_async_copy(ref, held_ref.at[place], sems.at[index]).start()

        @pl.when(here_ref[0] == 1)
        def _():
            place = lax.rem(here_ref[4] + away, RING)
            pltpu.make_async_copy(ref, held_ref.at[:, place], sems.at[index]).start()

    def wait():
        for index, ref in enumerate(stacks):
            pltpu.make_async_copy(ref, held_ref.at[0], sems.at[index]).wait()

    return wait


def product(here_ref, away, stacks, lifted, held_ref, left_ref, sems):
    second = jnp.where(here_ref[0] == 0, here_ref[3], here_ref[4])
    block = left_ref.shape[2]
    rows = lifted[0].shape[0]
    copies = []
    for index, ref in enumerate(stacks):
        place = lax.rem(second + away[index], RING)
        at = pl.ds(pl.multiple_of(place * block, block), block)
        group = [pltpu.make_async_copy(ref, held_ref.at[index], sems.at[index, 0])]
        for i, part in enumerate(lifted):
            to = left_ref.at[index, pl.ds(i * rows, rows)]
            group.append(pltpu.make_async_copy(part.at[:, at], to, sems.at[index, 1 + i]))
        for copy in group:
            copy.start()
        copies.append(group)

    def run(total):
        for index, group in enumerate(copies):
            for copy in group:
                copy.wait()
            part = jnp.dot(
                left_ref[index], held_ref[index].reshape(block, -1), preferred_element_type=F32
            )
            total = part if total is None else total + part
        return total

    return run


def product_scratch(stacks, lifted):
    count = len(stacks)
    rows, depth = lifted[0].shape
    return [
        pltpu.VMEM((count,) + stacks[0].shape, BF),
        pltpu.VMEM((count, len(lifted) * rows, depth // RING), BF),
        pltpu.SemaphoreType.DMA((count, 1 + len(lifted))),
    ]


def multiply_kernel(here_ref, *refs):
    stacks, lifted, (out_ref, *scratch) = refs[:EARLY], refs[EARLY : EARLY + 2], refs[EARLY + 2 :]
    out_ref[...] = product(here_ref, AWAY[:EARLY], stacks, lifted, *scratch)(None)


def multiply(here, stacks, lifted):
    tokens, width = 2 * lifted[0].shape[0], stacks[0].shape[2]
    return pl.pallas_call(
        multiply_kernel,
        in_specs=[scalars()] + [in_hbm()] * (len(stacks) + len(lifted)),
        out_specs=whole(),
        out_shape=shape((tokens, width), F32),
        scratch_shapes=product_scratch(stacks, lifted),
        compiler_params=params(60),
        cost_estimate=FREE,
        name="multiply",
    )(here, *stacks, *lifted)


def merge_kernel(here_ref, ngain_ref, acc_hbm, base_hbm, cot_hbm, *refs):
    stacks, lifted, refs = refs[: RING - EARLY], refs[RING - EARLY : RING - EARLY + 2], refs[RING - EARLY + 2 :]
    visual_ref, state_ref, stat_ref, acc_ref, base_ref, cot_ref, row_sems, *scratch = refs
    run = product(here_ref, AWAY[EARLY:], stacks, lifted, *scratch)
    copies = [
        pltpu.make_async_copy(a, b, row_sems.at[i])
        for i, (a, b) in enumerate(((acc_hbm, acc_ref), (base_hbm, base_ref), (cot_hbm, cot_ref)))
    ]
    for copy in copies:
        copy.start()
    total = run(None)
    for copy in copies:
        copy.wait()
    visual = (acc_ref[...] + total).astype(BF)
    visual_ref[...] = visual
    state = base_ref[...].astype(F32) + visual.astype(F32)
    state_ref[...] = state
    up = ngain_ref[...].astype(F32) * cot_ref[...].astype(F32)
    lane = lax.broadcasted_iota(jnp.int32, (state.shape[0], 128), 1)
    sums = jnp.where(
        lane == 0,
        jnp.sum(state * state, axis=1, keepdims=True),
        jnp.sum(up * state, axis=1, keepdims=True),
    )
    stat_ref[...] = sums.T[: stat_ref.shape[0]]


def merge(here, ngain, acc, base, cot, stacks, lifted):
    tokens, width = base.shape
    outs = [shape((tokens, width), BF), shape((tokens, width), F32), shape((8, tokens), F32)]
    return pl.pallas_call(
        merge_kernel,
        in_specs=[scalars(), whole()] + [in_hbm()] * (3 + len(stacks) + len(lifted)),
        out_specs=[whole()] * 3,
        out_shape=outs,
        scratch_shapes=[
            pltpu.VMEM((tokens, width), F32),
            pltpu.VMEM((tokens, width), BF),
            pltpu.VMEM((tokens, width), BF),
            pltpu.SemaphoreType.DMA((3,)),
        ]
        + product_scratch(stacks, lifted),
        compiler_params=params(24),
        cost_estimate=FREE,
        name="merge",
    )(here, ngain, acc, base, cot, *stacks, *lifted)


def add_kernel(sums_ref, got_ref, near_ref, turned_ref):
    count = sums_ref.shape[1] // 4
    cuts = [
        sums_ref[:, i * count : (i + 1) * count] + got_ref[:, (i ^ 1) * count : ((i ^ 1) + 1) * count]
        for i in range(4)
    ]
    near_ref[...] = jnp.concatenate(cuts, axis=1)
    turned_ref[...] = jnp.concatenate(cuts[2:] + cuts[:2], axis=1)


def add(sums, got):
    return pl.pallas_call(
        add_kernel,
        in_specs=[whole()] * 2,
        out_specs=[whole()] * 2,
        out_shape=[shape(sums.shape, F32)] * 2,
        compiler_params=params(4),
        cost_estimate=FREE,
        name="add",
    )(sums, got)


def pack_kernel(here_ref, slot_ref, visual_ref, after_ref, stay_ref, cross_ref):
    tokens = visual_ref.shape[0]
    slots = stay_ref.shape[0]
    for relative, out_ref in ((0, stay_ref), (1, cross_ref)):
        put = eq_hot((tokens, slots), 1, slot_ref[...] - (here_ref[2] ^ relative) * slots)
        out_ref[...] = lax.dot_general(
            put, visual_ref[...], (((0,), (0,)), ((), ())), preferred_element_type=F32
        ).astype(BF)


def pack(here, slot_col, visual, slots, after):
    tokens, width = visual.shape
    return pl.pallas_call(
        pack_kernel,
        in_specs=[scalars()] + [whole()] * 2 + [anywhere()],
        out_specs=[whole()] * 2,
        out_shape=[shape((slots // 2, width), BF)] * 2,
        compiler_params=params(8),
        cost_estimate=FREE,
        name="pack",
    )(here, slot_col, visual, after)


def braid_kernel(stay_ref, crossed_ref, out_ref):
    count, _, rows, _ = out_ref.shape
    for c in range(count):
        at = slice(c * rows, (c + 1) * rows)
        out_ref[c, 0] = stay_ref[at, :]
        out_ref[c, 1] = crossed_ref[at, :]


def braid(stay, crossed, count):
    rows, width = stay.shape
    return pl.pallas_call(
        braid_kernel,
        in_specs=[whole()] * 2,
        out_specs=whole(),
        out_shape=shape((count, 2, rows // count, width), BF),
        compiler_params=params(6),
        cost_estimate=FREE,
        name="braid",
    )(stay, crossed)


def backward_kernel(full_width, here_ref, ngain_ref, *refs):
    stats, stacks, refs = refs[:RING], refs[RING : 2 * RING], refs[2 * RING :]
    state_hbm, cot_hbm, own_ref, rest_ref, other_ref, other_rest_ref = refs[:6]
    picked_ref, sums_ref, state_ref, cot_ref, held_ref, row_sems, sems = refs[6:]
    row_copies = [
        pltpu.make_async_copy(a, b, row_sems.at[i])
        for i, (a, b) in enumerate(((state_hbm, state_ref), (cot_hbm, cot_ref)))
    ]
    for copy in row_copies:
        copy.start()
    wait_weight = fetch(here_ref, stacks, held_ref, sems)
    tokens = state_ref.shape[0]
    rows = tokens // 2 // RING
    total = stats[0][...]
    for ref in stats[1:]:
        total = total + ref[...]
    sums_ref[...] = total.T
    far, img = here_ref[1], here_ref[2]
    gain = ngain_ref[...].astype(F32)
    for copy in row_copies:
        copy.wait()
    for core in range(2):
        for away in range(RING):
            there = lax.rem(2 * far + img + away, RING)
            partner = lax.rem(there + img, 2)
            begin = partner * (tokens // 2) + core * (tokens // 4) + (there // 2) * (tokens // 8)
            at = pl.ds(pl.multiple_of(begin, rows), rows)
            sums = sums_ref[at, :]
            inv = lax.rsqrt(sums[:, 0:1] / full_width + 1e-06)
            inner = sums[:, 1:2] / full_width
            up = gain * cot_ref[at, :].astype(F32)
            grad = inv * up - state_ref[at, :] * (inv * inv * inv * inner)
            to = (core * RING + away) * rows
            picked_ref[to : to + rows, :] = grad.astype(BF)
    depth = own_ref.shape[1]
    wait_weight()
    block = depth // RING
    for step in range(RING):
        cols = slice(step * block, (step + 1) * block)
        both = lax.dot_general(
            picked_ref[...],
            held_ref[step].reshape(block, -1),
            (((1,), (1,)), ((), ())),
            preferred_element_type=F32,
        )
        start = 0
        for out_ref in (own_ref, rest_ref, other_ref, other_rest_ref):
            count = out_ref.shape[0]
            out_ref[:, cols] = both[start : start + count].astype(BF)
            start += count


def backward(here, state, cot, ngain, stats, stacks, full_width):
    tokens, width = state.shape
    depth = RING * stacks[0].shape[0] * stacks[0].shape[1]
    return pl.pallas_call(
        lambda *refs: backward_kernel(full_width, *refs),
        in_specs=[scalars()] + [whole()] * (1 + RING) + [in_hbm()] * (RING + 2),
        out_specs=[whole()] * 4,
        out_shape=[shape((n * tokens // 8, depth), BF) for n in (1, RING - 1, 1, RING - 1)],
        scratch_shapes=[
            pltpu.VMEM((tokens, width), BF),
            pltpu.VMEM((tokens, 8), F32),
            pltpu.VMEM((tokens, width), F32),
            pltpu.VMEM((tokens, width), BF),
            pltpu.VMEM((RING,) + stacks[0].shape, BF),
            pltpu.SemaphoreType.DMA((2,)),
            pltpu.SemaphoreType.DMA((RING,)),
        ],
        compiler_params=params(24),
        cost_estimate=FREE,
        name="backward",
    )(here, ngain, *stats, *stacks, state, cot)


def both(own_ref, got_ref, start, count):
    at = slice(start, start + count)
    return (own_ref[at, :].astype(F32) + got_ref[at, :].astype(F32)).astype(BF)


def pair_kernel(own_ref, got_ref, after_ref, next_ref, last_ref):
    rows = own_ref.shape[0] // (RING - 1)
    half = rows // 2
    next_ref[:half] = both(own_ref, got_ref, rows, half)
    next_ref[half:] = both(own_ref, got_ref, half, half)
    last_ref[:half] = both(own_ref, got_ref, rows + half, half)
    last_ref[half:] = both(own_ref, got_ref, 2 * rows, half)


def pair(own, got, after):
    rows, depth = got.shape[0] // (RING - 1), got.shape[1]
    return pl.pallas_call(
        pair_kernel,
        in_specs=[whole()] * 2 + [anywhere()],
        out_specs=[whole()] * 2,
        out_shape=[shape((rows, depth), BF)] * 2,
        compiler_params=params(8),
        cost_estimate=FREE,
        name="pair",
    )(own, got, after)


def relay_kernel(own_ref, got_ref, from_last_ref, from_next_ref, next_ref, last_ref):
    half = next_ref.shape[0]
    rows = 2 * half
    for start, came_ref, out_ref in (
        (0, from_last_ref, next_ref),
        (2 * rows + half, from_next_ref, last_ref),
    ):
        kept = both(own_ref, got_ref, start, half).astype(F32)
        out_ref[...] = (kept + came_ref[:half].astype(F32)).astype(BF)


def relay(own, got, from_last, from_next):
    rows, depth = from_last.shape
    return pl.pallas_call(
        relay_kernel,
        in_specs=[whole()] * 4,
        out_specs=[whole()] * 2,
        out_shape=[shape((rows // 2, depth), BF)] * 2,
        compiler_params=params(8),
        cost_estimate=FREE,
        name="relay",
    )(own, got, from_last, from_next)


def finish_kernel(here_ref, own_ref, got_ref, early_ref, late_ref, xw_ref, stat_ref, gain_ref, out_ref):
    window, tokens, width = xw_ref.shape
    full = window * width
    mean = stat_ref[:, 0:1]
    inv = stat_ref[:, 1:2]
    lifted = own_ref[...].astype(F32) + got_ref[...].astype(F32)
    lifted = lifted + early_ref[...].astype(F32) + late_ref[...].astype(F32)
    share = width // (RING * RING)
    scaled = []
    total = 0.0
    inner = 0.0
    for w in range(window):
        g = jnp.concatenate(
            [lifted[:, at : at + share] for at in range(w * share, full, window * share)], axis=1
        ) * gain_ref[w : w + 1].astype(F32)
        normed = (xw_ref[w].astype(F32) - mean) * inv
        total = total + jnp.sum(g, axis=1, keepdims=True)
        inner = inner + jnp.sum(g * normed, axis=1, keepdims=True)
        scaled.append((g, normed))
    total = total / full
    inner = inner / full
    rows = jnp.concatenate(
        [(inv * (g - total - normed * inner)).astype(BF) for g, normed in scaled], axis=0
    )
    out_ref[...] = jnp.dot(
        patch_major(tokens, window), rows, preferred_element_type=F32
    ).astype(BF)


def finish(here, step, own, got, early, late, xw, stat, gain):
    tokens, depth = late.shape
    window, width = gain.shape
    same = pl.BlockSpec((tokens, depth), lambda i, h: (step, 0))
    second = pl.BlockSpec((tokens, depth), lambda i, h: (1, 0))
    only = pl.BlockSpec((tokens, depth), lambda i, h: (0, 0))
    return pl.pallas_call(
        finish_kernel,
        grid_spec=pltpu.PrefetchScalarGridSpec(
            num_scalar_prefetch=1,
            grid=(1,),
            in_specs=[same, same, second, only]
            + [
                pl.BlockSpec((window, tokens, width), lambda i, h: (0, h[1] * 2 + step, 0)),
                pl.BlockSpec((tokens, 128), lambda i, h: (h[1] * 2 + step, 0)),
                pl.BlockSpec((window, width), lambda i, h: (0, 0)),
            ],
            out_specs=pl.BlockSpec((tokens * window, width), lambda i, h: (0, 0)),
        ),
        out_shape=shape((tokens * window, width), BF),
        compiler_params=params(12),
        cost_estimate=FREE,
        name="finish",
    )(here, own, got, early, late, xw, stat, gain)


def place_kernel(here_ref, pos_ref, came_ref, stream_ref, out_ref):
    rows, width = stream_ref.shape
    cut = width // 2
    slots = pos_ref.shape[0]
    put = eq_hot((slots, rows), 1, pos_ref[...])
    for relative in range(2):
        start = pl.multiple_of((here_ref[2] ^ relative) * cut, cut)
        at = pl.ds(start, cut)
        out_ref[:, at] = (
            stream_ref[:, at].astype(F32)
            + lax.dot_general(
                put,
                came_ref[:, relative].reshape(slots, cut),
                (((0,), (0,)), ((), ())),
                preferred_element_type=F32,
            )
        ).astype(BF)


def place(here, pos, came, stream):
    rows, width = stream.shape
    return pl.pallas_call(
        place_kernel,
        in_specs=[scalars()] + [whole()] * 3,
        out_specs=whole(),
        out_shape=shape((rows, width), BF),
        compiler_params=params(12),
        cost_estimate=FREE,
        name="place",
    )(here, pos, came, stream)


def lay_kernel(here_ref, *refs):
    blocks, (out_ref, sems) = refs[:-2], refs[-2:]
    rows = blocks[0].shape[0]
    copies = []
    for index, ref in enumerate(blocks):
        quarter, step = index // 2, index % 2
        owner = 2 * (here_ref[0] ^ (quarter // 2)) + (here_ref[1] ^ (quarter % 2))
        start = pl.multiple_of((2 * owner + step) * rows, rows)
        copies.append(pltpu.make_async_copy(ref, out_ref.at[pl.ds(start, rows)], sems.at[index]))
    for copy in copies:
        copy.start()
    for copy in copies:
        copy.wait()


def lay(here, blocks):
    rows, width = blocks[0].shape
    return pl.pallas_call(
        lay_kernel,
        in_specs=[scalars()] + [whole()] * len(blocks),
        out_specs=anywhere(),
        out_shape=shape((len(blocks) * rows, width), BF),
        scratch_shapes=[pltpu.SemaphoreType.DMA((len(blocks),))],
        compiler_params=params(4),
        cost_estimate=FREE,
        name="lay",
    )(here, *blocks)


def shards(features, ln_gain, ln_bias, projection, stream, norm_gain, cotangent, slots):
    n_img = lax.axis_size("img")
    n_ctx = lax.axis_size("ctx")
    n_tp = lax.axis_size("tp")
    merged = slots.shape[0]
    tok_rows, width = stream.shape
    owners = n_img * n_ctx
    capacity = 2 * merged // owners
    slot_count = owners * capacity
    full_width = width * n_tp
    cut = width // n_img

    img = lax.axis_index("img").astype(jnp.int32)
    tp = lax.axis_index("tp").astype(jnp.int32)
    core, far_half = tp % 2, tp // 2
    z, y = lax.axis_index("ctx") // RING, lax.axis_index("ctx") % RING
    here = jnp.stack([core, far_half, img, z, y]).astype(jnp.int32)

    flip = [(i, 1 - i) for i in range(n_img)]
    core_pairs = [(t, t ^ 1) for t in range(n_tp)]
    far_pairs = [(t, t ^ 2) for t in range(n_tp)]

    def along_x(array, by):
        pairs = []
        for i in range(n_img):
            for t in range(n_tp):
                x = (2 * (t // 2) + i + by) % RING
                pairs.append((i * n_tp + t, (x % 2) * n_tp + 2 * (x // 2) + t % 2))
        return lax.ppermute(array, ("img", "tp"), pairs)

    def along_ctx(array, axis, by):
        pairs = []
        for c in range(n_ctx):
            for t in range(n_tp):
                z, y = c // RING, c % RING
                if t % 2 == axis:
                    y = (y + by) % RING
                else:
                    z = (z + by) % RING
                pairs.append((c * n_tp + t, (z * RING + y) * n_tp + t))
        return lax.ppermute(array, ("ctx", "tp"), pairs)

    slots = jnp.roll(slots, -core * (merged // 2))
    target = slots // tok_rows
    ids = jnp.arange(merged)
    earlier = (target[:, None] == target[None, :]) & (ids[:, None] < ids[None, :])
    rank = jnp.sum(earlier.astype(jnp.int32), axis=0)
    slot = target * capacity + rank
    local = slots - target * tok_rows
    packed = jnp.max(
        jnp.where(jnp.arange(slot_count)[:, None] == slot[None, :], local[None, :], -1), axis=1
    )
    asked = lax.all_to_all(
        packed.reshape(owners, capacity), ("img", "ctx"), split_axis=0, concat_axis=0, tiled=True
    )
    columns = lax.dynamic_slice_in_dim(projection[0], img * cut, cut, axis=2).reshape(-1, cut)
    moves = (1, -1, 2)
    near_blocks = [along_ctx(columns, 0, by) for by in moves]
    paired = target * (n_img * capacity) + rank + img * capacity
    partner = lax.ppermute(paired, "img", flip)
    gain = ln_gain[0]
    lifted, xw, stat = layer_norm(here, features[0], gain, ln_bias[0])
    asked, lifted, stat, near_blocks, partner = lax.optimization_barrier(
        (asked, lifted, stat, near_blocks, partner)
    )
    paired = jnp.concatenate([paired, partner]).reshape(-1, 1)

    first = stack(here, [columns] + near_blocks)
    asked, first, lifted = lax.optimization_barrier((asked, first, lifted))

    asked = asked.reshape(n_img, n_ctx, capacity).transpose(1, 0, 2)
    asked = asked.reshape(slot_count, 1)
    held = collect(asked, stream, cotangent[0], first)
    came = lax.all_to_all(
        held.reshape(owners, n_img * capacity, width),
        ("img", "ctx"), split_axis=0, concat_axis=0, tiled=True,
    ).reshape(n_img * slot_count, width)

    stacks = [first] + [along_ctx(first, 1, by) for by in moves[:2]]
    stacks.append(along_ctx(stacks[1], 1, 1))

    pairs = []
    for i in range(n_img):
        for t in range(n_tp):
            x = (2 * (t // 2) + i + (1 if t % 2 == 0 else -1)) % RING
            pairs.append((i * n_tp + t, (x % 2) * n_tp + 2 * (x // 2) + t % 2))
    lifted = [lifted, lax.ppermute(lifted, ("img", "tp"), pairs)]

    own_gain = lax.dynamic_slice_in_dim(norm_gain, img * cut, cut, axis=1)
    acc = multiply(here, stacks[:EARLY], lifted)
    base, cot = unpack(paired, came, acc)
    visual, state, sums = merge(here, own_gain, acc, base, cot, stacks[EARLY:], lifted)

    near, turned = add(sums, lax.ppermute(sums, "tp", core_pairs))
    stats = [near] + [along_x(near if by == 2 else turned, by) for by in (1, 2, 3)]
    stay, cross = pack(here, paired, visual, n_img * slot_count, near)
    cross, stats = lax.optimization_barrier((cross, stats))
    crossed = lax.ppermute(cross, "img", flip)

    own, rest, other, other_rest = backward(here, state, cot, own_gain, stats, stacks, full_width)
    own, rest, other, other_rest, crossed = lax.optimization_barrier(
        (own, rest, other, other_rest, crossed)
    )
    got_rest = lax.ppermute(other_rest, "tp", core_pairs)
    got = lax.ppermute(other, "tp", core_pairs)
    to_next, to_last = pair(rest, got_rest, crossed)
    from_last, from_next = along_x(to_next, 1), along_x(to_last, -1)
    to_next, to_last = relay(rest, got_rest, from_last, from_next)
    late_last, late_next = along_x(to_next, 1), along_x(to_last, -1)

    send = braid(stay, crossed, n_ctx)
    arrived = lax.all_to_all(send, "ctx", split_axis=0, concat_axis=0, tiled=True)
    new_stream = place(here, asked, arrived, stream)

    out = [
        finish(here, step, own, got, early, late, xw, stat, gain)
        for step, (early, late) in enumerate(((from_next, late_last), (from_last, late_next)))
    ]
    beyond = [lax.ppermute(x, "tp", far_pairs) for x in out]
    beyond[1], new_stream = lax.optimization_barrier((beyond[1], new_stream))
    from_core = [lax.ppermute(x, "tp", core_pairs) for x in out + beyond]
    grad = lay(here, out + beyond + from_core)
    return (new_stream, grad[None])


def solution(mesh):
    placed = (
        P(None, ("img", "ctx"), None),
        P(),
        P(),
        P(None, None, "ctx", "tp"),
        P(("img", "ctx"), "tp"),
        P(None, "tp"),
        P(None, ("img", "ctx"), "tp"),
        P(("img", "ctx")),
    )
    return jax.shard_map(
        shards,
        mesh=mesh,
        in_specs=placed,
        out_specs=(P(("img", "ctx"), "tp"), P(None, ("img", "ctx"), None)),
        check_vma=False,
    )
```

```python
import jax
import jax.numpy as jnp
from jax import lax
from jax.experimental import pallas as pl
from jax.experimental.pallas import tpu as pltpu
from jax.sharding import PartitionSpec as P


BF = jnp.bfloat16
F32 = jnp.float32
FREE = pl.CostEstimate(flops=0, bytes_accessed=0, transcendentals=0)
RING = 4
AWAY = (0, 3, 1, 2)
EARLY = 2


def params(mib):
    return pltpu.CompilerParams(vmem_limit_bytes=mib * 1024 * 1024)


def whole():
    return pl.BlockSpec(memory_space=pltpu.VMEM)


def shape(dims, kind):
    return jax.ShapeDtypeStruct(dims, kind)


def scalars():
    return pl.BlockSpec(memory_space=pltpu.SMEM)


def in_hbm():
    return pl.BlockSpec(memory_space=pltpu.HBM)


def anywhere():
    return pl.BlockSpec(memory_space=pl.ANY)


def eq_hot(shape, dim, index):
    return (lax.broadcasted_iota(jnp.int32, shape, dim) == index).astype(BF)


def window_major(tokens, window):
    n = tokens * window
    row = lax.broadcasted_iota(jnp.int32, (n, n), 0)
    col = lax.broadcasted_iota(jnp.int32, (n, n), 1)
    return (col == (row % tokens) * window + row // tokens).astype(BF)


def patch_major(tokens, window):
    n = tokens * window
    row = lax.broadcasted_iota(jnp.int32, (n, n), 0)
    col = lax.broadcasted_iota(jnp.int32, (n, n), 1)
    return (col == (row % window) * tokens + row // window).astype(BF)


def norm_kernel(here_ref, x_ref, gain_ref, bias_ref, lifted_ref, xw_ref, stat_ref):
    window, width = gain_ref.shape
    tokens = x_ref.shape[0] // window
    full = window * width
    x = jnp.dot(window_major(tokens, window), x_ref[...], preferred_element_type=F32)
    parts = [x[w * tokens : (w + 1) * tokens] for w in range(window)]
    total = sum(jnp.sum(p, axis=1, keepdims=True) for p in parts)
    squares = sum(jnp.sum(p * p, axis=1, keepdims=True) for p in parts)
    mean = total / full
    inv = lax.rsqrt(squares / full - mean * mean + 1e-05)
    lifted = []
    for w, p in enumerate(parts):
        normed = (p - mean) * inv
        lifted.append(
            normed * gain_ref[w : w + 1].astype(F32) + bias_ref[w : w + 1].astype(F32)
        )
        xw_ref[w] = p.astype(BF)
    share = width // (RING * RING)
    for core in range(2):

        @pl.when(here_ref[0] == core)
        def _():
            blocks = [(a, b) for a in range(RING) for b in range(RING)]
            starts = [(a * RING + b if core == 0 else b * RING + a) * share for a, b in blocks]
            lifted_ref[...] = jnp.concatenate(
                [p[:, at : at + share] for at in starts for p in lifted], axis=1
            ).astype(BF)

    lane = lax.broadcasted_iota(jnp.int32, stat_ref.shape, 1)
    stat_ref[...] = jnp.where(lane == 0, mean, inv)


def layer_norm(here, features, gain, bias):
    rows, width = features.shape
    window = gain.shape[0]
    merged = rows // window
    block = 32
    steps = merged // block
    return pl.pallas_call(
        norm_kernel,
        grid_spec=pltpu.PrefetchScalarGridSpec(
            num_scalar_prefetch=1,
            grid=(steps,),
            in_specs=[
                pl.BlockSpec(
                    (block * window, width),
                    lambda i, c: (lax.rem(i + c[0] * (steps // 2), steps), 0),
                ),
                pl.BlockSpec((window, width), lambda i, c: (0, 0)),
                pl.BlockSpec((window, width), lambda i, c: (0, 0)),
            ],
            out_specs=[
                pl.BlockSpec((block, window * width), lambda i, c: (i, 0)),
                pl.BlockSpec((window, block, width), lambda i, c: (0, i, 0)),
                pl.BlockSpec((block, 128), lambda i, c: (i, 0)),
            ],
        ),
        out_shape=[
            shape((merged, window * width), BF),
            shape((window, merged, width), BF),
            shape((merged, 128), F32),
        ],
        compiler_params=params(58),
        cost_estimate=FREE,
        name="layer_norm",
    )(here, features, gain, bias)


def collect_kernel(pos_ref, stream_ref, cot_ref, after_ref, out_ref):
    slots = pos_ref.shape[0]
    rows, width = stream_ref.shape
    cut = width // 2
    pick = eq_hot((slots, rows), 1, pos_ref[...])
    for img in range(2):
        at = slice(img * cut, (img + 1) * cut)
        for place, ref in enumerate((stream_ref, cot_ref)):
            out_ref[img, :, place * cut : (place + 1) * cut] = jnp.dot(
                pick, ref[:, at], preferred_element_type=F32
            ).astype(BF)


def collect(pos, stream, cot, after):
    slots = pos.shape[0]
    rows, width = stream.shape
    return pl.pallas_call(
        collect_kernel,
        in_specs=[whole()] * 3 + [anywhere()],
        out_specs=whole(),
        out_shape=shape((2, slots, width), BF),
        compiler_params=params(20),
        cost_estimate=FREE,
        name="collect",
    )(pos, stream, cot, after)


def unpack_kernel(slot_ref, came_ref, after_ref, base_ref, cot_ref):
    tokens, width = base_ref.shape
    slots = came_ref.shape[0]
    take = eq_hot((tokens, slots), 1, slot_ref[...])
    for start, out_ref in ((0, base_ref), (width, cot_ref)):
        out_ref[...] = jnp.dot(
            take, came_ref[:, start : start + width], preferred_element_type=F32
        ).astype(BF)


def unpack(slot_col, came, after):
    tokens = slot_col.shape[0]
    slots, both = came.shape
    width = both // 2
    outs = [shape((tokens, width), BF)] * 2
    return pl.pallas_call(
        unpack_kernel,
        in_specs=[whole()] * 2 + [anywhere()],
        out_specs=[whole()] * 2,
        out_shape=outs,
        compiler_params=params(12),
        cost_estimate=FREE,
        name="unpack",
    )(slot_col, came, after)


def stack_kernel(here_ref, *refs):
    out_ref, sems = refs[RING:]
    first = jnp.where(here_ref[0] == 0, here_ref[4], here_ref[3])
    copies = [
        pltpu.make_async_copy(ref, out_ref.at[lax.rem(first + away, RING)], sems.at[index])
        for index, (away, ref) in enumerate(zip(AWAY, refs[:RING]))
    ]
    for copy in copies:
        copy.start()
    for copy in copies:
        copy.wait()


def stack(here, blocks):
    rows, width = blocks[0].shape
    return pl.pallas_call(
        stack_kernel,
        in_specs=[scalars()] + [in_hbm()] * RING,
        out_specs=whole(),
        out_shape=shape((RING, rows, width), BF),
        scratch_shapes=[pltpu.SemaphoreType.DMA((RING,))],
        compiler_params=params(6),
        cost_estimate=FREE,
        name="stack",
    )(here, *blocks)


def fetch(here_ref, stacks, held_ref, sems):
    for index, (away, ref) in enumerate(zip(AWAY, stacks)):

        @pl.when(here_ref[0] == 0)
        def _():
            place = lax.rem(here_ref[3] + away, RING)
            pltpu.make_async_copy(ref, held_ref.at[place], sems.at[index]).start()

        @pl.when(here_ref[0] == 1)
        def _():
            place = lax.rem(here_ref[4] + away, RING)
            pltpu.make_async_copy(ref, held_ref.at[:, place], sems.at[index]).start()

    def wait():
        for index, ref in enumerate(stacks):
            pltpu.make_async_copy(ref, held_ref.at[0], sems.at[index]).wait()

    return wait


def product(here_ref, away, stacks, lifted, held_ref, left_ref, sems):
    second = jnp.where(here_ref[0] == 0, here_ref[3], here_ref[4])
    block = left_ref.shape[2]
    rows = lifted[0].shape[0]
    copies = []
    for index, ref in enumerate(stacks):
        place = lax.rem(second + away[index], RING)
        at = pl.ds(pl.multiple_of(place * block, block), block)
        group = [pltpu.make_async_copy(ref, held_ref.at[index], sems.at[index, 0])]
        for i, part in enumerate(lifted):
            to = left_ref.at[index, pl.ds(i * rows, rows)]
            group.append(pltpu.make_async_copy(part.at[:, at], to, sems.at[index, 1 + i]))
        for copy in group:
            copy.start()
        copies.append(group)

    def run(total):
        for index, group in enumerate(copies):
            for copy in group:
                copy.wait()
            part = jnp.dot(
                left_ref[index], held_ref[index].reshape(block, -1), preferred_element_type=F32
            )
            total = part if total is None else total + part
        return total

    return run


def product_scratch(stacks, lifted):
    count = len(stacks)
    rows, depth = lifted[0].shape
    return [
        pltpu.VMEM((count,) + stacks[0].shape, BF),
        pltpu.VMEM((count, len(lifted) * rows, depth // RING), BF),
        pltpu.SemaphoreType.DMA((count, 1 + len(lifted))),
    ]


def multiply_kernel(here_ref, *refs):
    stacks, lifted, (out_ref, *scratch) = refs[:EARLY], refs[EARLY : EARLY + 2], refs[EARLY + 2 :]
    out_ref[...] = product(here_ref, AWAY[:EARLY], stacks, lifted, *scratch)(None)


def multiply(here, stacks, lifted):
    tokens, width = 2 * lifted[0].shape[0], stacks[0].shape[2]
    return pl.pallas_call(
        multiply_kernel,
        in_specs=[scalars()] + [in_hbm()] * (len(stacks) + len(lifted)),
        out_specs=whole(),
        out_shape=shape((tokens, width), F32),
        scratch_shapes=product_scratch(stacks, lifted),
        compiler_params=params(60),
        cost_estimate=FREE,
        name="multiply",
    )(here, *stacks, *lifted)


def merge_kernel(here_ref, ngain_ref, acc_hbm, base_hbm, cot_hbm, *refs):
    stacks, lifted, refs = refs[: RING - EARLY], refs[RING - EARLY : RING - EARLY + 2], refs[RING - EARLY + 2 :]
    visual_ref, state_ref, stat_ref, acc_ref, base_ref, cot_ref, row_sems, *scratch = refs
    run = product(here_ref, AWAY[EARLY:], stacks, lifted, *scratch)
    copies = [
        pltpu.make_async_copy(a, b, row_sems.at[i])
        for i, (a, b) in enumerate(((acc_hbm, acc_ref), (base_hbm, base_ref), (cot_hbm, cot_ref)))
    ]
    for copy in copies:
        copy.start()
    total = run(None)
    for copy in copies:
        copy.wait()
    visual = (acc_ref[...] + total).astype(BF)
    visual_ref[...] = visual
    state = base_ref[...].astype(F32) + visual.astype(F32)
    state_ref[...] = state
    up = ngain_ref[...].astype(F32) * cot_ref[...].astype(F32)
    lane = lax.broadcasted_iota(jnp.int32, (state.shape[0], 128), 1)
    sums = jnp.where(
        lane == 0,
        jnp.sum(state * state, axis=1, keepdims=True),
        jnp.sum(up * state, axis=1, keepdims=True),
    )
    stat_ref[...] = sums.T[: stat_ref.shape[0]]


def merge(here, ngain, acc, base, cot, stacks, lifted):
    tokens, width = base.shape
    outs = [shape((tokens, width), BF), shape((tokens, width), F32), shape((8, tokens), F32)]
    return pl.pallas_call(
        merge_kernel,
        in_specs=[scalars(), whole()] + [in_hbm()] * (3 + len(stacks) + len(lifted)),
        out_specs=[whole()] * 3,
        out_shape=outs,
        scratch_shapes=[
            pltpu.VMEM((tokens, width), F32),
            pltpu.VMEM((tokens, width), BF),
            pltpu.VMEM((tokens, width), BF),
            pltpu.SemaphoreType.DMA((3,)),
        ]
        + product_scratch(stacks, lifted),
        compiler_params=params(24),
        cost_estimate=FREE,
        name="merge",
    )(here, ngain, acc, base, cot, *stacks, *lifted)


def add_kernel(sums_ref, got_ref, near_ref, turned_ref):
    count = sums_ref.shape[1] // 4
    cuts = [
        sums_ref[:, i * count : (i + 1) * count] + got_ref[:, (i ^ 1) * count : ((i ^ 1) + 1) * count]
        for i in range(4)
    ]
    near_ref[...] = jnp.concatenate(cuts, axis=1)
    turned_ref[...] = jnp.concatenate(cuts[2:] + cuts[:2], axis=1)


def add(sums, got):
    return pl.pallas_call(
        add_kernel,
        in_specs=[whole()] * 2,
        out_specs=[whole()] * 2,
        out_shape=[shape(sums.shape, F32)] * 2,
        compiler_params=params(4),
        cost_estimate=FREE,
        name="add",
    )(sums, got)


def pack_kernel(here_ref, slot_ref, visual_ref, after_ref, stay_ref, cross_ref):
    tokens = visual_ref.shape[0]
    slots = stay_ref.shape[0]
    for relative, out_ref in ((0, stay_ref), (1, cross_ref)):
        put = eq_hot((tokens, slots), 1, slot_ref[...] - (here_ref[2] ^ relative) * slots)
        out_ref[...] = lax.dot_general(
            put, visual_ref[...], (((0,), (0,)), ((), ())), preferred_element_type=F32
        ).astype(BF)


def pack(here, slot_col, visual, slots, after):
    tokens, width = visual.shape
    return pl.pallas_call(
        pack_kernel,
        in_specs=[scalars()] + [whole()] * 2 + [anywhere()],
        out_specs=[whole()] * 2,
        out_shape=[shape((slots // 2, width), BF)] * 2,
        compiler_params=params(8),
        cost_estimate=FREE,
        name="pack",
    )(here, slot_col, visual, after)


def braid_kernel(stay_ref, crossed_ref, out_ref):
    count, _, rows, _ = out_ref.shape
    for c in range(count):
        at = slice(c * rows, (c + 1) * rows)
        out_ref[c, 0] = stay_ref[at, :]
        out_ref[c, 1] = crossed_ref[at, :]


def braid(stay, crossed, count):
    rows, width = stay.shape
    return pl.pallas_call(
        braid_kernel,
        in_specs=[whole()] * 2,
        out_specs=whole(),
        out_shape=shape((count, 2, rows // count, width), BF),
        compiler_params=params(6),
        cost_estimate=FREE,
        name="braid",
    )(stay, crossed)


def backward_kernel(full_width, here_ref, ngain_ref, *refs):
    stats, stacks, refs = refs[:RING], refs[RING : 2 * RING], refs[2 * RING :]
    state_hbm, cot_hbm, own_ref, rest_ref, other_ref, other_rest_ref = refs[:6]
    picked_ref, sums_ref, state_ref, cot_ref, held_ref, row_sems, sems = refs[6:]
    row_copies = [
        pltpu.make_async_copy(a, b, row_sems.at[i])
        for i, (a, b) in enumerate(((state_hbm, state_ref), (cot_hbm, cot_ref)))
    ]
    for copy in row_copies:
        copy.start()
    wait_weight = fetch(here_ref, stacks, held_ref, sems)
    tokens = state_ref.shape[0]
    rows = tokens // 2 // RING
    total = stats[0][...]
    for ref in stats[1:]:
        total = total + ref[...]
    sums_ref[...] = total.T
    far, img = here_ref[1], here_ref[2]
    gain = ngain_ref[...].astype(F32)
    for copy in row_copies:
        copy.wait()
    for core in range(2):
        for away in range(RING):
            there = lax.rem(2 * far + img + away, RING)
            partner = lax.rem(there + img, 2)
            begin = partner * (tokens // 2) + core * (tokens // 4) + (there // 2) * (tokens // 8)
            at = pl.ds(pl.multiple_of(begin, rows), rows)
            sums = sums_ref[at, :]
            inv = lax.rsqrt(sums[:, 0:1] / full_width + 1e-06)
            inner = sums[:, 1:2] / full_width
            up = gain * cot_ref[at, :].astype(F32)
            grad = inv * up - state_ref[at, :] * (inv * inv * inv * inner)
            to = (core * RING + away) * rows
            picked_ref[to : to + rows, :] = grad.astype(BF)
    depth = own_ref.shape[1]
    wait_weight()
    block = depth // RING
    for step in range(RING):
        cols = slice(step * block, (step + 1) * block)
        both = lax.dot_general(
            picked_ref[...],
            held_ref[step].reshape(block, -1),
            (((1,), (1,)), ((), ())),
            preferred_element_type=F32,
        )
        start = 0
        for out_ref in (own_ref, rest_ref, other_ref, other_rest_ref):
            count = out_ref.shape[0]
            out_ref[:, cols] = both[start : start + count].astype(BF)
            start += count


def backward(here, state, cot, ngain, stats, stacks, full_width):
    tokens, width = state.shape
    depth = RING * stacks[0].shape[0] * stacks[0].shape[1]
    return pl.pallas_call(
        lambda *refs: backward_kernel(full_width, *refs),
        in_specs=[scalars()] + [whole()] * (1 + RING) + [in_hbm()] * (RING + 2),
        out_specs=[whole()] * 4,
        out_shape=[shape((n * tokens // 8, depth), BF) for n in (1, RING - 1, 1, RING - 1)],
        scratch_shapes=[
            pltpu.VMEM((tokens, width), BF),
            pltpu.VMEM((tokens, 8), F32),
            pltpu.VMEM((tokens, width), F32),
            pltpu.VMEM((tokens, width), BF),
            pltpu.VMEM((RING,) + stacks[0].shape, BF),
            pltpu.SemaphoreType.DMA((2,)),
            pltpu.SemaphoreType.DMA((RING,)),
        ],
        compiler_params=params(24),
        cost_estimate=FREE,
        name="backward",
    )(here, ngain, *stats, *stacks, state, cot)


def both(own_ref, got_ref, start, count):
    at = slice(start, start + count)
    return (own_ref[at, :].astype(F32) + got_ref[at, :].astype(F32)).astype(BF)


def pair_kernel(own_ref, got_ref, after_ref, next_ref, last_ref):
    rows = own_ref.shape[0] // (RING - 1)
    half = rows // 2
    next_ref[:half] = both(own_ref, got_ref, rows, half)
    next_ref[half:] = both(own_ref, got_ref, half, half)
    last_ref[:half] = both(own_ref, got_ref, rows + half, half)
    last_ref[half:] = both(own_ref, got_ref, 2 * rows, half)


def pair(own, got, after):
    rows, depth = got.shape[0] // (RING - 1), got.shape[1]
    return pl.pallas_call(
        pair_kernel,
        in_specs=[whole()] * 2 + [anywhere()],
        out_specs=[whole()] * 2,
        out_shape=[shape((rows, depth), BF)] * 2,
        compiler_params=params(8),
        cost_estimate=FREE,
        name="pair",
    )(own, got, after)


def relay_kernel(own_ref, got_ref, from_last_ref, from_next_ref, next_ref, last_ref):
    half = next_ref.shape[0]
    rows = 2 * half
    for start, came_ref, out_ref in (
        (0, from_last_ref, next_ref),
        (2 * rows + half, from_next_ref, last_ref),
    ):
        kept = both(own_ref, got_ref, start, half).astype(F32)
        out_ref[...] = (kept + came_ref[:half].astype(F32)).astype(BF)


def relay(own, got, from_last, from_next):
    rows, depth = from_last.shape
    return pl.pallas_call(
        relay_kernel,
        in_specs=[whole()] * 4,
        out_specs=[whole()] * 2,
        out_shape=[shape((rows // 2, depth), BF)] * 2,
        compiler_params=params(8),
        cost_estimate=FREE,
        name="relay",
    )(own, got, from_last, from_next)


def finish_kernel(here_ref, own_ref, got_ref, early_ref, late_ref, xw_ref, stat_ref, gain_ref, out_ref):
    window, tokens, width = xw_ref.shape
    full = window * width
    mean = stat_ref[:, 0:1]
    inv = stat_ref[:, 1:2]
    lifted = own_ref[...].astype(F32) + got_ref[...].astype(F32)
    lifted = lifted + early_ref[...].astype(F32) + late_ref[...].astype(F32)
    share = width // (RING * RING)
    scaled = []
    total = 0.0
    inner = 0.0
    for w in range(window):
        g = jnp.concatenate(
            [lifted[:, at : at + share] for at in range(w * share, full, window * share)], axis=1
        ) * gain_ref[w : w + 1].astype(F32)
        normed = (xw_ref[w].astype(F32) - mean) * inv
        total = total + jnp.sum(g, axis=1, keepdims=True)
        inner = inner + jnp.sum(g * normed, axis=1, keepdims=True)
        scaled.append((g, normed))
    total = total / full
    inner = inner / full
    rows = jnp.concatenate(
        [(inv * (g - total - normed * inner)).astype(BF) for g, normed in scaled], axis=0
    )
    out_ref[...] = jnp.dot(
        patch_major(tokens, window), rows, preferred_element_type=F32
    ).astype(BF)


def finish(here, step, own, got, early, late, xw, stat, gain):
    tokens, depth = late.shape
    window, width = gain.shape
    same = pl.BlockSpec((tokens, depth), lambda i, h: (step, 0))
    second = pl.BlockSpec((tokens, depth), lambda i, h: (1, 0))
    only = pl.BlockSpec((tokens, depth), lambda i, h: (0, 0))
    return pl.pallas_call(
        finish_kernel,
        grid_spec=pltpu.PrefetchScalarGridSpec(
            num_scalar_prefetch=1,
            grid=(1,),
            in_specs=[same, same, second, only]
            + [
                pl.BlockSpec((window, tokens, width), lambda i, h: (0, h[1] * 2 + step, 0)),
                pl.BlockSpec((tokens, 128), lambda i, h: (h[1] * 2 + step, 0)),
                pl.BlockSpec((window, width), lambda i, h: (0, 0)),
            ],
            out_specs=pl.BlockSpec((tokens * window, width), lambda i, h: (0, 0)),
        ),
        out_shape=shape((tokens * window, width), BF),
        compiler_params=params(12),
        cost_estimate=FREE,
        name="finish",
    )(here, own, got, early, late, xw, stat, gain)


def place_kernel(here_ref, pos_ref, came_ref, stream_ref, out_ref):
    rows, width = stream_ref.shape
    cut = width // 2
    slots = pos_ref.shape[0]
    put = eq_hot((slots, rows), 1, pos_ref[...])
    for relative in range(2):
        start = pl.multiple_of((here_ref[2] ^ relative) * cut, cut)
        at = pl.ds(start, cut)
        out_ref[:, at] = (
            stream_ref[:, at].astype(F32)
            + lax.dot_general(
                put,
                came_ref[:, relative].reshape(slots, cut),
                (((0,), (0,)), ((), ())),
                preferred_element_type=F32,
            )
        ).astype(BF)


def place(here, pos, came, stream):
    rows, width = stream.shape
    return pl.pallas_call(
        place_kernel,
        in_specs=[scalars()] + [whole()] * 3,
        out_specs=whole(),
        out_shape=shape((rows, width), BF),
        compiler_params=params(12),
        cost_estimate=FREE,
        name="place",
    )(here, pos, came, stream)


def lay_kernel(here_ref, *refs):
    blocks, (out_ref, sems) = refs[:-2], refs[-2:]
    rows = blocks[0].shape[0]
    copies = []
    for index, ref in enumerate(blocks):
        quarter, step = index // 2, index % 2
        owner = 2 * (here_ref[0] ^ (quarter // 2)) + (here_ref[1] ^ (quarter % 2))
        start = pl.multiple_of((2 * owner + step) * rows, rows)
        copies.append(pltpu.make_async_copy(ref, out_ref.at[pl.ds(start, rows)], sems.at[index]))
    for copy in copies:
        copy.start()
    for copy in copies:
        copy.wait()


def lay(here, blocks):
    rows, width = blocks[0].shape
    return pl.pallas_call(
        lay_kernel,
        in_specs=[scalars()] + [whole()] * len(blocks),
        out_specs=anywhere(),
        out_shape=shape((len(blocks) * rows, width), BF),
        scratch_shapes=[pltpu.SemaphoreType.DMA((len(blocks),))],
        compiler_params=params(4),
        cost_estimate=FREE,
        name="lay",
    )(here, *blocks)


def shards(features, ln_gain, ln_bias, projection, stream, norm_gain, cotangent, slots):
    n_img = lax.axis_size("img")
    n_ctx = lax.axis_size("ctx")
    n_tp = lax.axis_size("tp")
    merged = slots.shape[0]
    tok_rows, width = stream.shape
    owners = n_img * n_ctx
    capacity = 2 * merged // owners
    slot_count = owners * capacity
    full_width = width * n_tp
    cut = width // n_img

    img = lax.axis_index("img").astype(jnp.int32)
    tp = lax.axis_index("tp").astype(jnp.int32)
    core, far_half = tp % 2, tp // 2
    z, y = lax.axis_index("ctx") // RING, lax.axis_index("ctx") % RING
    here = jnp.stack([core, far_half, img, z, y]).astype(jnp.int32)

    flip = [(i, 1 - i) for i in range(n_img)]
    core_pairs = [(t, t ^ 1) for t in range(n_tp)]
    far_pairs = [(t, t ^ 2) for t in range(n_tp)]

    def along_x(array, by):
        pairs = []
        for i in range(n_img):
            for t in range(n_tp):
                x = (2 * (t // 2) + i + by) % RING
                pairs.append((i * n_tp + t, (x % 2) * n_tp + 2 * (x // 2) + t % 2))
        return lax.ppermute(array, ("img", "tp"), pairs)

    def along_ctx(array, axis, by):
        pairs = []
        for c in range(n_ctx):
            for t in range(n_tp):
                z, y = c // RING, c % RING
                if t % 2 == axis:
                    y = (y + by) % RING
                else:
                    z = (z + by) % RING
                pairs.append((c * n_tp + t, (z * RING + y) * n_tp + t))
        return lax.ppermute(array, ("ctx", "tp"), pairs)

    slots = jnp.roll(slots, -core * (merged // 2))
    target = slots // tok_rows
    ids = jnp.arange(merged)
    earlier = (target[:, None] == target[None, :]) & (ids[:, None] < ids[None, :])
    rank = jnp.sum(earlier.astype(jnp.int32), axis=0)
    slot = target * capacity + rank
    local = slots - target * tok_rows
    packed = jnp.max(
        jnp.where(jnp.arange(slot_count)[:, None] == slot[None, :], local[None, :], -1), axis=1
    )
    asked = lax.all_to_all(
        packed.reshape(owners, capacity), ("img", "ctx"), split_axis=0, concat_axis=0, tiled=True
    )
    columns = lax.dynamic_slice_in_dim(projection[0], img * cut, cut, axis=2).reshape(-1, cut)
    moves = (1, -1, 2)
    near_blocks = [along_ctx(columns, 0, by) for by in moves]
    paired = target * (n_img * capacity) + rank + img * capacity
    partner = lax.ppermute(paired, "img", flip)
    gain = ln_gain[0]
    lifted, xw, stat = layer_norm(here, features[0], gain, ln_bias[0])
    asked, lifted, stat, near_blocks, partner = lax.optimization_barrier(
        (asked, lifted, stat, near_blocks, partner)
    )
    paired = jnp.concatenate([paired, partner]).reshape(-1, 1)

    first = stack(here, [columns] + near_blocks)
    asked, first, lifted = lax.optimization_barrier((asked, first, lifted))

    asked = asked.reshape(n_img, n_ctx, capacity).transpose(1, 0, 2)
    asked = asked.reshape(slot_count, 1)
    held = collect(asked, stream, cotangent[0], first)
    came = lax.all_to_all(
        held.reshape(owners, n_img * capacity, width),
        ("img", "ctx"), split_axis=0, concat_axis=0, tiled=True,
    ).reshape(n_img * slot_count, width)

    stacks = [first] + [along_ctx(first, 1, by) for by in moves[:2]]
    stacks.append(along_ctx(stacks[1], 1, 1))

    pairs = []
    for i in range(n_img):
        for t in range(n_tp):
            x = (2 * (t // 2) + i + (1 if t % 2 == 0 else -1)) % RING
            pairs.append((i * n_tp + t, (x % 2) * n_tp + 2 * (x // 2) + t % 2))
    lifted = [lifted, lax.ppermute(lifted, ("img", "tp"), pairs)]

    own_gain = lax.dynamic_slice_in_dim(norm_gain, img * cut, cut, axis=1)
    acc = multiply(here, stacks[:EARLY], lifted)
    base, cot = unpack(paired, came, acc)
    visual, state, sums = merge(here, own_gain, acc, base, cot, stacks[EARLY:], lifted)

    near, turned = add(sums, lax.ppermute(sums, "tp", core_pairs))
    stats = [near] + [along_x(near if by == 2 else turned, by) for by in (1, 2, 3)]
    stay, cross = pack(here, paired, visual, n_img * slot_count, near)
    cross, stats = lax.optimization_barrier((cross, stats))
    crossed = lax.ppermute(cross, "img", flip)

    own, rest, other, other_rest = backward(here, state, cot, own_gain, stats, stacks, full_width)
    own, rest, other, other_rest, crossed = lax.optimization_barrier(
        (own, rest, other, other_rest, crossed)
    )
    got_rest = lax.ppermute(other_rest, "tp", core_pairs)
    got = lax.ppermute(other, "tp", core_pairs)
    to_next, to_last = pair(rest, got_rest, crossed)
    from_last, from_next = along_x(to_next, 1), along_x(to_last, -1)
    to_next, to_last = relay(rest, got_rest, from_last, from_next)
    late_last, late_next = along_x(to_next, 1), along_x(to_last, -1)

    send = braid(stay, crossed, n_ctx)
    arrived = lax.all_to_all(send, "ctx", split_axis=0, concat_axis=0, tiled=True)
    new_stream = place(here, asked, arrived, stream)

    out = [
        finish(here, step, own, got, early, late, xw, stat, gain)
        for step, (early, late) in enumerate(((from_next, late_last), (from_last, late_next)))
    ]
    beyond = [lax.ppermute(x, "tp", far_pairs) for x in out]
    beyond[1], new_stream = lax.optimization_barrier((beyond[1], new_stream))
    from_core = [lax.ppermute(x, "tp", core_pairs) for x in out + beyond]
    grad = lay(here, out + beyond + from_core)
    return (new_stream, grad[None])


def solution(mesh):
    placed = (
        P(None, ("img", "ctx"), None),
        P(),
        P(),
        P(None, None, "ctx", "tp"),
        P(("img", "ctx"), "tp"),
        P(None, "tp"),
        P(None, ("img", "ctx"), "tp"),
        P(("img", "ctx")),
    )
    return jax.shard_map(
        shards,
        mesh=mesh,
        in_specs=placed,
        out_specs=(P(("img", "ctx"), "tp"), P(None, ("img", "ctx"), None)),
        check_vma=False,
    )
```
